32 devices in a mesh: seq: 8 (over y, x, core), head: 4 (over z).
Axes of the slice: x: 2, y: 2, z: 4, core: 2. Of those that a mesh axis runs over, the one named last changes fastest.
Arguments:
- fixed_point: bfloat16 [1024, 2048], P('seq'), may hold values from -7 to 7
- upstream: bfloat16 [1024, 2048], P('seq'), may hold values from -70 to 70
- norm_gain: float32 [2048], replicated, may hold values from 0.7 to 1.3
- query_weight: bfloat16 [2048, 1024], P(None, 'head'), may hold values from -0.35355339 to 0.35355339
- keyval_weight: bfloat16 [2048, 512], P(None, 'head'), may hold values from -0.143631065 to 0.143631065
- output_weight: bfloat16 [1024, 2048], P('head'), may hold values from -0.09375 to 0.09375
- log_norm: float32 [16, 1024], P('head', 'seq'), as said below
- attention_out: bfloat16 [1024, 1024], P('seq', 'head'), as said below
Outputs:
- adjoint: float32 [1024, 2048], P('seq')
The draws below stay inside these ranges and needn't reach their ends.
Inputs may be any that keep to these rules, and one draw needn't show every extreme that they name: log_norm[h, t] is the log of the sum over the keys that query t sees of exp(scores[h, t, j]), with scores computed from fixed_point, norm_gain, query_weight and keyval_weight as in the reference program. attention_out[t, h] is the sum over the keys that query t sees of exp(scores[h, t, j] - log_norm[h, t]) v_c(j), rounded to bfloat16.
All inputs are finite; a program needn't handle non-finite values.
Results may differ from the reference program's by a relative error of at most 0.012.
The reference program's roundings to bfloat16 on the way count: a program that leaves them out, or rounds other values in their place, can miss the bound.
Values may be sent and summed in bfloat16 or wider, within the bound.
No kernel may reach another device: no remote copies, remote signals or barrier semaphores. Data moves between devices by JAX's collectives and lax.ppermute only.
A program may use at most 64 MiB of HBM per device.

```python
import jax
import jax.numpy as jnp
from jax import lax

D = 2048
HEADS = 16
KV_HEADS = 4
HEAD_DIM = 64
TOK_DEV = 128
WIN_DEVS = 4
ITERS = 3
TOKENS = 1024


norm_eps = 1e-05


def layer_draw(key):
    subkeys = jax.random.split(jax.random.fold_in(key, 4099), 5)
    latent = jnp.clip(jax.random.normal(subkeys[0], (TOKENS, D), jnp.float32), -6.0, 6.0)
    gains = 1.0 + 0.15 * jax.random.uniform(subkeys[2], (D,), jnp.float32, -1.0, 1.0)
    query_weight = jnp.clip(jax.random.normal(subkeys[3], (D, HEADS * HEAD_DIM), jnp.float32), -6.0, 6.0) * (2.5 / D ** 0.5)
    keyval_weight = jnp.clip(jax.random.normal(subkeys[4], (D, KV_HEADS * 2 * HEAD_DIM), jnp.float32), -6.0, 6.0) / D ** 0.5
    return (latent.astype(jnp.bfloat16), gains, query_weight.astype(jnp.bfloat16), keyval_weight.astype(jnp.bfloat16))


def window_mask_drawn(block_id):
    key_pos = jnp.arange((WIN_DEVS + 1) * TOK_DEV).astype(jnp.int32)[None, :]
    query_pos = jnp.arange(TOK_DEV).astype(jnp.int32)[:, None]
    lowest = (WIN_DEVS - block_id) * TOK_DEV
    return (key_pos > query_pos) & (key_pos <= query_pos + WIN_DEVS * TOK_DEV) & (key_pos >= lowest)


def window_stats(key):
    latent, gains, query_weight, keyval_weight = layer_draw(key)
    group_size = HEADS // KV_HEADS
    block_total = TOKENS // TOK_DEV
    key_span = (WIN_DEVS + 1) * TOK_DEV
    latent_f = latent.astype(jnp.float32)
    normed = latent_f * lax.rsqrt(jnp.mean(latent_f * latent_f, axis=1, keepdims=True) + norm_eps)
    hidden = (normed * gains).astype(jnp.bfloat16)
    queries = jnp.dot(hidden, query_weight, preferred_element_type=jnp.float32).astype(jnp.bfloat16)
    keyval = jnp.dot(hidden, keyval_weight, preferred_element_type=jnp.float32).astype(jnp.bfloat16)
    padding = jnp.zeros((WIN_DEVS * TOK_DEV, KV_HEADS * 2 * HEAD_DIM), jnp.bfloat16)
    padded = jnp.concatenate([padding, keyval], axis=0)

    def one_block(block_id):
        first_row = block_id * TOK_DEV
        query_blk = lax.dynamic_slice_in_dim(queries, first_row, TOK_DEV, 0).astype(jnp.float32)
        query_blk = query_blk.reshape(TOK_DEV, KV_HEADS, group_size, HEAD_DIM)
        window = lax.dynamic_slice_in_dim(padded, first_row, key_span, 0).astype(jnp.float32)
        window = window.reshape(key_span, KV_HEADS, 2, HEAD_DIM)
        scores = jnp.einsum('rcge,pce->cgrp', query_blk, window[:, :, 0]) * HEAD_DIM ** (-0.5)
        allowed = window_mask_drawn(block_id)
        masked = jnp.where(allowed, scores, -1e+30)
        totals = jax.nn.logsumexp(masked, axis=-1)
        weights_blk = jnp.where(allowed, jnp.exp(scores - totals[..., None]), 0.0)
        outputs = jnp.einsum('cgrp,pce->rcge', weights_blk, window[:, :, 1]).reshape(TOK_DEV, HEADS * HEAD_DIM)
        return (totals.reshape(HEADS, TOK_DEV), outputs)
    totals, outputs = lax.map(one_block, jnp.arange(block_total).astype(jnp.int32))
    log_totals = jnp.transpose(totals, (1, 0, 2)).reshape(HEADS, TOKENS)
    return (log_totals, outputs.reshape(TOKENS, HEADS * HEAD_DIM))


def draw_fixed_point(key, part):
    return layer_draw(key)[0]


def draw_norm_gain(key, part):
    return layer_draw(key)[1]


def draw_query_weight(key, part):
    return layer_draw(key)[2]


def draw_keyval_weight(key, part):
    return layer_draw(key)[3]


def draw_log_norm(key, part):
    return window_stats(key)[0]


def draw_attention_out(key, part):
    return window_stats(key)[1].astype(jnp.bfloat16)


def draw_upstream(key, part):
    subkeys = jax.random.split(jax.random.fold_in(key, 9173), 4)
    position = jnp.arange(TOKENS).astype(jnp.float32)[:, None] / TOKENS
    rising = jnp.exp(jnp.log(3.0) * (position - 0.5))
    row_scale = jnp.exp(jax.random.uniform(subkeys[1], (TOKENS, 1), jnp.float32, -1.15, 1.15))
    column_scale = jnp.exp(jax.random.uniform(subkeys[2], (1, D), jnp.float32, -1.15, 1.15))
    noise_field = jnp.clip(jax.random.normal(subkeys[0], (TOKENS, D), jnp.float32), -4.0, 4.0)
    return (noise_field * rising * row_scale * column_scale).astype(jnp.bfloat16)


def block_levels(own_key, extent, shards, smallest, high):
    def one(dim, blocks):
        draws = jax.random.uniform(jax.random.fold_in(jax.random.fold_in(own_key, 6), dim), (blocks,), jnp.float32, smallest / len(shards), high / len(shards))
        return jnp.repeat(jnp.exp(draws), extent[dim] // blocks).reshape((-1,) + (1,) * (len(extent) - dim - 1))

    level = one(*shards[0])
    for cut in shards[1:]:
        level = level * one(*cut)
    return level


def gaussian(rng, extent, width, bound, pieces=(), dtype=jnp.bfloat16):
    factor_of = block_levels(rng, extent, pieces, -0.22, 0.18) if pieces else 1.0
    result = jax.random.normal(rng, extent, jnp.float32) * width * factor_of
    return jnp.minimum(jnp.maximum(result, -bound), bound).astype(dtype)


def setup_inputs(seed: int = 0) -> dict:
    streams_of = jax.random.split(jax.random.key(seed), 9)
    return {
        "fixed_point": draw_fixed_point(jax.random.fold_in(streams_of[8], 71), 0),
        "upstream": draw_upstream(jax.random.fold_in(streams_of[8], 71), 0),
        "norm_gain": draw_norm_gain(jax.random.fold_in(streams_of[8], 71), 0),
        "query_weight": draw_query_weight(jax.random.fold_in(streams_of[8], 71), 0),
        "keyval_weight": draw_keyval_weight(jax.random.fold_in(streams_of[8], 71), 0),
        "output_weight": gaussian(streams_of[5], (HEADS * HEAD_DIM, D), (4 * HEADS * HEAD_DIM) ** -0.5, 0.09375, ((0, 4),)),
        "log_norm": draw_log_norm(jax.random.fold_in(streams_of[8], 71), 0),
        "attention_out": draw_attention_out(jax.random.fold_in(streams_of[8], 71), 0),
    }


norm_eps = 1e-05
mix_eps = 1e-06

def window_mask(block_id):
    key_pos = jnp.arange((WIN_DEVS + 1) * TOK_DEV).astype(jnp.int32)[None, :]
    query_pos = jnp.arange(TOK_DEV).astype(jnp.int32)[:, None]
    lowest = (WIN_DEVS - block_id) * TOK_DEV
    return (key_pos > query_pos) & (key_pos <= query_pos + WIN_DEVS * TOK_DEV) & (key_pos >= lowest)

def reference(fixed_point, upstream, norm_gain, query_weight, keyval_weight, output_weight, log_norm, attention_out):
    group_size = HEADS // KV_HEADS
    block_total = TOKENS // TOK_DEV
    key_span = (WIN_DEVS + 1) * TOK_DEV
    score_scale = HEAD_DIM ** (-0.5)
    latent = fixed_point.astype(jnp.float32)
    inverse = lax.rsqrt(lax.optimization_barrier(jnp.mean(latent * latent, axis=1, keepdims=True)) + norm_eps)
    normed = latent * inverse
    hidden = (normed * norm_gain).astype(jnp.bfloat16)
    queries = jnp.dot(hidden, query_weight, preferred_element_type=jnp.float32).astype(jnp.bfloat16)
    keyval = jnp.dot(hidden, keyval_weight, preferred_element_type=jnp.float32).astype(jnp.bfloat16)
    padding = jnp.zeros((WIN_DEVS * TOK_DEV, KV_HEADS * 2 * HEAD_DIM), jnp.bfloat16)
    padded = jnp.concatenate([padding, keyval], axis=0)
    block_ids = jnp.arange(block_total).astype(jnp.int32)

    def apply_map(current):
        grad_out = jnp.dot(current.astype(jnp.bfloat16), output_weight.T, preferred_element_type=jnp.float32)
        grad_outb = grad_out.astype(jnp.bfloat16)
        row_terms = lax.optimization_barrier(jnp.sum((grad_out * attention_out.astype(jnp.float32)).reshape(TOKENS, HEADS, HEAD_DIM), axis=2))

        def one_block(block_id):
            first_row = block_id * TOK_DEV
            query_blk = lax.dynamic_slice_in_dim(queries, first_row, TOK_DEV, 0).astype(jnp.float32)
            query_blk = query_blk.reshape(TOK_DEV, KV_HEADS, group_size, HEAD_DIM)
            window = lax.dynamic_slice_in_dim(padded, first_row, key_span, 0).astype(jnp.float32)
            window = window.reshape(key_span, KV_HEADS, 2, HEAD_DIM)
            key_rows = window[:, :, 0]
            value_rows = window[:, :, 1]
            norms_blk = lax.dynamic_slice_in_dim(log_norm, first_row, TOK_DEV, 1).reshape(KV_HEADS, group_size, TOK_DEV)
            grad_blk = lax.dynamic_slice_in_dim(grad_outb, first_row, TOK_DEV, 0).astype(jnp.float32)
            grad_blk = grad_blk.reshape(TOK_DEV, KV_HEADS, group_size, HEAD_DIM)
            terms_blk = lax.dynamic_slice_in_dim(row_terms, first_row, TOK_DEV, 0).T.reshape(KV_HEADS, group_size, TOK_DEV)
            scores = jnp.einsum('rcge,pce->cgrp', query_blk, key_rows) * score_scale
            allowed = window_mask(block_id)
            weights_blk = jnp.where(allowed, jnp.exp(scores - norms_blk[..., None]), 0.0)
            weights_blk = lax.optimization_barrier(weights_blk.astype(jnp.bfloat16)).astype(jnp.float32)
            grad_prob = jnp.einsum('rcge,pce->cgrp', grad_blk, value_rows)
            grad_score = weights_blk * (grad_prob - terms_blk[..., None])
            grad_score = lax.optimization_barrier(grad_score.astype(jnp.bfloat16)).astype(jnp.float32)
            grad_query = jnp.einsum('cgrp,pce->rcge', grad_score, key_rows) * score_scale
            grad_query = grad_query.reshape(TOK_DEV, HEADS * HEAD_DIM).astype(jnp.bfloat16)
            grad_key = jnp.einsum('cgrp,rcge->pce', grad_score, query_blk) * score_scale
            grad_value = jnp.einsum('cgrp,rcge->pce', weights_blk, grad_blk)
            key_terms = jnp.stack([grad_key, grad_value], axis=2).reshape(key_span, KV_HEADS * 2 * HEAD_DIM)
            return (grad_query, key_terms)
        grad_query, key_terms = lax.map(one_block, block_ids)
        grad_query = grad_query.reshape(TOKENS, HEADS * HEAD_DIM)
        key_terms = key_terms.reshape(block_total, WIN_DEVS + 1, TOK_DEV, KV_HEADS * 2 * HEAD_DIM)
        collected = jnp.zeros((block_total + WIN_DEVS, TOK_DEV, KV_HEADS * 2 * HEAD_DIM), jnp.float32)
        for offset in range(WIN_DEVS + 1):
            collected = collected.at[offset:offset + block_total].add(key_terms[:, offset])
        grad_keyval = collected[WIN_DEVS:].reshape(TOKENS, KV_HEADS * 2 * HEAD_DIM).astype(jnp.bfloat16)
        grad_hidden = jnp.dot(grad_query, query_weight.T, preferred_element_type=jnp.float32)
        grad_hidden = grad_hidden + jnp.dot(grad_keyval, keyval_weight.T, preferred_element_type=jnp.float32)
        scaled = grad_hidden * norm_gain
        return inverse * (scaled - normed * lax.optimization_barrier(jnp.mean(scaled * normed, axis=1, keepdims=True)))
    cotangent = upstream.astype(jnp.float32)
    last_image = cotangent
    last_residual = cotangent
    current = cotangent
    for offset in range(ITERS):
        mapped = cotangent + apply_map(current)
        residual = mapped - current
        change = residual - last_residual
        mixing = jnp.mean(change * residual) / (jnp.mean(change * change) + mix_eps)
        current = mapped - mixing * (mapped - last_image)
        last_image = mapped
        last_residual = residual
    return current
```

```python
import jax
import jax.numpy as jnp
from jax import lax
from jax.sharding import PartitionSpec as P

WIN_DEVS = 4
norm_eps = 1e-05
mix_eps = 1e-06
F32 = jnp.float32
BF16 = jnp.bfloat16


def shifted(value, axis, steps):
    count = lax.axis_size(axis)
    initial, last = (max(0, -steps), min(count, count - steps))
    return lax.ppermute(value, axis, [(source, source + steps) for source in range(initial, last)])


def gathered(value, axis):
    count = lax.axis_size(axis)
    mine = lax.axis_index(axis)
    parts = [value]
    for step in range(1, count):
        parts.append(lax.ppermute(value, axis, [(i, (i - step) % count) for i in range(count)]))
    return jnp.roll(jnp.stack(parts), mine, axis=0)


def shards(
    fixed_point,
    upstream,
    norm_gain,
    query_weight,
    keyval_weight,
    output_weight,
    log_norm,
    attention_out,
):
    rows, width = fixed_point.shape
    head_width = keyval_weight.shape[1] // 2
    heads = log_norm.shape[0]
    seq_count = lax.axis_size("seq")
    head_count = lax.axis_size("head")
    block = lax.axis_index("seq")
    scale = head_width ** (-0.5)

    own_weight = jnp.concatenate([query_weight, keyval_weight], axis=1)
    share = width // seq_count
    piece = lax.dynamic_slice_in_dim(own_weight, block * share, share, 0)
    all_weight = lax.all_gather(piece, ("head", "seq"), tiled=True)
    cols = own_weight.shape[1]
    all_weight = all_weight.reshape(head_count, width, cols)

    latent = fixed_point.astype(F32)
    inverse = lax.rsqrt(jnp.mean(latent * latent, axis=1, keepdims=True) + norm_eps)
    normed = latent * inverse
    hidden = (normed * norm_gain).astype(BF16)
    keyval = jnp.dot(hidden, keyval_weight, preferred_element_type=F32).astype(BF16)
    earlier = [shifted(keyval, "seq", offset) for offset in range(WIN_DEVS, 0, -1)]
    queries = jnp.dot(hidden, query_weight, preferred_element_type=F32).astype(BF16)
    own_proj = jnp.concatenate([queries, keyval], axis=1)
    all_proj = lax.all_gather(own_proj, "head")

    window_keys = jnp.concatenate(earlier + [keyval], axis=0)
    key_rows = window_keys[:, :head_width]
    value_rows = window_keys[:, head_width:]
    query_heads = queries.reshape(rows, heads, head_width).transpose(1, 0, 2)
    key_pos = jnp.arange((WIN_DEVS + 1) * rows)[None, :]
    query_pos = jnp.arange(rows)[:, None]
    allowed = (key_pos > query_pos) & (key_pos <= query_pos + WIN_DEVS * rows)
    allowed = allowed & (key_pos >= (WIN_DEVS - block) * rows)
    saved_out = attention_out.astype(F32).reshape(rows, heads, head_width)

    scores = jnp.einsum("hre,pe->hrp", query_heads, key_rows, preferred_element_type=F32) * scale
    probs = jnp.where(allowed[None], jnp.exp(scores - log_norm[:, :, None]), 0.0).astype(BF16)

    scaled_out = output_weight.astype(F32) * norm_gain
    chain = jnp.einsum(
        "hdi,jd->hij", all_weight, scaled_out.astype(BF16), preferred_element_type=F32
    ).astype(BF16)
    chain = chain.reshape(head_count * cols, -1)
    normed_out = inverse * lax.dot_general(
        fixed_point, output_weight, (((1,), (1,)), ((), ())), preferred_element_type=F32
    )

    cotangent = upstream.astype(F32)
    entries = rows * seq_count * width

    def pull(grad_out):
        grad_outb = grad_out.astype(BF16).reshape(rows, heads, head_width).transpose(1, 0, 2)
        row_terms = jnp.sum(grad_out.reshape(rows, heads, head_width) * saved_out, axis=2).T
        grad_prob = jnp.einsum("hre,pe->hrp", grad_outb, value_rows, preferred_element_type=F32)
        grad_score = (probs.astype(F32) * (grad_prob - row_terms[:, :, None])).astype(BF16)
        grad_key = (
            jnp.einsum("hrp,hre->pe", grad_score, query_heads, preferred_element_type=F32) * scale
        )
        grad_value = jnp.einsum("hrp,hre->pe", probs, grad_outb, preferred_element_type=F32)
        key_terms = jnp.concatenate([grad_key, grad_value], axis=1)
        arrived = []
        for offset in range(1, WIN_DEVS + 1):
            first = (WIN_DEVS - offset) * rows
            arrived.append(shifted(key_terms[first : first + rows].astype(BF16), "seq", -offset))
        grad_query = (
            jnp.einsum("hrp,pe->rhe", grad_score, key_rows, preferred_element_type=F32) * scale
        )
        grad_query = grad_query.astype(BF16).reshape(rows, heads * head_width)
        collected = key_terms[WIN_DEVS * rows :]
        for part in arrived:
            collected = collected + part.astype(F32)
        own = jnp.concatenate([grad_query, collected.astype(BF16)], axis=1)
        every = gathered(own, "head")
        along = (
            jnp.sum(every.astype(F32) * all_proj.astype(F32), axis=(0, 2))[:, None] / width
        )
        return every, along

    def next_out(every, along):
        flat = every.transpose(1, 0, 2).reshape(rows, head_count * cols)
        through = jnp.dot(flat, chain, preferred_element_type=F32)
        return inverse * (through - along * normed_out)

    def field(every, along):
        grad_hidden = sum(
            lax.dot_general(
                every[i], all_weight[i], (((1,), (1,)), ((), ())), preferred_element_type=F32
            )
            for i in range(head_count)
        )
        return inverse * (grad_hidden * norm_gain - normed * along)

    def inner(a, b):
        return jnp.sum(a * b)

    grad_out = lax.dot_general(
        upstream, output_weight, (((1,), (1,)), ((), ())), preferred_element_type=F32
    )
    every1, along1 = pull(grad_out)
    every2, along2 = pull(next_out(every1, along1))
    first = field(every1, along1)
    every3, along3 = pull(next_out(every2, along2))
    second = field(every2, along2)
    third = field(every3, along3)

    start_change = first - cotangent
    change2 = second - first
    change3 = third - second
    totals = jnp.stack(
        [
            inner(start_change, first),
            inner(start_change, start_change),
            inner(change2, first),
            inner(change2, change2),
            inner(change2, second),
            inner(change2, change3),
            inner(change3, second),
            inner(change3, change3),
        ]
    )
    totals = lax.psum(totals, "seq") / entries
    s_r1, s_s, d2_v1, d2_d2, d2_v2, d2_d3, d3_v2, d3_d3 = [totals[i] for i in range(8)]
    mix1 = s_r1 / (s_s + mix_eps)
    keep1 = 1.0 - mix1
    mix2 = keep1 * (d2_v1 + keep1 * d2_d2) / (keep1 * keep1 * d2_d2 + mix_eps)
    keep2 = keep1 * (1.0 - mix2)
    cross = mix1 * (d2_v2 + keep2 * d2_d3) + keep2 * (d3_v2 + keep2 * d3_d3)
    square = mix1 * mix1 * d2_d2 + 2.0 * mix1 * keep2 * d2_d3 + keep2 * keep2 * d3_d3
    mix3 = cross / (square + mix_eps)
    return (
        cotangent + first + (1.0 - mix3 * mix1) * second + (keep2 * (1.0 - mix3)) * third
    )


def solution(mesh):
    in_specs = (
        P("seq", None),
        P("seq", None),
        P(),
        P(None, "head"),
        P(None, "head"),
        P("head", None),
        P("head", "seq"),
        P("seq", "head"),
    )
    out_specs = P("seq", None)
    return jax.shard_map(shards, mesh=mesh, in_specs=in_specs, out_specs=out_specs, check_vma=False)
```

```python
import jax
import jax.numpy as jnp
from jax import lax
from jax.sharding import PartitionSpec as P

WIN_DEVS = 4
norm_eps = 1e-05
mix_eps = 1e-06
F32 = jnp.float32
BF16 = jnp.bfloat16


def shifted(value, axis, steps):
    count = lax.axis_size(axis)
    initial, last = (max(0, -steps), min(count, count - steps))
    return lax.ppermute(value, axis, [(source, source + steps) for source in range(initial, last)])


def spread(value, axis):
    count = lax.axis_size(axis)
    copies = jnp.broadcast_to(value[None], (count,) + value.shape)
    return lax.all_to_all(copies, axis, 0, 0)


def shards(
    fixed_point,
    upstream,
    norm_gain,
    query_weight,
    keyval_weight,
    output_weight,
    log_norm,
    attention_out,
):
    rows, width = fixed_point.shape
    head_width = keyval_weight.shape[1] // 2
    heads = log_norm.shape[0]
    seq_count = lax.axis_size("seq")
    head_count = lax.axis_size("head")
    block = lax.axis_index("seq")
    scale = head_width ** (-0.5)

    own_weight = jnp.concatenate([query_weight, keyval_weight], axis=1)
    share = width // seq_count
    piece = lax.dynamic_slice_in_dim(own_weight, block * share, share, 0)
    all_weight = lax.all_gather(piece, ("head", "seq"), tiled=True)
    cols = own_weight.shape[1]
    all_weight = all_weight.reshape(head_count, width, cols)

    latent = fixed_point.astype(F32)
    inverse = lax.rsqrt(jnp.mean(latent * latent, axis=1, keepdims=True) + norm_eps)
    normed = latent * inverse
    hidden = (normed * norm_gain).astype(BF16)
    keyval = jnp.dot(hidden, keyval_weight, preferred_element_type=F32).astype(BF16)
    all_keyval = spread(keyval, "seq")
    padded = jnp.pad(all_keyval, ((WIN_DEVS, 0), (0, 0), (0, 0)))
    window_keys = lax.dynamic_slice_in_dim(padded, block, WIN_DEVS + 1, 0)
    window_keys = window_keys.reshape((WIN_DEVS + 1) * rows, 2 * head_width)
    queries = jnp.dot(hidden, query_weight, preferred_element_type=F32).astype(BF16)
    own_proj = jnp.concatenate([queries, keyval], axis=1)
    all_proj = spread(own_proj, "head")

    key_rows = window_keys[:, :head_width]
    value_rows = window_keys[:, head_width:]
    query_heads = queries.reshape(rows, heads, head_width).transpose(1, 0, 2)
    key_pos = jnp.arange((WIN_DEVS + 1) * rows)[None, :]
    query_pos = jnp.arange(rows)[:, None]
    allowed = (key_pos > query_pos) & (key_pos <= query_pos + WIN_DEVS * rows)
    allowed = allowed & (key_pos >= (WIN_DEVS - block) * rows)
    saved_out = attention_out.astype(F32).reshape(rows, heads, head_width)

    scores = jnp.einsum("hre,pe->hrp", query_heads, key_rows, preferred_element_type=F32) * scale
    probs = jnp.where(allowed[None], jnp.exp(scores - log_norm[:, :, None]), 0.0).astype(BF16)

    scaled_out = output_weight.astype(F32) * norm_gain
    chain = jnp.einsum(
        "hdi,jd->hij", all_weight, scaled_out.astype(BF16), preferred_element_type=F32
    ).astype(BF16)
    chain = chain.reshape(head_count * cols, -1)
    normed_out = inverse * lax.dot_general(
        fixed_point, output_weight, (((1,), (1,)), ((), ())), preferred_element_type=F32
    )

    cotangent = upstream.astype(F32)
    entries = rows * seq_count * width

    def pull(grad_out):
        grad_outb = grad_out.astype(BF16).reshape(rows, heads, head_width).transpose(1, 0, 2)
        row_terms = jnp.sum(grad_out.reshape(rows, heads, head_width) * saved_out, axis=2).T
        grad_prob = jnp.einsum("hre,pe->hrp", grad_outb, value_rows, preferred_element_type=F32)
        grad_score = (probs.astype(F32) * (grad_prob - row_terms[:, :, None])).astype(BF16)
        grad_key = (
            jnp.einsum("hrp,hre->pe", grad_score, query_heads, preferred_element_type=F32) * scale
        )
        grad_value = jnp.einsum("hrp,hre->pe", probs, grad_outb, preferred_element_type=F32)
        key_terms = jnp.concatenate([grad_key, grad_value], axis=1)
        terms = key_terms[: WIN_DEVS * rows].astype(BF16).reshape(WIN_DEVS, rows, 2 * head_width)
        slots = jnp.concatenate([terms, jnp.zeros((seq_count,) + terms.shape[1:], BF16)])
        slots = lax.dynamic_slice_in_dim(jnp.roll(slots, block, axis=0), WIN_DEVS, seq_count, 0)
        arrived = lax.all_to_all(slots, "seq", 0, 0)
        grad_query = (
            jnp.einsum("hrp,pe->rhe", grad_score, key_rows, preferred_element_type=F32) * scale
        )
        grad_query = grad_query.astype(BF16).reshape(rows, heads * head_width)
        collected = key_terms[WIN_DEVS * rows :]
        collected = collected + jnp.sum(arrived.astype(F32), axis=0)
        own = jnp.concatenate([grad_query, collected.astype(BF16)], axis=1)
        every = spread(own, "head")
        along = (
            jnp.sum(every.astype(F32) * all_proj.astype(F32), axis=(0, 2))[:, None] / width
        )
        return every, along

    def next_out(every, along):
        flat = every.transpose(1, 0, 2).reshape(rows, head_count * cols)
        through = jnp.dot(flat, chain, preferred_element_type=F32)
        return inverse * (through - along * normed_out)

    def field(every, along):
        grad_hidden = sum(
            lax.dot_general(
                every[i], all_weight[i], (((1,), (1,)), ((), ())), preferred_element_type=F32
            )
            for i in range(head_count)
        )
        return inverse * (grad_hidden * norm_gain - normed * along)

    grad_out = lax.dot_general(
        upstream, output_weight, (((1,), (1,)), ((), ())), preferred_element_type=F32
    )
    every1, along1 = pull(grad_out)
    every2, along2 = pull(next_out(every1, along1))
    first = field(every1, along1)
    every3, along3 = pull(next_out(every2, along2))
    second = field(every2, along2)
    third = field(every3, along3)

    start_change = first - cotangent
    change2 = second - first
    change3 = third - second
    pairs = [
        start_change * first,
        start_change * start_change,
        change2 * first,
        change2 * change2,
        change2 * second,
        change2 * change3,
        change3 * second,
        change3 * change3,
    ]
    totals = jnp.stack([jnp.sum(pair.reshape(-1, 128), axis=0) for pair in pairs])
    totals = jnp.sum(spread(totals, "seq"), axis=(0, 2)) / entries
    s_r1, s_s, d2_v1, d2_d2, d2_v2, d2_d3, d3_v2, d3_d3 = [totals[i] for i in range(8)]
    mix1 = s_r1 / (s_s + mix_eps)
    keep1 = 1.0 - mix1
    mix2 = keep1 * (d2_v1 + keep1 * d2_d2) / (keep1 * keep1 * d2_d2 + mix_eps)
    keep2 = keep1 * (1.0 - mix2)
    cross = mix1 * (d2_v2 + keep2 * d2_d3) + keep2 * (d3_v2 + keep2 * d3_d3)
    square = mix1 * mix1 * d2_d2 + 2.0 * mix1 * keep2 * d2_d3 + keep2 * keep2 * d3_d3
    mix3 = cross / (square + mix_eps)
    return (
        cotangent + first + (1.0 - mix3 * mix1) * second + (keep2 * (1.0 - mix3)) * third
    )


def solution(mesh):
    in_specs = (
        P("seq", None),
        P("seq", None),
        P(),
        P(None, "head"),
        P(None, "head"),
        P("head", None),
        P("head", "seq"),
        P("seq", "head"),
    )
    out_specs = P("seq", None)
    return jax.shard_map(shards, mesh=mesh, in_specs=in_specs, out_specs=out_specs, check_vma=False)
```

```python
import functools

import jax
import jax.numpy as jnp
from jax import lax
from jax.experimental import pallas as pl
from jax.experimental.pallas import tpu as pltpu
from jax.sharding import PartitionSpec as P

WIN_DEVS = 4
norm_eps = 1e-05
mix_eps = 1e-06
F32 = jnp.float32
BF16 = jnp.bfloat16
EXTRA = 16
NT = (((1,), (1,)), ((), ()))


def shape_of(shape, dtype):
    return jax.ShapeDtypeStruct(shape, dtype)


def local_call(body, outs, flops, moved, **more):
    return pl.pallas_call(
        body,
        out_shape=outs,
        compiler_params=pltpu.CompilerParams(vmem_limit_bytes=48 * 1024 * 1024),
        cost_estimate=pl.CostEstimate(flops=flops, bytes_accessed=moved, transcendentals=0),
        **more,
    )


def shifted(value, axis, steps):
    count = lax.axis_size(axis)
    initial, last = (max(0, -steps), min(count, count - steps))
    return lax.ppermute(value, axis, [(source, source + steps) for source in range(initial, last)])


def rotated(value, axis):
    count = lax.axis_size(axis)
    parts = [value]
    for step in range(1, count):
        parts.append(lax.ppermute(value, axis, [(i, (i - step) % count) for i in range(count)]))
    return parts


def doubled(value, axis, group):
    count = lax.axis_size(axis)
    mine = lax.axis_index(axis)
    parts = value[None]
    bits = []
    bit = group // 2
    while bit:
        other = lax.ppermute(parts, axis, [(i, i ^ bit) for i in range(count)])
        parts = jnp.concatenate([parts, other])
        bits.append(bit)
        bit //= 2
    shape = (2,) * len(bits) + value.shape
    parts = parts.reshape(shape)
    for place, bit in enumerate(reversed(bits)):
        swap = (mine & bit) != 0
        parts = jnp.where(swap, jnp.flip(parts, place), parts)
    parts = parts.transpose(tuple(range(len(bits)))[::-1] + tuple(range(len(bits), len(shape))))
    return parts.reshape((group,) + value.shape)


def norm_body(z_ref, gain_ref, kvw_ref, hidden_ref, kv_ref, kvf_ref, inv_ref):
    z = z_ref[...].astype(F32)
    inverse = lax.rsqrt(jnp.mean(z * z, axis=1, keepdims=True) + norm_eps)
    hidden = (z * inverse * gain_ref[...]).astype(BF16)
    hidden_ref[...] = hidden
    kvf = jnp.dot(hidden, kvw_ref[...], preferred_element_type=F32)
    kvf_ref[...] = kvf
    kv_ref[...] = kvf.astype(BF16)
    inv_ref[...] = jnp.broadcast_to(inverse, inv_ref.shape)


def lanes_of(value, heads):
    size = value.shape[0] // heads
    return jnp.concatenate([value[i * size : (i + 1) * size] for i in range(heads)], axis=1)


def start_body(heads, hidden_ref, qw_ref, up_ref, z_ref, ow_ref, inv_ref, ao_ref,
               qf_ref, qt_ref, go_ref, nt_ref, aot_ref):
    qf = jnp.dot(hidden_ref[...], qw_ref[...], preferred_element_type=F32)
    qf_ref[...] = qf
    qt_ref[...] = lanes_of(qf.T, heads).astype(BF16)
    out = lax.dot_general(up_ref[...], ow_ref[...], NT, preferred_element_type=F32)
    go_ref[...] = lanes_of(out.T, heads)
    base = lax.dot_general(z_ref[...], ow_ref[...], NT, preferred_element_type=F32)
    nt_ref[...] = lanes_of((base * inv_ref[:, :1]).T, heads)
    aot_ref[...] = lanes_of(ao_ref[...].astype(F32).T, heads)


def pull(heads, scale, go, aot, qt, kvw_ref, kt, probs, gq_ref, own_ref, term_refs):
    e = go.shape[0]
    rows = go.shape[1] // heads
    row_terms = jnp.sum(go * aot, axis=0, keepdims=True)
    gob = go.astype(BF16)
    grad_prob = jnp.dot(kvw_ref[:, e:], gob, preferred_element_type=F32)
    grad_score = (probs.astype(F32) * (grad_prob - row_terms)).astype(BF16)
    grad_key = lax.dot_general(grad_score, qt, NT, preferred_element_type=F32) * scale
    grad_value = lax.dot_general(probs, gob, NT, preferred_element_type=F32)
    terms = jnp.concatenate([grad_key, grad_value], axis=1)
    for offset in range(1, len(term_refs) + 1):
        first = (len(term_refs) - offset) * rows
        term_refs[offset - 1][...] = terms[first : first + rows].astype(BF16)
    own_ref[...] = terms[len(term_refs) * rows :]
    grad_query = jnp.dot(kt, grad_score, preferred_element_type=F32) * scale
    parts = [grad_query[:, i * rows : (i + 1) * rows] for i in range(heads)]
    gq_ref[...] = jnp.concatenate(parts, axis=0).T.astype(BF16)


def first_body(heads, scale, block_ref, *refs):
    windows = refs[: WIN_DEVS + 1]
    qt_ref, go_ref, aot_ref, ln_ref = refs[WIN_DEVS + 1 : WIN_DEVS + 5]
    kvw_ref, kt_ref, probs_ref, gq_ref, own_ref = refs[WIN_DEVS + 5 : WIN_DEVS + 10]
    term_refs = refs[WIN_DEVS + 10 :]
    rows = windows[0].shape[0]
    for place, ref in enumerate(windows):
        kvw_ref[place * rows : (place + 1) * rows, :] = ref[...]
    kvw = kvw_ref[...]
    e = kvw.shape[1] // 2
    kt_ref[...] = kvw.astype(F32).T[:e].astype(BF16)
    scores = jnp.dot(kvw[:, :e], qt_ref[...], preferred_element_type=F32) * scale
    norms = jnp.concatenate([ln_ref[i : i + 1, :] for i in range(heads)], axis=1)
    key_pos = lax.broadcasted_iota(jnp.int32, scores.shape, 0)
    query_pos = lax.broadcasted_iota(jnp.int32, scores.shape, 1) & (rows - 1)
    allowed = (key_pos > query_pos) & (key_pos <= query_pos + WIN_DEVS * rows)
    allowed = allowed & (key_pos >= (WIN_DEVS - block_ref[0]) * rows)
    probs = jnp.where(allowed, jnp.exp(scores - norms), 0.0).astype(BF16)
    probs_ref[...] = probs
    pull(heads, scale, go_ref[...], aot_ref[...], qt_ref[...], kvw_ref, kt_ref[...], probs,
         gq_ref, own_ref, term_refs)


def next_body(heads, parts, scale, *refs):
    gq_refs = refs[:parts]
    msg_refs = refs[parts : 2 * parts]
    chain_ref, inv_ref, nt_ref, qt_ref, aot_ref, kvw_ref, kt_ref, probs_ref = refs[
        2 * parts : 2 * parts + 8
    ]
    gq_ref, own_ref = refs[2 * parts + 8 : 2 * parts + 10]
    term_refs = refs[2 * parts + 10 :]
    rows, wide = gq_refs[0].shape
    narrow = msg_refs[0].shape[1]
    size = wide + narrow
    out = jnp.zeros((rows, wide), F32)
    along = jnp.zeros((EXTRA, rows), F32)
    for k in range(parts):
        chain = chain_ref[k * size : (k + 1) * size, :]
        out += jnp.dot(gq_refs[k][...], chain[:wide], preferred_element_type=F32)
        msg = msg_refs[k][...]
        out += jnp.dot(msg[:rows], chain[wide:], preferred_element_type=F32)
        along += msg[rows:].astype(F32)
    along = jnp.sum(along, axis=0, keepdims=True)
    along = jnp.concatenate([along] * heads, axis=1)
    go = lanes_of((out * inv_ref[:, :1]).T, heads)
    inv_row = jnp.concatenate([inv_ref[...].T[:1, :]] * heads, axis=1)
    go = go - inv_row * along * nt_ref[...]
    pull(heads, scale, go, aot_ref[...], qt_ref[...], kvw_ref, kt_ref[...], probs_ref[...],
         gq_ref, own_ref, term_refs)


def collect_body(width, own_ref, gq_ref, qf_ref, kvf_ref, *refs):
    msg_ref = refs[-1]
    rows = own_ref.shape[0]
    total = own_ref[...]
    for ref in refs[:-1]:
        total += ref[...].astype(F32)
    total = total.astype(BF16)
    msg_ref[:rows, :] = total
    prods = gq_ref[...].astype(F32) * qf_ref[...]
    partial = total.astype(F32) * kvf_ref[...]
    lanes = partial.shape[1]
    for first in range(0, prods.shape[1], lanes):
        partial += prods[:, first : first + lanes]
    along = jnp.sum(partial.T, axis=0, keepdims=True) * (1.0 / width)
    high = along.astype(BF16).astype(F32)
    place = lax.broadcasted_iota(jnp.int32, (EXTRA, rows), 0)
    extra = jnp.where(place == 0, high, jnp.where(place == 1, along - high, 0.0))
    msg_ref[rows:, :] = extra.astype(BF16)


def field_body(parts, steps, head_ref, *refs):
    count = parts * steps
    gq_refs = refs[:count]
    msg_refs = refs[count : 2 * count]
    w_ref, z_ref, up_ref, gain_ref, inv_ref = refs[2 * count : 2 * count + 5]
    v_ref, tot_ref, lhs_ref, along_ref = refs[2 * count + 5 :]
    rows, wide = gq_refs[0].shape
    cell = pl.program_id(0)

    @pl.when(cell == 0)
    def _():
        for step in range(steps):
            along = jnp.zeros((EXTRA, rows), F32)
            for k in range(parts):
                at = pl.ds(step * rows, rows)
                lhs_ref[k, at, :wide] = gq_refs[step * parts + k][...]
                msg = msg_refs[step * parts + k][...]
                lhs_ref[k, at, wide:] = msg[:rows]
                along += msg[rows:].astype(F32)
            along = jnp.broadcast_to(jnp.sum(along, axis=0, keepdims=True), (rows, rows))
            along_ref[step * rows : (step + 1) * rows, :] = along.T
        tot_ref[...] = jnp.zeros_like(tot_ref)

    head = head_ref[0]
    y = jnp.zeros((steps * rows, w_ref.shape[1]), F32)
    for k in range(parts):
        which = lax.rem(head + k, parts)
        y += lax.dot_general(lhs_ref[k], w_ref[which], NT, preferred_element_type=F32)
    inverse = inv_ref[:, :1]
    normed = z_ref[...].astype(F32) * inverse
    gain = gain_ref[...]
    fields = []
    for step in range(steps):
        at = slice(step * rows, (step + 1) * rows)
        field = inverse * (y[at] * gain - normed * along_ref[at, :1])
        v_ref[step] = field
        fields.append(field)
    first, second, third = fields
    change1 = first - up_ref[...].astype(F32)
    change2 = second - first
    change3 = third - second
    pairs = [
        (change1, first), (change1, change1), (change2, first), (change2, change2),
        (change2, second), (change2, change3), (change3, second), (change3, change3),
    ]
    sums = []
    for a, b in pairs:
        total = jnp.sum(a * b, axis=0, keepdims=True)
        lanes = tot_ref.shape[1]
        sums.append(sum(total[:, i : i + lanes] for i in range(0, total.shape[1], lanes)))
    tot_ref[...] += jnp.concatenate(sums, axis=0)


def mix_body(entries, tot_ref, up_ref, v_ref, out_ref):
    totals = jnp.sum(jnp.sum(tot_ref[...], axis=0), axis=1, keepdims=True) / entries
    s_r1, s_s, d2_v1, d2_d2, d2_v2, d2_d3, d3_v2, d3_d3 = [totals[i : i + 1] for i in range(8)]
    mix1 = s_r1 / (s_s + mix_eps)
    keep1 = 1.0 - mix1
    mix2 = keep1 * (d2_v1 + keep1 * d2_d2) / (keep1 * keep1 * d2_d2 + mix_eps)
    keep2 = keep1 * (1.0 - mix2)
    cross = mix1 * (d2_v2 + keep2 * d2_d3) + keep2 * (d3_v2 + keep2 * d3_d3)
    square = mix1 * mix1 * d2_d2 + 2.0 * mix1 * keep2 * d2_d3 + keep2 * keep2 * d3_d3
    mix3 = cross / (square + mix_eps)
    out_ref[...] = (
        up_ref[...].astype(F32)
        + v_ref[0]
        + (1.0 - mix3 * mix1) * v_ref[1]
        + keep2 * (1.0 - mix3) * v_ref[2]
    )


def shards(
    fixed_point,
    upstream,
    norm_gain,
    query_weight,
    keyval_weight,
    output_weight,
    log_norm,
    attention_out,
):
    rows, width = fixed_point.shape
    wide = query_weight.shape[1]
    narrow = keyval_weight.shape[1]
    size = wide + narrow
    e = narrow // 2
    heads = log_norm.shape[0]
    seq_count = lax.axis_size("seq")
    parts = lax.axis_size("head")
    block = lax.axis_index("seq")
    head = lax.axis_index("head")
    scale = e ** (-0.5)
    gain = norm_gain.reshape(1, width)
    span = (WIN_DEVS + 1) * rows
    group = min(8, seq_count)

    place = lax.rem(block, group)
    q_share, kv_share = wide // group, narrow // group

    def chosen(weight, share):
        total = weight.shape[1]
        pick = (
            jnp.arange(total)[None, :] == place * share + jnp.arange(share)[:, None]
        ).astype(BF16)
        return lax.dot_general(pick, weight, NT, preferred_element_type=F32).astype(BF16)

    own_cols = jnp.concatenate(
        [chosen(query_weight, q_share), chosen(keyval_weight, kv_share)], axis=0
    )
    every_cols = rotated(own_cols, "head")

    hidden, kv, kvf, inv = local_call(
        norm_body,
        [
            shape_of((rows, width), BF16),
            shape_of((rows, narrow), BF16),
            shape_of((rows, narrow), F32),
            shape_of((rows, rows), F32),
        ],
        2 * rows * width * narrow,
        2 * width * (2 * rows + narrow),
    )(fixed_point, gain, keyval_weight)
    earlier = [shifted(kv, "seq", offset) for offset in range(WIN_DEVS, 0, -1)]

    share = width // seq_count
    piece = jnp.concatenate(
        [
            lax.dynamic_slice_in_dim(query_weight, block * share, share, 0),
            lax.dynamic_slice_in_dim(keyval_weight, block * share, share, 0),
        ],
        axis=1,
    )
    all_weight = lax.all_gather(piece, ("head", "seq"), tiled=True)
    all_weight = all_weight.reshape(parts, width, size)

    qf, qt, go, nt, aot = local_call(
        functools.partial(start_body, heads),
        [
            shape_of((rows, wide), F32),
            shape_of((e, heads * rows), BF16),
            shape_of((e, heads * rows), F32),
            shape_of((e, heads * rows), F32),
            shape_of((e, heads * rows), F32),
        ],
        6 * rows * width * wide,
        4 * width * (2 * rows + wide),
    )(hidden, query_weight, upstream, fixed_point, output_weight, inv, attention_out)

    scaled_out = (output_weight.astype(F32) * gain).astype(BF16)
    chain_share = lax.dot_general(
        jnp.concatenate(every_cols, axis=0), scaled_out, NT, preferred_element_type=F32
    ).astype(BF16)
    chain = doubled(chain_share, "seq", group)
    chain = chain.reshape(group, parts, q_share + kv_share, wide).transpose(1, 0, 2, 3)
    chain = jnp.concatenate(
        [
            chain[:, :, :q_share].reshape(parts, wide, wide),
            chain[:, :, q_share:].reshape(parts, narrow, wide),
        ],
        axis=1,
    ).reshape(parts * size, wide)

    pull_outs = [shape_of((rows, wide), BF16), shape_of((rows, narrow), F32)]
    pull_outs += [shape_of((rows, narrow), BF16)] * WIN_DEVS
    pull_flops = 8 * span * e * heads * rows
    smem = pl.BlockSpec(memory_space=pltpu.SMEM)
    vmem = pl.BlockSpec(memory_space=pltpu.VMEM)

    def exchange(gq, own, terms):
        arrived = [shifted(term, "seq", -offset - 1) for offset, term in enumerate(terms)]
        every_gq = rotated(gq, "head")
        msg = local_call(
            functools.partial(collect_body, width),
            shape_of((rows + EXTRA, narrow), BF16),
            rows * size,
            rows * size * 4,
        )(own, gq, qf, kvf, *arrived)
        return every_gq, rotated(msg, "head")

    kvw, kt, probs, gq, own, *terms = local_call(
        functools.partial(first_body, heads, scale),
        [
            shape_of((span, narrow), BF16),
            shape_of((e, span), BF16),
            shape_of((span, heads * rows), BF16),
        ]
        + pull_outs,
        pull_flops * 5 // 4,
        span * heads * rows * 2,
        in_specs=[smem] + [vmem] * (WIN_DEVS + 5),
    )(block.reshape(1), *earlier, kv, qt, go, aot, log_norm)
    all_gq, all_msg = [], []
    for step in range(3):
        if step:
            gq, own, *terms = local_call(
                functools.partial(next_body, heads, parts, scale),
                pull_outs,
                pull_flops + 2 * rows * parts * size * wide,
                span * heads * rows * 2 + parts * size * wide * 2,
            )(*all_gq[-1], *all_msg[-1], chain, inv, nt, qt, aot, kvw, kt, probs)
        every_gq, every_msg = exchange(gq, own, terms)
        all_gq.append(every_gq)
        all_msg.append(every_msg)

    cell = 256 if width % 256 == 0 else width
    held = lambda shape: pl.BlockSpec(shape, lambda i: (0,) * len(shape))
    fields, totals = pl.pallas_call(
        functools.partial(field_body, parts, 3),
        grid=(width // cell,),
        in_specs=[smem]
        + [held((rows, wide))] * (3 * parts)
        + [held((rows + EXTRA, narrow))] * (3 * parts)
        + [
            pl.BlockSpec((parts, cell, size), lambda i: (0, i, 0)),
            pl.BlockSpec((rows, cell), lambda i: (0, i)),
            pl.BlockSpec((rows, cell), lambda i: (0, i)),
            pl.BlockSpec((1, cell), lambda i: (0, i)),
            held((rows, rows)),
        ],
        out_specs=[
            pl.BlockSpec((3, rows, cell), lambda i: (0, 0, i)),
            held((8, 128)),
        ],
        out_shape=[shape_of((3, rows, width), F32), shape_of((8, 128), F32)],
        scratch_shapes=[
            pltpu.VMEM((parts, 3 * rows, size), BF16),
            pltpu.VMEM((3 * rows, rows), F32),
        ],
        compiler_params=pltpu.CompilerParams(vmem_limit_bytes=48 * 1024 * 1024),
        cost_estimate=pl.CostEstimate(
            flops=6 * rows * parts * size * width,
            bytes_accessed=2 * parts * size * width,
            transcendentals=0,
        ),
    )(
        head.reshape(1),
        *[part for one in all_gq for part in one],
        *[part for one in all_msg for part in one],
        all_weight,
        fixed_point,
        upstream,
        gain,
        inv,
    )
    copies = jnp.broadcast_to(totals[None], (seq_count,) + totals.shape)
    totals = lax.all_to_all(copies, "seq", 0, 0)
    return local_call(
        functools.partial(mix_body, rows * seq_count * width),
        shape_of((rows, width), F32),
        8 * rows * width,
        18 * rows * width,
    )(totals, upstream, fields)


def solution(mesh):
    in_specs = (
        P("seq", None),
        P("seq", None),
        P(),
        P(None, "head"),
        P(None, "head"),
        P("head", None),
        P("head", "seq"),
        P("seq", "head"),
    )
    out_specs = P("seq", None)
    return jax.shard_map(shards, mesh=mesh, in_specs=in_specs, out_specs=out_specs, check_vma=False)
```

```python
import functools

import jax
import jax.numpy as jnp
from jax import lax
from jax.experimental import pallas as pl
from jax.experimental.pallas import tpu as pltpu
from jax.sharding import PartitionSpec as P

WIN_DEVS = 4
norm_eps = 1e-05
mix_eps = 1e-06
F32 = jnp.float32
BF16 = jnp.bfloat16
COLLECT = 50000
EXTRA = 16
NT = (((1,), (1,)), ((), ()))


def shape_of(shape, dtype):
    return jax.ShapeDtypeStruct(shape, dtype)


def local_call(body, outs, flops, moved, **more):
    return pl.pallas_call(
        body,
        out_shape=outs,
        compiler_params=pltpu.CompilerParams(vmem_limit_bytes=48 * 1024 * 1024),
        cost_estimate=pl.CostEstimate(flops=flops, bytes_accessed=moved, transcendentals=0),
        **more,
    )


def shifted(value, axis, steps):
    count = lax.axis_size(axis)
    initial, last = (max(0, -steps), min(count, count - steps))
    return lax.ppermute(value, axis, [(source, source + steps) for source in range(initial, last)])


def rotated(value, axis):
    count = lax.axis_size(axis)
    parts = [value]
    for step in range(1, count):
        parts.append(lax.ppermute(value, axis, [(i, (i - step) % count) for i in range(count)]))
    return parts


def shared(value, axis, group):
    count = lax.axis_size(axis)
    mine = lax.axis_index(axis)
    half = group // 2
    parts = [value]
    for offset in range(2, group, 2):
        parts.append(lax.ppermute(value, axis, [(i, i ^ offset) for i in range(count)]))
    even = jnp.stack(parts)
    odd = lax.ppermute(even, axis, [(i, i ^ 1) for i in range(count)])
    both = jnp.stack([even, odd], axis=1)
    bits = group.bit_length() - 1
    both = both.reshape((2,) * bits + value.shape)
    for place in range(bits):
        swap = (mine & (half >> place)) != 0
        both = jnp.where(swap, jnp.flip(both, place), both)
    return both.reshape((group,) + value.shape)


def spread(value, axis):
    count = lax.axis_size(axis)
    copies = jnp.broadcast_to(value[None], (count,) + value.shape)
    return lax.all_to_all(copies, axis, 0, 0)


def prep_body(share, block_ref, z_ref, gain_ref, qw_ref, kvw_ref,
              hidden_ref, kv_ref, kvf_ref, inv_ref, cols_ref, *piece_refs):
    z = z_ref[...].astype(F32)
    inverse = lax.rsqrt(jnp.mean(z * z, axis=1, keepdims=True) + norm_eps)
    hidden = (z * inverse * gain_ref[...]).astype(BF16)
    hidden_ref[...] = hidden
    kvf = jnp.dot(hidden, kvw_ref[...], preferred_element_type=F32)
    kvf_ref[...] = kvf
    kv_ref[...] = kvf.astype(BF16)
    inv_ref[...] = jnp.broadcast_to(inverse, inv_ref.shape)
    wide = qw_ref.shape[1]
    first = 0
    for ref in (qw_ref, kvw_ref):
        total = ref.shape[1]
        take = total * cols_ref.shape[0] // (wide + kvw_ref.shape[1])
        group = total // take
        at = lax.rem(block_ref[0], group) * take
        row = lax.broadcasted_iota(jnp.int32, (take, total), 0) + at
        pick = (row == lax.broadcasted_iota(jnp.int32, (take, total), 1)).astype(BF16)
        cols = lax.dot_general(pick, ref[...], NT, preferred_element_type=F32)
        cols_ref[first : first + take, :] = cols.astype(BF16)
        first += take
    for ref in piece_refs:
        rows = pl.ds(pl.multiple_of(block_ref[0] * share, share), share)
        ref[:, :wide] = qw_ref[rows, :]
        ref[:, wide:] = kvw_ref[rows, :]


def lanes_of(value, heads):
    size = value.shape[0] // heads
    return jnp.concatenate([value[i * size : (i + 1) * size] for i in range(heads)], axis=1)


def start_body(heads, hidden_ref, qw_ref, up_ref, z_ref, ow_ref, inv_ref, ao_ref,
               qf_ref, qt_ref, go_ref, nt_ref, aot_ref):
    qf = jnp.dot(hidden_ref[...], qw_ref[...], preferred_element_type=F32)
    qf_ref[...] = qf
    qt_ref[...] = lanes_of(qf.T, heads).astype(BF16)
    out = lax.dot_general(up_ref[...], ow_ref[...], NT, preferred_element_type=F32)
    go_ref[...] = lanes_of(out.T, heads)
    base = lax.dot_general(z_ref[...], ow_ref[...], NT, preferred_element_type=F32)
    nt_ref[...] = lanes_of((base * inv_ref[:, :1]).T, heads)
    aot_ref[...] = lanes_of(ao_ref[...].astype(F32).T, heads)


def pull(heads, scale, go, aot, qt, kvw_ref, probs, score_ref, own_ref, term_refs):
    e = go.shape[0]
    rows = go.shape[1] // heads
    row_terms = jnp.sum(go * aot, axis=0, keepdims=True)
    gob = go.astype(BF16)
    grad_prob = jnp.dot(kvw_ref[:, e:], gob, preferred_element_type=F32)
    grad_score = (probs.astype(F32) * (grad_prob - row_terms)).astype(BF16)
    score_ref[...] = grad_score
    grad_key = lax.dot_general(grad_score, qt, NT, preferred_element_type=F32) * scale
    grad_value = lax.dot_general(probs, gob, NT, preferred_element_type=F32)
    terms = jnp.concatenate([grad_key, grad_value], axis=1)
    for offset in range(1, len(term_refs) + 1):
        first = (len(term_refs) - offset) * rows
        term_refs[offset - 1][...] = terms[first : first + rows].astype(BF16)
    own_ref[...] = terms[len(term_refs) * rows :]


def query_body(heads, scale, kt_ref, score_ref, gq_ref):
    rows = gq_ref.shape[0]
    grad_query = jnp.dot(kt_ref[...], score_ref[...], preferred_element_type=F32) * scale
    parts = [grad_query[:, i * rows : (i + 1) * rows] for i in range(heads)]
    gq_ref[...] = jnp.concatenate(parts, axis=0).T.astype(BF16)


def first_body(heads, scale, block_ref, *refs):
    windows = refs[: WIN_DEVS + 1]
    qt_ref, go_ref, aot_ref, ln_ref = refs[WIN_DEVS + 1 : WIN_DEVS + 5]
    kvw_ref, kt_ref, probs_ref, score_ref, own_ref = refs[WIN_DEVS + 5 : WIN_DEVS + 10]
    term_refs = refs[WIN_DEVS + 10 :]
    rows = windows[0].shape[0]
    for place, ref in enumerate(windows):
        kvw_ref[place * rows : (place + 1) * rows, :] = ref[...]
    kvw = kvw_ref[...]
    e = kvw.shape[1] // 2
    kt_ref[...] = kvw.astype(F32).T[:e].astype(BF16)
    scores = jnp.dot(kvw[:, :e], qt_ref[...], preferred_element_type=F32) * scale
    norms = jnp.concatenate([ln_ref[i : i + 1, :] for i in range(heads)], axis=1)
    key_pos = lax.broadcasted_iota(jnp.int32, scores.shape, 0)
    query_pos = lax.broadcasted_iota(jnp.int32, scores.shape, 1) & (rows - 1)
    allowed = (key_pos > query_pos) & (key_pos <= query_pos + WIN_DEVS * rows)
    allowed = allowed & (key_pos >= (WIN_DEVS - block_ref[0]) * rows)
    probs = jnp.where(allowed, jnp.exp(scores - norms), 0.0).astype(BF16)
    probs_ref[...] = probs
    pull(heads, scale, go_ref[...], aot_ref[...], qt_ref[...], kvw_ref, probs,
         score_ref, own_ref, term_refs)


def next_body(heads, parts, scale, head_ref, *refs):
    gq_refs = refs[:parts]
    msg_refs = refs[parts : 2 * parts]
    chain_ref, inv_ref, nt_ref, qt_ref, aot_ref, kvw_ref, probs_ref = refs[
        2 * parts : 2 * parts + 7
    ]
    score_ref, own_ref = refs[2 * parts + 7 : 2 * parts + 9]
    term_refs = refs[2 * parts + 9 :]
    rows, wide = gq_refs[0].shape
    narrow = msg_refs[0].shape[1]
    out = jnp.zeros((rows, wide), F32)
    along = jnp.zeros((EXTRA, rows), F32)
    for k in range(parts):
        chain = chain_ref[lax.rem(head_ref[0] + k, parts)]
        out += jnp.dot(gq_refs[k][...], chain[:wide], preferred_element_type=F32)
        msg = msg_refs[k][...]
        out += jnp.dot(msg[:rows], chain[wide:], preferred_element_type=F32)
        along += msg[rows:].astype(F32)
    along = jnp.sum(along, axis=0, keepdims=True)
    along = jnp.concatenate([along] * heads, axis=1)
    go = lanes_of((out * inv_ref[:, :1]).T, heads)
    inv_row = jnp.concatenate([inv_ref[...].T[:1, :]] * heads, axis=1)
    go = go - inv_row * along * nt_ref[...]
    pull(heads, scale, go, aot_ref[...], qt_ref[...], kvw_ref, probs_ref[...],
         score_ref, own_ref, term_refs)


def collect_body(width, own_ref, gq_ref, qf_ref, kvf_ref, *refs):
    msg_ref = refs[-1]
    rows = own_ref.shape[0]
    total = own_ref[...]
    for ref in refs[:-1]:
        total += ref[...].astype(F32)
    total = total.astype(BF16)
    msg_ref[:rows, :] = total
    prods = gq_ref[...].astype(F32) * qf_ref[...]
    partial = total.astype(F32) * kvf_ref[...]
    lanes = partial.shape[1]
    for first in range(0, prods.shape[1], lanes):
        partial += prods[:, first : first + lanes]
    along = jnp.sum(partial.T, axis=0, keepdims=True) * (1.0 / width)
    high = along.astype(BF16).astype(F32)
    place = lax.broadcasted_iota(jnp.int32, (EXTRA, rows), 0)
    extra = jnp.where(place == 0, high, jnp.where(place == 1, along - high, 0.0))
    msg_ref[rows:, :] = extra.astype(BF16)


def field_body(parts, steps, head_ref, *refs):
    count = parts * steps
    gq_refs = refs[:count]
    msg_refs = refs[count : 2 * count]
    w_ref, z_ref, up_ref, gain_ref, inv_ref = refs[2 * count : 2 * count + 5]
    v_ref, tot_ref, lhs_ref, along_ref = refs[2 * count + 5 :]
    rows, wide = gq_refs[0].shape
    cell = pl.program_id(0)

    @pl.when(cell == 0)
    def _():
        for step in range(steps):
            along = jnp.zeros((EXTRA, rows), F32)
            for k in range(parts):
                at = slice(step * rows, (step + 1) * rows)
                size = wide + msg_refs[0].shape[1]
                lhs_ref[at, k * size : k * size + wide] = gq_refs[step * parts + k][...]
                msg = msg_refs[step * parts + k][...]
                lhs_ref[at, k * size + wide : (k + 1) * size] = msg[:rows]
                along += msg[rows:].astype(F32)
            along = jnp.broadcast_to(jnp.sum(along, axis=0, keepdims=True), (rows, rows))
            along_ref[step * rows : (step + 1) * rows, :] = along.T
        tot_ref[...] = jnp.zeros_like(tot_ref)

    head = head_ref[0]
    weight = jnp.concatenate([w_ref[lax.rem(head + k, parts)] for k in range(parts)], axis=1)
    y = lax.dot_general(lhs_ref[...], weight, NT, preferred_element_type=F32)
    inverse = inv_ref[:, :1]
    normed = z_ref[...].astype(F32) * inverse
    gain = gain_ref[...]
    fields = []
    for step in range(steps):
        at = slice(step * rows, (step + 1) * rows)
        field = inverse * (y[at] * gain - normed * along_ref[at, :1])
        v_ref[step] = field
        fields.append(field)
    first, second, third = fields
    change1 = first - up_ref[...].astype(F32)
    change2 = second - first
    change3 = third - second
    pairs = [
        (change1, first), (change1, change1), (change2, first), (change2, change2),
        (change2, second), (change2, change3), (change3, second), (change3, change3),
    ]
    sums = []
    for a, b in pairs:
        total = jnp.sum(a * b, axis=0, keepdims=True)
        lanes = tot_ref.shape[1]
        sums.append(sum(total[:, i : i + lanes] for i in range(0, total.shape[1], lanes)))
    tot_ref[...] += jnp.concatenate(sums, axis=0)


def mix_body(entries, tot_ref, up_ref, v_ref, out_ref):
    totals = jnp.sum(jnp.sum(tot_ref[...], axis=0), axis=1, keepdims=True) / entries
    s_r1, s_s, d2_v1, d2_d2, d2_v2, d2_d3, d3_v2, d3_d3 = [totals[i : i + 1] for i in range(8)]
    mix1 = s_r1 / (s_s + mix_eps)
    keep1 = 1.0 - mix1
    mix2 = keep1 * (d2_v1 + keep1 * d2_d2) / (keep1 * keep1 * d2_d2 + mix_eps)
    keep2 = keep1 * (1.0 - mix2)
    cross = mix1 * (d2_v2 + keep2 * d2_d3) + keep2 * (d3_v2 + keep2 * d3_d3)
    square = mix1 * mix1 * d2_d2 + 2.0 * mix1 * keep2 * d2_d3 + keep2 * keep2 * d3_d3
    mix3 = cross / (square + mix_eps)
    out_ref[...] = (
        up_ref[...].astype(F32)
        + v_ref[0]
        + (1.0 - mix3 * mix1) * v_ref[1]
        + keep2 * (1.0 - mix3) * v_ref[2]
    )


def shards(
    fixed_point,
    upstream,
    norm_gain,
    query_weight,
    keyval_weight,
    output_weight,
    log_norm,
    attention_out,
):
    rows, width = fixed_point.shape
    wide = query_weight.shape[1]
    narrow = keyval_weight.shape[1]
    size = wide + narrow
    e = narrow // 2
    heads = log_norm.shape[0]
    seq_count = lax.axis_size("seq")
    parts = lax.axis_size("head")
    block = lax.axis_index("seq")
    head = lax.axis_index("head")
    scale = e ** (-0.5)
    gain = norm_gain.reshape(1, width)
    span = (WIN_DEVS + 1) * rows
    group = min(8, seq_count)

    cols = size // group
    share = width // seq_count
    in_kernel = share % 16 == 0
    smem = pl.BlockSpec(memory_space=pltpu.SMEM)
    vmem = pl.BlockSpec(memory_space=pltpu.VMEM)
    hidden, kv, kvf, inv, own_cols, *piece = local_call(
        functools.partial(prep_body, share),
        [
            shape_of((rows, width), BF16),
            shape_of((rows, narrow), BF16),
            shape_of((rows, narrow), F32),
            shape_of((rows, rows), F32),
            shape_of((cols, width), BF16),
        ]
        + [shape_of((share, size), BF16)] * in_kernel,
        2 * rows * width * narrow,
        2 * width * (2 * rows + size),
        in_specs=[smem] + [vmem] * 4,
    )(block.reshape(1), fixed_point, gain, query_weight, keyval_weight)
    if not in_kernel:
        piece = [
            jnp.concatenate(
                [
                    lax.dynamic_slice_in_dim(weight, block * share, share, 0)
                    for weight in (query_weight, keyval_weight)
                ],
                axis=1,
            )
        ]
    all_weight = lax.all_gather(piece[0], ("head", "seq"), tiled=True)
    all_weight = all_weight.reshape(parts, width, size)
    every_cols = spread(own_cols, "head")
    earlier = [shifted(kv, "seq", offset) for offset in range(WIN_DEVS, 0, -1)]

    qf, qt, go, nt, aot = local_call(
        functools.partial(start_body, heads),
        [
            shape_of((rows, wide), F32),
            shape_of((e, heads * rows), BF16),
            shape_of((e, heads * rows), F32),
            shape_of((e, heads * rows), F32),
            shape_of((e, heads * rows), F32),
        ],
        6 * rows * width * wide,
        4 * width * (2 * rows + wide),
    )(hidden, query_weight, upstream, fixed_point, output_weight, inv, attention_out)

    pull_outs = [shape_of((span, heads * rows), BF16), shape_of((rows, narrow), F32)]
    pull_outs += [shape_of((rows, narrow), BF16)] * WIN_DEVS
    pull_flops = 6 * span * e * heads * rows
    scaled_out = (output_weight.astype(F32) * gain).astype(BF16)

    def exchange(score, own, terms, late):
        arrived = [shifted(term, "seq", -offset - 1) for offset, term in enumerate(terms)]
        gq = local_call(
            functools.partial(query_body, heads, scale),
            shape_of((rows, wide), BF16),
            2 * span * e * heads * rows,
            span * heads * rows * 2,
        )(kt, score)
        if late is not None:
            late = lax.optimization_barrier((late, gq))[0]
        every_gq = rotated(gq, "head")
        msg = local_call(
            functools.partial(collect_body, width),
            shape_of((rows + EXTRA, narrow), BF16),
            COLLECT * rows * size,
            rows * size * 4,
        )(own, gq, qf, kvf, *arrived)
        return every_gq, rotated(msg, "head"), late

    kvw, kt, probs, score, own, *terms = local_call(
        functools.partial(first_body, heads, scale),
        [
            shape_of((span, narrow), BF16),
            shape_of((e, span), BF16),
            shape_of((span, heads * rows), BF16),
        ]
        + pull_outs,
        pull_flops * 5 // 4,
        span * heads * rows * 2,
        in_specs=[smem] + [vmem] * (WIN_DEVS + 5),
    )(block.reshape(1), *earlier, kv, qt, go, aot, log_norm)
    all_gq, all_msg = [], []
    for step in range(3):
        if step:
            score, own, *terms = local_call(
                functools.partial(next_body, heads, parts, scale),
                pull_outs,
                pull_flops + 2 * rows * parts * size * wide,
                span * heads * rows * 2 + parts * size * wide * 2,
                in_specs=[smem] + [vmem] * (2 * parts + 7),
            )(head.reshape(1), *all_gq[-1], *all_msg[-1], chain, inv, nt, qt, aot, kvw, probs)
        every_gq, every_msg, late = exchange(score, own, terms, None if step else every_cols)
        all_gq.append(every_gq)
        all_msg.append(every_msg)
        if step == 0:
            chain_share = lax.dot_general(
                late.reshape(parts * cols, width), scaled_out, NT, preferred_element_type=F32
            ).astype(BF16)
            if group == seq_count:
                chain = spread(chain_share, "seq")
            else:
                chain = shared(chain_share, "seq", group)
            chain = chain.reshape(group, parts, cols, wide).transpose(1, 0, 2, 3)
            cut = wide // group
            chain = jnp.concatenate(
                [
                    chain[:, :, :cut].reshape(parts, wide, wide),
                    chain[:, :, cut:].reshape(parts, narrow, wide),
                ],
                axis=1,
            )

    cell = 512 if width % 512 == 0 else width
    held = lambda shape: pl.BlockSpec(shape, lambda i: (0,) * len(shape))
    fields, totals = pl.pallas_call(
        functools.partial(field_body, parts, 3),
        grid=(width // cell,),
        in_specs=[smem]
        + [held((rows, wide))] * (3 * parts)
        + [held((rows + EXTRA, narrow))] * (3 * parts)
        + [
            pl.BlockSpec((parts, cell, size), lambda i: (0, i, 0)),
            pl.BlockSpec((rows, cell), lambda i: (0, i)),
            pl.BlockSpec((rows, cell), lambda i: (0, i)),
            pl.BlockSpec((1, cell), lambda i: (0, i)),
            held((rows, rows)),
        ],
        out_specs=[
            pl.BlockSpec((3, rows, cell), lambda i: (0, 0, i)),
            held((8, 128)),
        ],
        out_shape=[shape_of((3, rows, width), F32), shape_of((8, 128), F32)],
        scratch_shapes=[
            pltpu.VMEM((3 * rows, parts * size), BF16),
            pltpu.VMEM((3 * rows, rows), F32),
        ],
        compiler_params=pltpu.CompilerParams(vmem_limit_bytes=48 * 1024 * 1024),
        cost_estimate=pl.CostEstimate(
            flops=6 * rows * parts * size * width,
            bytes_accessed=2 * parts * size * width,
            transcendentals=0,
        ),
    )(
        head.reshape(1),
        *[part for one in all_gq for part in one],
        *[part for one in all_msg for part in one],
        all_weight,
        fixed_point,
        upstream,
        gain,
        inv,
    )
    totals = spread(totals, "seq")
    return local_call(
        functools.partial(mix_body, rows * seq_count * width),
        shape_of((rows, width), F32),
        8 * rows * width,
        18 * rows * width,
    )(totals, upstream, fields)


def solution(mesh):
    in_specs = (
        P("seq", None),
        P("seq", None),
        P(),
        P(None, "head"),
        P(None, "head"),
        P("head", None),
        P("head", "seq"),
        P("seq", "head"),
    )
    out_specs = P("seq", None)
    return jax.shard_map(shards, mesh=mesh, in_specs=in_specs, out_specs=out_specs, check_vma=False)
```

```python
import functools

import jax
import jax.numpy as jnp
from jax import lax
from jax.experimental import pallas as pl
from jax.experimental.pallas import tpu as pltpu
from jax.sharding import PartitionSpec as P

WIN_DEVS = 4
norm_eps = 1e-05
mix_eps = 1e-06
F32 = jnp.float32
BF16 = jnp.bfloat16
COLLECT = 50000
EXTRA = 16
NT = (((1,), (1,)), ((), ()))


def shape_of(shape, dtype):
    return jax.ShapeDtypeStruct(shape, dtype)


def local_call(body, outs, flops, moved, **more):
    return pl.pallas_call(
        body,
        out_shape=outs,
        compiler_params=pltpu.CompilerParams(vmem_limit_bytes=48 * 1024 * 1024),
        cost_estimate=pl.CostEstimate(flops=flops, bytes_accessed=moved, transcendentals=0),
        **more,
    )


def shifted(value, axis, steps):
    count = lax.axis_size(axis)
    initial, last = (max(0, -steps), min(count, count - steps))
    return lax.ppermute(value, axis, [(source, source + steps) for source in range(initial, last)])


def rotated(value, axis):
    count = lax.axis_size(axis)
    parts = [value]
    for step in range(1, count):
        parts.append(lax.ppermute(value, axis, [(i, (i - step) % count) for i in range(count)]))
    return parts


def shared(value, axis, group):
    count = lax.axis_size(axis)
    mine = lax.axis_index(axis)
    half = group // 2
    parts = [value]
    for offset in range(2, group, 2):
        parts.append(lax.ppermute(value, axis, [(i, i ^ offset) for i in range(count)]))
    even = jnp.stack(parts)
    odd = lax.ppermute(even, axis, [(i, i ^ 1) for i in range(count)])
    both = jnp.stack([even, odd], axis=1)
    bits = group.bit_length() - 1
    both = both.reshape((2,) * bits + value.shape)
    for place in range(bits):
        swap = (mine & (half >> place)) != 0
        both = jnp.where(swap, jnp.flip(both, place), both)
    return both.reshape((group,) + value.shape)


def spread(value, axis):
    count = lax.axis_size(axis)
    copies = jnp.broadcast_to(value[None], (count,) + value.shape)
    return lax.all_to_all(copies, axis, 0, 0)


def columns_body(block_ref, qw_ref, kvw_ref, out_ref, q_tile, kv_tile, sems):
    tile = q_tile.shape[1]
    wide, narrow = qw_ref.shape[1], kvw_ref.shape[1]
    group = (wide + narrow) // out_ref.shape[1]
    place = lax.rem(block_ref[0], group)
    q_take, kv_take = wide // group, narrow // group
    q_at = place * q_take
    q_first = pl.multiple_of(q_at // tile * tile, tile)
    copies = [
        pltpu.make_async_copy(qw_ref.at[:, pl.ds(q_first, tile)], q_tile, sems.at[0]),
        pltpu.make_async_copy(kvw_ref, kv_tile, sems.at[1]),
    ]
    for copy in copies:
        copy.start()
    first = 0
    for copy, ref, at, take in (
        (copies[0], q_tile, q_at - q_first, q_take),
        (copies[1], kv_tile, place * kv_take, kv_take),
    ):
        copy.wait()
        total = ref.shape[1]
        row = lax.broadcasted_iota(jnp.int32, (take, total), 0) + at
        pick = (row == lax.broadcasted_iota(jnp.int32, (take, total), 1)).astype(BF16)
        cols = lax.dot_general(pick, ref[...], NT, preferred_element_type=F32).astype(BF16)
        for k in range(out_ref.shape[0]):
            out_ref[k, first : first + take, :] = cols
        first += take


def norm_body(z_ref, gain_ref, kvw_ref, hidden_ref, kv_ref, kvf_ref, inv_ref):
    z = z_ref[...].astype(F32)
    inverse = lax.rsqrt(jnp.mean(z * z, axis=1, keepdims=True) + norm_eps)
    hidden = (z * inverse * gain_ref[...]).astype(BF16)
    hidden_ref[...] = hidden
    kvf = jnp.dot(hidden, kvw_ref[...], preferred_element_type=F32)
    kvf_ref[...] = kvf
    kv_ref[...] = kvf.astype(BF16)
    inv_ref[...] = jnp.broadcast_to(inverse, inv_ref.shape)


def chain_body(cols_ref, ow_ref, gain_ref, out_ref):
    scaled = (ow_ref[...].astype(F32) * gain_ref[...]).astype(BF16)
    share = lax.dot_general(cols_ref[...], scaled, NT, preferred_element_type=F32).astype(BF16)
    for k in range(out_ref.shape[0]):
        out_ref[k] = share


def whole_of(ref, head, wide):
    cut = wide // ref.shape[0]
    parts = [ref[s, head, :cut, :] for s in range(ref.shape[0])]
    parts += [ref[s, head, cut:, :] for s in range(ref.shape[0])]
    return jnp.concatenate(parts, axis=0)


def lanes_of(value, heads):
    size = value.shape[0] // heads
    return jnp.concatenate([value[i * size : (i + 1) * size] for i in range(heads)], axis=1)


def start_body(heads, hidden_ref, qw_ref, up_ref, z_ref, ow_ref, inv_ref, ao_ref,
               qf_ref, qt_ref, go_ref, nt_ref, aot_ref):
    qf = jnp.dot(hidden_ref[...], qw_ref[...], preferred_element_type=F32)
    qf_ref[...] = qf
    qt_ref[...] = lanes_of(qf.T, heads).astype(BF16)
    out = lax.dot_general(up_ref[...], ow_ref[...], NT, preferred_element_type=F32)
    go_ref[...] = lanes_of(out.T, heads)
    base = lax.dot_general(z_ref[...], ow_ref[...], NT, preferred_element_type=F32)
    nt_ref[...] = lanes_of((base * inv_ref[:, :1]).T, heads)
    aot_ref[...] = lanes_of(ao_ref[...].astype(F32).T, heads)


def pull(heads, scale, go, aot, qt, kvw_ref, probs, score_ref, own_ref, term_refs):
    e = go.shape[0]
    rows = go.shape[1] // heads
    row_terms = jnp.sum(go * aot, axis=0, keepdims=True)
    gob = go.astype(BF16)
    grad_prob = jnp.dot(kvw_ref[:, e:], gob, preferred_element_type=F32)
    grad_score = (probs.astype(F32) * (grad_prob - row_terms)).astype(BF16)
    score_ref[...] = grad_score
    grad_key = lax.dot_general(grad_score, qt, NT, preferred_element_type=F32) * scale
    grad_value = lax.dot_general(probs, gob, NT, preferred_element_type=F32)
    terms = jnp.concatenate([grad_key, grad_value], axis=1)
    for offset in range(1, len(term_refs) + 1):
        first = (len(term_refs) - offset) * rows
        term_refs[offset - 1][...] = terms[first : first + rows].astype(BF16)
    own_ref[...] = terms[len(term_refs) * rows :]


def query_body(heads, scale, kt_ref, score_ref, gq_ref):
    rows = gq_ref.shape[0]
    grad_query = jnp.dot(kt_ref[...], score_ref[...], preferred_element_type=F32) * scale
    parts = [grad_query[:, i * rows : (i + 1) * rows] for i in range(heads)]
    gq_ref[...] = jnp.concatenate(parts, axis=0).T.astype(BF16)


def first_body(heads, scale, block_ref, *refs):
    windows = refs[: WIN_DEVS + 1]
    qt_ref, go_ref, aot_ref, ln_ref = refs[WIN_DEVS + 1 : WIN_DEVS + 5]
    kvw_ref, kt_ref, probs_ref, score_ref, own_ref = refs[WIN_DEVS + 5 : WIN_DEVS + 10]
    term_refs = refs[WIN_DEVS + 10 :]
    rows = windows[0].shape[0]
    for place, ref in enumerate(windows):
        kvw_ref[place * rows : (place + 1) * rows, :] = ref[...]
    kvw = kvw_ref[...]
    e = kvw.shape[1] // 2
    kt_ref[...] = kvw.astype(F32).T[:e].astype(BF16)
    scores = jnp.dot(kvw[:, :e], qt_ref[...], preferred_element_type=F32) * scale
    norms = jnp.concatenate([ln_ref[i : i + 1, :] for i in range(heads)], axis=1)
    key_pos = lax.broadcasted_iota(jnp.int32, scores.shape, 0)
    query_pos = lax.broadcasted_iota(jnp.int32, scores.shape, 1) & (rows - 1)
    allowed = (key_pos > query_pos) & (key_pos <= query_pos + WIN_DEVS * rows)
    allowed = allowed & (key_pos >= (WIN_DEVS - block_ref[0]) * rows)
    probs = jnp.where(allowed, jnp.exp(scores - norms), 0.0).astype(BF16)
    probs_ref[...] = probs
    pull(heads, scale, go_ref[...], aot_ref[...], qt_ref[...], kvw_ref, probs,
         score_ref, own_ref, term_refs)


def next_body(heads, parts, scale, head_ref, *refs):
    gq_refs = refs[:parts]
    msg_refs = refs[parts : 2 * parts]
    chain_ref, inv_ref, nt_ref, qt_ref, aot_ref, kvw_ref, probs_ref = refs[
        2 * parts : 2 * parts + 7
    ]
    score_ref, own_ref = refs[2 * parts + 7 : 2 * parts + 9]
    term_refs = refs[2 * parts + 9 :]
    rows, wide = gq_refs[0].shape
    narrow = msg_refs[0].shape[1]
    out = jnp.zeros((rows, wide), F32)
    along = jnp.zeros((EXTRA, rows), F32)
    for k in range(parts):
        chain = whole_of(chain_ref, lax.rem(head_ref[0] + k, parts), wide)
        out += jnp.dot(gq_refs[k][...], chain[:wide], preferred_element_type=F32)
        msg = msg_refs[k][...]
        out += jnp.dot(msg[:rows], chain[wide:], preferred_element_type=F32)
        along += msg[rows:].astype(F32)
    along = jnp.sum(along, axis=0, keepdims=True)
    along = jnp.concatenate([along] * heads, axis=1)
    go = lanes_of((out * inv_ref[:, :1]).T, heads)
    inv_row = jnp.concatenate([inv_ref[...].T[:1, :]] * heads, axis=1)
    go = go - inv_row * along * nt_ref[...]
    pull(heads, scale, go, aot_ref[...], qt_ref[...], kvw_ref, probs_ref[...],
         score_ref, own_ref, term_refs)


def collect_body(width, own_ref, gq_ref, qf_ref, kvf_ref, *refs):
    msg_ref = refs[-1]
    rows = own_ref.shape[0]
    total = own_ref[...]
    for ref in refs[:-1]:
        total += ref[...].astype(F32)
    total = total.astype(BF16)
    msg_ref[:rows, :] = total
    prods = gq_ref[...].astype(F32) * qf_ref[...]
    partial = total.astype(F32) * kvf_ref[...]
    lanes = partial.shape[1]
    for first in range(0, prods.shape[1], lanes):
        partial += prods[:, first : first + lanes]
    along = jnp.sum(partial.T, axis=0, keepdims=True) * (1.0 / width)
    high = along.astype(BF16).astype(F32)
    place = lax.broadcasted_iota(jnp.int32, (EXTRA, rows), 0)
    extra = jnp.where(place == 0, high, jnp.where(place == 1, along - high, 0.0))
    msg_ref[rows:, :] = extra.astype(BF16)


def field_body(parts, steps, head_ref, *refs):
    count = parts * steps
    gq_refs = refs[:count]
    msg_refs = refs[count : 2 * count]
    w_ref, z_ref, up_ref, gain_ref, inv_ref, *past = refs[2 * count : -3]
    v_ref, sent_ref, tot_ref = refs[-3:]
    rows, wide = gq_refs[0].shape
    half = w_ref.shape[3]
    head = head_ref[0]
    first = pl.multiple_of(lax.rem(head, z_ref.shape[1] // half) * half, half)
    at = pl.ds(first, half)
    y = jnp.zeros((steps * rows, half), F32)
    for k in range(parts):
        weight = whole_of(w_ref, lax.rem(head + k, parts), wide)
        lhs = [
            jnp.concatenate(
                [gq_refs[step * parts + k][...], msg_refs[step * parts + k][:rows, :]], axis=1
            )
            for step in range(steps)
        ]
        lhs = lhs[0] if steps == 1 else jnp.concatenate(lhs, axis=0)
        y += jnp.dot(lhs, weight, preferred_element_type=F32)
    inverse = inv_ref[:, :1]
    normed = z_ref[:, at].astype(F32) * inverse
    gain = gain_ref[:, at]
    fields = []
    for step in range(steps):
        along = jnp.zeros((EXTRA, rows), F32)
        for k in range(parts):
            along += msg_refs[step * parts + k][rows:, :].astype(F32)
        along = jnp.broadcast_to(jnp.sum(along, axis=0, keepdims=True), (rows, rows)).T[:, :1]
        field = inverse * (y[step * rows : (step + 1) * rows] * gain - normed * along)
        v_ref[step] = field
        sent_ref[step] = field.astype(BF16)
        fields.append(field)
    if steps == 2:
        one, two = fields
        change1 = one - up_ref[:, at].astype(F32)
        change2 = two - one
        pairs = [(change1, one), (change1, change1), (change2, one), (change2, change2),
                 (change2, two)]
    else:
        past_ref, past_tot_ref = past
        two = past_ref[1]
        change2 = two - past_ref[0]
        change3 = fields[0] - two
        pairs = [(change2, change3), (change3, two), (change3, change3)]
    sums = []
    lanes = tot_ref.shape[1]
    for a, b in pairs:
        total = jnp.sum(a * b, axis=0, keepdims=True)
        sums.append(sum(total[:, i : i + lanes] for i in range(0, half, lanes)))
    if steps == 2:
        tot_ref[...] = jnp.concatenate(sums + [jnp.zeros((3, lanes), F32)], axis=0)
    else:
        tot_ref[...] = jnp.concatenate([past_tot_ref[:5, :]] + sums, axis=0)


def mix_body(entries, head_ref, tot_ref, up_ref, *refs):
    totals = jnp.sum(jnp.sum(tot_ref[...], axis=0), axis=1, keepdims=True) / entries
    s_r1, s_s, d2_v1, d2_d2, d2_v2, d2_d3, d3_v2, d3_d3 = [totals[i : i + 1] for i in range(8)]
    mix1 = s_r1 / (s_s + mix_eps)
    keep1 = 1.0 - mix1
    mix2 = keep1 * (d2_v1 + keep1 * d2_d2) / (keep1 * keep1 * d2_d2 + mix_eps)
    keep2 = keep1 * (1.0 - mix2)
    cross = mix1 * (d2_v2 + keep2 * d2_d3) + keep2 * (d3_v2 + keep2 * d3_d3)
    square = mix1 * mix1 * d2_d2 + 2.0 * mix1 * keep2 * d2_d3 + keep2 * keep2 * d3_d3
    mix3 = cross / (square + mix_eps)
    out_ref = refs[-1]
    half = refs[0].shape[2]
    halves = up_ref.shape[1] // half
    for turn in range(halves):
        early_ref, late_ref = refs[turn], refs[halves + turn]
        side = lax.rem(head_ref[0] + turn, halves)
        at = pl.ds(pl.multiple_of(side * half, half), half)
        out_ref[:, at] = (
            up_ref[:, at].astype(F32)
            + early_ref[0].astype(F32)
            + (1.0 - mix3 * mix1) * early_ref[1].astype(F32)
            + keep2 * (1.0 - mix3) * late_ref[0].astype(F32)
        )


def shards(
    fixed_point,
    upstream,
    norm_gain,
    query_weight,
    keyval_weight,
    output_weight,
    log_norm,
    attention_out,
):
    rows, width = fixed_point.shape
    wide = query_weight.shape[1]
    narrow = keyval_weight.shape[1]
    size = wide + narrow
    e = narrow // 2
    heads = log_norm.shape[0]
    seq_count = lax.axis_size("seq")
    parts = lax.axis_size("head")
    block = lax.axis_index("seq")
    head = lax.axis_index("head")
    scale = e ** (-0.5)
    gain = norm_gain.reshape(1, width)
    span = (WIN_DEVS + 1) * rows
    group = min(8, seq_count)
    direct = group == seq_count

    cols = size // group
    smem = pl.BlockSpec(memory_space=pltpu.SMEM)
    vmem = pl.BlockSpec(memory_space=pltpu.VMEM)
    tile = 128 if wide % 128 == 0 and 128 % (wide // group) == 0 else wide
    own_cols = local_call(
        columns_body,
        shape_of((parts, cols, width), BF16),
        2 * width * size * cols,
        2 * width * (tile + narrow),
        in_specs=[smem] + [pl.BlockSpec(memory_space=pl.ANY)] * 2,
        scratch_shapes=[
            pltpu.VMEM((width, tile), BF16),
            pltpu.VMEM((width, narrow), BF16),
            pltpu.SemaphoreType.DMA((2,)),
        ],
    )(block.reshape(1), query_weight, keyval_weight)
    every_cols = lax.all_to_all(own_cols, "head", 0, 0)

    hidden, kv, kvf, inv = local_call(
        norm_body,
        [
            shape_of((rows, width), BF16),
            shape_of((rows, narrow), BF16),
            shape_of((rows, narrow), F32),
            shape_of((rows, rows), F32),
        ],
        2 * rows * width * narrow,
        2 * width * (2 * rows + narrow),
    )(fixed_point, gain, keyval_weight)
    earlier = [shifted(kv, "seq", offset) for offset in range(WIN_DEVS, 0, -1)]

    qf, qt, go, nt, aot = local_call(
        functools.partial(start_body, heads),
        [
            shape_of((rows, wide), F32),
            shape_of((e, heads * rows), BF16),
            shape_of((e, heads * rows), F32),
            shape_of((e, heads * rows), F32),
            shape_of((e, heads * rows), F32),
        ],
        6 * rows * width * wide,
        4 * width * (2 * rows + wide),
    )(hidden, query_weight, upstream, fixed_point, output_weight, inv, attention_out)

    pull_outs = [shape_of((span, heads * rows), BF16), shape_of((rows, narrow), F32)]
    pull_outs += [shape_of((rows, narrow), BF16)] * WIN_DEVS
    pull_flops = 6 * span * e * heads * rows

    def exchange(score, own, terms, late):
        arrived = [shifted(term, "seq", -offset - 1) for offset, term in enumerate(terms)]
        gq = local_call(
            functools.partial(query_body, heads, scale),
            shape_of((rows, wide), BF16),
            2 * span * e * heads * rows,
            span * heads * rows * 2,
        )(kt, score)
        if late is not None:
            late = lax.optimization_barrier((late, gq))[0]
        every_gq = rotated(gq, "head")
        msg = local_call(
            functools.partial(collect_body, width),
            shape_of((rows + EXTRA, narrow), BF16),
            COLLECT * rows * size,
            rows * size * 4,
        )(own, gq, qf, kvf, *arrived)
        return every_gq, rotated(msg, "head"), late

    kvw, kt, probs, score, own, *terms = local_call(
        functools.partial(first_body, heads, scale),
        [
            shape_of((span, narrow), BF16),
            shape_of((e, span), BF16),
            shape_of((span, heads * rows), BF16),
        ]
        + pull_outs,
        pull_flops * 5 // 4,
        span * heads * rows * 2,
        in_specs=[smem] + [vmem] * (WIN_DEVS + 5),
    )(block.reshape(1), *earlier, kv, qt, go, aot, log_norm)
    all_gq, all_msg = [], []
    for step in range(3):
        if step:
            score, own, *terms = local_call(
                functools.partial(next_body, heads, parts, scale),
                pull_outs,
                pull_flops + 2 * rows * parts * size * wide,
                span * heads * rows * 2 + parts * size * wide * 2,
                in_specs=[smem] + [vmem] * (2 * parts + 7),
            )(head.reshape(1), *all_gq[-1], *all_msg[-1], chain, inv, nt, qt, aot, kvw, probs)
        every_gq, every_msg, late = exchange(score, own, terms, None if step else every_cols)
        all_gq.append(every_gq)
        all_msg.append(every_msg)
        if step == 0:
            chain = local_call(
                chain_body,
                shape_of((group if direct else 1, parts * cols, wide), BF16),
                2 * parts * cols * width * wide,
                2 * width * (wide + parts * cols),
            )(late.reshape(parts * cols, width), output_weight, gain)
            if direct:
                chain = lax.all_to_all(chain, "seq", 0, 0)
            else:
                chain = shared(chain[0], "seq", group)
            chain = chain.reshape(group, parts, cols, wide)
            halves = 2 if parts % 2 == 0 else 1
            half = width // halves
            side = lax.rem(head, halves)
            mine = lax.dynamic_slice_in_dim(late, side * half, half, 2)
            mine = mine.reshape(parts * cols, half)
            if direct:
                weight = lax.all_gather(mine, "seq")
            else:
                weight = shared(mine, "seq", group)
            weight = weight.reshape(group, parts, cols, half)

    def fields(steps, past):
        gqs = [part for step in steps for part in all_gq[step]]
        msgs = [part for step in steps for part in all_msg[step]]
        return local_call(
            functools.partial(field_body, parts, len(steps)),
            [
                shape_of((len(steps), rows, half), F32),
                shape_of((len(steps), rows, half), BF16),
                shape_of((8, 128), F32),
            ],
            2 * len(steps) * rows * parts * size * half,
            2 * parts * size * half,
            in_specs=[smem] + [vmem] * (len(gqs) + len(msgs) + 5 + len(past)),
        )(head.reshape(1), *gqs, *msgs, weight, fixed_point, upstream, gain, inv, *past)

    def swapped(value):
        if halves == 1:
            return []
        return [lax.ppermute(value, "head", [(i, i ^ 1) for i in range(parts)])]

    all_gq[1], all_msg[1], _ = lax.optimization_barrier((all_gq[1], all_msg[1], all_msg[2][0]))
    v_early, early, totals = fields((0, 1), ())
    other_early = swapped(early)
    _, last, totals = fields((2,), (v_early, totals))
    totals = sum(swapped(totals), totals)
    other_last = swapped(last)
    totals = spread(totals, "seq")
    return local_call(
        functools.partial(mix_body, rows * seq_count * width),
        shape_of((rows, width), F32),
        8 * rows * width,
        18 * rows * width,
        in_specs=[smem] + [vmem] * (2 + 2 * halves),
    )(head.reshape(1), totals, upstream, early, *other_early, last, *other_last)


def solution(mesh):
    in_specs = (
        P("seq", None),
        P("seq", None),
        P(),
        P(None, "head"),
        P(None, "head"),
        P("head", None),
        P("head", "seq"),
        P("seq", "head"),
    )
    out_specs = P("seq", None)
    return jax.shard_map(shards, mesh=mesh, in_specs=in_specs, out_specs=out_specs, check_vma=False)
```

```python
import functools

import jax
import jax.numpy as jnp
from jax import lax
from jax.experimental import pallas as pl
from jax.experimental.pallas import tpu as pltpu
from jax.sharding import PartitionSpec as P

WIN_DEVS = 4
norm_eps = 1e-05
mix_eps = 1e-06
F32 = jnp.float32
BF16 = jnp.bfloat16
COLLECT = 50000
EXTRA = 16
NT = (((1,), (1,)), ((), ()))


def shape_of(shape, dtype):
    return jax.ShapeDtypeStruct(shape, dtype)


def local_call(body, outs, flops, moved, room, **more):
    return pl.pallas_call(
        body,
        out_shape=outs,
        compiler_params=pltpu.CompilerParams(vmem_limit_bytes=room * 1024 * 1024),
        cost_estimate=pl.CostEstimate(flops=flops, bytes_accessed=moved, transcendentals=0),
        **more,
    )


def shifted(value, axis, steps):
    count = lax.axis_size(axis)
    initial, last = (max(0, -steps), min(count, count - steps))
    return lax.ppermute(value, axis, [(source, source + steps) for source in range(initial, last)])


def rotated(value, axis):
    count = lax.axis_size(axis)
    parts = [value]
    for step in range(1, count):
        parts.append(lax.ppermute(value, axis, [(i, (i - step) % count) for i in range(count)]))
    return parts


def shared(value, axis, group):
    count = lax.axis_size(axis)
    mine = lax.axis_index(axis)
    half = group // 2
    parts = [value]
    for offset in range(2, group, 2):
        parts.append(lax.ppermute(value, axis, [(i, i ^ offset) for i in range(count)]))
    even = jnp.stack(parts)
    odd = lax.ppermute(even, axis, [(i, i ^ 1) for i in range(count)])
    both = jnp.stack([even, odd], axis=1)
    bits = group.bit_length() - 1
    both = both.reshape((2,) * bits + value.shape)
    for place in range(bits):
        swap = (mine & (half >> place)) != 0
        both = jnp.where(swap, jnp.flip(both, place), both)
    return both.reshape((group,) + value.shape)


def spread(value, axis):
    count = lax.axis_size(axis)
    copies = jnp.broadcast_to(value[None], (count,) + value.shape)
    return lax.all_to_all(copies, axis, 0, 0)


def columns_body(block_ref, qw_ref, kvw_ref, out_ref, q_tile, kv_tile, sems):
    tile = q_tile.shape[1]
    wide, narrow = qw_ref.shape[1], kvw_ref.shape[1]
    group = (wide + narrow) // out_ref.shape[1]
    place = lax.rem(block_ref[0], group)
    q_take, kv_take = wide // group, narrow // group
    q_at = place * q_take
    q_first = pl.multiple_of(q_at // tile * tile, tile)
    copies = [
        pltpu.make_async_copy(qw_ref.at[:, pl.ds(q_first, tile)], q_tile, sems.at[0]),
        pltpu.make_async_copy(kvw_ref, kv_tile, sems.at[1]),
    ]
    for copy in copies:
        copy.start()
    first = 0
    for copy, ref, at, take in (
        (copies[0], q_tile, q_at - q_first, q_take),
        (copies[1], kv_tile, place * kv_take, kv_take),
    ):
        copy.wait()
        total = ref.shape[1]
        row = lax.broadcasted_iota(jnp.int32, (take, total), 0) + at
        pick = (row == lax.broadcasted_iota(jnp.int32, (take, total), 1)).astype(BF16)
        cols = lax.dot_general(pick, ref[...], NT, preferred_element_type=F32).astype(BF16)
        for k in range(out_ref.shape[0]):
            out_ref[k, first : first + take, :] = cols
        first += take


def norm_body(z_ref, gain_ref, kvw_ref, hidden_ref, kv_ref, kvf_ref, inv_ref):
    z = z_ref[...].astype(F32)
    inverse = lax.rsqrt(jnp.mean(z * z, axis=1, keepdims=True) + norm_eps)
    hidden = (z * inverse * gain_ref[...]).astype(BF16)
    hidden_ref[...] = hidden
    kvf = jnp.dot(hidden, kvw_ref[...], preferred_element_type=F32)
    kvf_ref[...] = kvf
    kv_ref[...] = kvf.astype(BF16)
    inv_ref[...] = jnp.broadcast_to(inverse, inv_ref.shape)


def chain_body(cols_ref, ow_ref, gain_ref, out_ref):
    scaled = (ow_ref[...].astype(F32) * gain_ref[...]).astype(BF16)
    share = lax.dot_general(cols_ref[...], scaled, NT, preferred_element_type=F32).astype(BF16)
    for k in range(out_ref.shape[0]):
        out_ref[k] = share


def whole_of(ref, head, wide):
    cut = wide // ref.shape[0]
    parts = [ref[s, head, :cut, :] for s in range(ref.shape[0])]
    parts += [ref[s, head, cut:, :] for s in range(ref.shape[0])]
    return jnp.concatenate(parts, axis=0)


def lanes_of(value, heads):
    size = value.shape[0] // heads
    return jnp.concatenate([value[i * size : (i + 1) * size] for i in range(heads)], axis=1)


def start_body(heads, hidden_ref, qw_ref, up_ref, z_ref, ow_ref, inv_ref, ao_ref,
               qf_ref, qt_ref, go_ref, nt_ref, aot_ref):
    qf = jnp.dot(hidden_ref[...], qw_ref[...], preferred_element_type=F32)
    qf_ref[...] = qf
    qt_ref[...] = lanes_of(qf.T, heads).astype(BF16)
    out = lax.dot_general(up_ref[...], ow_ref[...], NT, preferred_element_type=F32)
    go_ref[...] = lanes_of(out.T, heads)
    base = lax.dot_general(z_ref[...], ow_ref[...], NT, preferred_element_type=F32)
    nt_ref[...] = lanes_of((base * inv_ref[:, :1]).T, heads)
    aot_ref[...] = lanes_of(ao_ref[...].astype(F32).T, heads)


def pull(heads, scale, go, aot, qt, kvw_ref, probs, score_ref, own_ref, term_refs):
    e = go.shape[0]
    rows = go.shape[1] // heads
    row_terms = jnp.sum(go * aot, axis=0, keepdims=True)
    gob = go.astype(BF16)
    grad_prob = jnp.dot(kvw_ref[:, e:], gob, preferred_element_type=F32)
    grad_score = (probs.astype(F32) * (grad_prob - row_terms)).astype(BF16)
    score_ref[...] = grad_score
    grad_key = lax.dot_general(grad_score, qt, NT, preferred_element_type=F32) * scale
    grad_value = lax.dot_general(probs, gob, NT, preferred_element_type=F32)
    terms = jnp.concatenate([grad_key, grad_value], axis=1)
    for offset in range(1, len(term_refs) + 1):
        first = (len(term_refs) - offset) * rows
        term_refs[offset - 1][...] = terms[first : first + rows].astype(BF16)
    own_ref[...] = terms[len(term_refs) * rows :]


def query_body(heads, scale, kt_ref, score_ref, gq_ref):
    rows = gq_ref.shape[0]
    grad_query = jnp.dot(kt_ref[...], score_ref[...], preferred_element_type=F32) * scale
    parts = [grad_query[:, i * rows : (i + 1) * rows] for i in range(heads)]
    gq_ref[...] = jnp.concatenate(parts, axis=0).T.astype(BF16)


def first_body(heads, scale, block_ref, *refs):
    windows = refs[: WIN_DEVS + 1]
    qt_ref, go_ref, aot_ref, ln_ref = refs[WIN_DEVS + 1 : WIN_DEVS + 5]
    kvw_ref, kt_ref, probs_ref, score_ref, own_ref = refs[WIN_DEVS + 5 : WIN_DEVS + 10]
    term_refs = refs[WIN_DEVS + 10 :]
    rows = windows[0].shape[0]
    for place, ref in enumerate(windows):
        kvw_ref[place * rows : (place + 1) * rows, :] = ref[...]
    kvw = kvw_ref[...]
    e = kvw.shape[1] // 2
    kt_ref[...] = kvw.astype(F32).T[:e].astype(BF16)
    scores = jnp.dot(kvw[:, :e], qt_ref[...], preferred_element_type=F32) * scale
    norms = jnp.concatenate([ln_ref[i : i + 1, :] for i in range(heads)], axis=1)
    key_pos = lax.broadcasted_iota(jnp.int32, scores.shape, 0)
    query_pos = lax.broadcasted_iota(jnp.int32, scores.shape, 1) & (rows - 1)
    allowed = (key_pos > query_pos) & (key_pos <= query_pos + WIN_DEVS * rows)
    allowed = allowed & (key_pos >= (WIN_DEVS - block_ref[0]) * rows)
    probs = jnp.where(allowed, jnp.exp(scores - norms), 0.0).astype(BF16)
    probs_ref[...] = probs
    pull(heads, scale, go_ref[...], aot_ref[...], qt_ref[...], kvw_ref, probs,
         score_ref, own_ref, term_refs)


def next_body(heads, parts, scale, head_ref, *refs):
    gq_refs = refs[:parts]
    msg_refs = refs[parts : 2 * parts]
    chain_ref, inv_ref, nt_ref, qt_ref, aot_ref, kvw_ref, probs_ref = refs[
        2 * parts : 2 * parts + 7
    ]
    score_ref, own_ref = refs[2 * parts + 7 : 2 * parts + 9]
    term_refs = refs[2 * parts + 9 :]
    rows, wide = gq_refs[0].shape
    narrow = msg_refs[0].shape[1]
    out = jnp.zeros((rows, wide), F32)
    along = jnp.zeros((EXTRA, rows), F32)
    for k in range(parts):
        chain = whole_of(chain_ref, lax.rem(head_ref[0] + k, parts), wide)
        out += jnp.dot(gq_refs[k][...], chain[:wide], preferred_element_type=F32)
        msg = msg_refs[k][...]
        out += jnp.dot(msg[:rows], chain[wide:], preferred_element_type=F32)
        along += msg[rows:].astype(F32)
    along = jnp.sum(along, axis=0, keepdims=True)
    along = jnp.concatenate([along] * heads, axis=1)
    go = lanes_of((out * inv_ref[:, :1]).T, heads)
    inv_row = jnp.concatenate([inv_ref[...].T[:1, :]] * heads, axis=1)
    go = go - inv_row * along * nt_ref[...]
    pull(heads, scale, go, aot_ref[...], qt_ref[...], kvw_ref, probs_ref[...],
         score_ref, own_ref, term_refs)


def collect_body(width, own_ref, gq_ref, qf_ref, kvf_ref, *refs):
    msg_ref = refs[-1]
    rows = own_ref.shape[0]
    total = own_ref[...]
    for ref in refs[:-1]:
        total += ref[...].astype(F32)
    total = total.astype(BF16)
    msg_ref[:rows, :] = total
    prods = gq_ref[...].astype(F32) * qf_ref[...]
    partial = total.astype(F32) * kvf_ref[...]
    lanes = partial.shape[1]
    for first in range(0, prods.shape[1], lanes):
        partial += prods[:, first : first + lanes]
    along = jnp.sum(partial.T, axis=0, keepdims=True) * (1.0 / width)
    high = along.astype(BF16).astype(F32)
    place = lax.broadcasted_iota(jnp.int32, (EXTRA, rows), 0)
    extra = jnp.where(place == 0, high, jnp.where(place == 1, along - high, 0.0))
    msg_ref[rows:, :] = extra.astype(BF16)


def field_body(parts, steps, head_ref, *refs):
    count = parts * steps
    gq_refs = refs[:count]
    msg_refs = refs[count : 2 * count]
    w_ref, z_ref, up_ref, gain_ref, inv_ref, *past = refs[2 * count : -3]
    v_ref, sent_ref, tot_ref = refs[-3:]
    rows, wide = gq_refs[0].shape
    half = w_ref.shape[3]
    head = head_ref[0]
    first = pl.multiple_of(lax.rem(head, z_ref.shape[1] // half) * half, half)
    at = pl.ds(first, half)
    y = jnp.zeros((steps * rows, half), F32)
    for k in range(parts):
        weight = whole_of(w_ref, lax.rem(head + k, parts), wide)
        lhs = [
            jnp.concatenate(
                [gq_refs[step * parts + k][...], msg_refs[step * parts + k][:rows, :]], axis=1
            )
            for step in range(steps)
        ]
        lhs = lhs[0] if steps == 1 else jnp.concatenate(lhs, axis=0)
        y += jnp.dot(lhs, weight, preferred_element_type=F32)
    inverse = inv_ref[:, :1]
    normed = z_ref[:, at].astype(F32) * inverse
    gain = gain_ref[:, at]
    fields = []
    for step in range(steps):
        along = jnp.zeros((EXTRA, rows), F32)
        for k in range(parts):
            along += msg_refs[step * parts + k][rows:, :].astype(F32)
        along = jnp.broadcast_to(jnp.sum(along, axis=0, keepdims=True), (rows, rows)).T[:, :1]
        field = inverse * (y[step * rows : (step + 1) * rows] * gain - normed * along)
        v_ref[step] = field
        sent_ref[step] = field.astype(BF16)
        fields.append(field)
    if steps == 2:
        one, two = fields
        change1 = one - up_ref[:, at].astype(F32)
        change2 = two - one
        pairs = [(change1, one), (change1, change1), (change2, one), (change2, change2),
                 (change2, two)]
    else:
        past_ref, past_tot_ref = past
        two = past_ref[1]
        change2 = two - past_ref[0]
        change3 = fields[0] - two
        pairs = [(change2, change3), (change3, two), (change3, change3)]
    sums = []
    lanes = tot_ref.shape[1]
    for a, b in pairs:
        total = jnp.sum(a * b, axis=0, keepdims=True)
        sums.append(sum(total[:, i : i + lanes] for i in range(0, half, lanes)))
    if steps == 2:
        tot_ref[...] = jnp.concatenate(sums + [jnp.zeros((3, lanes), F32)], axis=0)
    else:
        tot_ref[...] = jnp.concatenate([past_tot_ref[:5, :]] + sums, axis=0)


def mix_body(entries, head_ref, tot_ref, up_ref, *refs):
    totals = jnp.sum(jnp.sum(tot_ref[...], axis=0), axis=1, keepdims=True) / entries
    s_r1, s_s, d2_v1, d2_d2, d2_v2, d2_d3, d3_v2, d3_d3 = [totals[i : i + 1] for i in range(8)]
    mix1 = s_r1 / (s_s + mix_eps)
    keep1 = 1.0 - mix1
    mix2 = keep1 * (d2_v1 + keep1 * d2_d2) / (keep1 * keep1 * d2_d2 + mix_eps)
    keep2 = keep1 * (1.0 - mix2)
    cross = mix1 * (d2_v2 + keep2 * d2_d3) + keep2 * (d3_v2 + keep2 * d3_d3)
    square = mix1 * mix1 * d2_d2 + 2.0 * mix1 * keep2 * d2_d3 + keep2 * keep2 * d3_d3
    mix3 = cross / (square + mix_eps)
    out_ref = refs[-1]
    half = refs[0].shape[2]
    halves = up_ref.shape[1] // half
    for turn in range(halves):
        early_ref, late_ref = refs[turn], refs[halves + turn]
        side = lax.rem(head_ref[0] + turn, halves)
        at = pl.ds(pl.multiple_of(side * half, half), half)
        out_ref[:, at] = (
            up_ref[:, at].astype(F32)
            + early_ref[0].astype(F32)
            + (1.0 - mix3 * mix1) * early_ref[1].astype(F32)
            + keep2 * (1.0 - mix3) * late_ref[0].astype(F32)
        )


def shards(
    fixed_point,
    upstream,
    norm_gain,
    query_weight,
    keyval_weight,
    output_weight,
    log_norm,
    attention_out,
):
    rows, width = fixed_point.shape
    wide = query_weight.shape[1]
    narrow = keyval_weight.shape[1]
    size = wide + narrow
    e = narrow // 2
    heads = log_norm.shape[0]
    seq_count = lax.axis_size("seq")
    parts = lax.axis_size("head")
    block = lax.axis_index("seq")
    head = lax.axis_index("head")
    scale = e ** (-0.5)
    gain = norm_gain.reshape(1, width)
    span = (WIN_DEVS + 1) * rows
    group = min(8, seq_count)
    direct = group == seq_count

    cols = size // group
    smem = pl.BlockSpec(memory_space=pltpu.SMEM)
    vmem = pl.BlockSpec(memory_space=pltpu.VMEM)
    tile = 128 if wide % 128 == 0 and 128 % (wide // group) == 0 else wide
    own_cols = local_call(
        columns_body,
        shape_of((parts, cols, width), BF16),
        2 * width * size * cols,
        2 * width * (tile + narrow),
        6,
        in_specs=[smem] + [pl.BlockSpec(memory_space=pl.ANY)] * 2,
        scratch_shapes=[
            pltpu.VMEM((width, tile), BF16),
            pltpu.VMEM((width, narrow), BF16),
            pltpu.SemaphoreType.DMA((2,)),
        ],
    )(block.reshape(1), query_weight, keyval_weight)
    every_cols = lax.all_to_all(own_cols, "head", 0, 0)

    hidden, kv, kvf, inv = local_call(
        norm_body,
        [
            shape_of((rows, width), BF16),
            shape_of((rows, narrow), BF16),
            shape_of((rows, narrow), F32),
            shape_of((rows, rows), F32),
        ],
        2 * rows * width * narrow,
        2 * width * (2 * rows + narrow),
        8,
    )(fixed_point, gain, keyval_weight)
    earlier = [shifted(kv, "seq", offset) for offset in range(WIN_DEVS, 0, -1)]

    qf, qt, go, nt, aot = local_call(
        functools.partial(start_body, heads),
        [
            shape_of((rows, wide), F32),
            shape_of((e, heads * rows), BF16),
            shape_of((e, heads * rows), F32),
            shape_of((e, heads * rows), F32),
            shape_of((e, heads * rows), F32),
        ],
        6 * rows * width * wide,
        4 * width * (2 * rows + wide),
        10,
    )(hidden, query_weight, upstream, fixed_point, output_weight, inv, attention_out)

    pull_outs = [shape_of((span, heads * rows), BF16), shape_of((rows, narrow), F32)]
    pull_outs += [shape_of((rows, narrow), BF16)] * WIN_DEVS
    pull_flops = 6 * span * e * heads * rows

    def exchange(score, own, terms, late):
        arrived = [shifted(term, "seq", -offset - 1) for offset, term in enumerate(terms)]
        gq = local_call(
            functools.partial(query_body, heads, scale),
            shape_of((rows, wide), BF16),
            2 * span * e * heads * rows,
            span * heads * rows * 2,
            4,
        )(kt, score)
        if late is not None:
            late = lax.optimization_barrier((late, gq))[0]
        every_gq = rotated(gq, "head")
        msg = local_call(
            functools.partial(collect_body, width),
            shape_of((rows + EXTRA, narrow), BF16),
            COLLECT * rows * size,
            rows * size * 4,
            4,
        )(own, gq, qf, kvf, *arrived)
        return every_gq, rotated(msg, "head"), late

    kvw, kt, probs, score, own, *terms = local_call(
        functools.partial(first_body, heads, scale),
        [
            shape_of((span, narrow), BF16),
            shape_of((e, span), BF16),
            shape_of((span, heads * rows), BF16),
        ]
        + pull_outs,
        pull_flops * 5 // 4,
        span * heads * rows * 2,
        16,
        in_specs=[smem] + [vmem] * (WIN_DEVS + 5),
    )(block.reshape(1), *earlier, kv, qt, go, aot, log_norm)
    all_gq, all_msg = [], []
    for step in range(3):
        if step:
            score, own, *terms = local_call(
                functools.partial(next_body, heads, parts, scale),
                pull_outs,
                pull_flops + 2 * rows * parts * size * wide,
                span * heads * rows * 2 + parts * size * wide * 2,
                16,
                in_specs=[smem] + [vmem] * (2 * parts + 7),
            )(head.reshape(1), *all_gq[-1], *all_msg[-1], chain, inv, nt, qt, aot, kvw, probs)
        every_gq, every_msg, late = exchange(score, own, terms, None if step else every_cols)
        all_gq.append(every_gq)
        all_msg.append(every_msg)
        if step == 0:
            chain = local_call(
                chain_body,
                shape_of((group if direct else 1, parts * cols, wide), BF16),
                2 * parts * cols * width * wide,
                2 * width * (wide + parts * cols),
                8,
            )(late.reshape(parts * cols, width), output_weight, gain)
            if direct:
                chain = lax.all_to_all(chain, "seq", 0, 0)
            else:
                chain = shared(chain[0], "seq", group)
            chain = chain.reshape(group, parts, cols, wide)
            halves = 2 if parts % 2 == 0 else 1
            half = width // halves
            side = lax.rem(head, halves)
            mine = lax.dynamic_slice_in_dim(late, side * half, half, 2)
            mine = mine.reshape(parts * cols, half)
            if direct:
                weight = lax.all_gather(mine, "seq")
            else:
                weight = shared(mine, "seq", group)
            weight = weight.reshape(group, parts, cols, half)

    def fields(steps, past):
        gqs = [part for step in steps for part in all_gq[step]]
        msgs = [part for step in steps for part in all_msg[step]]
        return local_call(
            functools.partial(field_body, parts, len(steps)),
            [
                shape_of((len(steps), rows, half), F32),
                shape_of((len(steps), rows, half), BF16),
                shape_of((8, 128), F32),
            ],
            2 * len(steps) * rows * parts * size * half,
            2 * parts * size * half,
            20,
            in_specs=[smem] + [vmem] * (len(gqs) + len(msgs) + 5 + len(past)),
        )(head.reshape(1), *gqs, *msgs, weight, fixed_point, upstream, gain, inv, *past)

    def swapped(value):
        if halves == 1:
            return []
        return [lax.ppermute(value, "head", [(i, i ^ 1) for i in range(parts)])]

    all_gq[1], all_msg[1], _ = lax.optimization_barrier((all_gq[1], all_msg[1], score))
    v_early, early, totals = fields((0, 1), ())
    other_early = swapped(early)
    _, last, totals = fields((2,), (v_early, totals))
    totals = sum(swapped(totals), totals)
    other_last = swapped(last)
    totals = spread(totals, "seq")
    return local_call(
        functools.partial(mix_body, rows * seq_count * width),
        shape_of((rows, width), F32),
        8 * rows * width,
        18 * rows * width,
        10,
        in_specs=[smem] + [vmem] * (2 + 2 * halves),
    )(head.reshape(1), totals, upstream, early, *other_early, last, *other_last)


def solution(mesh):
    in_specs = (
        P("seq", None),
        P("seq", None),
        P(),
        P(None, "head"),
        P(None, "head"),
        P("head", None),
        P("head", "seq"),
        P("seq", "head"),
    )
    out_specs = P("seq", None)
    return jax.shard_map(shards, mesh=mesh, in_specs=in_specs, out_specs=out_specs, check_vma=False)
```

```python
import functools

import jax
import jax.numpy as jnp
from jax import lax
from jax.experimental import pallas as pl
from jax.experimental.pallas import tpu as pltpu
from jax.sharding import PartitionSpec as P

WIN_DEVS = 4
norm_eps = 1e-05
mix_eps = 1e-06
F32 = jnp.float32
BF16 = jnp.bfloat16
COLLECT = 50000
EXTRA = 16
NT = (((1,), (1,)), ((), ()))


def shape_of(shape, dtype):
    return jax.ShapeDtypeStruct(shape, dtype)


def local_call(body, outs, flops, moved, room, **more):
    return pl.pallas_call(
        body,
        out_shape=outs,
        compiler_params=pltpu.CompilerParams(vmem_limit_bytes=room * 1024 * 1024),
        cost_estimate=pl.CostEstimate(flops=flops, bytes_accessed=moved, transcendentals=0),
        **more,
    )


def shifted(value, axis, steps):
    count = lax.axis_size(axis)
    initial, last = (max(0, -steps), min(count, count - steps))
    return lax.ppermute(value, axis, [(source, source + steps) for source in range(initial, last)])


def shared(value, axis, group):
    count = lax.axis_size(axis)
    mine = lax.axis_index(axis)
    half = group // 2
    parts = [value]
    for offset in range(2, group, 2):
        parts.append(lax.ppermute(value, axis, [(i, i ^ offset) for i in range(count)]))
    even = jnp.stack(parts)
    odd = lax.ppermute(even, axis, [(i, i ^ 1) for i in range(count)])
    both = jnp.stack([even, odd], axis=1)
    bits = group.bit_length() - 1
    both = both.reshape((2,) * bits + value.shape)
    for place in range(bits):
        swap = (mine & (half >> place)) != 0
        both = jnp.where(swap, jnp.flip(both, place), both)
    return both.reshape((group,) + value.shape)


def columns_body(block_ref, qw_ref, kvw_ref, out_ref, q_tile, kv_tile, sems):
    tile = q_tile.shape[1]
    wide, narrow = qw_ref.shape[1], kvw_ref.shape[1]
    group = (wide + narrow) // out_ref.shape[1]
    place = lax.rem(block_ref[0], group)
    q_take, kv_take = wide // group, narrow // group
    q_at = place * q_take
    q_first = pl.multiple_of(q_at // tile * tile, tile)
    copies = [
        pltpu.make_async_copy(qw_ref.at[:, pl.ds(q_first, tile)], q_tile, sems.at[0]),
        pltpu.make_async_copy(kvw_ref, kv_tile, sems.at[1]),
    ]
    for copy in copies:
        copy.start()
    first = 0
    for copy, ref, at, take in (
        (copies[0], q_tile, q_at - q_first, q_take),
        (copies[1], kv_tile, place * kv_take, kv_take),
    ):
        copy.wait()
        total = ref.shape[1]
        row = lax.broadcasted_iota(jnp.int32, (take, total), 0) + at
        pick = (row == lax.broadcasted_iota(jnp.int32, (take, total), 1)).astype(BF16)
        cols = lax.dot_general(pick, ref[...], NT, preferred_element_type=F32).astype(BF16)
        for k in range(out_ref.shape[0]):
            out_ref[k, first : first + take, :] = cols
        first += take


def norm_body(z_ref, gain_ref, kvw_ref, hidden_ref, kv_ref, kvf_ref, inv_ref):
    z = z_ref[...].astype(F32)
    inverse = lax.rsqrt(jnp.mean(z * z, axis=1, keepdims=True) + norm_eps)
    hidden = (z * inverse * gain_ref[...]).astype(BF16)
    hidden_ref[...] = hidden
    kvf = jnp.dot(hidden, kvw_ref[...], preferred_element_type=F32)
    kvf_ref[...] = kvf
    for k in range(kv_ref.shape[0]):
        kv_ref[k] = kvf.astype(BF16)
    inv_ref[...] = jnp.broadcast_to(inverse, inv_ref.shape)


def chain_body(cols_ref, ow_ref, gain_ref, out_ref):
    scaled = (ow_ref[...].astype(F32) * gain_ref[...]).astype(BF16)
    share = lax.dot_general(cols_ref[...], scaled, NT, preferred_element_type=F32).astype(BF16)
    for k in range(out_ref.shape[0]):
        out_ref[k] = share


def whole_of(ref, head, wide):
    cut = wide // ref.shape[0]
    parts = [ref[s, head, :cut, :] for s in range(ref.shape[0])]
    parts += [ref[s, head, cut:, :] for s in range(ref.shape[0])]
    return jnp.concatenate(parts, axis=0)


def lanes_of(value, heads):
    size = value.shape[0] // heads
    return jnp.concatenate([value[i * size : (i + 1) * size] for i in range(heads)], axis=1)


def start_body(heads, hidden_ref, qw_ref, up_ref, z_ref, ow_ref, inv_ref, ao_ref,
               qf_ref, qt_ref, go_ref, nt_ref, aot_ref):
    qf = jnp.dot(hidden_ref[...], qw_ref[...], preferred_element_type=F32)
    qf_ref[...] = qf
    qt_ref[...] = lanes_of(qf.T, heads).astype(BF16)
    out = lax.dot_general(up_ref[...], ow_ref[...], NT, preferred_element_type=F32)
    go_ref[...] = lanes_of(out.T, heads)
    base = lax.dot_general(z_ref[...], ow_ref[...], NT, preferred_element_type=F32)
    nt_ref[...] = lanes_of((base * inv_ref[:, :1]).T, heads)
    aot_ref[...] = lanes_of(ao_ref[...].astype(F32).T, heads)


def pull(heads, scale, go, aot, qt, kvw_ref, probs, block, score_ref, own_ref, term_ref):
    e = go.shape[0]
    rows = go.shape[1] // heads
    row_terms = jnp.sum(go * aot, axis=0, keepdims=True)
    gob = go.astype(BF16)
    grad_prob = jnp.dot(kvw_ref[:, e:], gob, preferred_element_type=F32)
    grad_score = (probs.astype(F32) * (grad_prob - row_terms)).astype(BF16)
    score_ref[...] = grad_score
    grad_key = lax.dot_general(grad_score, qt, NT, preferred_element_type=F32) * scale
    grad_value = lax.dot_general(probs, gob, NT, preferred_element_type=F32)
    terms = jnp.concatenate([grad_key, grad_value], axis=1)
    own_ref[...] = terms[WIN_DEVS * rows :]
    slots = term_ref.shape[0]
    if slots == WIN_DEVS:
        for offset in range(1, WIN_DEVS + 1):
            first = (WIN_DEVS - offset) * rows
            term_ref[offset - 1] = terms[first : first + rows].astype(BF16)
        return
    for slot in range(slots):
        offset = block - slot
        part = jnp.zeros((rows, 2 * e), F32)
        for one in range(1, WIN_DEVS + 1):
            first = (WIN_DEVS - one) * rows
            part = jnp.where(offset == one, terms[first : first + rows], part)
        term_ref[slot] = part.astype(BF16)


def query_body(heads, scale, kt_ref, score_ref, gq_ref):
    rows = gq_ref.shape[1]
    grad_query = jnp.dot(kt_ref[...], score_ref[...], preferred_element_type=F32) * scale
    parts = [grad_query[:, i * rows : (i + 1) * rows] for i in range(heads)]
    grad_query = jnp.concatenate(parts, axis=0).T.astype(BF16)
    for k in range(gq_ref.shape[0]):
        gq_ref[k] = grad_query


def first_body(heads, scale, block_ref, window_ref, qt_ref, go_ref, aot_ref, ln_ref,
               kvw_ref, kt_ref, probs_ref, score_ref, own_ref, term_ref):
    block = block_ref[0]
    rows = window_ref.shape[1]
    for place in range(WIN_DEVS + 1):
        if window_ref.shape[0] == WIN_DEVS + 1:
            part = window_ref[place]
        else:
            index = block - WIN_DEVS + place
            part = window_ref[jnp.maximum(index, 0)]
            part = jnp.where(index >= 0, part.astype(F32), 0.0).astype(BF16)
        kvw_ref[place * rows : (place + 1) * rows, :] = part
    kvw = kvw_ref[...]
    e = kvw.shape[1] // 2
    kt_ref[...] = kvw.astype(F32).T[:e].astype(BF16)
    scores = jnp.dot(kvw[:, :e], qt_ref[...], preferred_element_type=F32) * scale
    norms = jnp.concatenate([ln_ref[i : i + 1, :] for i in range(heads)], axis=1)
    key_pos = lax.broadcasted_iota(jnp.int32, scores.shape, 0)
    query_pos = lax.broadcasted_iota(jnp.int32, scores.shape, 1) & (rows - 1)
    allowed = (key_pos > query_pos) & (key_pos <= query_pos + WIN_DEVS * rows)
    allowed = allowed & (key_pos >= (WIN_DEVS - block) * rows)
    probs = jnp.where(allowed, jnp.exp(scores - norms), 0.0).astype(BF16)
    probs_ref[...] = probs
    pull(heads, scale, go_ref[...], aot_ref[...], qt_ref[...], kvw_ref, probs, block,
         score_ref, own_ref, term_ref)


def next_body(heads, scale, block_ref, gq_ref, msg_ref, chain_ref, inv_ref, nt_ref, qt_ref,
              aot_ref, kvw_ref, probs_ref, score_ref, own_ref, term_ref):
    parts, rows, wide = gq_ref.shape
    out = jnp.zeros((rows, wide), F32)
    along = jnp.zeros((EXTRA, rows), F32)
    for k in range(parts):
        chain = whole_of(chain_ref, k, wide)
        lhs = jnp.concatenate([gq_ref[k], msg_ref[k, :rows, :]], axis=1)
        out += jnp.dot(lhs, chain, preferred_element_type=F32)
        along += msg_ref[k, rows:, :].astype(F32)
    along = jnp.sum(along, axis=0, keepdims=True)
    along = jnp.concatenate([along] * heads, axis=1)
    go = lanes_of((out * inv_ref[:, :1]).T, heads)
    inv_row = jnp.concatenate([inv_ref[...].T[:1, :]] * heads, axis=1)
    go = go - inv_row * along * nt_ref[...]
    pull(heads, scale, go, aot_ref[...], qt_ref[...], kvw_ref, probs_ref[...],
         block_ref[0], score_ref, own_ref, term_ref)


def collect_body(width, block_ref, own_ref, gq_ref, qf_ref, kvf_ref, arrived_ref, msg_ref):
    rows = own_ref.shape[0]
    total = own_ref[...]
    slots = arrived_ref.shape[0]
    for offset in range(1, WIN_DEVS + 1):
        if slots == WIN_DEVS:
            total += arrived_ref[offset - 1].astype(F32)
        else:
            index = block_ref[0] + offset
            part = arrived_ref[jnp.minimum(index, slots - 1)].astype(F32)
            total += jnp.where(index < slots, part, 0.0)
    total = total.astype(BF16)
    prods = gq_ref[0].astype(F32) * qf_ref[...]
    partial = total.astype(F32) * kvf_ref[...]
    lanes = partial.shape[1]
    for first in range(0, prods.shape[1], lanes):
        partial += prods[:, first : first + lanes]
    along = jnp.sum(partial.T, axis=0, keepdims=True) * (1.0 / width)
    high = along.astype(BF16).astype(F32)
    place = lax.broadcasted_iota(jnp.int32, (EXTRA, rows), 0)
    extra = jnp.where(place == 0, high, jnp.where(place == 1, along - high, 0.0)).astype(BF16)
    for k in range(msg_ref.shape[0]):
        msg_ref[k, :rows, :] = total
        msg_ref[k, rows:, :] = extra


def pack_body(place_ref, cols_ref, out_ref):
    slots, _, part = out_ref.shape
    half = 2 * part
    for core in range(2):
        at = pl.multiple_of(place_ref[0] * half + core * part, part)
        value = cols_ref[:, pl.ds(at, part)]
        for slot in range(core, slots, 2):
            out_ref[slot] = value


def field_body(steps, place_ref, *refs):
    gq_refs = refs[:steps]
    msg_refs = refs[steps : 2 * steps]
    own_ref, other_ref, z_ref, up_ref, gain_ref, inv_ref, *past = refs[2 * steps : -3]
    v_ref, sent_ref, tot_ref = refs[-3:]
    parts, rows, wide = gq_refs[0].shape
    part = own_ref.shape[3]
    lanes = tot_ref.shape[2]
    inverse = inv_ref[:, :1]
    alongs = []
    for step in range(steps):
        along = jnp.zeros((EXTRA, rows), F32)
        for k in range(parts):
            along += msg_refs[step][k, rows:, :].astype(F32)
        along = jnp.broadcast_to(jnp.sum(along, axis=0, keepdims=True), (rows, rows))
        alongs.append(along.T[:, :1])
    totals = None
    for turn, w_ref in enumerate((own_ref, other_ref)):
        sub = (place_ref[1] + turn) & 1
        inside = pl.ds(pl.multiple_of(sub * part, part), part)
        at = pl.ds(pl.multiple_of(place_ref[0] * (2 * part) + sub * part, part), part)
        y = jnp.zeros((steps * rows, part), F32)
        for k in range(parts):
            lhs = [
                jnp.concatenate([gq_refs[step][k], msg_refs[step][k, :rows, :]], axis=1)
                for step in range(steps)
            ]
            lhs = lhs[0] if steps == 1 else jnp.concatenate(lhs, axis=0)
            y += jnp.dot(lhs, whole_of(w_ref, k, wide), preferred_element_type=F32)
        normed = z_ref[:, at].astype(F32) * inverse
        gain = gain_ref[:, at]
        fields = []
        for step in range(steps):
            y_step = y[step * rows : (step + 1) * rows]
            field = inverse * (y_step * gain - normed * alongs[step])
            v_ref[step, :, inside] = field
            sent_ref[step, :, inside] = field.astype(BF16)
            fields.append(field)
        if steps == 2:
            one, two = fields
            change1 = one - up_ref[:, at].astype(F32)
            change2 = two - one
            pairs = [(change1, one), (change1, change1), (change2, one), (change2, change2),
                     (change2, two)]
        else:
            two = past[0][1, :, inside]
            change2 = two - past[0][0, :, inside]
            change3 = fields[0] - two
            pairs = [(change2, change3), (change3, two), (change3, change3)]
        sums = []
        for a, b in pairs:
            total = jnp.sum(a * b, axis=0, keepdims=True)
            sums.append(sum(total[:, i : i + lanes] for i in range(0, part, lanes)))
        totals = sums if totals is None else [a + b for a, b in zip(totals, sums)]
    if steps == 2:
        tot_ref[0] = jnp.concatenate(totals + [jnp.zeros((3, lanes), F32)], axis=0)
    else:
        totals = jnp.concatenate([past[1][0, :5, :]] + totals, axis=0)
        for k in range(tot_ref.shape[0]):
            tot_ref[k] = totals


def mix_body(entries, place_ref, tot_ref, up_ref, *refs):
    totals = jnp.sum(jnp.sum(tot_ref[...], axis=0), axis=1, keepdims=True) / entries
    s_r1, s_s, d2_v1, d2_d2, d2_v2, d2_d3, d3_v2, d3_d3 = [totals[i : i + 1] for i in range(8)]
    mix1 = s_r1 / (s_s + mix_eps)
    keep1 = 1.0 - mix1
    mix2 = keep1 * (d2_v1 + keep1 * d2_d2) / (keep1 * keep1 * d2_d2 + mix_eps)
    keep2 = keep1 * (1.0 - mix2)
    cross = mix1 * (d2_v2 + keep2 * d2_d3) + keep2 * (d3_v2 + keep2 * d3_d3)
    square = mix1 * mix1 * d2_d2 + 2.0 * mix1 * keep2 * d2_d3 + keep2 * keep2 * d3_d3
    mix3 = cross / (square + mix_eps)
    out_ref = refs[-1]
    half = refs[0].shape[2]
    halves = up_ref.shape[1] // half
    for turn in range(halves):
        early_ref, late_ref = refs[turn], refs[halves + turn]
        side = lax.rem(place_ref[0] + turn, halves)
        at = pl.ds(pl.multiple_of(side * half, half), half)
        out_ref[:, at] = (
            up_ref[:, at].astype(F32)
            + early_ref[0].astype(F32)
            + (1.0 - mix3 * mix1) * early_ref[1].astype(F32)
            + keep2 * (1.0 - mix3) * late_ref[0].astype(F32)
        )


def shards(
    fixed_point,
    upstream,
    norm_gain,
    query_weight,
    keyval_weight,
    output_weight,
    log_norm,
    attention_out,
):
    rows, width = fixed_point.shape
    wide = query_weight.shape[1]
    narrow = keyval_weight.shape[1]
    size = wide + narrow
    e = narrow // 2
    heads = log_norm.shape[0]
    seq_count = lax.axis_size("seq")
    parts = lax.axis_size("head")
    block = lax.axis_index("seq")
    head = lax.axis_index("head")
    scale = e ** (-0.5)
    gain = norm_gain.reshape(1, width)
    span = (WIN_DEVS + 1) * rows
    group = min(8, seq_count)
    direct = group == seq_count
    cols = size // group
    halves = 2 if parts % 2 == 0 else 1
    half = width // halves
    side = lax.rem(head, halves)
    core = lax.rem(block, 2) if direct else jnp.zeros_like(block)
    place = jnp.stack([side, core])
    smem = pl.BlockSpec(memory_space=pltpu.SMEM)
    vmem = pl.BlockSpec(memory_space=pltpu.VMEM)

    def over_heads(copies):
        return lax.all_to_all(copies, "head", 0, 0)

    tile = 128 if wide % 128 == 0 and 128 % (wide // group) == 0 else wide
    own_cols = local_call(
        columns_body,
        shape_of((parts, cols, width), BF16),
        2 * width * size * cols,
        2 * width * (tile + narrow),
        6,
        in_specs=[smem] + [pl.BlockSpec(memory_space=pltpu.HBM)] * 2,
        scratch_shapes=[
            pltpu.VMEM((width, tile), BF16),
            pltpu.VMEM((width, narrow), BF16),
            pltpu.SemaphoreType.DMA((2,)),
        ],
    )(block.reshape(1), query_weight, keyval_weight)
    every_cols = over_heads(own_cols)

    hidden, kv, kvf, inv = local_call(
        norm_body,
        [
            shape_of((rows, width), BF16),
            shape_of((seq_count if direct else 1, rows, narrow), BF16),
            shape_of((rows, narrow), F32),
            shape_of((rows, rows), F32),
        ],
        2 * rows * width * narrow,
        2 * width * (2 * rows + narrow),
        8,
    )(fixed_point, gain, keyval_weight)
    if direct:
        window = lax.all_to_all(kv, "seq", 0, 0)
    else:
        earlier = [shifted(kv[0], "seq", offset) for offset in range(WIN_DEVS, 0, -1)]
        window = jnp.stack(earlier + [kv[0]])

    qf, qt, go, nt, aot = local_call(
        functools.partial(start_body, heads),
        [
            shape_of((rows, wide), F32),
            shape_of((e, heads * rows), BF16),
            shape_of((e, heads * rows), F32),
            shape_of((e, heads * rows), F32),
            shape_of((e, heads * rows), F32),
        ],
        6 * rows * width * wide,
        4 * width * (2 * rows + wide),
        10,
    )(hidden, query_weight, upstream, fixed_point, output_weight, inv, attention_out)

    pull_outs = [
        shape_of((span, heads * rows), BF16),
        shape_of((rows, narrow), F32),
        shape_of((seq_count if direct else WIN_DEVS, rows, narrow), BF16),
    ]
    pull_flops = 6 * span * e * heads * rows

    def exchange(score, own, terms):
        if direct:
            arrived = lax.all_to_all(terms, "seq", 0, 0)
        else:
            arrived = jnp.stack([shifted(terms[i], "seq", -i - 1) for i in range(WIN_DEVS)])
        gq = local_call(
            functools.partial(query_body, heads, scale),
            shape_of((parts, rows, wide), BF16),
            2 * span * e * heads * rows,
            span * heads * rows * 2,
            4,
        )(kt, score)
        msg = local_call(
            functools.partial(collect_body, width),
            shape_of((parts, rows + EXTRA, narrow), BF16),
            COLLECT * rows * size,
            rows * size * 4,
            4,
            in_specs=[smem] + [vmem] * 5,
        )(block.reshape(1), own, gq, qf, kvf, arrived)
        return over_heads(gq), over_heads(msg), msg

    kvw, kt, probs, score, own, terms = local_call(
        functools.partial(first_body, heads, scale),
        [
            shape_of((span, narrow), BF16),
            shape_of((e, span), BF16),
            shape_of((span, heads * rows), BF16),
        ]
        + pull_outs,
        pull_flops * 5 // 4,
        span * heads * rows * 2,
        16,
        in_specs=[smem] + [vmem] * 5,
    )(block.reshape(1), window, qt, go, aot, log_norm)

    flat_cols = every_cols.reshape(parts * cols, width)
    chain = local_call(
        chain_body,
        shape_of((group if direct else 1, parts * cols, wide), BF16),
        2 * parts * cols * width * wide,
        2 * width * (wide + parts * cols),
        8,
    )(flat_cols, output_weight, gain)
    if direct:
        chain = lax.all_to_all(chain, "seq", 0, 0)
    else:
        chain = shared(chain[0], "seq", group)
    chain = chain.reshape(group, parts, cols, wide)

    all_gq, all_msg = [], []
    for step in range(3):
        if step:
            score, own, terms = local_call(
                functools.partial(next_body, heads, scale),
                pull_outs,
                pull_flops + 2 * rows * parts * size * wide,
                span * heads * rows * 2 + parts * size * wide * 2,
                16,
                in_specs=[smem] + [vmem] * 9,
            )(block.reshape(1), all_gq[-1], all_msg[-1], chain, inv, nt, qt, aot, kvw, probs)
        every_gq, every_msg, msg = exchange(score, own, terms)
        all_gq.append(every_gq)
        all_msg.append(every_msg)
        if step == 0:
            if direct:
                late_cols, _ = lax.optimization_barrier((flat_cols, msg))
                packed = local_call(
                    pack_body,
                    shape_of((group, parts * cols, half // 2), BF16),
                    0,
                    group * parts * cols * half,
                    8,
                    in_specs=[smem, vmem],
                )(place, late_cols)
                quarter = lax.all_to_all(packed, "seq", 0, 0)
                shape = (group, parts, cols, half // 2)
                own_w = quarter.reshape(shape)
            else:
                mine = lax.dynamic_slice_in_dim(flat_cols, side * half, half, 1)
                weight = shared(mine, "seq", group).reshape(group, parts, cols, half)
                own_w, other_w = weight[..., : half // 2], weight[..., half // 2 :]
        if step == 1 and direct:
            pairs = [(i, i ^ 1) for i in range(seq_count)]
            late, _ = lax.optimization_barrier((quarter, msg))
            other_w = lax.ppermute(late, "seq", pairs).reshape(shape)

    def fields(steps, past):
        copies = seq_count * parts if direct and len(steps) == 1 else 1
        return local_call(
            functools.partial(field_body, len(steps)),
            [
                shape_of((len(steps), rows, half), F32),
                shape_of((len(steps), rows, half), BF16),
                shape_of((copies, 8, 128), F32),
            ],
            2 * len(steps) * rows * parts * size * half,
            2 * parts * size * half,
            20,
            in_specs=[smem] + [vmem] * (2 * len(steps) + 6 + len(past)),
        )(
            place,
            *[all_gq[i] for i in steps],
            *[all_msg[i] for i in steps],
            own_w,
            other_w,
            fixed_point,
            upstream,
            gain,
            inv,
            *past,
        )

    def swapped(value):
        if halves == 1:
            return []
        return [lax.ppermute(value, "head", [(i, i ^ 1) for i in range(parts)])]

    all_gq[1], all_msg[1], _ = lax.optimization_barrier((all_gq[1], all_msg[1], score))
    v_early, early, totals = fields((0, 1), ())
    other_early = swapped(early)
    _, last, totals = fields((2,), (v_early, totals))
    if direct:
        totals = lax.all_to_all(totals, ("seq", "head"), 0, 0)
    else:
        totals = lax.psum(totals, ("seq", "head"))
    other_last = swapped(last)
    entries = rows * seq_count * width * (parts // halves)
    return local_call(
        functools.partial(mix_body, entries),
        shape_of((rows, width), F32),
        8 * rows * width,
        18 * rows * width,
        10,
        in_specs=[smem] + [vmem] * (2 + 2 * halves),
    )(place, totals, upstream, early, *other_early, last, *other_last)


def solution(mesh):
    in_specs = (
        P("seq", None),
        P("seq", None),
        P(),
        P(None, "head"),
        P(None, "head"),
        P("head", None),
        P("head", "seq"),
        P("seq", "head"),
    )
    out_specs = P("seq", None)
    return jax.shard_map(shards, mesh=mesh, in_specs=in_specs, out_specs=out_specs, check_vma=False)
```

```python
import functools

import jax
import jax.numpy as jnp
from jax import lax
from jax.experimental import pallas as pl
from jax.experimental.pallas import tpu as pltpu
from jax.sharding import PartitionSpec as P

WIN_DEVS = 4
norm_eps = 1e-05
mix_eps = 1e-06
F32 = jnp.float32
BF16 = jnp.bfloat16
COLLECT = 50000
EXTRA = 16
NT = (((1,), (1,)), ((), ()))


def shape_of(shape, dtype):
    return jax.ShapeDtypeStruct(shape, dtype)


def local_call(body, outs, flops, moved, room, **more):
    return pl.pallas_call(
        body,
        out_shape=outs,
        compiler_params=pltpu.CompilerParams(vmem_limit_bytes=room * 1024 * 1024),
        cost_estimate=pl.CostEstimate(flops=flops, bytes_accessed=moved, transcendentals=0),
        **more,
    )


def shifted(value, axis, steps):
    count = lax.axis_size(axis)
    initial, last = (max(0, -steps), min(count, count - steps))
    return lax.ppermute(value, axis, [(source, source + steps) for source in range(initial, last)])


def rotated(value, axis):
    count = lax.axis_size(axis)
    parts = [value]
    for step in range(1, count):
        parts.append(lax.ppermute(value, axis, [(i, (i - step) % count) for i in range(count)]))
    return parts


def doubled(value, axis, group, gates):
    count = lax.axis_size(axis)
    near, bit = [value[None]], group // 2
    for gate in gates:
        near = list(lax.optimization_barrier((tuple(near), gate))[0])
        pairs = [(i, i ^ bit) for i in range(count)]
        if bit == 1:
            return near + [lax.ppermute(part, axis, pairs) for part in near]
        if len(near) > 1:
            near = [jnp.concatenate(near)]
        near.append(lax.ppermute(near[0], axis, pairs))
        bit //= 2


def assemble(place, out_ref, refs):
    group = out_ref.shape[0]
    entries = [(ref, j) for ref in refs for j in range(ref.shape[0])]
    for j, (ref, at) in enumerate(entries):
        distance, bit, rest = 0, group // 2, j
        while rest:
            distance += bit * (rest & 1)
            rest >>= 1
            bit //= 2
        out_ref[lax.bitwise_xor(place, jnp.int32(distance))] = ref[at]


def spread(value, axis):
    count = lax.axis_size(axis)
    copies = jnp.broadcast_to(value[None], (count,) + value.shape)
    return lax.all_to_all(copies, axis, 0, 0)


def columns_body(block_ref, qw_ref, kvw_ref, out_ref, piece_ref, q_tile, kv_tile, sems):
    tile = q_tile.shape[1]
    wide, narrow = qw_ref.shape[1], kvw_ref.shape[1]
    group = (wide + narrow) // out_ref.shape[1]
    place = lax.rem(block_ref[0], group)
    q_take, kv_take = wide // group, narrow // group
    q_at = place * q_take
    q_first = pl.multiple_of(q_at // tile * tile, tile)
    copies = [
        pltpu.make_async_copy(qw_ref.at[:, pl.ds(q_first, tile)], q_tile, sems.at[0]),
        pltpu.make_async_copy(kvw_ref, kv_tile, sems.at[1]),
    ]
    share = piece_ref.shape[0]
    if share:
        rows = pl.ds(pl.multiple_of(block_ref[0] * share, share), share)
        copies += [
            pltpu.make_async_copy(qw_ref.at[rows], piece_ref.at[:, :wide], sems.at[2]),
            pltpu.make_async_copy(kvw_ref.at[rows], piece_ref.at[:, wide:], sems.at[3]),
        ]
    for copy in copies:
        copy.start()
    first = 0
    for copy, ref, at, take in (
        (copies[0], q_tile, q_at - q_first, q_take),
        (copies[1], kv_tile, place * kv_take, kv_take),
    ):
        copy.wait()
        total = ref.shape[1]
        row = lax.broadcasted_iota(jnp.int32, (take, total), 0) + at
        pick = (row == lax.broadcasted_iota(jnp.int32, (take, total), 1)).astype(BF16)
        cols = lax.dot_general(pick, ref[...], NT, preferred_element_type=F32).astype(BF16)
        for k in range(out_ref.shape[0]):
            out_ref[k, first : first + take, :] = cols
        first += take
    for copy in copies[2:]:
        copy.wait()


def norm_body(z_ref, gain_ref, kvw_ref, hidden_ref, kv_ref, kvf_ref, inv_ref):
    z = z_ref[...].astype(F32)
    inverse = lax.rsqrt(jnp.mean(z * z, axis=1, keepdims=True) + norm_eps)
    hidden = (z * inverse * gain_ref[...]).astype(BF16)
    hidden_ref[...] = hidden
    kvf = jnp.dot(hidden, kvw_ref[...], preferred_element_type=F32)
    kvf_ref[...] = kvf
    kv_ref[...] = kvf.astype(BF16)
    inv_ref[...] = jnp.broadcast_to(inverse, inv_ref.shape)


def chain_body(cols_ref, ow_ref, gain_ref, out_ref):
    scaled = (ow_ref[...].astype(F32) * gain_ref[...]).astype(BF16)
    share = lax.dot_general(cols_ref[...], scaled, NT, preferred_element_type=F32)
    out_ref[...] = share.astype(BF16)


def whole_of(ref, head, wide):
    cut = wide // ref.shape[0]
    parts = [ref[s, head, :cut, :] for s in range(ref.shape[0])]
    parts += [ref[s, head, cut:, :] for s in range(ref.shape[0])]
    return jnp.concatenate(parts, axis=0)


def lanes_of(value, heads):
    size = value.shape[0] // heads
    return jnp.concatenate([value[i * size : (i + 1) * size] for i in range(heads)], axis=1)


def start_body(heads, hidden_ref, qw_ref, up_ref, z_ref, ow_ref, inv_ref, ao_ref,
               qf_ref, qt_ref, go_ref, nt_ref, aot_ref):
    qf = jnp.dot(hidden_ref[...], qw_ref[...], preferred_element_type=F32)
    qf_ref[...] = qf
    qt_ref[...] = lanes_of(qf.T, heads).astype(BF16)
    out = lax.dot_general(up_ref[...], ow_ref[...], NT, preferred_element_type=F32)
    go_ref[...] = lanes_of(out.T, heads)
    base = lax.dot_general(z_ref[...], ow_ref[...], NT, preferred_element_type=F32)
    nt_ref[...] = lanes_of((base * inv_ref[:, :1]).T, heads)
    aot_ref[...] = lanes_of(ao_ref[...].astype(F32).T, heads)


def pull(heads, scale, go, aot, qt, kvw_ref, probs, score_ref, own_ref, term_refs):
    e = go.shape[0]
    rows = go.shape[1] // heads
    row_terms = jnp.sum(go * aot, axis=0, keepdims=True)
    gob = go.astype(BF16)
    grad_prob = jnp.dot(kvw_ref[:, e:], gob, preferred_element_type=F32)
    grad_score = (probs.astype(F32) * (grad_prob - row_terms)).astype(BF16)
    score_ref[...] = grad_score
    grad_key = lax.dot_general(grad_score, qt, NT, preferred_element_type=F32) * scale
    grad_value = lax.dot_general(probs, gob, NT, preferred_element_type=F32)
    terms = jnp.concatenate([grad_key, grad_value], axis=1)
    for offset in range(1, len(term_refs) + 1):
        first = (len(term_refs) - offset) * rows
        term_refs[offset - 1][...] = terms[first : first + rows].astype(BF16)
    own_ref[...] = terms[len(term_refs) * rows :]


def query_body(heads, scale, kt_ref, score_ref, gq_ref):
    rows = gq_ref.shape[0]
    grad_query = jnp.dot(kt_ref[...], score_ref[...], preferred_element_type=F32) * scale
    parts = [grad_query[:, i * rows : (i + 1) * rows] for i in range(heads)]
    gq_ref[...] = jnp.concatenate(parts, axis=0).T.astype(BF16)


def first_body(heads, scale, block_ref, *refs):
    windows = refs[: WIN_DEVS + 1]
    qt_ref, go_ref, aot_ref, ln_ref = refs[WIN_DEVS + 1 : WIN_DEVS + 5]
    kvw_ref, kt_ref, probs_ref, score_ref, own_ref = refs[WIN_DEVS + 5 : WIN_DEVS + 10]
    term_refs = refs[WIN_DEVS + 10 :]
    rows = windows[0].shape[0]
    for place, ref in enumerate(windows):
        kvw_ref[place * rows : (place + 1) * rows, :] = ref[...]
    kvw = kvw_ref[...]
    e = kvw.shape[1] // 2
    kt_ref[...] = kvw.astype(F32).T[:e].astype(BF16)
    scores = jnp.dot(kvw[:, :e], qt_ref[...], preferred_element_type=F32) * scale
    norms = jnp.concatenate([ln_ref[i : i + 1, :] for i in range(heads)], axis=1)
    key_pos = lax.broadcasted_iota(jnp.int32, scores.shape, 0)
    query_pos = lax.broadcasted_iota(jnp.int32, scores.shape, 1) & (rows - 1)
    allowed = (key_pos > query_pos) & (key_pos <= query_pos + WIN_DEVS * rows)
    allowed = allowed & (key_pos >= (WIN_DEVS - block_ref[0]) * rows)
    probs = jnp.where(allowed, jnp.exp(scores - norms), 0.0).astype(BF16)
    probs_ref[...] = probs
    pull(heads, scale, go_ref[...], aot_ref[...], qt_ref[...], kvw_ref, probs,
         score_ref, own_ref, term_refs)


def next_body(heads, parts, scale, spot_ref, *refs):
    gq_refs = refs[:parts]
    msg_refs = refs[parts : 2 * parts]
    chain_refs = refs[2 * parts : 2 * parts + 4]
    inv_ref, nt_ref, qt_ref, aot_ref, kvw_ref, probs_ref = refs[2 * parts + 4 : 2 * parts + 10]
    score_ref, own_ref = refs[2 * parts + 10 : 2 * parts + 12]
    term_refs = refs[2 * parts + 12 : -1]
    chain_ref = refs[-1]
    assemble(spot_ref[1], chain_ref, chain_refs)
    rows, wide = gq_refs[0].shape
    narrow = msg_refs[0].shape[1]
    out = jnp.zeros((rows, wide), F32)
    along = jnp.zeros((EXTRA, rows), F32)
    for k in range(parts):
        chain = whole_of(chain_ref, lax.rem(spot_ref[0] + k, parts), wide)
        out += jnp.dot(gq_refs[k][...], chain[:wide], preferred_element_type=F32)
        msg = msg_refs[k][...]
        out += jnp.dot(msg[:rows], chain[wide:], preferred_element_type=F32)
        along += msg[rows:].astype(F32)
    along = jnp.sum(along, axis=0, keepdims=True)
    along = jnp.concatenate([along] * heads, axis=1)
    go = lanes_of((out * inv_ref[:, :1]).T, heads)
    inv_row = jnp.concatenate([inv_ref[...].T[:1, :]] * heads, axis=1)
    go = go - inv_row * along * nt_ref[...]
    pull(heads, scale, go, aot_ref[...], qt_ref[...], kvw_ref, probs_ref[...],
         score_ref, own_ref, term_refs)


def collect_body(width, own_ref, gq_ref, qf_ref, kvf_ref, *refs):
    msg_ref = refs[-1]
    rows = own_ref.shape[0]
    total = own_ref[...]
    for ref in refs[:-1]:
        total += ref[...].astype(F32)
    total = total.astype(BF16)
    msg_ref[:rows, :] = total
    prods = gq_ref[...].astype(F32) * qf_ref[...]
    partial = total.astype(F32) * kvf_ref[...]
    lanes = partial.shape[1]
    for first in range(0, prods.shape[1], lanes):
        partial += prods[:, first : first + lanes]
    along = jnp.sum(partial.T, axis=0, keepdims=True) * (1.0 / width)
    high = along.astype(BF16).astype(F32)
    place = lax.broadcasted_iota(jnp.int32, (EXTRA, rows), 0)
    extra = jnp.where(place == 0, high, jnp.where(place == 1, along - high, 0.0))
    msg_ref[rows:, :] = extra.astype(BF16)


def field_body(parts, steps, head_ref, *refs):
    count = parts * steps
    gq_refs = refs[:count]
    msg_refs = refs[count : 2 * count]
    w_refs = refs[2 * count : 2 * count + parts]
    z_ref, up_ref, gain_ref, inv_ref = refs[2 * count + parts : 2 * count + parts + 4]
    v_ref, tot_ref, lhs_ref, along_ref = refs[2 * count + parts + 4 :]
    rows, wide = gq_refs[0].shape
    cell = pl.program_id(0)

    @pl.when(cell == 0)
    def _():
        for step in range(steps):
            along = jnp.zeros((EXTRA, rows), F32)
            for k in range(parts):
                at = slice(step * rows, (step + 1) * rows)
                size = wide + msg_refs[0].shape[1]
                first = lax.rem(head_ref[0] + k, parts) * size
                gq_at = pl.ds(pl.multiple_of(first, 128), wide)
                lhs_ref[at, gq_at] = gq_refs[step * parts + k][...]
                msg = msg_refs[step * parts + k][...]
                msg_at = pl.ds(pl.multiple_of(first + wide, 128), msg.shape[1])
                lhs_ref[at, msg_at] = msg[:rows]
                along += msg[rows:].astype(F32)
            along = jnp.broadcast_to(jnp.sum(along, axis=0, keepdims=True), (rows, rows))
            along_ref[step * rows : (step + 1) * rows, :] = along.T
        tot_ref[...] = jnp.zeros_like(tot_ref)

    weight = jnp.concatenate([ref[0] for ref in w_refs], axis=1)
    y = lax.dot_general(lhs_ref[...], weight, NT, preferred_element_type=F32)
    inverse = inv_ref[:, :1]
    normed = z_ref[...].astype(F32) * inverse
    gain = gain_ref[...]
    fields = []
    for step in range(steps):
        at = slice(step * rows, (step + 1) * rows)
        field = inverse * (y[at] * gain - normed * along_ref[at, :1])
        v_ref[step] = field
        fields.append(field)
    first, second, third = fields
    change1 = first - up_ref[...].astype(F32)
    change2 = second - first
    change3 = third - second
    pairs = [
        (change1, first), (change1, change1), (change2, first), (change2, change2),
        (change2, second), (change2, change3), (change3, second), (change3, change3),
    ]
    sums = []
    for a, b in pairs:
        total = jnp.sum(a * b, axis=0, keepdims=True)
        lanes = tot_ref.shape[1]
        sums.append(sum(total[:, i : i + lanes] for i in range(0, total.shape[1], lanes)))
    tot_ref[...] += jnp.concatenate(sums, axis=0)


def mix_body(entries, tot_ref, up_ref, v_ref, out_ref):
    totals = jnp.sum(jnp.sum(tot_ref[...], axis=0), axis=1, keepdims=True) / entries
    s_r1, s_s, d2_v1, d2_d2, d2_v2, d2_d3, d3_v2, d3_d3 = [totals[i : i + 1] for i in range(8)]
    mix1 = s_r1 / (s_s + mix_eps)
    keep1 = 1.0 - mix1
    mix2 = keep1 * (d2_v1 + keep1 * d2_d2) / (keep1 * keep1 * d2_d2 + mix_eps)
    keep2 = keep1 * (1.0 - mix2)
    cross = mix1 * (d2_v2 + keep2 * d2_d3) + keep2 * (d3_v2 + keep2 * d3_d3)
    square = mix1 * mix1 * d2_d2 + 2.0 * mix1 * keep2 * d2_d3 + keep2 * keep2 * d3_d3
    mix3 = cross / (square + mix_eps)
    out_ref[...] = (
        up_ref[...].astype(F32)
        + v_ref[0]
        + (1.0 - mix3 * mix1) * v_ref[1]
        + keep2 * (1.0 - mix3) * v_ref[2]
    )


def shards(
    fixed_point,
    upstream,
    norm_gain,
    query_weight,
    keyval_weight,
    output_weight,
    log_norm,
    attention_out,
):
    rows, width = fixed_point.shape
    wide = query_weight.shape[1]
    narrow = keyval_weight.shape[1]
    size = wide + narrow
    e = narrow // 2
    heads = log_norm.shape[0]
    seq_count = lax.axis_size("seq")
    parts = lax.axis_size("head")
    block = lax.axis_index("seq")
    head = lax.axis_index("head")
    scale = e ** (-0.5)
    gain = norm_gain.reshape(1, width)
    span = (WIN_DEVS + 1) * rows
    group = min(8, seq_count)

    cols = size // group
    share = width // seq_count
    in_kernel = share % 16 == 0
    spot = jnp.stack([head, lax.rem(block, group)])
    smem = pl.BlockSpec(memory_space=pltpu.SMEM)
    vmem = pl.BlockSpec(memory_space=pltpu.VMEM)
    tile = 128 if wide % 128 == 0 and 128 % (wide // group) == 0 else wide
    own_cols, piece = local_call(
        columns_body,
        [
            shape_of((parts, cols, width), BF16),
            shape_of((share if in_kernel else 16, size), BF16),
        ],
        2 * width * size * cols,
        2 * width * (tile + narrow),
        6,
        in_specs=[smem] + [pl.BlockSpec(memory_space=pltpu.HBM)] * 2,
        scratch_shapes=[
            pltpu.VMEM((width, tile), BF16),
            pltpu.VMEM((width, narrow), BF16),
            pltpu.SemaphoreType.DMA((4,)),
        ],
    )(block.reshape(1), query_weight, keyval_weight)
    if not in_kernel:
        piece = jnp.concatenate(
            [
                lax.dynamic_slice_in_dim(weight, block * share, share, 0)
                for weight in (query_weight, keyval_weight)
            ],
            axis=1,
        )
    all_weight = lax.all_gather(piece, ("head", "seq"), tiled=True)
    all_weight = all_weight.reshape(parts, width, size)
    every_cols = lax.all_to_all(own_cols, "head", 0, 0)

    hidden, kv, kvf, inv = local_call(
        norm_body,
        [
            shape_of((rows, width), BF16),
            shape_of((rows, narrow), BF16),
            shape_of((rows, narrow), F32),
            shape_of((rows, rows), F32),
        ],
        2 * rows * width * narrow,
        2 * width * (2 * rows + narrow),
        8,
    )(fixed_point, gain, keyval_weight)
    earlier = [shifted(kv, "seq", offset) for offset in range(WIN_DEVS, 0, -1)]

    qf, qt, go, nt, aot = local_call(
        functools.partial(start_body, heads),
        [
            shape_of((rows, wide), F32),
            shape_of((e, heads * rows), BF16),
            shape_of((e, heads * rows), F32),
            shape_of((e, heads * rows), F32),
            shape_of((e, heads * rows), F32),
        ],
        6 * rows * width * wide,
        4 * width * (2 * rows + wide),
        10,
    )(hidden, query_weight, upstream, fixed_point, output_weight, inv, attention_out)

    pull_outs = [shape_of((span, heads * rows), BF16), shape_of((rows, narrow), F32)]
    pull_outs += [shape_of((rows, narrow), BF16)] * WIN_DEVS
    pull_flops = 6 * span * e * heads * rows

    def exchange(score, own, terms):
        arrived = [shifted(term, "seq", -offset - 1) for offset, term in enumerate(terms)]
        gq = local_call(
            functools.partial(query_body, heads, scale),
            shape_of((rows, wide), BF16),
            2 * span * e * heads * rows,
            span * heads * rows * 2,
            4,
        )(kt, score)
        every_gq = rotated(gq, "head")
        msg = local_call(
            functools.partial(collect_body, width),
            shape_of((rows + EXTRA, narrow), BF16),
            COLLECT * rows * size,
            rows * size * 4,
            4,
        )(own, gq, qf, kvf, *arrived)
        return every_gq, rotated(msg, "head"), msg, gq

    kvw, kt, probs, score, own, *terms = local_call(
        functools.partial(first_body, heads, scale),
        [
            shape_of((span, narrow), BF16),
            shape_of((e, span), BF16),
            shape_of((span, heads * rows), BF16),
        ]
        + pull_outs,
        pull_flops * 5 // 4,
        span * heads * rows * 2,
        16,
        in_specs=[smem] + [vmem] * (WIN_DEVS + 5),
    )(block.reshape(1), *earlier, kv, qt, go, aot, log_norm)
    all_gq, all_msg = [], []
    for step in range(3):
        if step:
            score, own, *terms = local_call(
                functools.partial(next_body, heads, parts, scale),
                pull_outs,
                pull_flops + 2 * rows * parts * size * wide,
                span * heads * rows * 2 + parts * size * wide * 2,
                16,
                in_specs=[smem] + [vmem] * (2 * parts + 10),
                scratch_shapes=[pltpu.VMEM((group, parts, cols, wide), BF16)],
            )(spot, *all_gq[-1], *all_msg[-1], *chain, inv, nt, qt, aot, kvw, probs)
        every_gq, every_msg, msg, gq = exchange(score, own, terms)
        all_gq.append(every_gq)
        all_msg.append(every_msg)
        if step == 0:
            every_cols, _ = lax.optimization_barrier((every_cols, gq))
            share = local_call(
                chain_body,
                shape_of((parts * cols, wide), BF16),
                2 * parts * cols * width * wide,
                2 * width * (wide + parts * cols),
                8,
            )(every_cols.reshape(parts * cols, width), output_weight, gain)
            share = share.reshape(parts, cols, wide)
            chain = doubled(share, "seq", group, (share, msg, (every_gq[1:], every_msg[1:3])))

    cell = 512 if width % 512 == 0 else width
    held = lambda shape: pl.BlockSpec(shape, lambda i: (0,) * len(shape))
    fields, totals = pl.pallas_call(
        functools.partial(field_body, parts, 3),
        grid=(width // cell,),
        in_specs=[smem]
        + [held((rows, wide))] * (3 * parts)
        + [held((rows + EXTRA, narrow))] * (3 * parts)
        + [
            *[pl.BlockSpec((1, cell, size), functools.partial(lambda k, i: (k, i, 0), k))
              for k in range(parts)],
            pl.BlockSpec((rows, cell), lambda i: (0, i)),
            pl.BlockSpec((rows, cell), lambda i: (0, i)),
            pl.BlockSpec((1, cell), lambda i: (0, i)),
            held((rows, rows)),
        ],
        out_specs=[
            pl.BlockSpec((3, rows, cell), lambda i: (0, 0, i)),
            held((8, 128)),
        ],
        out_shape=[shape_of((3, rows, width), F32), shape_of((8, 128), F32)],
        scratch_shapes=[
            pltpu.VMEM((3 * rows, parts * size), BF16),
            pltpu.VMEM((3 * rows, rows), F32),
        ],
        compiler_params=pltpu.CompilerParams(vmem_limit_bytes=50 * 1024 * 1024),
        cost_estimate=pl.CostEstimate(
            flops=6 * rows * parts * size * width,
            bytes_accessed=2 * parts * size * width,
            transcendentals=0,
        ),
    )(
        head.reshape(1),
        *[part for one in all_gq for part in one],
        *[part for one in all_msg for part in one],
        *[all_weight] * parts,
        fixed_point,
        upstream,
        gain,
        inv,
    )
    totals = spread(totals, "seq")
    return local_call(
        functools.partial(mix_body, rows * seq_count * width),
        shape_of((rows, width), F32),
        8 * rows * width,
        18 * rows * width,
        10,
    )(totals, upstream, fields)


def solution(mesh):
    in_specs = (
        P("seq", None),
        P("seq", None),
        P(),
        P(None, "head"),
        P(None, "head"),
        P("head", None),
        P("head", "seq"),
        P("seq", "head"),
    )
    out_specs = P("seq", None)
    return jax.shard_map(shards, mesh=mesh, in_specs=in_specs, out_specs=out_specs, check_vma=False)
```

```python
import functools

import jax
import jax.numpy as jnp
from jax import lax
from jax.experimental import pallas as pl
from jax.experimental.pallas import tpu as pltpu
from jax.sharding import PartitionSpec as P

WIN_DEVS = 4
norm_eps = 1e-05
mix_eps = 1e-06
F32 = jnp.float32
BF16 = jnp.bfloat16
COLLECT = 50000
EXTRA = 16
NT = (((1,), (1,)), ((), ()))


def shape_of(shape, dtype):
    return jax.ShapeDtypeStruct(shape, dtype)


def local_call(body, outs, flops, moved, room, **more):
    return pl.pallas_call(
        body,
        out_shape=outs,
        compiler_params=pltpu.CompilerParams(vmem_limit_bytes=room * 1024 * 1024),
        cost_estimate=pl.CostEstimate(flops=flops, bytes_accessed=moved, transcendentals=0),
        **more,
    )


def shifted(value, axis, steps):
    count = lax.axis_size(axis)
    initial, last = (max(0, -steps), min(count, count - steps))
    return lax.ppermute(value, axis, [(source, source + steps) for source in range(initial, last)])


def rotated(value, axis):
    count = lax.axis_size(axis)
    parts = [value]
    for step in range(1, count):
        parts.append(lax.ppermute(value, axis, [(i, (i - step) % count) for i in range(count)]))
    return parts


def doubled(value, axis, group, gates):
    count = lax.axis_size(axis)
    near, bit = [value[None]], group // 2
    for gate in gates:
        near = list(lax.optimization_barrier((tuple(near), gate))[0])
        pairs = [(i, i ^ bit) for i in range(count)]
        if bit == 1:
            return near + [lax.ppermute(part, axis, pairs) for part in near]
        if len(near) > 1:
            near = [jnp.concatenate(near)]
        near.append(lax.ppermute(near[0], axis, pairs))
        bit //= 2


def assemble(place, out_ref, refs):
    group = out_ref.shape[0]
    entries = [(ref, j) for ref in refs for j in range(ref.shape[0])]
    for j, (ref, at) in enumerate(entries):
        distance, bit, rest = 0, group // 2, j
        while rest:
            distance += bit * (rest & 1)
            rest >>= 1
            bit //= 2
        out_ref[lax.bitwise_xor(place, jnp.int32(distance))] = ref[at]


def spread(value, axis):
    count = lax.axis_size(axis)
    copies = jnp.broadcast_to(value[None], (count,) + value.shape)
    return lax.all_to_all(copies, axis, 0, 0)


def prep_body(block_ref, gain_ref, qw_ref, kvw_ref, z_ref, cols_ref, hidden_ref, kv_ref, kvf_ref,
              inv_ref, q_tile, kv_tile, z_tile, sems):
    tile = q_tile.shape[1]
    wide, narrow = qw_ref.shape[1], kvw_ref.shape[1]
    group = (wide + narrow) // cols_ref.shape[0]
    place = lax.rem(block_ref[0], group)
    q_take, kv_take = wide // group, narrow // group
    q_at = place * q_take
    q_first = pl.multiple_of(q_at // tile * tile, tile)
    copies = [
        pltpu.make_async_copy(qw_ref.at[:, pl.ds(q_first, tile)], q_tile, sems.at[0]),
        pltpu.make_async_copy(kvw_ref, kv_tile, sems.at[1]),
        pltpu.make_async_copy(z_ref, z_tile, sems.at[2]),
    ]
    for copy in copies:
        copy.start()
    first = 0
    for copy, ref, at, take in (
        (copies[0], q_tile, q_at - q_first, q_take),
        (copies[1], kv_tile, place * kv_take, kv_take),
    ):
        copy.wait()
        total = ref.shape[1]
        row = lax.broadcasted_iota(jnp.int32, (take, total), 0) + at
        pick = (row == lax.broadcasted_iota(jnp.int32, (take, total), 1)).astype(BF16)
        cols = lax.dot_general(pick, ref[...], NT, preferred_element_type=F32)
        cols_ref[first : first + take, :] = cols.astype(BF16)
        first += take
    copies[2].wait()
    z = z_tile[...].astype(F32)
    inverse = lax.rsqrt(jnp.mean(z * z, axis=1, keepdims=True) + norm_eps)
    hidden = (z * inverse * gain_ref[...]).astype(BF16)
    hidden_ref[...] = hidden
    kvf = jnp.dot(hidden, kv_tile[...], preferred_element_type=F32)
    kvf_ref[...] = kvf
    kv_ref[...] = kvf.astype(BF16)
    inv_ref[...] = jnp.broadcast_to(inverse, inv_ref.shape)


def chain_body(cols_ref, ow_ref, gain_ref, out_ref):
    scaled = (ow_ref[...].astype(F32) * gain_ref[...]).astype(BF16)
    share = lax.dot_general(cols_ref[...], scaled, NT, preferred_element_type=F32)
    out_ref[...] = share.astype(BF16)


def whole_of(ref, head, wide):
    cut = wide // ref.shape[0]
    parts = [ref[s, head, :cut, :] for s in range(ref.shape[0])]
    parts += [ref[s, head, cut:, :] for s in range(ref.shape[0])]
    return jnp.concatenate(parts, axis=0)


def lanes_of(value, heads):
    size = value.shape[0] // heads
    return jnp.concatenate([value[i * size : (i + 1) * size] for i in range(heads)], axis=1)


def start_body(heads, hidden_ref, inv_ref, qw_ref, ow_ref, up_ref, z_ref, ao_ref,
               qf_ref, qt_ref, go_ref, nt_ref, aot_ref,
               qw_tile, ow_tile, up_tile, z_tile, ao_tile, sems):
    copies = [
        pltpu.make_async_copy(source, target, sems.at[i])
        for i, (source, target) in enumerate(
            ((ow_ref, ow_tile), (up_ref, up_tile), (z_ref, z_tile), (qw_ref, qw_tile),
             (ao_ref, ao_tile))
        )
    ]
    for copy in copies:
        copy.start()
    for copy in copies[:3]:
        copy.wait()
    out = lax.dot_general(up_tile[...], ow_tile[...], NT, preferred_element_type=F32)
    go_ref[...] = lanes_of(out.T, heads)
    base = lax.dot_general(z_tile[...], ow_tile[...], NT, preferred_element_type=F32)
    nt_ref[...] = lanes_of((base * inv_ref[:, :1]).T, heads)
    copies[3].wait()
    qf = jnp.dot(hidden_ref[...], qw_tile[...], preferred_element_type=F32)
    qf_ref[...] = qf
    qt_ref[...] = lanes_of(qf.T, heads).astype(BF16)
    copies[4].wait()
    aot_ref[...] = lanes_of(ao_tile[...].astype(F32).T, heads)


def pull(heads, scale, go, aot, qt, kvw_ref, probs, score_ref, own_ref, term_refs):
    e = go.shape[0]
    rows = go.shape[1] // heads
    row_terms = jnp.sum(go * aot, axis=0, keepdims=True)
    gob = go.astype(BF16)
    grad_prob = jnp.dot(kvw_ref[:, e:], gob, preferred_element_type=F32)
    grad_score = (probs.astype(F32) * (grad_prob - row_terms)).astype(BF16)
    score_ref[...] = grad_score
    grad_key = lax.dot_general(grad_score, qt, NT, preferred_element_type=F32) * scale
    grad_value = lax.dot_general(probs, gob, NT, preferred_element_type=F32)
    terms = jnp.concatenate([grad_key, grad_value], axis=1)
    for offset in range(1, len(term_refs) + 1):
        first = (len(term_refs) - offset) * rows
        term_refs[offset - 1][...] = terms[first : first + rows].astype(BF16)
    own_ref[...] = terms[len(term_refs) * rows :]


def query_body(heads, scale, kt_ref, score_ref, gq_ref):
    rows = gq_ref.shape[0]
    grad_query = jnp.dot(kt_ref[...], score_ref[...], preferred_element_type=F32) * scale
    parts = [grad_query[:, i * rows : (i + 1) * rows] for i in range(heads)]
    gq_ref[...] = jnp.concatenate(parts, axis=0).T.astype(BF16)


def first_body(heads, scale, block_ref, *refs):
    windows = refs[: WIN_DEVS + 1]
    qt_ref, go_ref, aot_ref, ln_ref = refs[WIN_DEVS + 1 : WIN_DEVS + 5]
    kvw_ref, kt_ref, probs_ref, score_ref, own_ref = refs[WIN_DEVS + 5 : WIN_DEVS + 10]
    term_refs = refs[WIN_DEVS + 10 :]
    rows = windows[0].shape[0]
    for place, ref in enumerate(windows):
        kvw_ref[place * rows : (place + 1) * rows, :] = ref[...]
    kvw = kvw_ref[...]
    e = kvw.shape[1] // 2
    kt_ref[...] = kvw.astype(F32).T[:e].astype(BF16)
    scores = jnp.dot(kvw[:, :e], qt_ref[...], preferred_element_type=F32) * scale
    norms = jnp.concatenate([ln_ref[i : i + 1, :] for i in range(heads)], axis=1)
    key_pos = lax.broadcasted_iota(jnp.int32, scores.shape, 0)
    query_pos = lax.broadcasted_iota(jnp.int32, scores.shape, 1) & (rows - 1)
    allowed = (key_pos > query_pos) & (key_pos <= query_pos + WIN_DEVS * rows)
    allowed = allowed & (key_pos >= (WIN_DEVS - block_ref[0]) * rows)
    probs = jnp.where(allowed, jnp.exp(scores - norms), 0.0).astype(BF16)
    probs_ref[...] = probs
    pull(heads, scale, go_ref[...], aot_ref[...], qt_ref[...], kvw_ref, probs,
         score_ref, own_ref, term_refs)


def gather_up(parts, spot_ref, gq_refs, msg_refs, lhs_tile):
    rows = gq_refs[0].shape[0]
    along = jnp.zeros((EXTRA, rows), F32)
    for k in range(parts):
        msg = msg_refs[k][...]
        lhs = jnp.concatenate([gq_refs[k][...], msg[:rows]], axis=1)
        lhs_tile[lax.rem(spot_ref[0] + k, parts)] = lhs
        along += msg[rows:].astype(F32)
    return along


def next_body(heads, parts, scale, fresh, spot_ref, *refs):
    gq_refs = refs[:parts]
    msg_refs = refs[parts : 2 * parts]
    refs = refs[2 * parts :]
    inv_ref, nt_ref, qt_ref, aot_ref, kvw_ref, probs_ref, *refs = refs
    *refs, lhs_tile, sem = refs
    if fresh:
        *parts_refs, score_ref, own_ref, lhs_ref, row_ref, chain_ref = refs[:9]
        term_refs = refs[9:]
        assemble(spot_ref[1], chain_ref, parts_refs)
    else:
        chain_ref, score_ref, own_ref, lhs_ref, row_ref = refs[:5]
        term_refs = refs[5:]
    along = gather_up(parts, spot_ref, gq_refs, msg_refs, lhs_tile)
    row_ref[...] = along
    copy = pltpu.make_async_copy(lhs_tile, lhs_ref, sem)
    copy.start()
    rows, wide = gq_refs[0].shape
    out = jnp.zeros((rows, wide), F32)
    for k in range(parts):
        chain = whole_of(chain_ref, lax.bitwise_xor(jnp.int32(k), spot_ref[0]), wide)
        out += jnp.dot(lhs_tile[k], chain, preferred_element_type=F32)
    along = jnp.sum(along, axis=0, keepdims=True)
    along = jnp.concatenate([along] * heads, axis=1)
    go = lanes_of((out * inv_ref[:, :1]).T, heads)
    inv_row = jnp.concatenate([inv_ref[...].T[:1, :]] * heads, axis=1)
    go = go - inv_row * along * nt_ref[...]
    pull(heads, scale, go, aot_ref[...], qt_ref[...], kvw_ref, probs_ref[...],
         score_ref, own_ref, term_refs)
    copy.wait()


def pack_body(parts, spot_ref, *refs):
    lhs_ref, row_ref, lhs_tile, sem = refs[2 * parts :]
    row_ref[...] = gather_up(parts, spot_ref, refs[:parts], refs[parts : 2 * parts], lhs_tile)
    copy = pltpu.make_async_copy(lhs_tile, lhs_ref, sem)
    copy.start()
    copy.wait()


def collect_body(width, own_ref, gq_ref, qf_ref, kvf_ref, *refs):
    msg_ref = refs[-1]
    rows = own_ref.shape[0]
    total = own_ref[...]
    for ref in refs[:-1]:
        total += ref[...].astype(F32)
    total = total.astype(BF16)
    msg_ref[:rows, :] = total
    prods = gq_ref[...].astype(F32) * qf_ref[...]
    partial = total.astype(F32) * kvf_ref[...]
    lanes = partial.shape[1]
    for first in range(0, prods.shape[1], lanes):
        partial += prods[:, first : first + lanes]
    along = jnp.sum(partial.T, axis=0, keepdims=True) * (1.0 / width)
    high = along.astype(BF16).astype(F32)
    place = lax.broadcasted_iota(jnp.int32, (EXTRA, rows), 0)
    extra = jnp.where(place == 0, high, jnp.where(place == 1, along - high, 0.0))
    msg_ref[rows:, :] = extra.astype(BF16)


def field_body(parts, steps, wide, *refs):
    packed = refs[: 2 * steps]
    w_ref, z_ref, up_ref, gain_ref, inv_ref, v_ref, tot_ref, lhs_ref, along_ref = refs[
        2 * steps :
    ]
    rows = packed[0].shape[1]
    cell = pl.program_id(0)

    @pl.when(cell == 0)
    def _():
        for step in range(steps):
            at = slice(step * rows, (step + 1) * rows)
            for k in range(parts):
                lhs_ref[k, at, :] = packed[2 * step][k]
            along = jnp.sum(packed[2 * step + 1][...], axis=0, keepdims=True)
            along = jnp.broadcast_to(along, (rows, rows))
            along_ref[at, :] = along.T
        tot_ref[...] = jnp.zeros_like(tot_ref)

    y = jnp.zeros((steps * rows, v_ref.shape[2]), F32)
    cut = wide // w_ref.shape[1]
    for k in range(parts):
        weight = [w_ref[k, s, :cut, :] for s in range(w_ref.shape[1])]
        weight += [w_ref[k, s, cut:, :] for s in range(w_ref.shape[1])]
        weight = jnp.concatenate(weight, axis=0)
        y += jnp.dot(lhs_ref[k], weight, preferred_element_type=F32)
    inverse = inv_ref[:, :1]
    normed = z_ref[...].astype(F32) * inverse
    gain = gain_ref[...]
    fields = []
    for step in range(steps):
        at = slice(step * rows, (step + 1) * rows)
        field = inverse * (y[at] * gain - normed * along_ref[at, :1])
        v_ref[step] = field
        fields.append(field)
    first, second, third = fields
    change1 = first - up_ref[...].astype(F32)
    change2 = second - first
    change3 = third - second
    pairs = [
        (change1, first), (change1, change1), (change2, first), (change2, change2),
        (change2, second), (change2, change3), (change3, second), (change3, change3),
    ]
    sums = []
    for a, b in pairs:
        total = jnp.sum(a * b, axis=0, keepdims=True)
        lanes = tot_ref.shape[1]
        sums.append(sum(total[:, i : i + lanes] for i in range(0, total.shape[1], lanes)))
    tot_ref[...] += jnp.concatenate(sums, axis=0)


def mix_body(entries, tot_ref, up_ref, v_ref, out_ref):
    totals = jnp.sum(jnp.sum(tot_ref[...], axis=0), axis=1, keepdims=True) / entries
    s_r1, s_s, d2_v1, d2_d2, d2_v2, d2_d3, d3_v2, d3_d3 = [totals[i : i + 1] for i in range(8)]
    mix1 = s_r1 / (s_s + mix_eps)
    keep1 = 1.0 - mix1
    mix2 = keep1 * (d2_v1 + keep1 * d2_d2) / (keep1 * keep1 * d2_d2 + mix_eps)
    keep2 = keep1 * (1.0 - mix2)
    cross = mix1 * (d2_v2 + keep2 * d2_d3) + keep2 * (d3_v2 + keep2 * d3_d3)
    square = mix1 * mix1 * d2_d2 + 2.0 * mix1 * keep2 * d2_d3 + keep2 * keep2 * d3_d3
    mix3 = cross / (square + mix_eps)
    out_ref[...] = (
        up_ref[...].astype(F32)
        + v_ref[0]
        + (1.0 - mix3 * mix1) * v_ref[1]
        + keep2 * (1.0 - mix3) * v_ref[2]
    )


def shards(
    fixed_point,
    upstream,
    norm_gain,
    query_weight,
    keyval_weight,
    output_weight,
    log_norm,
    attention_out,
):
    rows, width = fixed_point.shape
    wide = query_weight.shape[1]
    narrow = keyval_weight.shape[1]
    size = wide + narrow
    e = narrow // 2
    heads = log_norm.shape[0]
    seq_count = lax.axis_size("seq")
    parts = lax.axis_size("head")
    block = lax.axis_index("seq")
    head = lax.axis_index("head")
    scale = e ** (-0.5)
    gain = norm_gain.reshape(1, width)
    span = (WIN_DEVS + 1) * rows
    group = min(8, seq_count)

    cols = size // group
    spot = jnp.stack([head, lax.rem(block, group)])
    smem = pl.BlockSpec(memory_space=pltpu.SMEM)
    vmem = pl.BlockSpec(memory_space=pltpu.VMEM)
    hbm = pl.BlockSpec(memory_space=pltpu.HBM)

    def pinned(value):
        return pltpu.with_memory_space_constraint(value, pltpu.HBM)

    tile = 128 if wide % 128 == 0 and 128 % (wide // group) == 0 else wide
    own_cols, hidden, kv, kvf, inv = local_call(
        prep_body,
        [
            shape_of((cols, width), BF16),
            shape_of((rows, width), BF16),
            shape_of((rows, narrow), BF16),
            shape_of((rows, narrow), F32),
            shape_of((rows, rows), F32),
        ],
        2 * width * size * cols,
        2 * width * (tile + narrow + rows),
        10,
        in_specs=[smem, vmem] + [hbm] * 3,
        scratch_shapes=[
            pltpu.VMEM((width, tile), BF16),
            pltpu.VMEM((width, narrow), BF16),
            pltpu.VMEM((rows, width), BF16),
            pltpu.SemaphoreType.DMA((3,)),
        ],
    )(block.reshape(1), gain, pinned(query_weight), pinned(keyval_weight), pinned(fixed_point))
    if group == seq_count:
        all_weight = lax.all_gather(own_cols, ("head", "seq"))
    else:
        share = width // seq_count
        piece = [
            lax.dynamic_slice_in_dim(weight, block * share, share, 0).reshape(share, group, -1)
            for weight in (query_weight, keyval_weight)
        ]
        piece = jnp.concatenate(piece, axis=2)
        all_weight = lax.all_gather(piece, ("head", "seq"))
        all_weight = all_weight.reshape(parts, width, group, cols).transpose(0, 2, 3, 1)
    all_weight = all_weight.reshape(parts, group, cols, width)
    every_cols, bit = own_cols[None], 1
    while bit < parts:
        pairs = [(i, i ^ bit) for i in range(parts)]
        other = lax.ppermute(every_cols, "head", pairs)
        every_cols = jnp.concatenate([every_cols, other])
        bit *= 2
    earlier = [shifted(kv, "seq", offset) for offset in range(WIN_DEVS, 0, -1)]

    qf, qt, go, nt, aot = local_call(
        functools.partial(start_body, heads),
        [
            shape_of((rows, wide), F32),
            shape_of((e, heads * rows), BF16),
            shape_of((e, heads * rows), F32),
            shape_of((e, heads * rows), F32),
            shape_of((e, heads * rows), F32),
        ],
        6 * rows * width * wide,
        4 * width * (2 * rows + wide),
        14,
        in_specs=[vmem] * 2 + [hbm] * 5,
        scratch_shapes=[
            pltpu.VMEM((width, wide), BF16),
            pltpu.VMEM((wide, width), BF16),
            pltpu.VMEM((rows, width), BF16),
            pltpu.VMEM((rows, width), BF16),
            pltpu.VMEM((rows, wide), BF16),
            pltpu.SemaphoreType.DMA((5,)),
        ],
    )(
        hidden,
        inv,
        pinned(query_weight),
        pinned(output_weight),
        pinned(upstream),
        pinned(fixed_point),
        pinned(attention_out),
    )

    pull_outs = [shape_of((span, heads * rows), BF16), shape_of((rows, narrow), F32)]
    pull_outs += [shape_of((rows, narrow), BF16)] * WIN_DEVS
    pull_flops = 6 * span * e * heads * rows

    def exchange(score, own, terms):
        arrived = [shifted(term, "seq", -offset - 1) for offset, term in enumerate(terms)]
        gq = local_call(
            functools.partial(query_body, heads, scale),
            shape_of((rows, wide), BF16),
            2 * span * e * heads * rows,
            span * heads * rows * 2,
            4,
        )(kt, score)
        every_gq = rotated(gq, "head")
        msg = local_call(
            functools.partial(collect_body, width),
            shape_of((rows + EXTRA, narrow), BF16),
            COLLECT * rows * size,
            rows * size * 4,
            4,
        )(own, gq, qf, kvf, *arrived)
        return every_gq, rotated(msg, "head"), msg, gq

    kvw, kt, probs, score, own, *terms = local_call(
        functools.partial(first_body, heads, scale),
        [
            shape_of((span, narrow), BF16),
            shape_of((e, span), BF16),
            shape_of((span, heads * rows), BF16),
        ]
        + pull_outs,
        pull_flops * 5 // 4,
        span * heads * rows * 2,
        16,
        in_specs=[smem] + [vmem] * (WIN_DEVS + 5),
    )(block.reshape(1), *earlier, kv, qt, go, aot, log_norm)
    packed = []
    lhs_outs = [pltpu.HBM((parts, rows, size), BF16), shape_of((EXTRA, rows), F32)]
    lhs_scratch = [pltpu.VMEM((parts, rows, size), BF16), pltpu.SemaphoreType.DMA(())]
    chain_shape = shape_of((group, parts, cols, wide), BF16)
    for step in range(3):
        if step:
            score, own, lhs, row, *terms = local_call(
                functools.partial(next_body, heads, parts, scale, step == 1),
                pull_outs[:2]
                + lhs_outs
                + [chain_shape] * (step == 1)
                + pull_outs[2:],
                pull_flops + 2 * rows * parts * size * wide,
                span * heads * rows * 2 + parts * size * wide * 2,
                16,
                in_specs=[smem] + [vmem] * (2 * parts + 6 + len(chain)),
                out_specs=[vmem] * 2 + [hbm] + [vmem] * (1 + (step == 1) + WIN_DEVS),
                scratch_shapes=lhs_scratch,
            )(spot, *every_gq, *every_msg, inv, nt, qt, aot, kvw, probs, *chain)
            packed += [lhs, row]
            if step == 1:
                chain, *terms = terms
                chain = [chain]
        every_gq, every_msg, msg, gq = exchange(score, own, terms)
        if step == 0:
            every_cols, _ = lax.optimization_barrier((every_cols, gq))
            share = local_call(
                chain_body,
                shape_of((parts * cols, wide), BF16),
                2 * parts * cols * width * wide,
                2 * width * (wide + parts * cols),
                8,
            )(every_cols.reshape(parts * cols, width), output_weight, gain)
            share = share.reshape(parts, cols, wide)
            chain = doubled(share, "seq", group, (share, msg, (every_gq[1:], every_msg[1:])))

    packed += local_call(
        functools.partial(pack_body, parts),
        lhs_outs,
        0,
        parts * rows * size * 4,
        4,
        in_specs=[smem] + [vmem] * (2 * parts),
        out_specs=[hbm, vmem],
        scratch_shapes=lhs_scratch,
    )(spot, *every_gq, *every_msg)

    cell = 512 if width % 512 == 0 else width
    held = lambda shape: pl.BlockSpec(shape, lambda i: (0,) * len(shape))
    fields, totals = pl.pallas_call(
        functools.partial(field_body, parts, 3, wide),
        grid=(width // cell,),
        in_specs=[held((parts, rows, size)), held((EXTRA, rows))] * 3
        + [
            pl.BlockSpec((parts, group, cols, cell), lambda i: (0, 0, 0, i)),
            pl.BlockSpec((rows, cell), lambda i: (0, i)),
            pl.BlockSpec((rows, cell), lambda i: (0, i)),
            pl.BlockSpec((1, cell), lambda i: (0, i)),
            held((rows, rows)),
        ],
        out_specs=[
            pl.BlockSpec((3, rows, cell), lambda i: (0, 0, i)),
            held((8, 128)),
        ],
        out_shape=[shape_of((3, rows, width), F32), shape_of((8, 128), F32)],
        scratch_shapes=[
            pltpu.VMEM((parts, 3 * rows, size), BF16),
            pltpu.VMEM((3 * rows, rows), F32),
        ],
        compiler_params=pltpu.CompilerParams(vmem_limit_bytes=32 * 1024 * 1024),
        cost_estimate=pl.CostEstimate(
            flops=6 * rows * parts * size * width,
            bytes_accessed=2 * parts * size * width,
            transcendentals=0,
        ),
    )(
        *[pinned(part) for part in packed],
        pinned(all_weight),
        pinned(fixed_point),
        pinned(upstream),
        gain,
        pinned(inv),
    )
    totals = spread(totals, "seq")
    return local_call(
        functools.partial(mix_body, rows * seq_count * width),
        shape_of((rows, width), F32),
        8 * rows * width,
        18 * rows * width,
        10,
    )(totals, upstream, fields)


def solution(mesh):
    in_specs = (
        P("seq", None),
        P("seq", None),
        P(),
        P(None, "head"),
        P(None, "head"),
        P("head", None),
        P("head", "seq"),
        P("seq", "head"),
    )
    out_specs = P("seq", None)
    return jax.shard_map(shards, mesh=mesh, in_specs=in_specs, out_specs=out_specs, check_vma=False)
```

```python
import functools

import jax
import jax.numpy as jnp
from jax import lax
from jax.experimental import pallas as pl
from jax.experimental.pallas import tpu as pltpu
from jax.sharding import PartitionSpec as P

WIN_DEVS = 4
norm_eps = 1e-05
mix_eps = 1e-06
F32 = jnp.float32
BF16 = jnp.bfloat16
COLLECT = 50000
EXTRA = 16
NT = (((1,), (1,)), ((), ()))


def shape_of(shape, dtype):
    return jax.ShapeDtypeStruct(shape, dtype)


def local_call(body, outs, flops, moved, room, **more):
    return pl.pallas_call(
        body,
        out_shape=outs,
        compiler_params=pltpu.CompilerParams(vmem_limit_bytes=room * 1024 * 1024),
        cost_estimate=pl.CostEstimate(flops=flops, bytes_accessed=moved, transcendentals=0),
        **more,
    )


def shifted(value, axis, steps):
    count = lax.axis_size(axis)
    initial, last = (max(0, -steps), min(count, count - steps))
    return lax.ppermute(value, axis, [(source, source + steps) for source in range(initial, last)])


def rotated(value, axis):
    count = lax.axis_size(axis)
    parts = [value]
    for step in range(1, count):
        parts.append(lax.ppermute(value, axis, [(i, (i - step) % count) for i in range(count)]))
    return parts


def doubled(value, axis, group, gates):
    count = lax.axis_size(axis)
    near, bit = [value[None]], group // 2
    for gate in gates:
        near = list(lax.optimization_barrier((tuple(near), gate))[0])
        pairs = [(i, i ^ bit) for i in range(count)]
        if bit == 1:
            return near + [lax.ppermute(part, axis, pairs) for part in near]
        if len(near) > 1:
            near = [jnp.concatenate(near)]
        near.append(lax.ppermute(near[0], axis, pairs))
        bit //= 2


def assemble(place, wide, out_ref, refs):
    group = sum(ref.shape[0] for ref in refs)
    cut = wide // group
    rest_cut = refs[0].shape[2] - cut
    entries = [(ref, j) for ref in refs for j in range(ref.shape[0])]
    for j, (ref, at) in enumerate(entries):
        distance, bit, rest = 0, group // 2, j
        while rest:
            distance += bit * (rest & 1)
            rest >>= 1
            bit //= 2
        index = lax.bitwise_xor(place, jnp.int32(distance))
        first = pl.multiple_of(index * cut, cut)
        second = pl.multiple_of(wide + index * rest_cut, rest_cut)
        for k in range(out_ref.shape[0]):
            out_ref[k, pl.ds(first, cut), :] = ref[at, k, :cut, :]
            out_ref[k, pl.ds(second, rest_cut), :] = ref[at, k, cut:, :]


def prep_body(block_ref, gain_ref, qw_ref, kvw_ref, z_ref, cols_ref, hidden_ref, kv_ref, kvf_ref,
              inv_ref, q_tile, kv_tile, z_tile, sems):
    tile = q_tile.shape[1]
    wide, narrow = qw_ref.shape[1], kvw_ref.shape[1]
    group = (wide + narrow) // cols_ref.shape[0]
    place = lax.rem(block_ref[0], group)
    q_take, kv_take = wide // group, narrow // group
    q_at = place * q_take
    q_first = pl.multiple_of(q_at // tile * tile, tile)
    copies = [
        pltpu.make_async_copy(qw_ref.at[:, pl.ds(q_first, tile)], q_tile, sems.at[0]),
        pltpu.make_async_copy(kvw_ref, kv_tile, sems.at[1]),
        pltpu.make_async_copy(z_ref, z_tile, sems.at[2]),
    ]
    for copy in copies:
        copy.start()
    first = 0
    for copy, ref, at, take in (
        (copies[0], q_tile, q_at - q_first, q_take),
        (copies[1], kv_tile, place * kv_take, kv_take),
    ):
        copy.wait()
        total = ref.shape[1]
        row = lax.broadcasted_iota(jnp.int32, (take, total), 0) + at
        pick = (row == lax.broadcasted_iota(jnp.int32, (take, total), 1)).astype(BF16)
        cols = lax.dot_general(pick, ref[...], NT, preferred_element_type=F32)
        cols_ref[first : first + take, :] = cols.astype(BF16)
        first += take
    copies[2].wait()
    z = z_tile[...].astype(F32)
    inverse = lax.rsqrt(jnp.mean(z * z, axis=1, keepdims=True) + norm_eps)
    hidden = (z * inverse * gain_ref[...]).astype(BF16)
    hidden_ref[...] = hidden
    kvf = jnp.dot(hidden, kv_tile[...], preferred_element_type=F32)
    kvf_ref[...] = kvf
    kv_ref[...] = kvf.astype(BF16)
    inv_ref[...] = jnp.broadcast_to(inverse, inv_ref.shape)


def chain_body(cols_ref, ow_ref, gain_ref, out_ref):
    scaled = (ow_ref[...].astype(F32) * gain_ref[...]).astype(BF16)
    share = lax.dot_general(cols_ref[...], scaled, NT, preferred_element_type=F32)
    out_ref[...] = share.astype(BF16)


def lanes_of(value, heads):
    size = value.shape[0] // heads
    return jnp.concatenate([value[i * size : (i + 1) * size] for i in range(heads)], axis=1)


def start_body(heads, hidden_ref, inv_ref, qw_ref, ow_ref, up_ref, z_ref, ao_ref,
               qf_ref, qt_ref, go_ref, nt_ref, aot_ref,
               qw_tile, ow_tile, up_tile, z_tile, ao_tile, sems):
    copies = [
        pltpu.make_async_copy(source, target, sems.at[i])
        for i, (source, target) in enumerate(
            ((ow_ref, ow_tile), (up_ref, up_tile), (z_ref, z_tile), (qw_ref, qw_tile),
             (ao_ref, ao_tile))
        )
    ]
    for copy in copies:
        copy.start()
    for copy in copies[:3]:
        copy.wait()
    out = lax.dot_general(up_tile[...], ow_tile[...], NT, preferred_element_type=F32)
    go_ref[...] = lanes_of(out.T, heads)
    base = lax.dot_general(z_tile[...], ow_tile[...], NT, preferred_element_type=F32)
    nt_ref[...] = lanes_of((base * inv_ref[:, :1]).T, heads)
    copies[3].wait()
    qf = jnp.dot(hidden_ref[...], qw_tile[...], preferred_element_type=F32)
    qf_ref[...] = qf
    qt_ref[...] = lanes_of(qf.T, heads).astype(BF16)
    copies[4].wait()
    aot_ref[...] = lanes_of(ao_tile[...].astype(F32).T, heads)


def pull(heads, scale, go, aot, qt, kvw_ref, probs, score_ref, own_ref, term_refs):
    e = go.shape[0]
    rows = go.shape[1] // heads
    row_terms = jnp.sum(go * aot, axis=0, keepdims=True)
    gob = go.astype(BF16)
    grad_prob = jnp.dot(kvw_ref[:, e:], gob, preferred_element_type=F32)
    grad_score = (probs.astype(F32) * (grad_prob - row_terms)).astype(BF16)
    score_ref[...] = grad_score
    grad_key = lax.dot_general(grad_score, qt, NT, preferred_element_type=F32) * scale
    grad_value = lax.dot_general(probs, gob, NT, preferred_element_type=F32)
    terms = jnp.concatenate([grad_key, grad_value], axis=1)
    for offset in range(1, len(term_refs) + 1):
        first = (len(term_refs) - offset) * rows
        term_refs[offset - 1][...] = terms[first : first + rows].astype(BF16)
    own_ref[...] = terms[len(term_refs) * rows :]


def query_body(heads, scale, kt_ref, score_ref, gq_ref):
    rows = gq_ref.shape[0]
    grad_query = jnp.dot(kt_ref[...], score_ref[...], preferred_element_type=F32) * scale
    parts = [grad_query[:, i * rows : (i + 1) * rows] for i in range(heads)]
    gq_ref[...] = jnp.concatenate(parts, axis=0).T.astype(BF16)


def first_body(heads, scale, block_ref, *refs):
    windows = refs[: WIN_DEVS + 1]
    qt_ref, go_ref, aot_ref, ln_ref = refs[WIN_DEVS + 1 : WIN_DEVS + 5]
    kvw_ref, kt_ref, probs_ref, score_ref, own_ref = refs[WIN_DEVS + 5 : WIN_DEVS + 10]
    term_refs = refs[WIN_DEVS + 10 :]
    rows = windows[0].shape[0]
    for place, ref in enumerate(windows):
        kvw_ref[place * rows : (place + 1) * rows, :] = ref[...]
    kvw = kvw_ref[...]
    e = kvw.shape[1] // 2
    kt_ref[...] = kvw.astype(F32).T[:e].astype(BF16)
    scores = jnp.dot(kvw[:, :e], qt_ref[...], preferred_element_type=F32) * scale
    norms = jnp.concatenate([ln_ref[i : i + 1, :] for i in range(heads)], axis=1)
    key_pos = lax.broadcasted_iota(jnp.int32, scores.shape, 0)
    query_pos = lax.broadcasted_iota(jnp.int32, scores.shape, 1) & (rows - 1)
    allowed = (key_pos > query_pos) & (key_pos <= query_pos + WIN_DEVS * rows)
    allowed = allowed & (key_pos >= (WIN_DEVS - block_ref[0]) * rows)
    probs = jnp.where(allowed, jnp.exp(scores - norms), 0.0).astype(BF16)
    probs_ref[...] = probs
    pull(heads, scale, go_ref[...], aot_ref[...], qt_ref[...], kvw_ref, probs,
         score_ref, own_ref, term_refs)


def gather_up(parts, spot_ref, msg_refs, lhs_tile):
    rows = lhs_tile.shape[1]
    along = jnp.zeros((EXTRA, rows), F32)
    for k in range(parts):
        msg = msg_refs[k][...]
        lhs_tile[lax.rem(spot_ref[0] + k, parts)] = msg[:rows]
        along += msg[rows:, :rows].astype(F32)
    return along


def next_body(heads, parts, scale, fresh, spot_ref, *refs):
    msg_refs, refs = refs[:parts], refs[parts:]
    inv_ref, nt_ref, qt_ref, aot_ref, kvw_ref, probs_ref, *refs = refs
    if fresh:
        *parts_refs, score_ref, own_ref, lhs_ref, row_ref, chain_ref = refs[:9]
        term_refs = refs[9:]
        assemble(spot_ref[1], chain_ref.shape[2], chain_ref, parts_refs)
    else:
        chain_ref, score_ref, own_ref, lhs_ref, row_ref = refs[:5]
        term_refs = refs[5:]
    along = gather_up(parts, spot_ref, msg_refs, lhs_ref)
    row_ref[...] = along
    rows, wide = lhs_ref.shape[1], chain_ref.shape[2]
    out = jnp.zeros((rows, wide), F32)
    for k in range(parts):
        chain = chain_ref[lax.bitwise_xor(jnp.int32(k), spot_ref[0])]
        out += jnp.dot(lhs_ref[k], chain, preferred_element_type=F32)
    along = jnp.sum(along, axis=0, keepdims=True)
    along = jnp.concatenate([along] * heads, axis=1)
    go = lanes_of((out * inv_ref[:, :1]).T, heads)
    inv_row = jnp.concatenate([inv_ref[...].T[:1, :]] * heads, axis=1)
    go = go - inv_row * along * nt_ref[...]
    pull(heads, scale, go, aot_ref[...], qt_ref[...], kvw_ref, probs_ref[...],
         score_ref, own_ref, term_refs)


def collect_body(width, own_ref, gq_ref, qf_ref, kvf_ref, *refs):
    msg_ref = refs[-1]
    rows = own_ref.shape[0]
    total = own_ref[...]
    for ref in refs[:-1]:
        total += ref[...].astype(F32)
    total = total.astype(BF16)
    wide = gq_ref.shape[1]
    msg_ref[:rows, :wide] = gq_ref[...]
    msg_ref[:rows, wide:] = total
    prods = gq_ref[...].astype(F32) * qf_ref[...]
    partial = total.astype(F32) * kvf_ref[...]
    lanes = partial.shape[1]
    for first in range(0, prods.shape[1], lanes):
        partial += prods[:, first : first + lanes]
    along = jnp.sum(partial.T, axis=0, keepdims=True) * (1.0 / width)
    high = along.astype(BF16).astype(F32)
    place = lax.broadcasted_iota(jnp.int32, (EXTRA, rows), 0)
    extra = jnp.where(place == 0, high, jnp.where(place == 1, along - high, 0.0))
    msg_ref[rows:, :] = jnp.zeros((EXTRA, msg_ref.shape[1]), BF16)
    msg_ref[rows:, :rows] = extra.astype(BF16)


def field_body(parts, wide, spot_ref, *refs):
    msg_refs, refs = refs[:parts], refs[parts:]
    lhs1_ref, row1_ref, lhs2_ref, row2_ref, *refs = refs
    *w_refs, z_ref, up_ref, gain_ref, inv_ref, v_ref, tot_ref, lhs3_ref, w_ref = refs
    rows, part = v_ref.shape[1:]
    head = spot_ref[0]
    row3 = gather_up(parts, spot_ref, msg_refs, lhs3_ref)
    assemble(spot_ref[1], wide, w_ref, w_refs)
    y = jnp.zeros((3 * rows, part), F32)
    for k in range(parts):
        lhs = jnp.concatenate([lhs1_ref[k], lhs2_ref[k], lhs3_ref[k]], axis=0)
        weight = w_ref[lax.bitwise_xor(jnp.int32(k), head)]
        y += jnp.dot(lhs, weight, preferred_element_type=F32)
    at = pl.ds(pl.multiple_of(head * part, part), part)
    inverse = inv_ref[:, :1]
    normed = z_ref[:, at].astype(F32) * inverse
    gain = gain_ref[:, at]
    fields = []
    for step, row in enumerate((row1_ref[...], row2_ref[...], row3)):
        along = jnp.broadcast_to(jnp.sum(row, axis=0, keepdims=True), (rows, rows)).T[:, :1]
        y_step = y[step * rows : (step + 1) * rows]
        fields.append(inverse * (y_step * gain - normed * along))
        v_ref[step] = fields[step]
    first, second, third = fields
    change1 = first - up_ref[:, at].astype(F32)
    change2 = second - first
    change3 = third - second
    pairs = [
        (change1, first), (change1, change1), (change2, first), (change2, change2),
        (change2, second), (change2, change3), (change3, second), (change3, change3),
    ]
    lanes = tot_ref.shape[2]
    sums = []
    for a, b in pairs:
        total = jnp.sum(a * b, axis=0, keepdims=True)
        sums.append(sum(total[:, i : i + lanes] for i in range(0, part, lanes)))
    totals = jnp.concatenate(sums, axis=0)
    for k in range(tot_ref.shape[0]):
        tot_ref[k] = totals


def mix_body(entries, spot_ref, tot_ref, up_ref, v_ref, out_ref):
    totals = jnp.sum(jnp.sum(tot_ref[...], axis=0), axis=1, keepdims=True) / entries
    s_r1, s_s, d2_v1, d2_d2, d2_v2, d2_d3, d3_v2, d3_d3 = [totals[i : i + 1] for i in range(8)]
    mix1 = s_r1 / (s_s + mix_eps)
    keep1 = 1.0 - mix1
    mix2 = keep1 * (d2_v1 + keep1 * d2_d2) / (keep1 * keep1 * d2_d2 + mix_eps)
    keep2 = keep1 * (1.0 - mix2)
    cross = mix1 * (d2_v2 + keep2 * d2_d3) + keep2 * (d3_v2 + keep2 * d3_d3)
    square = mix1 * mix1 * d2_d2 + 2.0 * mix1 * keep2 * d2_d3 + keep2 * keep2 * d3_d3
    mix3 = cross / (square + mix_eps)
    part = out_ref.shape[1]
    at = pl.ds(pl.multiple_of(spot_ref[0] * part, part), part)
    mixed = (
        up_ref[:, at].astype(F32)
        + v_ref[0]
        + (1.0 - mix3 * mix1) * v_ref[1]
        + keep2 * (1.0 - mix3) * v_ref[2]
    )
    out_ref[...] = mixed.astype(BF16)


def join_body(spot_ref, *refs):
    out_ref = refs[-1]
    parts = len(refs) - 1
    part = refs[0].shape[1]
    for k in range(parts):
        first = lax.rem(spot_ref[0] + k, parts) * part
        out_ref[:, pl.ds(pl.multiple_of(first, part), part)] = refs[k][...].astype(F32)


def shards(
    fixed_point,
    upstream,
    norm_gain,
    query_weight,
    keyval_weight,
    output_weight,
    log_norm,
    attention_out,
):
    rows, width = fixed_point.shape
    wide = query_weight.shape[1]
    narrow = keyval_weight.shape[1]
    size = wide + narrow
    e = narrow // 2
    heads = log_norm.shape[0]
    seq_count = lax.axis_size("seq")
    parts = lax.axis_size("head")
    block = lax.axis_index("seq")
    head = lax.axis_index("head")
    scale = e ** (-0.5)
    gain = norm_gain.reshape(1, width)
    span = (WIN_DEVS + 1) * rows
    group = min(8, seq_count)

    cols = size // group
    spot = jnp.stack([head, lax.rem(block, group)])
    smem = pl.BlockSpec(memory_space=pltpu.SMEM)
    vmem = pl.BlockSpec(memory_space=pltpu.VMEM)
    hbm = pl.BlockSpec(memory_space=pltpu.HBM)

    def pinned(value):
        return pltpu.with_memory_space_constraint(value, pltpu.HBM)

    tile = 128 if wide % 128 == 0 and 128 % (wide // group) == 0 else wide
    own_cols, hidden, kv, kvf, inv = local_call(
        prep_body,
        [
            shape_of((cols, width), BF16),
            shape_of((rows, width), BF16),
            shape_of((rows, narrow), BF16),
            shape_of((rows, narrow), F32),
            shape_of((rows, rows), F32),
        ],
        2 * width * size * cols,
        2 * width * (tile + narrow + rows),
        10,
        in_specs=[smem, vmem] + [hbm] * 3,
        scratch_shapes=[
            pltpu.VMEM((width, tile), BF16),
            pltpu.VMEM((width, narrow), BF16),
            pltpu.VMEM((rows, width), BF16),
            pltpu.SemaphoreType.DMA((3,)),
        ],
    )(block.reshape(1), gain, pinned(query_weight), pinned(keyval_weight), pinned(fixed_point))
    every_cols, bit = own_cols[None], 1
    while bit < parts:
        pairs = [(i, i ^ bit) for i in range(parts)]
        other = lax.ppermute(every_cols, "head", pairs)
        every_cols = jnp.concatenate([every_cols, other])
        bit *= 2
    earlier = [shifted(kv, "seq", offset) for offset in range(WIN_DEVS, 0, -1)]

    qf, qt, go, nt, aot = local_call(
        functools.partial(start_body, heads),
        [
            shape_of((rows, wide), F32),
            shape_of((e, heads * rows), BF16),
            shape_of((e, heads * rows), F32),
            shape_of((e, heads * rows), F32),
            shape_of((e, heads * rows), F32),
        ],
        6 * rows * width * wide,
        4 * width * (2 * rows + wide),
        14,
        in_specs=[vmem] * 2 + [hbm] * 5,
        scratch_shapes=[
            pltpu.VMEM((width, wide), BF16),
            pltpu.VMEM((wide, width), BF16),
            pltpu.VMEM((rows, width), BF16),
            pltpu.VMEM((rows, width), BF16),
            pltpu.VMEM((rows, wide), BF16),
            pltpu.SemaphoreType.DMA((5,)),
        ],
    )(
        hidden,
        inv,
        pinned(query_weight),
        pinned(output_weight),
        pinned(upstream),
        pinned(fixed_point),
        pinned(attention_out),
    )

    pull_outs = [shape_of((span, heads * rows), BF16), shape_of((rows, narrow), F32)]
    pull_outs += [shape_of((rows, narrow), BF16)] * WIN_DEVS
    pull_flops = 6 * span * e * heads * rows

    def exchange(score, own, terms):
        arrived = [shifted(term, "seq", -offset - 1) for offset, term in enumerate(terms)]
        gq = local_call(
            functools.partial(query_body, heads, scale),
            shape_of((rows, wide), BF16),
            2 * span * e * heads * rows,
            span * heads * rows * 2,
            4,
        )(kt, score)
        msg = local_call(
            functools.partial(collect_body, width),
            shape_of((rows + EXTRA, size), BF16),
            COLLECT * rows * size,
            rows * size * 4,
            4,
        )(own, gq, qf, kvf, *arrived)
        return rotated(msg, "head"), msg, gq

    kvw, kt, probs, score, own, *terms = local_call(
        functools.partial(first_body, heads, scale),
        [
            shape_of((span, narrow), BF16),
            shape_of((e, span), BF16),
            shape_of((span, heads * rows), BF16),
        ]
        + pull_outs,
        pull_flops * 5 // 4,
        span * heads * rows * 2,
        16,
        in_specs=[smem] + [vmem] * (WIN_DEVS + 5),
    )(block.reshape(1), *earlier, kv, qt, go, aot, log_norm)
    packed = []
    chain_shape = shape_of((parts, size, wide), BF16)
    for step in range(3):
        if step:
            score, own, lhs, row, *terms = local_call(
                functools.partial(next_body, heads, parts, scale, step == 1),
                pull_outs[:2]
                + [shape_of((parts, rows, size), BF16), shape_of((EXTRA, rows), F32)]
                + [chain_shape] * (step == 1)
                + pull_outs[2:],
                pull_flops + 2 * rows * parts * size * wide,
                span * heads * rows * 2 + parts * size * wide * 2,
                16,
                in_specs=[smem] + [vmem] * (parts + 6 + len(chain)),
            )(spot, *every_msg, inv, nt, qt, aot, kvw, probs, *chain)
            packed += [lhs, row]
            if step == 1:
                chain, *terms = terms
                chain = [chain]
        every_msg, msg, gq = exchange(score, own, terms)
        if step == 0:
            every_cols, _ = lax.optimization_barrier((every_cols, gq))
            share = local_call(
                chain_body,
                shape_of((parts * cols, wide), BF16),
                2 * parts * cols * width * wide,
                2 * width * (wide + parts * cols),
                8,
            )(every_cols.reshape(parts * cols, width), output_weight, gain)
            share = share.reshape(parts, cols, wide)
            chain = doubled(share, "seq", group, (share, msg, tuple(every_msg[1:])))
            part = width // parts
            mine = lax.dynamic_slice_in_dim(every_cols, head * part, part, 2)
            weight = [mine[None]]
        bit = group >> (step + 1)
        weight = list(lax.optimization_barrier((tuple(weight), msg))[0])
        pairs = [(i, i ^ bit) for i in range(seq_count)]
        if bit > 1:
            if len(weight) > 1:
                weight = [jnp.concatenate(weight)]
            other = lax.ppermute(weight[0], "seq", pairs)
            other, *every_msg = lax.optimization_barrier((other, *every_msg))
            weight.append(other)
        else:
            weight = [jnp.concatenate(weight)]
            weight.append(lax.ppermute(weight[0], "seq", pairs))

    small = seq_count * parts <= 64
    fields, totals = local_call(
        functools.partial(field_body, parts, wide),
        [
            shape_of((3, rows, part), F32),
            shape_of((seq_count * parts if small else 1, 8, 128), F32),
        ],
        6 * rows * parts * size * part,
        2 * parts * size * part,
        20,
        in_specs=[smem] + [vmem] * (parts + 8 + len(weight)),
        scratch_shapes=[
            pltpu.VMEM((parts, rows, size), BF16),
            pltpu.VMEM((parts, size, part), BF16),
        ],
    )(spot, *every_msg, *packed, *weight, fixed_point, upstream, gain, inv)
    if small:
        totals = lax.all_to_all(totals, ("seq", "head"), 0, 0)
    else:
        totals = lax.psum(totals, ("seq", "head"))
    mixed = local_call(
        functools.partial(mix_body, rows * seq_count * width),
        shape_of((rows, part), BF16),
        8 * rows * part,
        18 * rows * part,
        6,
        in_specs=[smem] + [vmem] * 3,
    )(spot, totals, upstream, fields)
    every_mixed = rotated(mixed, "head")
    return local_call(
        join_body,
        shape_of((rows, width), F32),
        0,
        6 * rows * width,
        6,
        in_specs=[smem] + [vmem] * parts,
    )(spot, *every_mixed)


def solution(mesh):
    in_specs = (
        P("seq", None),
        P("seq", None),
        P(),
        P(None, "head"),
        P(None, "head"),
        P("head", None),
        P("head", "seq"),
        P("seq", "head"),
    )
    out_specs = P("seq", None)
    return jax.shard_map(shards, mesh=mesh, in_specs=in_specs, out_specs=out_specs, check_vma=False)
```

```python
import functools

import jax
import jax.numpy as jnp
from jax import lax
from jax.experimental import pallas as pl
from jax.experimental.pallas import tpu as pltpu
from jax.sharding import PartitionSpec as P

WIN_DEVS = 4
norm_eps = 1e-05
mix_eps = 1e-06
F32 = jnp.float32
BF16 = jnp.bfloat16
COLLECT = 50000
EXTRA = 16
NT = (((1,), (1,)), ((), ()))


def shape_of(shape, dtype):
    return jax.ShapeDtypeStruct(shape, dtype)


def local_call(body, outs, flops, moved, room, **more):
    return pl.pallas_call(
        body,
        out_shape=outs,
        compiler_params=pltpu.CompilerParams(vmem_limit_bytes=room * 1024 * 1024),
        cost_estimate=pl.CostEstimate(flops=flops, bytes_accessed=moved, transcendentals=0),
        **more,
    )


def shifted(value, axis, steps):
    count = lax.axis_size(axis)
    initial, last = (max(0, -steps), min(count, count - steps))
    return lax.ppermute(value, axis, [(source, source + steps) for source in range(initial, last)])


def rotated(value, axis):
    count = lax.axis_size(axis)
    parts = [value]
    for step in range(1, count):
        parts.append(lax.ppermute(value, axis, [(i, (i - step) % count) for i in range(count)]))
    return parts


def doubled(value, axis, group, gates):
    count = lax.axis_size(axis)
    near, bit = [value[None]], group // 2
    for gate in gates:
        near = list(lax.optimization_barrier((tuple(near), gate))[0])
        pairs = [(i, i ^ bit) for i in range(count)]
        if bit == 1:
            return near + [lax.ppermute(part, axis, pairs) for part in near]
        if len(near) > 1:
            near = [jnp.concatenate(near)]
        near.append(lax.ppermute(near[0], axis, pairs))
        bit //= 2


def assemble(place, wide, out_ref, refs):
    group = sum(ref.shape[0] for ref in refs)
    cut = wide // group
    rest_cut = refs[0].shape[2] - cut
    entries = [(ref, j) for ref in refs for j in range(ref.shape[0])]
    for j, (ref, at) in enumerate(entries):
        distance, bit, rest = 0, group // 2, j
        while rest:
            distance += bit * (rest & 1)
            rest >>= 1
            bit //= 2
        index = lax.bitwise_xor(place, jnp.int32(distance))
        first = pl.multiple_of(index * cut, cut)
        second = pl.multiple_of(wide + index * rest_cut, rest_cut)
        for k in range(out_ref.shape[0]):
            out_ref[k, pl.ds(first, cut), :] = ref[at, k, :cut, :]
            out_ref[k, pl.ds(second, rest_cut), :] = ref[at, k, cut:, :]


def prep_body(block_ref, qw_ref, kvw_ref, z_ref, gain_ref, cols_ref, hidden_ref, kv_ref, kvf_ref,
              inv_ref, q_tile, kv_tile, z_tile, gain_tile, sems):
    tile = q_tile.shape[1]
    wide, narrow = qw_ref.shape[1], kvw_ref.shape[1]
    group = (wide + narrow) // cols_ref.shape[0]
    place = lax.rem(block_ref[0], group)
    q_take, kv_take = wide // group, narrow // group
    q_at = place * q_take
    q_first = pl.multiple_of(q_at // tile * tile, tile)
    copies = [
        pltpu.make_async_copy(qw_ref.at[:, pl.ds(q_first, tile)], q_tile, sems.at[0]),
        pltpu.make_async_copy(kvw_ref, kv_tile, sems.at[1]),
        pltpu.make_async_copy(z_ref, z_tile, sems.at[2]),
        pltpu.make_async_copy(gain_ref, gain_tile, sems.at[3]),
    ]
    for copy in copies:
        copy.start()
    first = 0
    for copy, ref, at, take in (
        (copies[0], q_tile, q_at - q_first, q_take),
        (copies[1], kv_tile, place * kv_take, kv_take),
    ):
        copy.wait()
        total = ref.shape[1]
        row = lax.broadcasted_iota(jnp.int32, (take, total), 0) + at
        pick = (row == lax.broadcasted_iota(jnp.int32, (take, total), 1)).astype(BF16)
        cols = lax.dot_general(pick, ref[...], NT, preferred_element_type=F32)
        cols_ref[first : first + take, :] = cols.astype(BF16)
        first += take
    copies[2].wait()
    copies[3].wait()
    z = z_tile[...].astype(F32)
    inverse = lax.rsqrt(jnp.mean(z * z, axis=1, keepdims=True) + norm_eps)
    hidden = (z * inverse * gain_tile[...]).astype(BF16)
    hidden_ref[...] = hidden
    kvf = jnp.dot(hidden, kv_tile[...], preferred_element_type=F32)
    kvf_ref[...] = kvf
    kv_ref[...] = kvf.astype(BF16)
    inv_ref[...] = jnp.broadcast_to(inverse, inv_ref.shape)


def chain_body(cols_ref, scaled_ref, out_ref):
    share = lax.dot_general(cols_ref[...], scaled_ref[...], NT, preferred_element_type=F32)
    out_ref[...] = share.astype(BF16)


def lanes_of(value, heads):
    size = value.shape[0] // heads
    return jnp.concatenate([value[i * size : (i + 1) * size] for i in range(heads)], axis=1)


def start_body(heads, hidden_ref, inv_ref, qw_ref, ow_ref, up_ref, z_ref, ao_ref, gain_ref, ln_ref,
               qf_ref, qt_ref, go_ref, nt_ref, aot_ref, scaled_ref, norms_ref,
               qw_tile, ow_tile, up_tile, z_tile, ao_tile, gain_tile, sems):
    copies = [
        pltpu.make_async_copy(source, target, sems.at[i])
        for i, (source, target) in enumerate(
            ((ow_ref, ow_tile), (up_ref, up_tile), (z_ref, z_tile), (qw_ref, qw_tile),
             (ao_ref, ao_tile), (gain_ref, gain_tile), (ln_ref, norms_ref))
        )
    ]
    for copy in copies:
        copy.start()
    for copy in copies[:3]:
        copy.wait()
    out = lax.dot_general(up_tile[...], ow_tile[...], NT, preferred_element_type=F32)
    go_ref[...] = lanes_of(out.T, heads)
    base = lax.dot_general(z_tile[...], ow_tile[...], NT, preferred_element_type=F32)
    nt_ref[...] = lanes_of((base * inv_ref[:, :1]).T, heads)
    copies[3].wait()
    qf = jnp.dot(hidden_ref[...], qw_tile[...], preferred_element_type=F32)
    qf_ref[...] = qf
    qt_ref[...] = lanes_of(qf.T, heads).astype(BF16)
    for copy in copies[4:]:
        copy.wait()
    scaled_ref[...] = (ow_tile[...].astype(F32) * gain_tile[...]).astype(BF16)
    aot_ref[...] = lanes_of(ao_tile[...].astype(F32).T, heads)


def pull(heads, scale, go, aot, qt, kvw_ref, probs, score_ref, own_ref, term_refs):
    e = go.shape[0]
    rows = go.shape[1] // heads
    row_terms = jnp.sum(go * aot, axis=0, keepdims=True)
    gob = go.astype(BF16)
    grad_prob = jnp.dot(kvw_ref[:, e:], gob, preferred_element_type=F32)
    grad_score = (probs.astype(F32) * (grad_prob - row_terms)).astype(BF16)
    score_ref[...] = grad_score
    grad_key = lax.dot_general(grad_score, qt, NT, preferred_element_type=F32) * scale
    grad_value = lax.dot_general(probs, gob, NT, preferred_element_type=F32)
    terms = jnp.concatenate([grad_key, grad_value], axis=1)
    for offset in range(1, len(term_refs) + 1):
        first = (len(term_refs) - offset) * rows
        term_refs[offset - 1][...] = terms[first : first + rows].astype(BF16)
    own_ref[...] = terms[len(term_refs) * rows :]


def query_body(heads, scale, kt_ref, score_ref, gq_ref):
    rows = gq_ref.shape[0]
    grad_query = jnp.dot(kt_ref[...], score_ref[...], preferred_element_type=F32) * scale
    parts = [grad_query[:, i * rows : (i + 1) * rows] for i in range(heads)]
    gq_ref[...] = jnp.concatenate(parts, axis=0).T.astype(BF16)


def first_body(heads, scale, block_ref, *refs):
    windows = refs[: WIN_DEVS + 1]
    qt_ref, go_ref, aot_ref, ln_ref = refs[WIN_DEVS + 1 : WIN_DEVS + 5]
    kvw_ref, kt_ref, probs_ref, score_ref, own_ref = refs[WIN_DEVS + 5 : WIN_DEVS + 10]
    term_refs = refs[WIN_DEVS + 10 :]
    rows = windows[0].shape[0]
    for place, ref in enumerate(windows):
        kvw_ref[place * rows : (place + 1) * rows, :] = ref[...]
    kvw = kvw_ref[...]
    e = kvw.shape[1] // 2
    kt_ref[...] = kvw.astype(F32).T[:e].astype(BF16)
    scores = jnp.dot(kvw[:, :e], qt_ref[...], preferred_element_type=F32) * scale
    norms = jnp.concatenate([ln_ref[i : i + 1, :] for i in range(heads)], axis=1)
    key_pos = lax.broadcasted_iota(jnp.int32, scores.shape, 0)
    query_pos = lax.broadcasted_iota(jnp.int32, scores.shape, 1) & (rows - 1)
    allowed = (key_pos > query_pos) & (key_pos <= query_pos + WIN_DEVS * rows)
    allowed = allowed & (key_pos >= (WIN_DEVS - block_ref[0]) * rows)
    probs = jnp.where(allowed, jnp.exp(scores - norms), 0.0).astype(BF16)
    probs_ref[...] = probs
    pull(heads, scale, go_ref[...], aot_ref[...], qt_ref[...], kvw_ref, probs,
         score_ref, own_ref, term_refs)


def next_body(heads, parts, scale, fresh, spot_ref, *refs):
    msg_refs, refs = refs[:parts], refs[parts:]
    inv_ref, nt_ref, qt_ref, aot_ref, kvw_ref, probs_ref, *refs = refs
    if fresh:
        *parts_refs, score_ref, own_ref, lhs_ref, row_ref, chain_ref = refs[:9]
        term_refs = refs[9:]
        assemble(spot_ref[1], chain_ref.shape[2], chain_ref, parts_refs)
    else:
        chain_ref, score_ref, own_ref, lhs_ref, row_ref = refs[:5]
        term_refs = refs[5:]
    rows, wide = lhs_ref.shape[1], chain_ref.shape[2]
    out = jnp.zeros((rows, wide), F32)
    along = jnp.zeros((EXTRA, rows), F32)
    for k in range(parts):
        index = lax.rem(spot_ref[0] + k, parts)
        msg = msg_refs[k][...]
        chain = chain_ref[lax.bitwise_xor(index, spot_ref[0])]
        out += jnp.dot(msg[:rows], chain, preferred_element_type=F32)
        lhs_ref[index] = msg[:rows]
        along += msg[rows:, :rows].astype(F32)
    row_ref[...] = along
    along = jnp.sum(along, axis=0, keepdims=True)
    along = jnp.concatenate([along] * heads, axis=1)
    go = lanes_of((out * inv_ref[:, :1]).T, heads)
    inv_row = jnp.concatenate([inv_ref[...].T[:1, :]] * heads, axis=1)
    go = go - inv_row * along * nt_ref[...]
    pull(heads, scale, go, aot_ref[...], qt_ref[...], kvw_ref, probs_ref[...],
         score_ref, own_ref, term_refs)


def collect_body(width, own_ref, gq_ref, qf_ref, kvf_ref, *refs):
    msg_ref = refs[-1]
    rows = own_ref.shape[0]
    total = own_ref[...]
    for ref in refs[:-1]:
        total += ref[...].astype(F32)
    total = total.astype(BF16)
    ahead = msg_ref.shape[1] - total.shape[1]
    if ahead:
        msg_ref[:rows, :ahead] = gq_ref[...]
    msg_ref[:rows, ahead:] = total
    prods = gq_ref[...].astype(F32) * qf_ref[...]
    partial = total.astype(F32) * kvf_ref[...]
    lanes = partial.shape[1]
    for first in range(0, prods.shape[1], lanes):
        partial += prods[:, first : first + lanes]
    along = jnp.sum(partial.T, axis=0, keepdims=True) * (1.0 / width)
    high = along.astype(BF16).astype(F32)
    place = lax.broadcasted_iota(jnp.int32, (EXTRA, rows), 0)
    extra = jnp.where(place == 0, high, jnp.where(place == 1, along - high, 0.0))
    msg_ref[rows:, :] = jnp.zeros((EXTRA, msg_ref.shape[1]), BF16)
    msg_ref[rows:, :rows] = extra.astype(BF16)


def field_body(parts, wide, spot_ref, *refs):
    gq_refs, msg_refs, refs = refs[:parts], refs[parts : 2 * parts], refs[2 * parts :]
    lhs1_ref, row1_ref, lhs2_ref, row2_ref, *refs = refs
    *w_refs, z_ref, up_ref, gain_ref, inv_ref, v_ref, tot_ref, lhs3_ref, w_ref = refs
    rows, part = v_ref.shape[1:]
    head = spot_ref[0]
    row3 = jnp.zeros((EXTRA, rows), F32)
    for k in range(parts):
        msg = msg_refs[k][...]
        lhs3_ref[lax.rem(head + k, parts)] = jnp.concatenate(
            [gq_refs[k][...], msg[:rows]], axis=1
        )
        row3 += msg[rows:, :rows].astype(F32)
    assemble(spot_ref[1], wide, w_ref, w_refs)
    y = jnp.zeros((3 * rows, part), F32)
    for k in range(parts):
        lhs = jnp.concatenate([lhs1_ref[k], lhs2_ref[k], lhs3_ref[k]], axis=0)
        weight = w_ref[lax.bitwise_xor(jnp.int32(k), head)]
        y += jnp.dot(lhs, weight, preferred_element_type=F32)
    at = pl.ds(pl.multiple_of(head * part, part), part)
    inverse = inv_ref[:, :1]
    normed = z_ref[:, at].astype(F32) * inverse
    gain = gain_ref[:, at]
    fields = []
    for step, row in enumerate((row1_ref[...], row2_ref[...], row3)):
        along = jnp.broadcast_to(jnp.sum(row, axis=0, keepdims=True), (rows, rows)).T[:, :1]
        y_step = y[step * rows : (step + 1) * rows]
        fields.append(inverse * (y_step * gain - normed * along))
        v_ref[step] = fields[step]
    first, second, third = fields
    change1 = first - up_ref[:, at].astype(F32)
    change2 = second - first
    change3 = third - second
    pairs = [
        (change1, first), (change1, change1), (change2, first), (change2, change2),
        (change2, second), (change2, change3), (change3, second), (change3, change3),
    ]
    lanes = tot_ref.shape[2]
    sums = []
    for a, b in pairs:
        total = jnp.sum(a * b, axis=0, keepdims=True)
        sums.append(sum(total[:, i : i + lanes] for i in range(0, part, lanes)))
    totals = jnp.concatenate(sums, axis=0)
    for k in range(tot_ref.shape[0]):
        tot_ref[k] = totals


def mix_body(entries, spot_ref, tot_ref, up_ref, v_ref, out_ref):
    totals = jnp.sum(jnp.sum(tot_ref[...], axis=0), axis=1, keepdims=True) / entries
    s_r1, s_s, d2_v1, d2_d2, d2_v2, d2_d3, d3_v2, d3_d3 = [totals[i : i + 1] for i in range(8)]
    mix1 = s_r1 / (s_s + mix_eps)
    keep1 = 1.0 - mix1
    mix2 = keep1 * (d2_v1 + keep1 * d2_d2) / (keep1 * keep1 * d2_d2 + mix_eps)
    keep2 = keep1 * (1.0 - mix2)
    cross = mix1 * (d2_v2 + keep2 * d2_d3) + keep2 * (d3_v2 + keep2 * d3_d3)
    square = mix1 * mix1 * d2_d2 + 2.0 * mix1 * keep2 * d2_d3 + keep2 * keep2 * d3_d3
    mix3 = cross / (square + mix_eps)
    part = out_ref.shape[1]
    at = pl.ds(pl.multiple_of(spot_ref[0] * part, part), part)
    mixed = (
        up_ref[:, at].astype(F32)
        + v_ref[0]
        + (1.0 - mix3 * mix1) * v_ref[1]
        + keep2 * (1.0 - mix3) * v_ref[2]
    )
    out_ref[...] = mixed.astype(BF16)


def join_body(spot_ref, *refs):
    out_ref = refs[-1]
    parts = len(refs) - 1
    part = refs[0].shape[1]
    for k in range(parts):
        first = lax.rem(spot_ref[0] + k, parts) * part
        out_ref[:, pl.ds(pl.multiple_of(first, part), part)] = refs[k][...].astype(F32)


def shards(
    fixed_point,
    upstream,
    norm_gain,
    query_weight,
    keyval_weight,
    output_weight,
    log_norm,
    attention_out,
):
    rows, width = fixed_point.shape
    wide = query_weight.shape[1]
    narrow = keyval_weight.shape[1]
    size = wide + narrow
    e = narrow // 2
    heads = log_norm.shape[0]
    seq_count = lax.axis_size("seq")
    parts = lax.axis_size("head")
    block = lax.axis_index("seq")
    head = lax.axis_index("head")
    scale = e ** (-0.5)
    gain = norm_gain.reshape(1, width)
    span = (WIN_DEVS + 1) * rows
    group = min(8, seq_count)

    cols = size // group
    spot = jnp.stack([head, lax.rem(block, group)])
    smem = pl.BlockSpec(memory_space=pltpu.SMEM)
    vmem = pl.BlockSpec(memory_space=pltpu.VMEM)
    hbm = pl.BlockSpec(memory_space=pltpu.HBM)

    def pinned(value):
        return pltpu.with_memory_space_constraint(value, pltpu.HBM)

    tile = 128 if wide % 128 == 0 and 128 % (wide // group) == 0 else wide
    own_cols, hidden, kv, kvf, inv = local_call(
        prep_body,
        [
            shape_of((cols, width), BF16),
            shape_of((rows, width), BF16),
            shape_of((rows, narrow), BF16),
            shape_of((rows, narrow), F32),
            shape_of((rows, rows), F32),
        ],
        2 * width * size * cols,
        2 * width * (tile + narrow + rows),
        10,
        in_specs=[smem] + [hbm] * 4,
        scratch_shapes=[
            pltpu.VMEM((width, tile), BF16),
            pltpu.VMEM((width, narrow), BF16),
            pltpu.VMEM((rows, width), BF16),
            pltpu.VMEM((1, width), F32),
            pltpu.SemaphoreType.DMA((4,)),
        ],
    )(
        block.reshape(1),
        pinned(query_weight),
        pinned(keyval_weight),
        pinned(fixed_point),
        pinned(gain),
    )
    every_cols, bit = own_cols[None], 1
    while bit < parts:
        pairs = [(i, i ^ bit) for i in range(parts)]
        other = lax.ppermute(every_cols, "head", pairs)
        every_cols = jnp.concatenate([every_cols, other])
        bit *= 2
    earlier = [shifted(kv, "seq", offset) for offset in range(WIN_DEVS, 0, -1)]

    qf, qt, go, nt, aot, scaled, norms = local_call(
        functools.partial(start_body, heads),
        [
            shape_of((rows, wide), F32),
            shape_of((e, heads * rows), BF16),
            shape_of((e, heads * rows), F32),
            shape_of((e, heads * rows), F32),
            shape_of((e, heads * rows), F32),
            shape_of((wide, width), BF16),
            shape_of((heads, rows), F32),
        ],
        6 * rows * width * wide,
        4 * width * (2 * rows + wide),
        14,
        in_specs=[vmem] * 2 + [hbm] * 7,
        scratch_shapes=[
            pltpu.VMEM((width, wide), BF16),
            pltpu.VMEM((wide, width), BF16),
            pltpu.VMEM((rows, width), BF16),
            pltpu.VMEM((rows, width), BF16),
            pltpu.VMEM((rows, wide), BF16),
            pltpu.VMEM((1, width), F32),
            pltpu.SemaphoreType.DMA((7,)),
        ],
    )(
        hidden,
        inv,
        pinned(query_weight),
        pinned(output_weight),
        pinned(upstream),
        pinned(fixed_point),
        pinned(attention_out),
        pinned(gain),
        pinned(log_norm),
    )

    pull_outs = [shape_of((span, heads * rows), BF16), shape_of((rows, narrow), F32)]
    pull_outs += [shape_of((rows, narrow), BF16)] * WIN_DEVS
    pull_flops = 6 * span * e * heads * rows

    def exchange(score, own, terms, split):
        arrived = [shifted(term, "seq", -offset - 1) for offset, term in enumerate(terms)]
        gq = local_call(
            functools.partial(query_body, heads, scale),
            shape_of((rows, wide), BF16),
            2 * span * e * heads * rows,
            span * heads * rows * 2,
            4,
        )(kt, score)
        ahead = rotated(gq, "head") if split else []
        msg = local_call(
            functools.partial(collect_body, width),
            shape_of((rows + EXTRA, narrow if split else size), BF16),
            COLLECT * rows * size,
            rows * size * 4,
            4,
        )(own, gq, qf, kvf, *arrived)
        return rotated(msg, "head"), msg, gq, ahead

    kvw, kt, probs, score, own, *terms = local_call(
        functools.partial(first_body, heads, scale),
        [
            shape_of((span, narrow), BF16),
            shape_of((e, span), BF16),
            shape_of((span, heads * rows), BF16),
        ]
        + pull_outs,
        pull_flops * 5 // 4,
        span * heads * rows * 2,
        16,
        in_specs=[smem] + [vmem] * (WIN_DEVS + 5),
    )(block.reshape(1), *earlier, kv, qt, go, aot, norms)
    packed = []
    chain_shape = shape_of((parts, size, wide), BF16)
    for step in range(3):
        if step:
            score, own, lhs, row, *terms = local_call(
                functools.partial(next_body, heads, parts, scale, step == 1),
                pull_outs[:2]
                + [shape_of((parts, rows, size), BF16), shape_of((EXTRA, rows), F32)]
                + [chain_shape] * (step == 1)
                + pull_outs[2:],
                pull_flops + 2 * rows * parts * size * wide,
                span * heads * rows * 2 + parts * size * wide * 2,
                16,
                in_specs=[smem] + [vmem] * (parts + 6 + len(chain)),
            )(spot, *every_msg, inv, nt, qt, aot, kvw, probs, *chain)
            packed += [lhs, row]
            if step == 1:
                chain, *terms = terms
                chain = [chain]
        every_msg, msg, gq, ahead = exchange(score, own, terms, step == 2)
        if step == 0:
            every_cols, _ = lax.optimization_barrier((every_cols, gq))
            share = local_call(
                chain_body,
                shape_of((parts * cols, wide), BF16),
                2 * parts * cols * width * wide,
                2 * width * (wide + parts * cols),
                8,
            )(every_cols.reshape(parts * cols, width), scaled)
            share = share.reshape(parts, cols, wide)
            chain = doubled(share, "seq", group, (share, msg, tuple(every_msg[1:])))
            part = width // parts
            mine = lax.dynamic_slice_in_dim(every_cols, head * part, part, 2)
            weight = [mine[None]]
        bit = group >> (step + 1)
        gate = gq if bit == 1 else msg
        weight = list(lax.optimization_barrier((tuple(weight), gate))[0])
        pairs = [(i, i ^ bit) for i in range(seq_count)]
        if bit > 1:
            if len(weight) > 1:
                weight = [jnp.concatenate(weight)]
            other = lax.ppermute(weight[0], "seq", pairs)
            other, *every_msg = lax.optimization_barrier((other, *every_msg))
            weight.append(other)
        else:
            weight = [jnp.concatenate(weight)]
            weight.append(lax.ppermute(weight[0], "seq", pairs))

    small = seq_count * parts <= 64
    fields, totals = local_call(
        functools.partial(field_body, parts, wide),
        [
            shape_of((3, rows, part), F32),
            shape_of((seq_count * parts if small else 1, 8, 128), F32),
        ],
        6 * rows * parts * size * part,
        2 * parts * size * part,
        20,
        in_specs=[smem] + [vmem] * (2 * parts + 8 + len(weight)),
        scratch_shapes=[
            pltpu.VMEM((parts, rows, size), BF16),
            pltpu.VMEM((parts, size, part), BF16),
        ],
    )(spot, *ahead, *every_msg, *packed, *weight, fixed_point, upstream, gain, inv)
    if small:
        totals = lax.all_to_all(totals, ("seq", "head"), 0, 0)
    else:
        totals = lax.psum(totals, ("seq", "head"))
    mixed = local_call(
        functools.partial(mix_body, rows * seq_count * width),
        shape_of((rows, part), BF16),
        8 * rows * part,
        18 * rows * part,
        6,
        in_specs=[smem] + [vmem] * 3,
    )(spot, totals, upstream, fields)
    every_mixed = rotated(mixed, "head")
    return local_call(
        join_body,
        shape_of((rows, width), F32),
        0,
        6 * rows * width,
        6,
        in_specs=[smem] + [vmem] * parts,
    )(spot, *every_mixed)


def solution(mesh):
    in_specs = (
        P("seq", None),
        P("seq", None),
        P(),
        P(None, "head"),
        P(None, "head"),
        P("head", None),
        P("head", "seq"),
        P("seq", "head"),
    )
    out_specs = P("seq", None)
    return jax.shard_map(shards, mesh=mesh, in_specs=in_specs, out_specs=out_specs, check_vma=False)
```

```python
import functools

import jax
import jax.numpy as jnp
from jax import lax
from jax.experimental import pallas as pl
from jax.experimental.pallas import tpu as pltpu
from jax.sharding import PartitionSpec as P

WIN_DEVS = 4
norm_eps = 1e-05
mix_eps = 1e-06
F32 = jnp.float32
BF16 = jnp.bfloat16
COLLECT = 50000
EXTRA = 16
NT = (((1,), (1,)), ((), ()))


def shape_of(shape, dtype):
    return jax.ShapeDtypeStruct(shape, dtype)


def local_call(body, outs, flops, moved, room, **more):
    return pl.pallas_call(
        body,
        out_shape=outs,
        compiler_params=pltpu.CompilerParams(vmem_limit_bytes=room * 1024 * 1024),
        cost_estimate=pl.CostEstimate(flops=flops, bytes_accessed=moved, transcendentals=0),
        **more,
    )


def shifted(value, axis, steps):
    count = lax.axis_size(axis)
    initial, last = (max(0, -steps), min(count, count - steps))
    return lax.ppermute(value, axis, [(source, source + steps) for source in range(initial, last)])


def rotated(value, axis):
    count = lax.axis_size(axis)
    parts = [value]
    for step in range(1, count):
        parts.append(lax.ppermute(value, axis, [(i, (i - step) % count) for i in range(count)]))
    return parts


def doubled(value, axis, group, gates):
    count = lax.axis_size(axis)
    near, bit = [value[None]], group // 2
    for gate in gates:
        near = list(lax.optimization_barrier((tuple(near), gate))[0])
        pairs = [(i, i ^ bit) for i in range(count)]
        if len(near) > 1:
            near = [jnp.concatenate(near)]
        if bit == 1:
            return near + [lax.ppermute(near[0], axis, pairs)]
        near.append(lax.ppermute(near[0], axis, pairs))
        bit //= 2


def assemble(place, wide, out_ref, refs):
    group = sum(ref.shape[0] for ref in refs)
    cut = wide // group
    rest_cut = refs[0].shape[2] - cut
    entries = [(ref, j) for ref in refs for j in range(ref.shape[0])]
    for j, (ref, at) in enumerate(entries):
        distance, bit, rest = 0, group // 2, j
        while rest:
            distance += bit * (rest & 1)
            rest >>= 1
            bit //= 2
        index = lax.bitwise_xor(place, jnp.int32(distance))
        first = pl.multiple_of(index * cut, cut)
        second = pl.multiple_of(wide + index * rest_cut, rest_cut)
        for k in range(out_ref.shape[0]):
            out_ref[k, pl.ds(first, cut), :] = ref[at, k, :cut, :]
            out_ref[k, pl.ds(second, rest_cut), :] = ref[at, k, cut:, :]


def prep_body(block_ref, qw_ref, kvw_ref, z_ref, gain_ref, cols_ref, hidden_ref, kv_ref, kvf_ref,
              inv_ref, q_tile, kv_tile, z_tile, gain_tile, sems):
    tile = q_tile.shape[1]
    wide, narrow = qw_ref.shape[1], kvw_ref.shape[1]
    group = (wide + narrow) // cols_ref.shape[0]
    place = lax.rem(block_ref[0], group)
    q_take, kv_take = wide // group, narrow // group
    q_at = place * q_take
    q_first = pl.multiple_of(q_at // tile * tile, tile)
    copies = [
        pltpu.make_async_copy(qw_ref.at[:, pl.ds(q_first, tile)], q_tile, sems.at[0]),
        pltpu.make_async_copy(kvw_ref, kv_tile, sems.at[1]),
        pltpu.make_async_copy(z_ref, z_tile, sems.at[2]),
        pltpu.make_async_copy(gain_ref, gain_tile, sems.at[3]),
    ]
    for copy in copies:
        copy.start()
    first = 0
    for copy, ref, at, take in (
        (copies[0], q_tile, q_at - q_first, q_take),
        (copies[1], kv_tile, place * kv_take, kv_take),
    ):
        copy.wait()
        total = ref.shape[1]
        row = lax.broadcasted_iota(jnp.int32, (take, total), 0) + at
        pick = (row == lax.broadcasted_iota(jnp.int32, (take, total), 1)).astype(BF16)
        cols = lax.dot_general(pick, ref[...], NT, preferred_element_type=F32)
        cols_ref[first : first + take, :] = cols.astype(BF16)
        first += take
    copies[2].wait()
    copies[3].wait()
    z = z_tile[...].astype(F32)
    inverse = lax.rsqrt(jnp.mean(z * z, axis=1, keepdims=True) + norm_eps)
    hidden = (z * inverse * gain_tile[...]).astype(BF16)
    hidden_ref[...] = hidden
    kvf = jnp.dot(hidden, kv_tile[...], preferred_element_type=F32)
    kvf_ref[...] = kvf
    kv_ref[...] = kvf.astype(BF16)
    inv_ref[...] = jnp.broadcast_to(inverse, inv_ref.shape)


def chain_body(cols_ref, scaled_ref, out_ref):
    share = lax.dot_general(cols_ref[...], scaled_ref[...], NT, preferred_element_type=F32)
    out_ref[...] = share.astype(BF16)


def lanes_of(value, heads):
    size = value.shape[0] // heads
    return jnp.concatenate([value[i * size : (i + 1) * size] for i in range(heads)], axis=1)


def start_body(heads, hidden_ref, inv_ref, qw_ref, ow_ref, up_ref, z_ref, ao_ref, gain_ref, ln_ref,
               qf_ref, qt_ref, go_ref, nt_ref, aot_ref, scaled_ref, norms_ref,
               qw_tile, ow_tile, up_tile, z_tile, ao_tile, gain_tile, sems):
    copies = [
        pltpu.make_async_copy(source, target, sems.at[i])
        for i, (source, target) in enumerate(
            ((ow_ref, ow_tile), (up_ref, up_tile), (z_ref, z_tile), (qw_ref, qw_tile),
             (ao_ref, ao_tile), (gain_ref, gain_tile), (ln_ref, norms_ref))
        )
    ]
    for copy in copies:
        copy.start()
    for copy in copies[:3]:
        copy.wait()
    out = lax.dot_general(up_tile[...], ow_tile[...], NT, preferred_element_type=F32)
    go_ref[...] = lanes_of(out.T, heads)
    base = lax.dot_general(z_tile[...], ow_tile[...], NT, preferred_element_type=F32)
    nt_ref[...] = lanes_of((base * inv_ref[:, :1]).T, heads)
    copies[3].wait()
    qf = jnp.dot(hidden_ref[...], qw_tile[...], preferred_element_type=F32)
    qf_ref[...] = qf
    qt_ref[...] = lanes_of(qf.T, heads).astype(BF16)
    for copy in copies[4:]:
        copy.wait()
    scaled_ref[...] = (ow_tile[...].astype(F32) * gain_tile[...]).astype(BF16)
    aot_ref[...] = lanes_of(ao_tile[...].astype(F32).T, heads)


def pull(heads, scale, go, aot, qt, kvw_ref, probs, score_ref, own_ref, term_refs):
    e = go.shape[0]
    rows = go.shape[1] // heads
    row_terms = jnp.sum(go * aot, axis=0, keepdims=True)
    gob = go.astype(BF16)
    grad_prob = jnp.dot(kvw_ref[:, e:], gob, preferred_element_type=F32)
    grad_score = (probs.astype(F32) * (grad_prob - row_terms)).astype(BF16)
    score_ref[...] = grad_score
    grad_key = lax.dot_general(grad_score, qt, NT, preferred_element_type=F32) * scale
    grad_value = lax.dot_general(probs, gob, NT, preferred_element_type=F32)
    terms = jnp.concatenate([grad_key, grad_value], axis=1)
    for offset in range(1, len(term_refs) + 1):
        first = (len(term_refs) - offset) * rows
        term_refs[offset - 1][...] = terms[first : first + rows].astype(BF16)
    own_ref[...] = terms[len(term_refs) * rows :]


def query_body(heads, scale, kt_ref, score_ref, gq_ref):
    rows = gq_ref.shape[0]
    grad_query = jnp.dot(kt_ref[...], score_ref[...], preferred_element_type=F32) * scale
    parts = [grad_query[:, i * rows : (i + 1) * rows] for i in range(heads)]
    gq_ref[...] = jnp.concatenate(parts, axis=0).T.astype(BF16)


def first_body(heads, scale, block_ref, *refs):
    windows = refs[: WIN_DEVS + 1]
    qt_ref, go_ref, aot_ref, ln_ref = refs[WIN_DEVS + 1 : WIN_DEVS + 5]
    kvw_ref, kt_ref, probs_ref, score_ref, own_ref = refs[WIN_DEVS + 5 : WIN_DEVS + 10]
    term_refs = refs[WIN_DEVS + 10 :]
    rows = windows[0].shape[0]
    for place, ref in enumerate(windows):
        kvw_ref[place * rows : (place + 1) * rows, :] = ref[...]
    kvw = kvw_ref[...]
    e = kvw.shape[1] // 2
    kt_ref[...] = kvw.astype(F32).T[:e].astype(BF16)
    scores = jnp.dot(kvw[:, :e], qt_ref[...], preferred_element_type=F32) * scale
    norms = jnp.concatenate([ln_ref[i : i + 1, :] for i in range(heads)], axis=1)
    key_pos = lax.broadcasted_iota(jnp.int32, scores.shape, 0)
    query_pos = lax.broadcasted_iota(jnp.int32, scores.shape, 1) & (rows - 1)
    allowed = (key_pos > query_pos) & (key_pos <= query_pos + WIN_DEVS * rows)
    allowed = allowed & (key_pos >= (WIN_DEVS - block_ref[0]) * rows)
    probs = jnp.where(allowed, jnp.exp(scores - norms), 0.0).astype(BF16)
    probs_ref[...] = probs
    pull(heads, scale, go_ref[...], aot_ref[...], qt_ref[...], kvw_ref, probs,
         score_ref, own_ref, term_refs)


def next_body(heads, parts, scale, fresh, spot_ref, *refs):
    gq_refs, refs = ([], refs) if fresh else (refs[:parts], refs[parts:])
    msg_refs, refs = refs[:parts], refs[parts:]
    inv_ref, nt_ref, qt_ref, aot_ref, kvw_ref, probs_ref, *refs = refs
    if fresh:
        *parts_refs, score_ref, own_ref, lhs_ref, row_ref, chain_ref = refs[:7]
        term_refs = refs[7:]
        assemble(spot_ref[1], chain_ref.shape[2], chain_ref, parts_refs)
    else:
        chain_ref, score_ref, own_ref, lhs_ref, row_ref = refs[:5]
        term_refs = refs[5:]
    rows, wide = lhs_ref.shape[1], chain_ref.shape[2]
    out = jnp.zeros((rows, wide), F32)
    along = jnp.zeros((EXTRA, rows), F32)
    for k in range(parts):
        index = lax.rem(spot_ref[0] + k, parts)
        msg = msg_refs[k][...]
        chain = chain_ref[lax.bitwise_xor(index, spot_ref[0])]
        lhs = msg[:rows]
        if gq_refs:
            lhs = jnp.concatenate([gq_refs[k][...], lhs], axis=1)
        out += jnp.dot(lhs, chain, preferred_element_type=F32)
        lhs_ref[index] = lhs
        along += msg[rows:, :rows].astype(F32)
    row_ref[...] = along
    along = jnp.sum(along, axis=0, keepdims=True)
    along = jnp.concatenate([along] * heads, axis=1)
    go = lanes_of((out * inv_ref[:, :1]).T, heads)
    inv_row = jnp.concatenate([inv_ref[...].T[:1, :]] * heads, axis=1)
    go = go - inv_row * along * nt_ref[...]
    pull(heads, scale, go, aot_ref[...], qt_ref[...], kvw_ref, probs_ref[...],
         score_ref, own_ref, term_refs)


def collect_body(width, own_ref, gq_ref, qf_ref, kvf_ref, *refs):
    msg_ref = refs[-1]
    rows = own_ref.shape[0]
    total = own_ref[...]
    for ref in refs[:-1]:
        total += ref[...].astype(F32)
    total = total.astype(BF16)
    ahead = msg_ref.shape[1] - total.shape[1]
    if ahead:
        msg_ref[:rows, :ahead] = gq_ref[...]
        msg_ref[rows:, :] = jnp.zeros((EXTRA, msg_ref.shape[1]), BF16)
    msg_ref[:rows, ahead:] = total
    prods = gq_ref[...].astype(F32) * qf_ref[...]
    partial = total.astype(F32) * kvf_ref[...]
    lanes = partial.shape[1]
    for first in range(0, prods.shape[1], lanes):
        partial += prods[:, first : first + lanes]
    along = jnp.sum(partial.T, axis=0, keepdims=True) * (1.0 / width)
    high = along.astype(BF16).astype(F32)
    place = lax.broadcasted_iota(jnp.int32, (EXTRA, rows), 0)
    extra = jnp.where(place == 0, high, jnp.where(place == 1, along - high, 0.0))
    msg_ref[rows:, :rows] = extra.astype(BF16)


def field_body(parts, wide, spot_ref, *refs):
    gq_refs, msg_refs, refs = refs[:parts], refs[parts : 2 * parts], refs[2 * parts :]
    lhs1_ref, row1_ref, lhs2_ref, row2_ref, *refs = refs
    *w_refs, z_ref, up_ref, gain_ref, inv_ref, v_ref, tot_ref, lhs3_ref, w_ref = refs
    rows, part = v_ref.shape[1:]
    head = spot_ref[0]
    row3 = jnp.zeros((EXTRA, rows), F32)
    for k in range(parts):
        msg = msg_refs[k][...]
        lhs3_ref[lax.rem(head + k, parts)] = jnp.concatenate(
            [gq_refs[k][...], msg[:rows]], axis=1
        )
        row3 += msg[rows:].astype(F32)
    assemble(spot_ref[1], wide, w_ref, w_refs)
    y = jnp.zeros((3 * rows, part), F32)
    for k in range(parts):
        lhs = jnp.concatenate([lhs1_ref[k], lhs2_ref[k], lhs3_ref[k]], axis=0)
        weight = w_ref[lax.bitwise_xor(jnp.int32(k), head)]
        y += jnp.dot(lhs, weight, preferred_element_type=F32)
    at = pl.ds(pl.multiple_of(head * part, part), part)
    inverse = inv_ref[:, :1]
    normed = z_ref[:, at].astype(F32) * inverse
    gain = gain_ref[:, at]
    fields = []
    for step, row in enumerate((row1_ref[...], row2_ref[...], row3)):
        along = jnp.broadcast_to(jnp.sum(row, axis=0, keepdims=True), (rows, rows)).T[:, :1]
        y_step = y[step * rows : (step + 1) * rows]
        fields.append(inverse * (y_step * gain - normed * along))
        v_ref[step] = fields[step]
    first, second, third = fields
    change1 = first - up_ref[:, at].astype(F32)
    change2 = second - first
    change3 = third - second
    pairs = [
        (change1, first), (change1, change1), (change2, first), (change2, change2),
        (change2, second), (change2, change3), (change3, second), (change3, change3),
    ]
    lanes = tot_ref.shape[2]
    sums = []
    for a, b in pairs:
        total = jnp.sum(a * b, axis=0, keepdims=True)
        sums.append(sum(total[:, i : i + lanes] for i in range(0, part, lanes)))
    totals = jnp.concatenate(sums, axis=0)
    for k in range(tot_ref.shape[0]):
        tot_ref[k] = totals


def mix_body(entries, spot_ref, tot_ref, up_ref, v_ref, out_ref):
    totals = jnp.sum(jnp.sum(tot_ref[...], axis=0), axis=1, keepdims=True) / entries
    s_r1, s_s, d2_v1, d2_d2, d2_v2, d2_d3, d3_v2, d3_d3 = [totals[i : i + 1] for i in range(8)]
    mix1 = s_r1 / (s_s + mix_eps)
    keep1 = 1.0 - mix1
    mix2 = keep1 * (d2_v1 + keep1 * d2_d2) / (keep1 * keep1 * d2_d2 + mix_eps)
    keep2 = keep1 * (1.0 - mix2)
    cross = mix1 * (d2_v2 + keep2 * d2_d3) + keep2 * (d3_v2 + keep2 * d3_d3)
    square = mix1 * mix1 * d2_d2 + 2.0 * mix1 * keep2 * d2_d3 + keep2 * keep2 * d3_d3
    mix3 = cross / (square + mix_eps)
    part = out_ref.shape[1]
    at = pl.ds(pl.multiple_of(spot_ref[0] * part, part), part)
    mixed = (
        up_ref[:, at].astype(F32)
        + v_ref[0]
        + (1.0 - mix3 * mix1) * v_ref[1]
        + keep2 * (1.0 - mix3) * v_ref[2]
    )
    out_ref[...] = mixed.astype(BF16)


def join_body(spot_ref, *refs):
    out_ref = refs[-1]
    parts = len(refs) - 1
    part = refs[0].shape[1]
    for k in range(parts):
        first = lax.rem(spot_ref[0] + k, parts) * part
        out_ref[:, pl.ds(pl.multiple_of(first, part), part)] = refs[k][...].astype(F32)


def shards(
    fixed_point,
    upstream,
    norm_gain,
    query_weight,
    keyval_weight,
    output_weight,
    log_norm,
    attention_out,
):
    rows, width = fixed_point.shape
    wide = query_weight.shape[1]
    narrow = keyval_weight.shape[1]
    size = wide + narrow
    e = narrow // 2
    heads = log_norm.shape[0]
    seq_count = lax.axis_size("seq")
    parts = lax.axis_size("head")
    block = lax.axis_index("seq")
    head = lax.axis_index("head")
    scale = e ** (-0.5)
    gain = norm_gain.reshape(1, width)
    span = (WIN_DEVS + 1) * rows
    group = min(8, seq_count)

    cols = size // group
    spot = jnp.stack([head, lax.rem(block, group)])
    smem = pl.BlockSpec(memory_space=pltpu.SMEM)
    vmem = pl.BlockSpec(memory_space=pltpu.VMEM)
    hbm = pl.BlockSpec(memory_space=pltpu.HBM)

    def pinned(value):
        return pltpu.with_memory_space_constraint(value, pltpu.HBM)

    tile = 128 if wide % 128 == 0 and 128 % (wide // group) == 0 else wide
    own_cols, hidden, kv, kvf, inv = local_call(
        prep_body,
        [
            shape_of((cols, width), BF16),
            shape_of((rows, width), BF16),
            shape_of((rows, narrow), BF16),
            shape_of((rows, narrow), F32),
            shape_of((rows, rows), F32),
        ],
        2 * width * size * cols,
        2 * width * (tile + narrow + rows),
        10,
        in_specs=[smem] + [hbm] * 4,
        scratch_shapes=[
            pltpu.VMEM((width, tile), BF16),
            pltpu.VMEM((width, narrow), BF16),
            pltpu.VMEM((rows, width), BF16),
            pltpu.VMEM((1, width), F32),
            pltpu.SemaphoreType.DMA((4,)),
        ],
    )(
        block.reshape(1),
        pinned(query_weight),
        pinned(keyval_weight),
        pinned(fixed_point),
        pinned(gain),
    )
    every_cols, bit = own_cols[None], 1
    while bit < parts:
        pairs = [(i, i ^ bit) for i in range(parts)]
        other = lax.ppermute(every_cols, "head", pairs)
        every_cols = jnp.concatenate([every_cols, other])
        bit *= 2
    earlier = [shifted(kv, "seq", offset) for offset in range(WIN_DEVS, 0, -1)]

    qf, qt, go, nt, aot, scaled, norms = local_call(
        functools.partial(start_body, heads),
        [
            shape_of((rows, wide), F32),
            shape_of((e, heads * rows), BF16),
            shape_of((e, heads * rows), F32),
            shape_of((e, heads * rows), F32),
            shape_of((e, heads * rows), F32),
            shape_of((wide, width), BF16),
            shape_of((heads, rows), F32),
        ],
        6 * rows * width * wide,
        4 * width * (2 * rows + wide),
        14,
        in_specs=[vmem] * 2 + [hbm] * 7,
        scratch_shapes=[
            pltpu.VMEM((width, wide), BF16),
            pltpu.VMEM((wide, width), BF16),
            pltpu.VMEM((rows, width), BF16),
            pltpu.VMEM((rows, width), BF16),
            pltpu.VMEM((rows, wide), BF16),
            pltpu.VMEM((1, width), F32),
            pltpu.SemaphoreType.DMA((7,)),
        ],
    )(
        hidden,
        inv,
        pinned(query_weight),
        pinned(output_weight),
        pinned(upstream),
        pinned(fixed_point),
        pinned(attention_out),
        pinned(gain),
        pinned(log_norm),
    )

    pull_outs = [shape_of((span, heads * rows), BF16), shape_of((rows, narrow), F32)]
    pull_outs += [shape_of((rows, narrow), BF16)] * WIN_DEVS
    pull_flops = 6 * span * e * heads * rows

    def exchange(score, own, terms, split):
        arrived = [shifted(term, "seq", -offset - 1) for offset, term in enumerate(terms)]
        gq = local_call(
            functools.partial(query_body, heads, scale),
            shape_of((rows, wide), BF16),
            2 * span * e * heads * rows,
            span * heads * rows * 2,
            4,
        )(kt, score)
        ahead = rotated(gq, "head") if split else []
        msg = local_call(
            functools.partial(collect_body, width),
            shape_of((rows + EXTRA, narrow if split else size), BF16),
            COLLECT * rows * size,
            rows * size * 4,
            4,
        )(own, gq, qf, kvf, *arrived)
        return rotated(msg, "head"), msg, ahead

    kvw, kt, probs, score, own, *terms = local_call(
        functools.partial(first_body, heads, scale),
        [
            shape_of((span, narrow), BF16),
            shape_of((e, span), BF16),
            shape_of((span, heads * rows), BF16),
        ]
        + pull_outs,
        pull_flops * 5 // 4,
        span * heads * rows * 2,
        16,
        in_specs=[smem] + [vmem] * (WIN_DEVS + 5),
    )(block.reshape(1), *earlier, kv, qt, go, aot, norms)
    packed, marks = [], []
    chain_shape = shape_of((parts, size, wide), BF16)
    for step in range(3):
        if step:
            score, own, lhs, row, *terms = local_call(
                functools.partial(next_body, heads, parts, scale, step == 1),
                pull_outs[:2]
                + [shape_of((parts, rows, size), BF16), shape_of((EXTRA, rows), F32)]
                + [chain_shape] * (step == 1)
                + pull_outs[2:],
                pull_flops + 2 * rows * parts * size * wide,
                span * heads * rows * 2 + parts * size * wide * 2,
                16,
                in_specs=[smem] + [vmem] * (len(ahead) + parts + 6 + len(chain)),
            )(spot, *ahead, *every_msg, inv, nt, qt, aot, kvw, probs, *chain)
            packed += [lhs, row]
            if step == 1:
                chain, *terms = terms
                chain = [chain]
        if step == 0:
            every_cols, _ = lax.optimization_barrier((every_cols, score))
            share = local_call(
                chain_body,
                shape_of((parts * cols, wide), BF16),
                2 * parts * cols * width * wide,
                2 * width * (wide + parts * cols),
                8,
            )(every_cols.reshape(parts * cols, width), scaled)
            share = share.reshape(parts, cols, wide)
            *terms, share = lax.optimization_barrier((*terms, share))
        every_msg, msg, ahead = exchange(score, own, terms, step > 0)
        if step == 0:
            chain = doubled(share, "seq", group, (share, msg, (ahead[1:], every_msg[1:])))
        marks.append(dict(msg=msg, sent=(ahead[1:], every_msg[1:])))

    part = width // parts
    mine = lax.dynamic_slice_in_dim(every_cols, head * part, part, 2)
    weight = doubled(mine, "seq", group, (marks[0]["msg"], marks[0]["sent"], marks[1]["sent"]))
    small = seq_count * parts <= 64
    fields, totals = local_call(
        functools.partial(field_body, parts, wide),
        [
            shape_of((3, rows, part), F32),
            shape_of((seq_count * parts if small else 1, 8, 128), F32),
        ],
        6 * rows * parts * size * part,
        2 * parts * size * part,
        20,
        in_specs=[smem] + [vmem] * (2 * parts + 8 + len(weight)),
        scratch_shapes=[
            pltpu.VMEM((parts, rows, size), BF16),
            pltpu.VMEM((parts, size, part), BF16),
        ],
    )(spot, *ahead, *every_msg, *packed, *weight, fixed_point, upstream, gain, inv)
    if small:
        totals = lax.all_to_all(totals, ("seq", "head"), 0, 0)
    else:
        totals = lax.psum(totals, ("seq", "head"))
    mixed = local_call(
        functools.partial(mix_body, rows * seq_count * width),
        shape_of((rows, part), BF16),
        8 * rows * part,
        18 * rows * part,
        6,
        in_specs=[smem] + [vmem] * 3,
    )(spot, totals, upstream, fields)
    every_mixed = rotated(mixed, "head")
    return local_call(
        join_body,
        shape_of((rows, width), F32),
        0,
        6 * rows * width,
        6,
        in_specs=[smem] + [vmem] * parts,
    )(spot, *every_mixed)


def solution(mesh):
    in_specs = (
        P("seq", None),
        P("seq", None),
        P(),
        P(None, "head"),
        P(None, "head"),
        P("head", None),
        P("head", "seq"),
        P("seq", "head"),
    )
    out_specs = P("seq", None)
    return jax.shard_map(shards, mesh=mesh, in_specs=in_specs, out_specs=out_specs, check_vma=False)
```

```python
import functools

import jax
import jax.numpy as jnp
from jax import lax
from jax.experimental import pallas as pl
from jax.experimental.pallas import tpu as pltpu
from jax.sharding import PartitionSpec as P

WIN_DEVS = 4
norm_eps = 1e-05
mix_eps = 1e-06
F32 = jnp.float32
BF16 = jnp.bfloat16
COLLECT = 50000
EXTRA = 16
NT = (((1,), (1,)), ((), ()))


def shape_of(shape, dtype):
    return jax.ShapeDtypeStruct(shape, dtype)


def local_call(body, outs, flops, moved, room, **more):
    return pl.pallas_call(
        body,
        out_shape=outs,
        compiler_params=pltpu.CompilerParams(vmem_limit_bytes=room * 1024 * 1024),
        cost_estimate=pl.CostEstimate(flops=flops, bytes_accessed=moved, transcendentals=0),
        **more,
    )


def shifted(value, axis, steps):
    count = lax.axis_size(axis)
    initial, last = (max(0, -steps), min(count, count - steps))
    return lax.ppermute(value, axis, [(source, source + steps) for source in range(initial, last)])


def rotated(value, axis):
    count = lax.axis_size(axis)
    parts = [value]
    for step in range(1, count):
        parts.append(lax.ppermute(value, axis, [(i, (i - step) % count) for i in range(count)]))
    return parts


def doubled(value, axis, group, gates):
    count = lax.axis_size(axis)
    near, bit = [value[None]], group // 2
    for gate in gates:
        near = list(lax.optimization_barrier((tuple(near), gate))[0])
        pairs = [(i, i ^ bit) for i in range(count)]
        if len(near) > 1:
            near = [jnp.concatenate(near)]
        if bit == 1:
            return near + [lax.ppermute(near[0], axis, pairs)]
        near.append(lax.ppermute(near[0], axis, pairs))
        bit //= 2


def assemble(place, wide, out_ref, refs):
    group = sum(ref.shape[0] for ref in refs)
    cut = wide // group
    rest_cut = refs[0].shape[2] - cut
    entries = [(ref, j) for ref in refs for j in range(ref.shape[0])]
    for j, (ref, at) in enumerate(entries):
        distance, bit, rest = 0, group // 2, j
        while rest:
            distance += bit * (rest & 1)
            rest >>= 1
            bit //= 2
        index = lax.bitwise_xor(place, jnp.int32(distance))
        first = pl.multiple_of(index * cut, cut)
        second = pl.multiple_of(wide + index * rest_cut, rest_cut)
        for k in range(out_ref.shape[0]):
            out_ref[k, pl.ds(first, cut), :] = ref[at, k, :cut, :]
            out_ref[k, pl.ds(second, rest_cut), :] = ref[at, k, cut:, :]


def prep_body(block_ref, qw_ref, kvw_ref, z_ref, gain_ref, cols_ref, hidden_ref, kv_ref, kvf_ref,
              inv_ref, q_tile, kv_tile, z_tile, gain_tile, sems):
    tile = q_tile.shape[1]
    wide, narrow = qw_ref.shape[1], kvw_ref.shape[1]
    group = (wide + narrow) // cols_ref.shape[0]
    place = lax.rem(block_ref[0], group)
    q_take, kv_take = wide // group, narrow // group
    q_at = place * q_take
    q_first = pl.multiple_of(q_at // tile * tile, tile)
    copies = [
        pltpu.make_async_copy(qw_ref.at[:, pl.ds(q_first, tile)], q_tile, sems.at[0]),
        pltpu.make_async_copy(kvw_ref, kv_tile, sems.at[1]),
        pltpu.make_async_copy(z_ref, z_tile, sems.at[2]),
        pltpu.make_async_copy(gain_ref, gain_tile, sems.at[3]),
    ]
    for copy in copies:
        copy.start()
    first = 0
    for copy, ref, at, take in (
        (copies[0], q_tile, q_at - q_first, q_take),
        (copies[1], kv_tile, place * kv_take, kv_take),
    ):
        copy.wait()
        total = ref.shape[1]
        row = lax.broadcasted_iota(jnp.int32, (take, total), 0) + at
        pick = (row == lax.broadcasted_iota(jnp.int32, (take, total), 1)).astype(BF16)
        cols = lax.dot_general(pick, ref[...], NT, preferred_element_type=F32)
        cols_ref[first : first + take, :] = cols.astype(BF16)
        first += take
    copies[2].wait()
    copies[3].wait()
    z = z_tile[...].astype(F32)
    inverse = lax.rsqrt(jnp.mean(z * z, axis=1, keepdims=True) + norm_eps)
    hidden = (z * inverse * gain_tile[...]).astype(BF16)
    hidden_ref[...] = hidden
    kvf = jnp.dot(hidden, kv_tile[...], preferred_element_type=F32)
    kvf_ref[...] = kvf
    kv_ref[...] = kvf.astype(BF16)
    inv_ref[...] = jnp.broadcast_to(inverse, inv_ref.shape)


def chain_body(cols_ref, scaled_ref, out_ref):
    share = lax.dot_general(cols_ref[...], scaled_ref[...], NT, preferred_element_type=F32)
    out_ref[...] = share.astype(BF16)


def lanes_of(value, heads):
    size = value.shape[0] // heads
    return jnp.concatenate([value[i * size : (i + 1) * size] for i in range(heads)], axis=1)


def start_body(heads, hidden_ref, inv_ref, qw_ref, ow_ref, up_ref, z_ref, ao_ref, gain_ref, ln_ref,
               qf_ref, qt_ref, go_ref, nt_ref, aot_ref, scaled_ref, norms_ref,
               qw_tile, ow_tile, up_tile, z_tile, ao_tile, gain_tile, sems):
    copies = [
        pltpu.make_async_copy(source, target, sems.at[i])
        for i, (source, target) in enumerate(
            ((ow_ref, ow_tile), (up_ref, up_tile), (z_ref, z_tile), (qw_ref, qw_tile),
             (ao_ref, ao_tile), (gain_ref, gain_tile), (ln_ref, norms_ref))
        )
    ]
    for copy in copies:
        copy.start()
    for copy in copies[:3]:
        copy.wait()
    out = lax.dot_general(up_tile[...], ow_tile[...], NT, preferred_element_type=F32)
    go_ref[...] = lanes_of(out.T, heads)
    base = lax.dot_general(z_tile[...], ow_tile[...], NT, preferred_element_type=F32)
    nt_ref[...] = lanes_of((base * inv_ref[:, :1]).T, heads)
    copies[3].wait()
    qf = jnp.dot(hidden_ref[...], qw_tile[...], preferred_element_type=F32)
    qf_ref[...] = qf
    qt_ref[...] = lanes_of(qf.T, heads).astype(BF16)
    for copy in copies[4:]:
        copy.wait()
    scaled_ref[...] = (ow_tile[...].astype(F32) * gain_tile[...]).astype(BF16)
    aot_ref[...] = lanes_of(ao_tile[...].astype(F32).T, heads)


def pull(heads, scale, go, aot, qt, kvw_ref, probs, score_ref, own_ref, term_refs):
    e = go.shape[0]
    rows = go.shape[1] // heads
    row_terms = jnp.sum(go * aot, axis=0, keepdims=True)
    gob = go.astype(BF16)
    grad_prob = jnp.dot(kvw_ref[:, e:], gob, preferred_element_type=F32)
    grad_score = (probs.astype(F32) * (grad_prob - row_terms)).astype(BF16)
    score_ref[...] = grad_score
    grad_key = lax.dot_general(grad_score, qt, NT, preferred_element_type=F32) * scale
    grad_value = lax.dot_general(probs, gob, NT, preferred_element_type=F32)
    terms = jnp.concatenate([grad_key, grad_value], axis=1)
    for offset in range(1, len(term_refs) + 1):
        first = (len(term_refs) - offset) * rows
        term_refs[offset - 1][...] = terms[first : first + rows].astype(BF16)
    own_ref[...] = terms[len(term_refs) * rows :]


def query_body(heads, scale, kt_ref, score_ref, gq_ref):
    rows = gq_ref.shape[0]
    grad_query = jnp.dot(kt_ref[...], score_ref[...], preferred_element_type=F32) * scale
    parts = [grad_query[:, i * rows : (i + 1) * rows] for i in range(heads)]
    gq_ref[...] = jnp.concatenate(parts, axis=0).T.astype(BF16)


def first_body(heads, scale, block_ref, *refs):
    windows = refs[: WIN_DEVS + 1]
    qt_ref, go_ref, aot_ref, ln_ref = refs[WIN_DEVS + 1 : WIN_DEVS + 5]
    kvw_ref, kt_ref, probs_ref, score_ref, own_ref = refs[WIN_DEVS + 5 : WIN_DEVS + 10]
    term_refs = refs[WIN_DEVS + 10 :]
    rows = windows[0].shape[0]
    for place, ref in enumerate(windows):
        kvw_ref[place * rows : (place + 1) * rows, :] = ref[...]
    kvw = kvw_ref[...]
    e = kvw.shape[1] // 2
    kt_ref[...] = kvw.astype(F32).T[:e].astype(BF16)
    scores = jnp.dot(kvw[:, :e], qt_ref[...], preferred_element_type=F32) * scale
    norms = jnp.concatenate([ln_ref[i : i + 1, :] for i in range(heads)], axis=1)
    key_pos = lax.broadcasted_iota(jnp.int32, scores.shape, 0)
    query_pos = lax.broadcasted_iota(jnp.int32, scores.shape, 1) & (rows - 1)
    allowed = (key_pos > query_pos) & (key_pos <= query_pos + WIN_DEVS * rows)
    allowed = allowed & (key_pos >= (WIN_DEVS - block_ref[0]) * rows)
    probs = jnp.where(allowed, jnp.exp(scores - norms), 0.0).astype(BF16)
    probs_ref[...] = probs
    pull(heads, scale, go_ref[...], aot_ref[...], qt_ref[...], kvw_ref, probs,
         score_ref, own_ref, term_refs)


def next_body(heads, parts, scale, fresh, spot_ref, *refs):
    gq_refs, refs = ([], refs) if fresh else (refs[:parts], refs[parts:])
    msg_refs, refs = refs[:parts], refs[parts:]
    inv_ref, nt_ref, qt_ref, aot_ref, kvw_ref, probs_ref, *refs = refs
    if fresh:
        *parts_refs, score_ref, own_ref, lhs_ref, row_ref, chain_ref = refs[:7]
        term_refs = refs[7:]
        assemble(spot_ref[1], chain_ref.shape[2], chain_ref, parts_refs)
    else:
        chain_ref, score_ref, own_ref, lhs_ref, row_ref = refs[:5]
        term_refs = refs[5:]
    rows, wide = lhs_ref.shape[1], chain_ref.shape[2]
    out = jnp.zeros((rows, wide), F32)
    along = jnp.zeros((EXTRA, rows), F32)
    for k in range(parts):
        index = lax.rem(spot_ref[0] + k, parts)
        msg = msg_refs[k][...]
        chain = chain_ref[k]
        lhs = msg[:rows]
        if gq_refs:
            lhs = jnp.concatenate([gq_refs[k][...], lhs], axis=1)
        out += jnp.dot(lhs, chain, preferred_element_type=F32)
        lhs_ref[index] = lhs
        along += msg[rows:, :rows].astype(F32)
    row_ref[...] = along
    along = jnp.sum(along, axis=0, keepdims=True)
    along = jnp.concatenate([along] * heads, axis=1)
    go = lanes_of((out * inv_ref[:, :1]).T, heads)
    inv_row = jnp.concatenate([inv_ref[...].T[:1, :]] * heads, axis=1)
    go = go - inv_row * along * nt_ref[...]
    pull(heads, scale, go, aot_ref[...], qt_ref[...], kvw_ref, probs_ref[...],
         score_ref, own_ref, term_refs)


def collect_body(width, own_ref, gq_ref, qf_ref, kvf_ref, *refs):
    msg_ref = refs[-1]
    rows = own_ref.shape[0]
    total = own_ref[...]
    for ref in refs[:-1]:
        total += ref[...].astype(F32)
    total = total.astype(BF16)
    ahead = msg_ref.shape[1] - total.shape[1]
    if ahead:
        msg_ref[:rows, :ahead] = gq_ref[...]
        msg_ref[rows:, :] = jnp.zeros((EXTRA, msg_ref.shape[1]), BF16)
    msg_ref[:rows, ahead:] = total
    prods = gq_ref[...].astype(F32) * qf_ref[...]
    partial = total.astype(F32) * kvf_ref[...]
    lanes = partial.shape[1]
    for first in range(0, prods.shape[1], lanes):
        partial += prods[:, first : first + lanes]
    along = jnp.sum(partial.T, axis=0, keepdims=True) * (1.0 / width)
    high = along.astype(BF16).astype(F32)
    place = lax.broadcasted_iota(jnp.int32, (EXTRA, rows), 0)
    extra = jnp.where(place == 0, high, jnp.where(place == 1, along - high, 0.0))
    msg_ref[rows:, :rows] = extra.astype(BF16)


def field_body(parts, wide, spot_ref, *refs):
    gq_refs, msg_refs, refs = refs[:parts], refs[parts : 2 * parts], refs[2 * parts :]
    lhs1_ref, row1_ref, lhs2_ref, row2_ref, *refs = refs
    *w_refs, z_ref, up_ref, gain_ref, inv_ref, v_ref, tot_ref, lhs3_ref, w_ref = refs
    rows, part = v_ref.shape[1:]
    head = spot_ref[0]
    row3 = jnp.zeros((EXTRA, rows), F32)
    for k in range(parts):
        msg = msg_refs[k][...]
        lhs3_ref[lax.rem(head + k, parts)] = jnp.concatenate(
            [gq_refs[k][...], msg[:rows]], axis=1
        )
        row3 += msg[rows:].astype(F32)
    assemble(spot_ref[1], wide, w_ref, w_refs)
    y = jnp.zeros((3 * rows, part), F32)
    for k in range(parts):
        lhs = jnp.concatenate([lhs1_ref[k], lhs2_ref[k], lhs3_ref[k]], axis=0)
        weight = w_ref[lax.rem(k - head + parts, parts)]
        y += jnp.dot(lhs, weight, preferred_element_type=F32)
    at = pl.ds(pl.multiple_of(head * part, part), part)
    inverse = inv_ref[:, :1]
    normed = z_ref[:, at].astype(F32) * inverse
    gain = gain_ref[:, at]
    fields = []
    for step, row in enumerate((row1_ref[...], row2_ref[...], row3)):
        along = jnp.broadcast_to(jnp.sum(row, axis=0, keepdims=True), (rows, rows)).T[:, :1]
        y_step = y[step * rows : (step + 1) * rows]
        fields.append(inverse * (y_step * gain - normed * along))
        v_ref[step] = fields[step]
    first, second, third = fields
    change1 = first - up_ref[:, at].astype(F32)
    change2 = second - first
    change3 = third - second
    pairs = [
        (change1, first), (change1, change1), (change2, first), (change2, change2),
        (change2, second), (change2, change3), (change3, second), (change3, change3),
    ]
    lanes = tot_ref.shape[2]
    sums = []
    for a, b in pairs:
        total = jnp.sum(a * b, axis=0, keepdims=True)
        sums.append(sum(total[:, i : i + lanes] for i in range(0, part, lanes)))
    totals = jnp.concatenate(sums, axis=0)
    for k in range(tot_ref.shape[0]):
        tot_ref[k] = totals


def mix_body(entries, spot_ref, tot_ref, up_ref, v_ref, out_ref):
    totals = jnp.sum(jnp.sum(tot_ref[...], axis=0), axis=1, keepdims=True) / entries
    s_r1, s_s, d2_v1, d2_d2, d2_v2, d2_d3, d3_v2, d3_d3 = [totals[i : i + 1] for i in range(8)]
    mix1 = s_r1 / (s_s + mix_eps)
    keep1 = 1.0 - mix1
    mix2 = keep1 * (d2_v1 + keep1 * d2_d2) / (keep1 * keep1 * d2_d2 + mix_eps)
    keep2 = keep1 * (1.0 - mix2)
    cross = mix1 * (d2_v2 + keep2 * d2_d3) + keep2 * (d3_v2 + keep2 * d3_d3)
    square = mix1 * mix1 * d2_d2 + 2.0 * mix1 * keep2 * d2_d3 + keep2 * keep2 * d3_d3
    mix3 = cross / (square + mix_eps)
    part = out_ref.shape[1]
    at = pl.ds(pl.multiple_of(spot_ref[0] * part, part), part)
    mixed = (
        up_ref[:, at].astype(F32)
        + v_ref[0]
        + (1.0 - mix3 * mix1) * v_ref[1]
        + keep2 * (1.0 - mix3) * v_ref[2]
    )
    out_ref[...] = mixed.astype(BF16)


def join_body(spot_ref, *refs):
    out_ref = refs[-1]
    parts = len(refs) - 1
    part = refs[0].shape[1]
    for k in range(parts):
        first = lax.rem(spot_ref[0] + k, parts) * part
        out_ref[:, pl.ds(pl.multiple_of(first, part), part)] = refs[k][...].astype(F32)


def shards(
    fixed_point,
    upstream,
    norm_gain,
    query_weight,
    keyval_weight,
    output_weight,
    log_norm,
    attention_out,
):
    rows, width = fixed_point.shape
    wide = query_weight.shape[1]
    narrow = keyval_weight.shape[1]
    size = wide + narrow
    e = narrow // 2
    heads = log_norm.shape[0]
    seq_count = lax.axis_size("seq")
    parts = lax.axis_size("head")
    block = lax.axis_index("seq")
    head = lax.axis_index("head")
    scale = e ** (-0.5)
    gain = norm_gain.reshape(1, width)
    span = (WIN_DEVS + 1) * rows
    group = min(8, seq_count)

    cols = size // group
    spot = jnp.stack([head, lax.rem(block, group)])
    smem = pl.BlockSpec(memory_space=pltpu.SMEM)
    vmem = pl.BlockSpec(memory_space=pltpu.VMEM)
    hbm = pl.BlockSpec(memory_space=pltpu.HBM)

    def pinned(value):
        return pltpu.with_memory_space_constraint(value, pltpu.HBM)

    tile = 128 if wide % 128 == 0 and 128 % (wide // group) == 0 else wide
    own_cols, hidden, kv, kvf, inv = local_call(
        prep_body,
        [
            shape_of((cols, width), BF16),
            shape_of((rows, width), BF16),
            shape_of((rows, narrow), BF16),
            shape_of((rows, narrow), F32),
            shape_of((rows, rows), F32),
        ],
        2 * width * size * cols,
        2 * width * (tile + narrow + rows),
        10,
        in_specs=[smem] + [hbm] * 4,
        scratch_shapes=[
            pltpu.VMEM((width, tile), BF16),
            pltpu.VMEM((width, narrow), BF16),
            pltpu.VMEM((rows, width), BF16),
            pltpu.VMEM((1, width), F32),
            pltpu.SemaphoreType.DMA((4,)),
        ],
    )(
        block.reshape(1),
        pinned(query_weight),
        pinned(keyval_weight),
        pinned(fixed_point),
        pinned(gain),
    )
    every_cols = jnp.stack(rotated(own_cols, "head"))
    earlier = [shifted(kv, "seq", offset) for offset in range(WIN_DEVS, 0, -1)]

    qf, qt, go, nt, aot, scaled, norms = local_call(
        functools.partial(start_body, heads),
        [
            shape_of((rows, wide), F32),
            shape_of((e, heads * rows), BF16),
            shape_of((e, heads * rows), F32),
            shape_of((e, heads * rows), F32),
            shape_of((e, heads * rows), F32),
            shape_of((wide, width), BF16),
            shape_of((heads, rows), F32),
        ],
        6 * rows * width * wide,
        4 * width * (2 * rows + wide),
        14,
        in_specs=[vmem] * 2 + [hbm] * 7,
        scratch_shapes=[
            pltpu.VMEM((width, wide), BF16),
            pltpu.VMEM((wide, width), BF16),
            pltpu.VMEM((rows, width), BF16),
            pltpu.VMEM((rows, width), BF16),
            pltpu.VMEM((rows, wide), BF16),
            pltpu.VMEM((1, width), F32),
            pltpu.SemaphoreType.DMA((7,)),
        ],
    )(
        hidden,
        inv,
        pinned(query_weight),
        pinned(output_weight),
        pinned(upstream),
        pinned(fixed_point),
        pinned(attention_out),
        pinned(gain),
        pinned(log_norm),
    )

    pull_outs = [shape_of((span, heads * rows), BF16), shape_of((rows, narrow), F32)]
    pull_outs += [shape_of((rows, narrow), BF16)] * WIN_DEVS
    pull_flops = 6 * span * e * heads * rows

    def exchange(score, own, terms, split):
        arrived = [shifted(term, "seq", -offset - 1) for offset, term in enumerate(terms)]
        gq = local_call(
            functools.partial(query_body, heads, scale),
            shape_of((rows, wide), BF16),
            2 * span * e * heads * rows,
            span * heads * rows * 2,
            4,
        )(kt, score)
        ahead = rotated(gq, "head") if split else []
        msg = local_call(
            functools.partial(collect_body, width),
            shape_of((rows + EXTRA, narrow if split else size), BF16),
            COLLECT * rows * size,
            rows * size * 4,
            4,
        )(own, gq, qf, kvf, *arrived)
        return rotated(msg, "head"), msg, ahead

    kvw, kt, probs, score, own, *terms = local_call(
        functools.partial(first_body, heads, scale),
        [
            shape_of((span, narrow), BF16),
            shape_of((e, span), BF16),
            shape_of((span, heads * rows), BF16),
        ]
        + pull_outs,
        pull_flops * 5 // 4,
        span * heads * rows * 2,
        16,
        in_specs=[smem] + [vmem] * (WIN_DEVS + 5),
    )(block.reshape(1), *earlier, kv, qt, go, aot, norms)
    packed, marks = [], []
    chain_shape = shape_of((parts, size, wide), BF16)
    for step in range(3):
        if step:
            score, own, lhs, row, *terms = local_call(
                functools.partial(next_body, heads, parts, scale, step == 1),
                pull_outs[:2]
                + [shape_of((parts, rows, size), BF16), shape_of((EXTRA, rows), F32)]
                + [chain_shape] * (step == 1)
                + pull_outs[2:],
                pull_flops + 2 * rows * parts * size * wide,
                span * heads * rows * 2 + parts * size * wide * 2,
                16,
                in_specs=[smem] + [vmem] * (len(ahead) + parts + 6 + len(chain)),
            )(spot, *ahead, *every_msg, inv, nt, qt, aot, kvw, probs, *chain)
            packed += [lhs, row]
            if step == 1:
                chain, *terms = terms
                chain = [chain]
        if step == 0:
            every_cols, _ = lax.optimization_barrier((every_cols, score))
            share = local_call(
                chain_body,
                shape_of((parts * cols, wide), BF16),
                2 * parts * cols * width * wide,
                2 * width * (wide + parts * cols),
                8,
            )(every_cols.reshape(parts * cols, width), scaled)
            share = share.reshape(parts, cols, wide)
            *terms, share = lax.optimization_barrier((*terms, share))
        every_msg, msg, ahead = exchange(score, own, terms, step > 0)
        if step == 0:
            chain = doubled(share, "seq", group, (share, msg, (ahead[1:], every_msg[1:])))
        marks.append(dict(msg=msg, sent=(ahead[1:], every_msg[1:])))

    part = width // parts
    mine = lax.dynamic_slice_in_dim(every_cols, head * part, part, 2)
    weight = doubled(mine, "seq", group, (marks[0]["msg"], marks[0]["sent"], marks[1]["sent"]))
    small = seq_count * parts <= 64
    fields, totals = local_call(
        functools.partial(field_body, parts, wide),
        [
            shape_of((3, rows, part), F32),
            shape_of((seq_count * parts if small else 1, 8, 128), F32),
        ],
        6 * rows * parts * size * part,
        2 * parts * size * part,
        20,
        in_specs=[smem] + [vmem] * (2 * parts + 8 + len(weight)),
        scratch_shapes=[
            pltpu.VMEM((parts, rows, size), BF16),
            pltpu.VMEM((parts, size, part), BF16),
        ],
    )(spot, *ahead, *every_msg, *packed, *weight, fixed_point, upstream, gain, inv)
    if small:
        totals = lax.all_to_all(totals, ("seq", "head"), 0, 0)
    else:
        totals = lax.psum(totals, ("seq", "head"))
    mixed = local_call(
        functools.partial(mix_body, rows * seq_count * width),
        shape_of((rows, part), BF16),
        8 * rows * part,
        18 * rows * part,
        6,
        in_specs=[smem] + [vmem] * 3,
    )(spot, totals, upstream, fields)
    every_mixed = rotated(mixed, "head")
    return local_call(
        join_body,
        shape_of((rows, width), F32),
        0,
        6 * rows * width,
        6,
        in_specs=[smem] + [vmem] * parts,
    )(spot, *every_mixed)


def solution(mesh):
    in_specs = (
        P("seq", None),
        P("seq", None),
        P(),
        P(None, "head"),
        P(None, "head"),
        P("head", None),
        P("head", "seq"),
        P("seq", "head"),
    )
    out_specs = P("seq", None)
    return jax.shard_map(shards, mesh=mesh, in_specs=in_specs, out_specs=out_specs, check_vma=False)
```

```python
import functools

import jax
import jax.numpy as jnp
from jax import lax
from jax.experimental import pallas as pl
from jax.experimental.pallas import tpu as pltpu
from jax.sharding import PartitionSpec as P

WIN_DEVS = 4
norm_eps = 1e-05
mix_eps = 1e-06
F32 = jnp.float32
BF16 = jnp.bfloat16
COLLECT = 50000
EXTRA = 16
NT = (((1,), (1,)), ((), ()))


def shape_of(shape, dtype):
    return jax.ShapeDtypeStruct(shape, dtype)


def local_call(body, outs, flops, moved, room, **more):
    return pl.pallas_call(
        body,
        out_shape=outs,
        compiler_params=pltpu.CompilerParams(vmem_limit_bytes=room * 1024 * 1024),
        cost_estimate=pl.CostEstimate(flops=flops, bytes_accessed=moved, transcendentals=0),
        **more,
    )


def shifted(value, axis, steps):
    count = lax.axis_size(axis)
    initial, last = (max(0, -steps), min(count, count - steps))
    return lax.ppermute(value, axis, [(source, source + steps) for source in range(initial, last)])


def rotated(value, axis):
    count = lax.axis_size(axis)
    parts = [value]
    for step in range(1, count):
        parts.append(lax.ppermute(value, axis, [(i, (i - step) % count) for i in range(count)]))
    return parts


def doubled(value, axis, group, gates):
    count = lax.axis_size(axis)
    near, bit = [value[None]], group // 2
    for gate in gates:
        near = list(lax.optimization_barrier((tuple(near), gate))[0])
        pairs = [(i, i ^ bit) for i in range(count)]
        if len(near) > 1:
            near = [jnp.concatenate(near)]
        if bit == 1:
            return near + [lax.ppermute(near[0], axis, pairs)]
        near.append(lax.ppermute(near[0], axis, pairs))
        bit //= 2


def assemble(place, wide, out_ref, refs):
    group = sum(ref.shape[0] for ref in refs)
    cut = wide // group
    rest_cut = refs[0].shape[2] - cut
    entries = [(ref, j) for ref in refs for j in range(ref.shape[0])]
    for j, (ref, at) in enumerate(entries):
        distance, bit, rest = 0, group // 2, j
        while rest:
            distance += bit * (rest & 1)
            rest >>= 1
            bit //= 2
        index = lax.bitwise_xor(place, jnp.int32(distance))
        first = pl.multiple_of(index * cut, cut)
        second = pl.multiple_of(wide + index * rest_cut, rest_cut)
        for k in range(out_ref.shape[0]):
            out_ref[k, pl.ds(first, cut), :] = ref[at, k, :cut, :]
            out_ref[k, pl.ds(second, rest_cut), :] = ref[at, k, cut:, :]


def prep_body(block_ref, qw_ref, kvw_ref, z_ref, gain_ref, cols_ref, hidden_ref, kv_ref, kvf_ref,
              inv_ref, z_tile, q_tile, kv_tile, gain_tile, sems):
    tile = q_tile.shape[1]
    wide, narrow = qw_ref.shape[1], kvw_ref.shape[1]
    group = (wide + narrow) // cols_ref.shape[0]
    place = lax.rem(block_ref[0], group)
    q_take, kv_take = wide // group, narrow // group
    q_at = place * q_take
    q_first = pl.multiple_of(q_at // tile * tile, tile)
    copies = [
        pltpu.make_async_copy(qw_ref.at[:, pl.ds(q_first, tile)], q_tile, sems.at[0]),
        pltpu.make_async_copy(kvw_ref, kv_tile, sems.at[1]),
        pltpu.make_async_copy(z_ref, z_tile, sems.at[2]),
        pltpu.make_async_copy(gain_ref, gain_tile, sems.at[3]),
    ]
    for copy in copies:
        copy.start()
    first = 0
    for copy, ref, at, take in (
        (copies[0], q_tile, q_at - q_first, q_take),
        (copies[1], kv_tile, place * kv_take, kv_take),
    ):
        copy.wait()
        total = ref.shape[1]
        row = lax.broadcasted_iota(jnp.int32, (take, total), 0) + at
        pick = (row == lax.broadcasted_iota(jnp.int32, (take, total), 1)).astype(BF16)
        cols = lax.dot_general(pick, ref[...], NT, preferred_element_type=F32)
        cols_ref[first : first + take, :] = cols.astype(BF16)
        first += take
    copies[2].wait()
    copies[3].wait()
    z = z_tile[...].astype(F32)
    inverse = lax.rsqrt(jnp.mean(z * z, axis=1, keepdims=True) + norm_eps)
    hidden = (z * inverse * gain_tile[...]).astype(BF16)
    hidden_ref[...] = hidden
    kvf = jnp.dot(hidden, kv_tile[...], preferred_element_type=F32)
    kvf_ref[...] = kvf
    kv_ref[...] = kvf.astype(BF16)
    inv_ref[...] = jnp.broadcast_to(inverse, inv_ref.shape)


def chain_body(cols_ref, scaled_ref, out_ref):
    share = lax.dot_general(cols_ref[...], scaled_ref[...], NT, preferred_element_type=F32)
    out_ref[...] = share.astype(BF16)


def lanes_of(value, heads):
    size = value.shape[0] // heads
    return jnp.concatenate([value[i * size : (i + 1) * size] for i in range(heads)], axis=1)


def start_body(heads, hidden_ref, inv_ref, z_ref, gain_ref, qw_ref, up_ref, ow_ref, ao_ref, ln_ref,
               qf_ref, qt_ref, go_ref, nt_ref, aot_ref, scaled_ref, norms_ref,
               ow_tile, ao_tile, sems):
    copies = [
        pltpu.make_async_copy(source, target, sems.at[i])
        for i, (source, target) in enumerate(
            ((ow_ref, ow_tile), (ao_ref, ao_tile), (ln_ref, norms_ref))
        )
    ]
    for copy in copies:
        copy.start()
    qf = jnp.dot(hidden_ref[...], qw_ref[...], preferred_element_type=F32)
    qf_ref[...] = qf
    qt_ref[...] = lanes_of(qf.T, heads).astype(BF16)
    for copy in copies:
        copy.wait()
    aot_ref[...] = lanes_of(ao_tile[...].astype(F32).T, heads)
    weight = ow_tile[...]
    out = lax.dot_general(up_ref[...], weight, NT, preferred_element_type=F32)
    go_ref[...] = lanes_of(out.T, heads)
    base = lax.dot_general(z_ref[...], weight, NT, preferred_element_type=F32)
    nt_ref[...] = lanes_of((base * inv_ref[:, :1]).T, heads)
    scaled_ref[...] = (weight.astype(F32) * gain_ref[...]).astype(BF16)


def pull(heads, scale, go, aot, qt, kvw_ref, probs, score_ref, own_ref, term_refs):
    e = go.shape[0]
    rows = go.shape[1] // heads
    row_terms = jnp.sum(go * aot, axis=0, keepdims=True)
    gob = go.astype(BF16)
    grad_prob = jnp.dot(kvw_ref[:, e:], gob, preferred_element_type=F32)
    grad_score = (probs.astype(F32) * (grad_prob - row_terms)).astype(BF16)
    score_ref[...] = grad_score
    grad_key = lax.dot_general(grad_score, qt, NT, preferred_element_type=F32) * scale
    grad_value = lax.dot_general(probs, gob, NT, preferred_element_type=F32)
    terms = jnp.concatenate([grad_key, grad_value], axis=1)
    for offset in range(1, len(term_refs) + 1):
        first = (len(term_refs) - offset) * rows
        term_refs[offset - 1][...] = terms[first : first + rows].astype(BF16)
    own_ref[...] = terms[len(term_refs) * rows :]


def query_body(heads, scale, kt_ref, score_ref, gq_ref):
    rows = gq_ref.shape[0]
    grad_query = jnp.dot(kt_ref[...], score_ref[...], preferred_element_type=F32) * scale
    parts = [grad_query[:, i * rows : (i + 1) * rows] for i in range(heads)]
    gq_ref[...] = jnp.concatenate(parts, axis=0).T.astype(BF16)


def first_body(heads, scale, block_ref, *refs):
    windows = refs[: WIN_DEVS + 1]
    qt_ref, go_ref, aot_ref, ln_ref = refs[WIN_DEVS + 1 : WIN_DEVS + 5]
    kvw_ref, kt_ref, probs_ref, score_ref, own_ref = refs[WIN_DEVS + 5 : WIN_DEVS + 10]
    term_refs = refs[WIN_DEVS + 10 :]
    rows = windows[0].shape[0]
    for place, ref in enumerate(windows):
        kvw_ref[place * rows : (place + 1) * rows, :] = ref[...]
    kvw = kvw_ref[...]
    e = kvw.shape[1] // 2
    kt_ref[...] = kvw.astype(F32).T[:e].astype(BF16)
    scores = jnp.dot(kvw[:, :e], qt_ref[...], preferred_element_type=F32) * scale
    norms = jnp.concatenate([ln_ref[i : i + 1, :] for i in range(heads)], axis=1)
    key_pos = lax.broadcasted_iota(jnp.int32, scores.shape, 0)
    query_pos = lax.broadcasted_iota(jnp.int32, scores.shape, 1) & (rows - 1)
    allowed = (key_pos > query_pos) & (key_pos <= query_pos + WIN_DEVS * rows)
    allowed = allowed & (key_pos >= (WIN_DEVS - block_ref[0]) * rows)
    probs = jnp.where(allowed, jnp.exp(scores - norms), 0.0).astype(BF16)
    probs_ref[...] = probs
    pull(heads, scale, go_ref[...], aot_ref[...], qt_ref[...], kvw_ref, probs,
         score_ref, own_ref, term_refs)


def next_body(heads, parts, scale, fresh, spot_ref, *refs):
    gq_refs, refs = ([], refs) if fresh else (refs[:parts], refs[parts:])
    msg_refs, refs = refs[:parts], refs[parts:]
    inv_ref, nt_ref, qt_ref, aot_ref, kvw_ref, probs_ref, *refs = refs
    if fresh:
        *parts_refs, score_ref, own_ref, lhs_ref, row_ref, chain_ref = refs[:7]
        term_refs = refs[7:]
        assemble(spot_ref[1], chain_ref.shape[2], chain_ref, parts_refs)
    else:
        chain_ref, score_ref, own_ref, lhs_ref, row_ref = refs[:5]
        term_refs = refs[5:]
    rows, wide = lhs_ref.shape[1], chain_ref.shape[2]
    out = jnp.zeros((rows, wide), F32)
    along = jnp.zeros((EXTRA, rows), F32)
    for k in range(parts):
        index = lax.rem(spot_ref[0] + k, parts)
        msg = msg_refs[k][...]
        chain = chain_ref[k]
        lhs = msg[:rows]
        if gq_refs:
            lhs = jnp.concatenate([gq_refs[k][...], lhs], axis=1)
        out += jnp.dot(lhs, chain, preferred_element_type=F32)
        lhs_ref[index] = lhs
        along += msg[rows:, :rows].astype(F32)
    row_ref[...] = along
    along = jnp.sum(along, axis=0, keepdims=True)
    along = jnp.concatenate([along] * heads, axis=1)
    go = lanes_of((out * inv_ref[:, :1]).T, heads)
    inv_row = jnp.concatenate([inv_ref[...].T[:1, :]] * heads, axis=1)
    go = go - inv_row * along * nt_ref[...]
    pull(heads, scale, go, aot_ref[...], qt_ref[...], kvw_ref, probs_ref[...],
         score_ref, own_ref, term_refs)


def collect_body(width, own_ref, gq_ref, qf_ref, kvf_ref, *refs):
    msg_ref = refs[-1]
    rows = own_ref.shape[0]
    total = own_ref[...]
    for ref in refs[:-1]:
        total += ref[...].astype(F32)
    total = total.astype(BF16)
    ahead = msg_ref.shape[1] - total.shape[1]
    if ahead:
        msg_ref[:rows, :ahead] = gq_ref[...]
        msg_ref[rows:, :] = jnp.zeros((EXTRA, msg_ref.shape[1]), BF16)
    msg_ref[:rows, ahead:] = total
    prods = gq_ref[...].astype(F32) * qf_ref[...]
    partial = total.astype(F32) * kvf_ref[...]
    lanes = partial.shape[1]
    for first in range(0, prods.shape[1], lanes):
        partial += prods[:, first : first + lanes]
    along = jnp.sum(partial.T, axis=0, keepdims=True) * (1.0 / width)
    high = along.astype(BF16).astype(F32)
    place = lax.broadcasted_iota(jnp.int32, (EXTRA, rows), 0)
    extra = jnp.where(place == 0, high, jnp.where(place == 1, along - high, 0.0))
    msg_ref[rows:, :rows] = extra.astype(BF16)


def field_body(parts, wide, spot_ref, *refs):
    gq_refs, msg_refs, refs = refs[:parts], refs[parts : 2 * parts], refs[2 * parts :]
    lhs1_ref, row1_ref, lhs2_ref, row2_ref, *refs = refs
    *w_refs, z_ref, up_ref, gain_ref, inv_ref, v_ref, tot_ref, lhs3_ref, w_ref = refs
    rows, part = v_ref.shape[1:]
    head = spot_ref[0]
    row3 = jnp.zeros((EXTRA, rows), F32)
    for k in range(parts):
        msg = msg_refs[k][...]
        lhs3_ref[lax.rem(head + k, parts)] = jnp.concatenate(
            [gq_refs[k][...], msg[:rows]], axis=1
        )
        row3 += msg[rows:].astype(F32)
    assemble(spot_ref[1], wide, w_ref, w_refs)
    y = jnp.zeros((3 * rows, part), F32)
    for k in range(parts):
        lhs = jnp.concatenate([lhs1_ref[k], lhs2_ref[k], lhs3_ref[k]], axis=0)
        weight = w_ref[lax.rem(k - head + parts, parts)]
        y += jnp.dot(lhs, weight, preferred_element_type=F32)
    at = pl.ds(pl.multiple_of(head * part, part), part)
    inverse = inv_ref[:, :1]
    normed = z_ref[:, at].astype(F32) * inverse
    gain = gain_ref[:, at]
    fields = []
    for step, row in enumerate((row1_ref[...], row2_ref[...], row3)):
        along = jnp.broadcast_to(jnp.sum(row, axis=0, keepdims=True), (rows, rows)).T[:, :1]
        y_step = y[step * rows : (step + 1) * rows]
        fields.append(inverse * (y_step * gain - normed * along))
        v_ref[step] = fields[step]
    first, second, third = fields
    change1 = first - up_ref[:, at].astype(F32)
    change2 = second - first
    change3 = third - second
    pairs = [
        (change1, first), (change1, change1), (change2, first), (change2, change2),
        (change2, second), (change2, change3), (change3, second), (change3, change3),
    ]
    lanes = tot_ref.shape[2]
    sums = []
    for a, b in pairs:
        total = jnp.sum(a * b, axis=0, keepdims=True)
        sums.append(sum(total[:, i : i + lanes] for i in range(0, part, lanes)))
    totals = jnp.concatenate(sums, axis=0)
    for k in range(tot_ref.shape[0]):
        tot_ref[k] = totals


def mix_body(entries, spot_ref, tot_ref, up_ref, v_ref, out_ref):
    totals = jnp.sum(jnp.sum(tot_ref[...], axis=0), axis=1, keepdims=True) / entries
    s_r1, s_s, d2_v1, d2_d2, d2_v2, d2_d3, d3_v2, d3_d3 = [totals[i : i + 1] for i in range(8)]
    mix1 = s_r1 / (s_s + mix_eps)
    keep1 = 1.0 - mix1
    mix2 = keep1 * (d2_v1 + keep1 * d2_d2) / (keep1 * keep1 * d2_d2 + mix_eps)
    keep2 = keep1 * (1.0 - mix2)
    cross = mix1 * (d2_v2 + keep2 * d2_d3) + keep2 * (d3_v2 + keep2 * d3_d3)
    square = mix1 * mix1 * d2_d2 + 2.0 * mix1 * keep2 * d2_d3 + keep2 * keep2 * d3_d3
    mix3 = cross / (square + mix_eps)
    part = out_ref.shape[1]
    at = pl.ds(pl.multiple_of(spot_ref[0] * part, part), part)
    mixed = (
        up_ref[:, at].astype(F32)
        + v_ref[0]
        + (1.0 - mix3 * mix1) * v_ref[1]
        + keep2 * (1.0 - mix3) * v_ref[2]
    )
    out_ref[...] = mixed.astype(BF16)


def join_body(spot_ref, *refs):
    out_ref = refs[-1]
    parts = len(refs) - 1
    part = refs[0].shape[1]
    for k in range(parts):
        first = lax.rem(spot_ref[0] + k, parts) * part
        out_ref[:, pl.ds(pl.multiple_of(first, part), part)] = refs[k][...].astype(F32)


def shards(
    fixed_point,
    upstream,
    norm_gain,
    query_weight,
    keyval_weight,
    output_weight,
    log_norm,
    attention_out,
):
    rows, width = fixed_point.shape
    wide = query_weight.shape[1]
    narrow = keyval_weight.shape[1]
    size = wide + narrow
    e = narrow // 2
    heads = log_norm.shape[0]
    seq_count = lax.axis_size("seq")
    parts = lax.axis_size("head")
    block = lax.axis_index("seq")
    head = lax.axis_index("head")
    scale = e ** (-0.5)
    gain = norm_gain.reshape(1, width)
    span = (WIN_DEVS + 1) * rows
    group = min(8, seq_count)

    cols = size // group
    spot = jnp.stack([head, lax.rem(block, group)])
    smem = pl.BlockSpec(memory_space=pltpu.SMEM)
    vmem = pl.BlockSpec(memory_space=pltpu.VMEM)
    hbm = pl.BlockSpec(memory_space=pltpu.HBM)

    def pinned(value):
        return pltpu.with_memory_space_constraint(value, pltpu.HBM)

    tile = 128 if wide % 128 == 0 and 128 % (wide // group) == 0 else wide
    own_cols, hidden, kv, kvf, inv, near_z = local_call(
        prep_body,
        [
            shape_of((cols, width), BF16),
            shape_of((rows, width), BF16),
            shape_of((rows, narrow), BF16),
            shape_of((rows, narrow), F32),
            shape_of((rows, rows), F32),
            shape_of((rows, width), BF16),
        ],
        2 * width * size * cols,
        2 * width * (tile + narrow + rows),
        10,
        in_specs=[smem] + [hbm] * 4,
        scratch_shapes=[
            pltpu.VMEM((width, tile), BF16),
            pltpu.VMEM((width, narrow), BF16),
            pltpu.VMEM((1, width), F32),
            pltpu.SemaphoreType.DMA((4,)),
        ],
    )(
        block.reshape(1),
        pinned(query_weight),
        pinned(keyval_weight),
        pinned(fixed_point),
        pinned(gain),
    )
    every_cols = jnp.stack(rotated(own_cols, "head"))
    earlier = [shifted(kv, "seq", offset) for offset in range(WIN_DEVS, 0, -1)]

    qf, qt, go, nt, aot, scaled, norms = local_call(
        functools.partial(start_body, heads),
        [
            shape_of((rows, wide), F32),
            shape_of((e, heads * rows), BF16),
            shape_of((e, heads * rows), F32),
            shape_of((e, heads * rows), F32),
            shape_of((e, heads * rows), F32),
            shape_of((wide, width), BF16),
            shape_of((heads, rows), F32),
        ],
        6 * rows * width * wide,
        4 * width * (2 * rows + wide),
        14,
        in_specs=[vmem] * 6 + [hbm] * 3,
        scratch_shapes=[
            pltpu.VMEM((wide, width), BF16),
            pltpu.VMEM((rows, wide), BF16),
            pltpu.SemaphoreType.DMA((3,)),
        ],
    )(
        hidden,
        inv,
        near_z,
        gain,
        query_weight,
        upstream,
        pinned(output_weight),
        pinned(attention_out),
        pinned(log_norm),
    )

    pull_outs = [shape_of((span, heads * rows), BF16), shape_of((rows, narrow), F32)]
    pull_outs += [shape_of((rows, narrow), BF16)] * WIN_DEVS
    pull_flops = 6 * span * e * heads * rows

    def exchange(score, own, terms, split):
        arrived = [shifted(term, "seq", -offset - 1) for offset, term in enumerate(terms)]
        gq = local_call(
            functools.partial(query_body, heads, scale),
            shape_of((rows, wide), BF16),
            2 * span * e * heads * rows,
            span * heads * rows * 2,
            4,
        )(kt, score)
        ahead = rotated(gq, "head") if split else []
        msg = local_call(
            functools.partial(collect_body, width),
            shape_of((rows + EXTRA, narrow if split else size), BF16),
            COLLECT * rows * size,
            rows * size * 4,
            4,
        )(own, gq, qf, kvf, *arrived)
        return rotated(msg, "head"), msg, ahead

    kvw, kt, probs, score, own, *terms = local_call(
        functools.partial(first_body, heads, scale),
        [
            shape_of((span, narrow), BF16),
            shape_of((e, span), BF16),
            shape_of((span, heads * rows), BF16),
        ]
        + pull_outs,
        pull_flops * 5 // 4,
        span * heads * rows * 2,
        16,
        in_specs=[smem] + [vmem] * (WIN_DEVS + 5),
    )(block.reshape(1), *earlier, kv, qt, go, aot, norms)
    packed, marks = [], []
    chain_shape = shape_of((parts, size, wide), BF16)
    for step in range(3):
        if step:
            score, own, lhs, row, *terms = local_call(
                functools.partial(next_body, heads, parts, scale, step == 1),
                pull_outs[:2]
                + [shape_of((parts, rows, size), BF16), shape_of((EXTRA, rows), F32)]
                + [chain_shape] * (step == 1)
                + pull_outs[2:],
                pull_flops + 2 * rows * parts * size * wide,
                span * heads * rows * 2 + parts * size * wide * 2,
                16,
                in_specs=[smem] + [vmem] * (len(ahead) + parts + 6 + len(chain)),
            )(spot, *ahead, *every_msg, inv, nt, qt, aot, kvw, probs, *chain)
            packed += [lhs, row]
            if step == 1:
                chain, *terms = terms
                chain = [chain]
        if step == 0:
            every_cols, _ = lax.optimization_barrier((every_cols, score))
            share = local_call(
                chain_body,
                shape_of((parts * cols, wide), BF16),
                2 * parts * cols * width * wide,
                2 * width * (wide + parts * cols),
                8,
            )(every_cols.reshape(parts * cols, width), scaled)
            share = share.reshape(parts, cols, wide)
            *terms, share = lax.optimization_barrier((*terms, share))
        every_msg, msg, ahead = exchange(score, own, terms, step > 0)
        if step == 0:
            chain = doubled(share, "seq", group, (share, msg, (ahead[1:], every_msg[1:])))
        marks.append(dict(msg=msg, sent=(ahead[1:], every_msg[1:])))

    part = width // parts
    mine = lax.dynamic_slice_in_dim(every_cols, head * part, part, 2)
    weight = doubled(mine, "seq", group, (marks[0]["msg"], marks[0]["sent"], marks[1]["sent"]))
    small = seq_count * parts <= 64
    fields, totals = local_call(
        functools.partial(field_body, parts, wide),
        [
            shape_of((3, rows, part), F32),
            shape_of((seq_count * parts if small else 1, 8, 128), F32),
        ],
        6 * rows * parts * size * part,
        2 * parts * size * part,
        20,
        in_specs=[smem] + [vmem] * (2 * parts + 8 + len(weight)),
        scratch_shapes=[
            pltpu.VMEM((parts, rows, size), BF16),
            pltpu.VMEM((parts, size, part), BF16),
        ],
    )(spot, *ahead, *every_msg, *packed, *weight, fixed_point, upstream, gain, inv)
    if small:
        totals = lax.all_to_all(totals, ("seq", "head"), 0, 0)
    else:
        totals = lax.psum(totals, ("seq", "head"))
    mixed = local_call(
        functools.partial(mix_body, rows * seq_count * width),
        shape_of((rows, part), BF16),
        8 * rows * part,
        18 * rows * part,
        6,
        in_specs=[smem] + [vmem] * 3,
    )(spot, totals, upstream, fields)
    every_mixed = rotated(mixed, "head")
    return local_call(
        join_body,
        shape_of((rows, width), F32),
        0,
        6 * rows * width,
        6,
        in_specs=[smem] + [vmem] * parts,
    )(spot, *every_mixed)


def solution(mesh):
    in_specs = (
        P("seq", None),
        P("seq", None),
        P(),
        P(None, "head"),
        P(None, "head"),
        P("head", None),
        P("head", "seq"),
        P("seq", "head"),
    )
    out_specs = P("seq", None)
    return jax.shard_map(shards, mesh=mesh, in_specs=in_specs, out_specs=out_specs, check_vma=False)
```

```python
import functools

import jax
import jax.numpy as jnp
from jax import lax
from jax.experimental import pallas as pl
from jax.experimental.pallas import tpu as pltpu
from jax.sharding import PartitionSpec as P

WIN_DEVS = 4
norm_eps = 1e-05
mix_eps = 1e-06
F32 = jnp.float32
BF16 = jnp.bfloat16
COLLECT = 50000
EXTRA = 16
NT = (((1,), (1,)), ((), ()))


def shape_of(shape, dtype):
    return jax.ShapeDtypeStruct(shape, dtype)


def local_call(body, outs, flops, moved, room, **more):
    return pl.pallas_call(
        body,
        out_shape=outs,
        compiler_params=pltpu.CompilerParams(vmem_limit_bytes=room * 1024 * 1024),
        cost_estimate=pl.CostEstimate(flops=flops, bytes_accessed=moved, transcendentals=0),
        **more,
    )


def shifted(value, axis, steps):
    count = lax.axis_size(axis)
    initial, last = (max(0, -steps), min(count, count - steps))
    return lax.ppermute(value, axis, [(source, source + steps) for source in range(initial, last)])


def rotated(value, axis):
    count = lax.axis_size(axis)
    parts = [value]
    for step in range(1, count):
        parts.append(lax.ppermute(value, axis, [(i, (i - step) % count) for i in range(count)]))
    return parts


def doubled(value, axis, group, gates, join):
    count = lax.axis_size(axis)
    near, bit = [value[None]], group // 2
    for gate in gates:
        near = list(lax.optimization_barrier((tuple(near), gate))[0])
        pairs = [(i, i ^ bit) for i in range(count)]
        near = [join(near)]
        if bit == 1:
            return near + [lax.ppermute(near[0], axis, pairs)]
        near.append(lax.ppermute(near[0], axis, pairs))
        bit //= 2


def assemble(place, wide, out_ref, refs):
    group = sum(ref.shape[0] for ref in refs)
    cut = wide // group
    rest_cut = refs[0].shape[2] - cut
    entries = [(ref, j) for ref in refs for j in range(ref.shape[0])]
    for j, (ref, at) in enumerate(entries):
        distance, bit, rest = 0, group // 2, j
        while rest:
            distance += bit * (rest & 1)
            rest >>= 1
            bit //= 2
        index = lax.bitwise_xor(place, jnp.int32(distance))
        first = pl.multiple_of(index * cut, cut)
        second = pl.multiple_of(wide + index * rest_cut, rest_cut)
        for k in range(out_ref.shape[0]):
            out_ref[k, pl.ds(first, cut), :] = ref[at, k, :cut, :]
            out_ref[k, pl.ds(second, rest_cut), :] = ref[at, k, cut:, :]


def prep_body(block_ref, qw_ref, kvw_ref, z_ref, gain_ref, cols_ref, hidden_ref, kv_ref, kvf_ref,
              inv_ref, z_tile, q_tile, kv_tile, gain_tile, sems):
    tile = q_tile.shape[1]
    wide, narrow = qw_ref.shape[1], kvw_ref.shape[1]
    group = (wide + narrow) // cols_ref.shape[0]
    place = lax.rem(block_ref[0], group)
    q_take, kv_take = wide // group, narrow // group
    q_at = place * q_take
    q_first = pl.multiple_of(q_at // tile * tile, tile)
    copies = [
        pltpu.make_async_copy(qw_ref.at[:, pl.ds(q_first, tile)], q_tile, sems.at[0]),
        pltpu.make_async_copy(kvw_ref, kv_tile, sems.at[1]),
        pltpu.make_async_copy(z_ref, z_tile, sems.at[2]),
        pltpu.make_async_copy(gain_ref, gain_tile, sems.at[3]),
    ]
    for copy in copies:
        copy.start()
    first = 0
    for copy, ref, at, take in (
        (copies[0], q_tile, q_at - q_first, q_take),
        (copies[1], kv_tile, place * kv_take, kv_take),
    ):
        copy.wait()
        total = ref.shape[1]
        row = lax.broadcasted_iota(jnp.int32, (take, total), 0) + at
        pick = (row == lax.broadcasted_iota(jnp.int32, (take, total), 1)).astype(BF16)
        cols = lax.dot_general(pick, ref[...], NT, preferred_element_type=F32)
        cols_ref[first : first + take, :] = cols.astype(BF16)
        first += take
    copies[2].wait()
    copies[3].wait()
    z = z_tile[...].astype(F32)
    inverse = lax.rsqrt(jnp.mean(z * z, axis=1, keepdims=True) + norm_eps)
    hidden = (z * inverse * gain_tile[...]).astype(BF16)
    hidden_ref[...] = hidden
    kvf = jnp.dot(hidden, kv_tile[...], preferred_element_type=F32)
    kvf_ref[...] = kvf
    kv_ref[...] = kvf.astype(BF16)
    inv_ref[...] = jnp.broadcast_to(inverse, inv_ref.shape)


def chain_body(spot_ref, *refs):
    *cols_refs, scaled_ref, share_ref, quarter_ref = refs
    part = quarter_ref.shape[2]
    at = pl.ds(pl.multiple_of(spot_ref[0] * part, part), part)
    cols = jnp.concatenate([ref[...] for ref in cols_refs], axis=0)
    share = lax.dot_general(cols, scaled_ref[...], NT, preferred_element_type=F32).astype(BF16)
    size = cols_refs[0].shape[0]
    for k, ref in enumerate(cols_refs):
        share_ref[k] = share[k * size : (k + 1) * size]
        quarter_ref[k] = ref[:, at]


def join_parts_body(*refs):
    first = 0
    for ref in refs[:-1]:
        refs[-1][first : first + ref.shape[0]] = ref[...]
        first += ref.shape[0]


def joined(parts):
    if len(parts) == 1:
        return parts[0]
    shape = (sum(part.shape[0] for part in parts),) + parts[0].shape[1:]
    moved = 4 * functools.reduce(lambda a, b: a * b, shape)
    return local_call(join_parts_body, shape_of(shape, BF16), 0, moved, 6)(*parts)


def lanes_of(value, heads):
    size = value.shape[0] // heads
    return jnp.concatenate([value[i * size : (i + 1) * size] for i in range(heads)], axis=1)


def start_body(heads, hidden_ref, inv_ref, z_ref, gain_ref, qw_ref, up_ref, ow_ref, ao_ref, ln_ref,
               qf_ref, qt_ref, go_ref, nt_ref, aot_ref, scaled_ref, norms_ref,
               ow_tile, ao_tile, sems):
    copies = [
        pltpu.make_async_copy(source, target, sems.at[i])
        for i, (source, target) in enumerate(
            ((ow_ref, ow_tile), (ao_ref, ao_tile), (ln_ref, norms_ref))
        )
    ]
    for copy in copies:
        copy.start()
    qf = jnp.dot(hidden_ref[...], qw_ref[...], preferred_element_type=F32)
    qf_ref[...] = qf
    qt_ref[...] = lanes_of(qf.T, heads).astype(BF16)
    for copy in copies:
        copy.wait()
    aot_ref[...] = lanes_of(ao_tile[...].astype(F32).T, heads)
    weight = ow_tile[...]
    out = lax.dot_general(up_ref[...], weight, NT, preferred_element_type=F32)
    go_ref[...] = lanes_of(out.T, heads)
    base = lax.dot_general(z_ref[...], weight, NT, preferred_element_type=F32)
    nt_ref[...] = lanes_of((base * inv_ref[:, :1]).T, heads)
    scaled_ref[...] = (weight.astype(F32) * gain_ref[...]).astype(BF16)


def pull(heads, scale, go, aot, qt, kvw_ref, probs, score_ref, own_ref, term_refs):
    e = go.shape[0]
    rows = go.shape[1] // heads
    row_terms = jnp.sum(go * aot, axis=0, keepdims=True)
    gob = go.astype(BF16)
    grad_prob = jnp.dot(kvw_ref[:, e:], gob, preferred_element_type=F32)
    grad_score = (probs.astype(F32) * (grad_prob - row_terms)).astype(BF16)
    score_ref[...] = grad_score
    grad_key = lax.dot_general(grad_score, qt, NT, preferred_element_type=F32) * scale
    grad_value = lax.dot_general(probs, gob, NT, preferred_element_type=F32)
    terms = jnp.concatenate([grad_key, grad_value], axis=1)
    for offset in range(1, len(term_refs) + 1):
        first = (len(term_refs) - offset) * rows
        term_refs[offset - 1][...] = terms[first : first + rows].astype(BF16)
    own_ref[...] = terms[len(term_refs) * rows :]


def query_body(heads, scale, kt_ref, score_ref, gq_ref):
    rows = gq_ref.shape[0]
    grad_query = jnp.dot(kt_ref[...], score_ref[...], preferred_element_type=F32) * scale
    parts = [grad_query[:, i * rows : (i + 1) * rows] for i in range(heads)]
    gq_ref[...] = jnp.concatenate(parts, axis=0).T.astype(BF16)


def first_body(heads, scale, block_ref, *refs):
    windows = refs[: WIN_DEVS + 1]
    qt_ref, go_ref, aot_ref, ln_ref = refs[WIN_DEVS + 1 : WIN_DEVS + 5]
    kvw_ref, kt_ref, probs_ref, score_ref, own_ref = refs[WIN_DEVS + 5 : WIN_DEVS + 10]
    term_refs = refs[WIN_DEVS + 10 :]
    rows = windows[0].shape[0]
    for place, ref in enumerate(windows):
        kvw_ref[place * rows : (place + 1) * rows, :] = ref[...]
    kvw = kvw_ref[...]
    e = kvw.shape[1] // 2
    kt_ref[...] = kvw.astype(F32).T[:e].astype(BF16)
    scores = jnp.dot(kvw[:, :e], qt_ref[...], preferred_element_type=F32) * scale
    norms = jnp.concatenate([ln_ref[i : i + 1, :] for i in range(heads)], axis=1)
    key_pos = lax.broadcasted_iota(jnp.int32, scores.shape, 0)
    query_pos = lax.broadcasted_iota(jnp.int32, scores.shape, 1) & (rows - 1)
    allowed = (key_pos > query_pos) & (key_pos <= query_pos + WIN_DEVS * rows)
    allowed = allowed & (key_pos >= (WIN_DEVS - block_ref[0]) * rows)
    probs = jnp.where(allowed, jnp.exp(scores - norms), 0.0).astype(BF16)
    probs_ref[...] = probs
    pull(heads, scale, go_ref[...], aot_ref[...], qt_ref[...], kvw_ref, probs,
         score_ref, own_ref, term_refs)


def next_body(heads, parts, scale, fresh, spot_ref, *refs):
    gq_refs, refs = ([], refs) if fresh else (refs[:parts], refs[parts:])
    msg_refs, refs = refs[:parts], refs[parts:]
    inv_ref, nt_ref, qt_ref, aot_ref, kvw_ref, probs_ref, *refs = refs
    if fresh:
        *parts_refs, score_ref, own_ref, lhs_ref, row_ref, chain_ref = refs[:7]
        term_refs = refs[7:]
        assemble(spot_ref[1], chain_ref.shape[2], chain_ref, parts_refs)
    else:
        chain_ref, score_ref, own_ref, lhs_ref, row_ref = refs[:5]
        term_refs = refs[5:]
    rows, wide = lhs_ref.shape[1], chain_ref.shape[2]
    out = jnp.zeros((rows, wide), F32)
    along = jnp.zeros((EXTRA, rows), F32)
    for k in range(parts):
        index = lax.rem(spot_ref[0] + k, parts)
        msg = msg_refs[k][...]
        chain = chain_ref[k]
        lhs = msg[:rows]
        if gq_refs:
            lhs = jnp.concatenate([gq_refs[k][...], lhs], axis=1)
        out += jnp.dot(lhs, chain, preferred_element_type=F32)
        lhs_ref[index] = lhs
        along += msg[rows:, :rows].astype(F32)
    row_ref[...] = along
    along = jnp.sum(along, axis=0, keepdims=True)
    along = jnp.concatenate([along] * heads, axis=1)
    go = lanes_of((out * inv_ref[:, :1]).T, heads)
    inv_row = jnp.concatenate([inv_ref[...].T[:1, :]] * heads, axis=1)
    go = go - inv_row * along * nt_ref[...]
    pull(heads, scale, go, aot_ref[...], qt_ref[...], kvw_ref, probs_ref[...],
         score_ref, own_ref, term_refs)


def collect_body(width, own_ref, gq_ref, qf_ref, kvf_ref, *refs):
    msg_ref = refs[-1]
    rows = own_ref.shape[0]
    total = own_ref[...]
    for ref in refs[:-1]:
        total += ref[...].astype(F32)
    total = total.astype(BF16)
    ahead = msg_ref.shape[1] - total.shape[1]
    if ahead:
        msg_ref[:rows, :ahead] = gq_ref[...]
        msg_ref[rows:, :] = jnp.zeros((EXTRA, msg_ref.shape[1]), BF16)
    msg_ref[:rows, ahead:] = total
    prods = gq_ref[...].astype(F32) * qf_ref[...]
    partial = total.astype(F32) * kvf_ref[...]
    lanes = partial.shape[1]
    for first in range(0, prods.shape[1], lanes):
        partial += prods[:, first : first + lanes]
    along = jnp.sum(partial.T, axis=0, keepdims=True) * (1.0 / width)
    high = along.astype(BF16).astype(F32)
    place = lax.broadcasted_iota(jnp.int32, (EXTRA, rows), 0)
    extra = jnp.where(place == 0, high, jnp.where(place == 1, along - high, 0.0))
    msg_ref[rows:, :rows] = extra.astype(BF16)


def field_body(parts, wide, spot_ref, *refs):
    gq_refs, msg_refs, refs = refs[:parts], refs[parts : 2 * parts], refs[2 * parts :]
    lhs1_ref, row1_ref, lhs2_ref, row2_ref, *refs = refs
    *w_refs, z_ref, up_ref, gain_ref, inv_ref, v_ref, tot_ref, lhs3_ref, w_ref = refs
    rows, part = v_ref.shape[1:]
    head = spot_ref[0]
    row3 = jnp.zeros((EXTRA, rows), F32)
    for k in range(parts):
        msg = msg_refs[k][...]
        lhs3_ref[lax.rem(head + k, parts)] = jnp.concatenate(
            [gq_refs[k][...], msg[:rows]], axis=1
        )
        row3 += msg[rows:].astype(F32)
    assemble(spot_ref[1], wide, w_ref, w_refs)
    y = jnp.zeros((3 * rows, part), F32)
    for k in range(parts):
        lhs = jnp.concatenate([lhs1_ref[k], lhs2_ref[k], lhs3_ref[k]], axis=0)
        weight = w_ref[lax.rem(k - head + parts, parts)]
        y += jnp.dot(lhs, weight, preferred_element_type=F32)
    at = pl.ds(pl.multiple_of(head * part, part), part)
    inverse = inv_ref[:, :1]
    normed = z_ref[:, at].astype(F32) * inverse
    gain = gain_ref[:, at]
    fields = []
    for step, row in enumerate((row1_ref[...], row2_ref[...], row3)):
        along = jnp.broadcast_to(jnp.sum(row, axis=0, keepdims=True), (rows, rows)).T[:, :1]
        y_step = y[step * rows : (step + 1) * rows]
        fields.append(inverse * (y_step * gain - normed * along))
        v_ref[step] = fields[step]
    first, second, third = fields
    change1 = first - up_ref[:, at].astype(F32)
    change2 = second - first
    change3 = third - second
    pairs = [
        (change1, first), (change1, change1), (change2, first), (change2, change2),
        (change2, second), (change2, change3), (change3, second), (change3, change3),
    ]
    lanes = tot_ref.shape[2]
    sums = []
    for a, b in pairs:
        total = jnp.sum(a * b, axis=0, keepdims=True)
        sums.append(sum(total[:, i : i + lanes] for i in range(0, part, lanes)))
    totals = jnp.concatenate(sums, axis=0)
    for k in range(tot_ref.shape[0]):
        tot_ref[k] = totals


def mix_body(entries, spot_ref, tot_ref, up_ref, v_ref, out_ref):
    totals = jnp.sum(jnp.sum(tot_ref[...], axis=0), axis=1, keepdims=True) / entries
    s_r1, s_s, d2_v1, d2_d2, d2_v2, d2_d3, d3_v2, d3_d3 = [totals[i : i + 1] for i in range(8)]
    mix1 = s_r1 / (s_s + mix_eps)
    keep1 = 1.0 - mix1
    mix2 = keep1 * (d2_v1 + keep1 * d2_d2) / (keep1 * keep1 * d2_d2 + mix_eps)
    keep2 = keep1 * (1.0 - mix2)
    cross = mix1 * (d2_v2 + keep2 * d2_d3) + keep2 * (d3_v2 + keep2 * d3_d3)
    square = mix1 * mix1 * d2_d2 + 2.0 * mix1 * keep2 * d2_d3 + keep2 * keep2 * d3_d3
    mix3 = cross / (square + mix_eps)
    part = out_ref.shape[1]
    at = pl.ds(pl.multiple_of(spot_ref[0] * part, part), part)
    mixed = (
        up_ref[:, at].astype(F32)
        + v_ref[0]
        + (1.0 - mix3 * mix1) * v_ref[1]
        + keep2 * (1.0 - mix3) * v_ref[2]
    )
    out_ref[...] = mixed.astype(BF16)


def join_body(spot_ref, *refs):
    out_ref = refs[-1]
    parts = len(refs) - 1
    part = refs[0].shape[1]
    for k in range(parts):
        first = lax.rem(spot_ref[0] + k, parts) * part
        out_ref[:, pl.ds(pl.multiple_of(first, part), part)] = refs[k][...].astype(F32)


def shards(
    fixed_point,
    upstream,
    norm_gain,
    query_weight,
    keyval_weight,
    output_weight,
    log_norm,
    attention_out,
):
    rows, width = fixed_point.shape
    wide = query_weight.shape[1]
    narrow = keyval_weight.shape[1]
    size = wide + narrow
    e = narrow // 2
    heads = log_norm.shape[0]
    seq_count = lax.axis_size("seq")
    parts = lax.axis_size("head")
    block = lax.axis_index("seq")
    head = lax.axis_index("head")
    scale = e ** (-0.5)
    gain = norm_gain.reshape(1, width)
    span = (WIN_DEVS + 1) * rows
    group = min(8, seq_count)

    cols = size // group
    spot = jnp.stack([head, lax.rem(block, group)])
    smem = pl.BlockSpec(memory_space=pltpu.SMEM)
    vmem = pl.BlockSpec(memory_space=pltpu.VMEM)
    hbm = pl.BlockSpec(memory_space=pltpu.HBM)

    def pinned(value):
        return pltpu.with_memory_space_constraint(value, pltpu.HBM)

    tile = 128 if wide % 128 == 0 and 128 % (wide // group) == 0 else wide
    own_cols, hidden, kv, kvf, inv, near_z = local_call(
        prep_body,
        [
            shape_of((cols, width), BF16),
            shape_of((rows, width), BF16),
            shape_of((rows, narrow), BF16),
            shape_of((rows, narrow), F32),
            shape_of((rows, rows), F32),
            shape_of((rows, width), BF16),
        ],
        2 * width * size * cols,
        2 * width * (tile + narrow + rows),
        10,
        in_specs=[smem] + [hbm] * 4,
        scratch_shapes=[
            pltpu.VMEM((width, tile), BF16),
            pltpu.VMEM((width, narrow), BF16),
            pltpu.VMEM((1, width), F32),
            pltpu.SemaphoreType.DMA((4,)),
        ],
    )(
        block.reshape(1),
        pinned(query_weight),
        pinned(keyval_weight),
        pinned(fixed_point),
        pinned(gain),
    )
    every_cols = rotated(own_cols, "head")
    earlier = [shifted(kv, "seq", offset) for offset in range(WIN_DEVS, 0, -1)]

    qf, qt, go, nt, aot, scaled, norms = local_call(
        functools.partial(start_body, heads),
        [
            shape_of((rows, wide), F32),
            shape_of((e, heads * rows), BF16),
            shape_of((e, heads * rows), F32),
            shape_of((e, heads * rows), F32),
            shape_of((e, heads * rows), F32),
            shape_of((wide, width), BF16),
            shape_of((heads, rows), F32),
        ],
        6 * rows * width * wide,
        4 * width * (2 * rows + wide),
        14,
        in_specs=[vmem] * 6 + [hbm] * 3,
        scratch_shapes=[
            pltpu.VMEM((wide, width), BF16),
            pltpu.VMEM((rows, wide), BF16),
            pltpu.SemaphoreType.DMA((3,)),
        ],
    )(
        hidden,
        inv,
        near_z,
        gain,
        query_weight,
        upstream,
        pinned(output_weight),
        pinned(attention_out),
        pinned(log_norm),
    )

    pull_outs = [shape_of((span, heads * rows), BF16), shape_of((rows, narrow), F32)]
    pull_outs += [shape_of((rows, narrow), BF16)] * WIN_DEVS
    pull_flops = 6 * span * e * heads * rows

    def exchange(score, own, terms, split):
        arrived = [shifted(term, "seq", -offset - 1) for offset, term in enumerate(terms)]
        gq = local_call(
            functools.partial(query_body, heads, scale),
            shape_of((rows, wide), BF16),
            2 * span * e * heads * rows,
            span * heads * rows * 2,
            4,
        )(kt, score)
        ahead = rotated(gq, "head") if split else []
        msg = local_call(
            functools.partial(collect_body, width),
            shape_of((rows + EXTRA, narrow if split else size), BF16),
            COLLECT * rows * size,
            rows * size * 4,
            4,
        )(own, gq, qf, kvf, *arrived)
        return rotated(msg, "head"), msg, ahead

    kvw, kt, probs, score, own, *terms = local_call(
        functools.partial(first_body, heads, scale),
        [
            shape_of((span, narrow), BF16),
            shape_of((e, span), BF16),
            shape_of((span, heads * rows), BF16),
        ]
        + pull_outs,
        pull_flops * 5 // 4,
        span * heads * rows * 2,
        16,
        in_specs=[smem] + [vmem] * (WIN_DEVS + 5),
    )(block.reshape(1), *earlier, kv, qt, go, aot, norms)
    packed, marks = [], []
    chain_shape = shape_of((parts, size, wide), BF16)
    for step in range(3):
        if step:
            score, own, lhs, row, *terms = local_call(
                functools.partial(next_body, heads, parts, scale, step == 1),
                pull_outs[:2]
                + [shape_of((parts, rows, size), BF16), shape_of((EXTRA, rows), F32)]
                + [chain_shape] * (step == 1)
                + pull_outs[2:],
                pull_flops + 2 * rows * parts * size * wide,
                span * heads * rows * 2 + parts * size * wide * 2,
                16,
                in_specs=[smem] + [vmem] * (len(ahead) + parts + 6 + len(chain)),
            )(spot, *ahead, *every_msg, inv, nt, qt, aot, kvw, probs, *chain)
            packed += [lhs, row]
            if step == 1:
                chain, *terms = terms
                chain = [chain]
        if step == 0:
            *every_cols, _ = lax.optimization_barrier((*every_cols, score))
            part = width // parts
            share, mine = local_call(
                chain_body,
                [shape_of((parts, cols, wide), BF16), shape_of((parts, cols, part), BF16)],
                2 * parts * cols * width * wide,
                2 * width * (wide + parts * cols),
                8,
                in_specs=[smem] + [vmem] * (parts + 1),
            )(spot, *every_cols, scaled)
            *terms, share = lax.optimization_barrier((*terms, share))
        every_msg, msg, ahead = exchange(score, own, terms, step > 0)
        if step == 0:
            chain = doubled(share, "seq", group, (share, msg, (ahead[1:], every_msg[1:])), joined)
        marks.append(dict(msg=msg, sent=(ahead[1:], every_msg[1:])))

    weight = doubled(mine, "seq", group, (marks[0]["msg"], marks[0]["sent"], marks[1]["sent"]), jnp.concatenate)
    small = seq_count * parts <= 64
    fields, totals = local_call(
        functools.partial(field_body, parts, wide),
        [
            shape_of((3, rows, part), F32),
            shape_of((seq_count * parts if small else 1, 8, 128), F32),
        ],
        6 * rows * parts * size * part,
        2 * parts * size * part,
        20,
        in_specs=[smem] + [vmem] * (2 * parts + 8 + len(weight)),
        scratch_shapes=[
            pltpu.VMEM((parts, rows, size), BF16),
            pltpu.VMEM((parts, size, part), BF16),
        ],
    )(spot, *ahead, *every_msg, *packed, *weight, fixed_point, upstream, gain, inv)
    if small:
        totals = lax.all_to_all(totals, ("seq", "head"), 0, 0)
    else:
        totals = lax.psum(totals, ("seq", "head"))
    mixed = local_call(
        functools.partial(mix_body, rows * seq_count * width),
        shape_of((rows, part), BF16),
        8 * rows * part,
        18 * rows * part,
        6,
        in_specs=[smem] + [vmem] * 3,
    )(spot, totals, upstream, fields)
    every_mixed = rotated(mixed, "head")
    return local_call(
        join_body,
        shape_of((rows, width), F32),
        0,
        6 * rows * width,
        6,
        in_specs=[smem] + [vmem] * parts,
    )(spot, *every_mixed)


def solution(mesh):
    in_specs = (
        P("seq", None),
        P("seq", None),
        P(),
        P(None, "head"),
        P(None, "head"),
        P("head", None),
        P("head", "seq"),
        P("seq", "head"),
    )
    out_specs = P("seq", None)
    return jax.shard_map(shards, mesh=mesh, in_specs=in_specs, out_specs=out_specs, check_vma=False)
```

```python
import functools

import jax
import jax.numpy as jnp
from jax import lax
from jax.experimental import pallas as pl
from jax.experimental.pallas import tpu as pltpu
from jax.sharding import PartitionSpec as P

WIN_DEVS = 4
norm_eps = 1e-05
mix_eps = 1e-06
F32 = jnp.float32
BF16 = jnp.bfloat16
COLLECT = 50000
EXTRA = 16
NT = (((1,), (1,)), ((), ()))


def shape_of(shape, dtype):
    return jax.ShapeDtypeStruct(shape, dtype)


def local_call(body, outs, flops, moved, room, **more):
    return pl.pallas_call(
        body,
        out_shape=outs,
        compiler_params=pltpu.CompilerParams(vmem_limit_bytes=room * 1024 * 1024),
        cost_estimate=pl.CostEstimate(flops=flops, bytes_accessed=moved, transcendentals=0),
        **more,
    )


def shifted(value, axis, steps):
    count = lax.axis_size(axis)
    initial, last = (max(0, -steps), min(count, count - steps))
    return lax.ppermute(value, axis, [(source, source + steps) for source in range(initial, last)])


def rotated(value, axis):
    count = lax.axis_size(axis)
    parts = [value]
    for step in range(1, count):
        parts.append(lax.ppermute(value, axis, [(i, (i - step) % count) for i in range(count)]))
    return parts


def doubled(value, axis, group, gates):
    count = lax.axis_size(axis)
    near, bit = list(value), group // 2
    for gate in gates:
        near = list(lax.optimization_barrier((tuple(near), gate))[0])
        pairs = [(i, i ^ bit) for i in range(count)]
        if len(near) > 1:
            near = [jnp.concatenate(near)]
        if bit == 1:
            return near + [lax.ppermute(near[0], axis, pairs)]
        near.append(lax.ppermute(near[0], axis, pairs))
        bit //= 2


def assemble(place, wide, out_ref, refs):
    group = sum(ref.shape[0] for ref in refs)
    cut = wide // group
    rest_cut = refs[0].shape[2] - cut
    entries = [(ref, j) for ref in refs for j in range(ref.shape[0])]
    for j, (ref, at) in enumerate(entries):
        distance, bit, rest = 0, group // 2, j
        while rest:
            distance += bit * (rest & 1)
            rest >>= 1
            bit //= 2
        index = lax.bitwise_xor(place, jnp.int32(distance))
        first = pl.multiple_of(index * cut, cut)
        second = pl.multiple_of(wide + index * rest_cut, rest_cut)
        for k in range(out_ref.shape[0]):
            out_ref[k, pl.ds(first, cut), :] = ref[at, k, :cut, :]
            out_ref[k, pl.ds(second, rest_cut), :] = ref[at, k, cut:, :]


def prep_body(block_ref, qw_ref, kvw_ref, z_ref, gain_ref, cols_ref, hidden_ref, kv_ref, kvf_ref,
              inv_ref, q_tile, kv_tile, z_tile, gain_tile, sems):
    tile = q_tile.shape[1]
    wide, narrow = qw_ref.shape[1], kvw_ref.shape[1]
    group = (wide + narrow) // cols_ref.shape[0]
    place = lax.rem(block_ref[0], group)
    q_take, kv_take = wide // group, narrow // group
    q_at = place * q_take
    q_first = pl.multiple_of(q_at // tile * tile, tile)
    copies = [
        pltpu.make_async_copy(qw_ref.at[:, pl.ds(q_first, tile)], q_tile, sems.at[0]),
        pltpu.make_async_copy(kvw_ref, kv_tile, sems.at[1]),
        pltpu.make_async_copy(z_ref, z_tile, sems.at[2]),
        pltpu.make_async_copy(gain_ref, gain_tile, sems.at[3]),
    ]
    for copy in copies:
        copy.start()
    first = 0
    for copy, ref, at, take in (
        (copies[0], q_tile, q_at - q_first, q_take),
        (copies[1], kv_tile, place * kv_take, kv_take),
    ):
        copy.wait()
        total = ref.shape[1]
        row = lax.broadcasted_iota(jnp.int32, (take, total), 0) + at
        pick = (row == lax.broadcasted_iota(jnp.int32, (take, total), 1)).astype(BF16)
        cols = lax.dot_general(pick, ref[...], NT, preferred_element_type=F32)
        cols_ref[first : first + take, :] = cols.astype(BF16)
        first += take
    copies[2].wait()
    copies[3].wait()
    z = z_tile[...].astype(F32)
    inverse = lax.rsqrt(jnp.mean(z * z, axis=1, keepdims=True) + norm_eps)
    hidden = (z * inverse * gain_tile[...]).astype(BF16)
    hidden_ref[...] = hidden
    kvf = jnp.dot(hidden, kv_tile[...], preferred_element_type=F32)
    kvf_ref[...] = kvf
    kv_ref[...] = kvf.astype(BF16)
    inv_ref[...] = jnp.broadcast_to(inverse, inv_ref.shape)


def chain_body(cols_ref, scaled_ref, out_ref):
    share = lax.dot_general(cols_ref[...], scaled_ref[...], NT, preferred_element_type=F32)
    out_ref[...] = share.astype(BF16)


def lanes_of(value, heads):
    size = value.shape[0] // heads
    return jnp.concatenate([value[i * size : (i + 1) * size] for i in range(heads)], axis=1)


def start_body(heads, hidden_ref, inv_ref, qw_ref, ow_ref, up_ref, z_ref, ao_ref, gain_ref, ln_ref,
               qf_ref, qt_ref, go_ref, nt_ref, aot_ref, scaled_ref, norms_ref,
               qw_tile, ow_tile, up_tile, z_tile, ao_tile, gain_tile, sems):
    copies = [
        pltpu.make_async_copy(source, target, sems.at[i])
        for i, (source, target) in enumerate(
            ((ow_ref, ow_tile), (up_ref, up_tile), (z_ref, z_tile), (qw_ref, qw_tile),
             (ao_ref, ao_tile), (gain_ref, gain_tile), (ln_ref, norms_ref))
        )
    ]
    for copy in copies:
        copy.start()
    for copy in copies[:3]:
        copy.wait()
    out = lax.dot_general(up_tile[...], ow_tile[...], NT, preferred_element_type=F32)
    go_ref[...] = lanes_of(out.T, heads)
    base = lax.dot_general(z_tile[...], ow_tile[...], NT, preferred_element_type=F32)
    nt_ref[...] = lanes_of((base * inv_ref[:, :1]).T, heads)
    copies[3].wait()
    qf = jnp.dot(hidden_ref[...], qw_tile[...], preferred_element_type=F32)
    qf_ref[...] = qf
    qt_ref[...] = lanes_of(qf.T, heads).astype(BF16)
    for copy in copies[4:]:
        copy.wait()
    scaled_ref[...] = (ow_tile[...].astype(F32) * gain_tile[...]).astype(BF16)
    aot_ref[...] = lanes_of(ao_tile[...].astype(F32).T, heads)


def pull(heads, scale, go, aot, qt, kvw_ref, probs, score_ref, own_ref, term_refs):
    e = go.shape[0]
    rows = go.shape[1] // heads
    row_terms = jnp.sum(go * aot, axis=0, keepdims=True)
    gob = go.astype(BF16)
    grad_prob = jnp.dot(kvw_ref[:, e:], gob, preferred_element_type=F32)
    grad_score = (probs.astype(F32) * (grad_prob - row_terms)).astype(BF16)
    score_ref[...] = grad_score
    grad_key = lax.dot_general(grad_score, qt, NT, preferred_element_type=F32) * scale
    grad_value = lax.dot_general(probs, gob, NT, preferred_element_type=F32)
    terms = jnp.concatenate([grad_key, grad_value], axis=1)
    for offset in range(1, len(term_refs) + 1):
        first = (len(term_refs) - offset) * rows
        term_refs[offset - 1][...] = terms[first : first + rows].astype(BF16)
    own_ref[...] = terms[len(term_refs) * rows :]


def query_body(heads, scale, kt_ref, score_ref, gq_ref):
    rows = gq_ref.shape[0]
    grad_query = jnp.dot(kt_ref[...], score_ref[...], preferred_element_type=F32) * scale
    parts = [grad_query[:, i * rows : (i + 1) * rows] for i in range(heads)]
    gq_ref[...] = jnp.concatenate(parts, axis=0).T.astype(BF16)


def first_body(heads, scale, block_ref, *refs):
    windows = refs[: WIN_DEVS + 1]
    qt_ref, go_ref, aot_ref, ln_ref = refs[WIN_DEVS + 1 : WIN_DEVS + 5]
    kvw_ref, kt_ref, probs_ref, score_ref, own_ref = refs[WIN_DEVS + 5 : WIN_DEVS + 10]
    term_refs = refs[WIN_DEVS + 10 :]
    rows = windows[0].shape[0]
    for place, ref in enumerate(windows):
        kvw_ref[place * rows : (place + 1) * rows, :] = ref[...]
    kvw = kvw_ref[...]
    e = kvw.shape[1] // 2
    kt_ref[...] = kvw.astype(F32).T[:e].astype(BF16)
    scores = jnp.dot(kvw[:, :e], qt_ref[...], preferred_element_type=F32) * scale
    norms = jnp.concatenate([ln_ref[i : i + 1, :] for i in range(heads)], axis=1)
    key_pos = lax.broadcasted_iota(jnp.int32, scores.shape, 0)
    query_pos = lax.broadcasted_iota(jnp.int32, scores.shape, 1) & (rows - 1)
    allowed = (key_pos > query_pos) & (key_pos <= query_pos + WIN_DEVS * rows)
    allowed = allowed & (key_pos >= (WIN_DEVS - block_ref[0]) * rows)
    probs = jnp.where(allowed, jnp.exp(scores - norms), 0.0).astype(BF16)
    probs_ref[...] = probs
    pull(heads, scale, go_ref[...], aot_ref[...], qt_ref[...], kvw_ref, probs,
         score_ref, own_ref, term_refs)


def next_body(heads, parts, scale, fresh, spot_ref, *refs):
    gq_refs, refs = ([], refs) if fresh else (refs[:parts], refs[parts:])
    msg_refs, refs = refs[:parts], refs[parts:]
    inv_ref, nt_ref, qt_ref, aot_ref, kvw_ref, probs_ref, *refs = refs
    if fresh:
        *parts_refs, score_ref, own_ref, lhs_ref, row_ref, chain_ref = refs[:7]
        term_refs = refs[7:]
        assemble(spot_ref[1], chain_ref.shape[2], chain_ref, parts_refs)
    else:
        chain_ref, score_ref, own_ref, lhs_ref, row_ref = refs[:5]
        term_refs = refs[5:]
    rows, wide = lhs_ref.shape[1], chain_ref.shape[2]
    out = jnp.zeros((rows, wide), F32)
    along = jnp.zeros((EXTRA, rows), F32)
    for k in range(parts):
        index = lax.rem(spot_ref[0] + k, parts)
        msg = msg_refs[k][...]
        chain = chain_ref[k]
        lhs = msg[:rows]
        if gq_refs:
            lhs = jnp.concatenate([gq_refs[k][...], lhs], axis=1)
        out += jnp.dot(lhs, chain, preferred_element_type=F32)
        lhs_ref[index] = lhs
        along += msg[rows:, :rows].astype(F32)
    row_ref[...] = along
    along = jnp.sum(along, axis=0, keepdims=True)
    along = jnp.concatenate([along] * heads, axis=1)
    go = lanes_of((out * inv_ref[:, :1]).T, heads)
    inv_row = jnp.concatenate([inv_ref[...].T[:1, :]] * heads, axis=1)
    go = go - inv_row * along * nt_ref[...]
    pull(heads, scale, go, aot_ref[...], qt_ref[...], kvw_ref, probs_ref[...],
         score_ref, own_ref, term_refs)


def collect_body(width, own_ref, gq_ref, qf_ref, kvf_ref, *refs):
    msg_ref = refs[-1]
    rows = own_ref.shape[0]
    total = own_ref[...]
    for ref in refs[:-1]:
        total += ref[...].astype(F32)
    total = total.astype(BF16)
    ahead = msg_ref.shape[1] - total.shape[1]
    if ahead:
        msg_ref[:rows, :ahead] = gq_ref[...]
        msg_ref[rows:, :] = jnp.zeros((EXTRA, msg_ref.shape[1]), BF16)
    msg_ref[:rows, ahead:] = total
    prods = gq_ref[...].astype(F32) * qf_ref[...]
    partial = total.astype(F32) * kvf_ref[...]
    lanes = partial.shape[1]
    for first in range(0, prods.shape[1], lanes):
        partial += prods[:, first : first + lanes]
    along = jnp.sum(partial.T, axis=0, keepdims=True) * (1.0 / width)
    high = along.astype(BF16).astype(F32)
    place = lax.broadcasted_iota(jnp.int32, (EXTRA, rows), 0)
    extra = jnp.where(place == 0, high, jnp.where(place == 1, along - high, 0.0))
    msg_ref[rows:, :rows] = extra.astype(BF16)


def field_body(parts, wide, spot_ref, *refs):
    gq_refs, msg_refs, refs = refs[:parts], refs[parts : 2 * parts], refs[2 * parts :]
    lhs1_ref, row1_ref, lhs2_ref, row2_ref, *refs = refs
    *w_refs, z_ref, up_ref, gain_ref, inv_ref, v_ref, tot_ref, lhs3_ref, w_ref = refs
    rows, part = v_ref.shape[1:]
    head = spot_ref[0]
    row3 = jnp.zeros((EXTRA, rows), F32)
    for k in range(parts):
        msg = msg_refs[k][...]
        lhs3_ref[lax.rem(head + k, parts)] = jnp.concatenate(
            [gq_refs[k][...], msg[:rows]], axis=1
        )
        row3 += msg[rows:].astype(F32)
    assemble(spot_ref[1], wide, w_ref, w_refs)
    y = jnp.zeros((3 * rows, part), F32)
    for k in range(parts):
        lhs = jnp.concatenate([lhs1_ref[k], lhs2_ref[k], lhs3_ref[k]], axis=0)
        weight = w_ref[lax.rem(k - head + parts, parts)]
        y += jnp.dot(lhs, weight, preferred_element_type=F32)
    at = pl.ds(pl.multiple_of(head * part, part), part)
    inverse = inv_ref[:, :1]
    normed = z_ref[:, at].astype(F32) * inverse
    gain = gain_ref[:, at]
    fields = []
    for step, row in enumerate((row1_ref[...], row2_ref[...], row3)):
        along = jnp.broadcast_to(jnp.sum(row, axis=0, keepdims=True), (rows, rows)).T[:, :1]
        y_step = y[step * rows : (step + 1) * rows]
        fields.append(inverse * (y_step * gain - normed * along))
        v_ref[step] = fields[step]
    first, second, third = fields
    change1 = first - up_ref[:, at].astype(F32)
    change2 = second - first
    change3 = third - second
    pairs = [
        (change1, first), (change1, change1), (change2, first), (change2, change2),
        (change2, second), (change2, change3), (change3, second), (change3, change3),
    ]
    lanes = tot_ref.shape[2]
    sums = []
    for a, b in pairs:
        total = jnp.sum(a * b, axis=0, keepdims=True)
        sums.append(sum(total[:, i : i + lanes] for i in range(0, part, lanes)))
    totals = jnp.concatenate(sums, axis=0)
    for k in range(tot_ref.shape[0]):
        tot_ref[k] = totals


def mix_body(entries, spot_ref, tot_ref, up_ref, v_ref, out_ref):
    totals = jnp.sum(jnp.sum(tot_ref[...], axis=0), axis=1, keepdims=True) / entries
    s_r1, s_s, d2_v1, d2_d2, d2_v2, d2_d3, d3_v2, d3_d3 = [totals[i : i + 1] for i in range(8)]
    mix1 = s_r1 / (s_s + mix_eps)
    keep1 = 1.0 - mix1
    mix2 = keep1 * (d2_v1 + keep1 * d2_d2) / (keep1 * keep1 * d2_d2 + mix_eps)
    keep2 = keep1 * (1.0 - mix2)
    cross = mix1 * (d2_v2 + keep2 * d2_d3) + keep2 * (d3_v2 + keep2 * d3_d3)
    square = mix1 * mix1 * d2_d2 + 2.0 * mix1 * keep2 * d2_d3 + keep2 * keep2 * d3_d3
    mix3 = cross / (square + mix_eps)
    part = out_ref.shape[1]
    at = pl.ds(pl.multiple_of(spot_ref[0] * part, part), part)
    mixed = (
        up_ref[:, at].astype(F32)
        + v_ref[0]
        + (1.0 - mix3 * mix1) * v_ref[1]
        + keep2 * (1.0 - mix3) * v_ref[2]
    )
    out_ref[...] = mixed.astype(BF16)


def join_body(spot_ref, *refs):
    out_ref = refs[-1]
    parts = len(refs) - 1
    part = refs[0].shape[1]
    for k in range(parts):
        first = lax.rem(spot_ref[0] + k, parts) * part
        out_ref[:, pl.ds(pl.multiple_of(first, part), part)] = refs[k][...].astype(F32)


def shards(
    fixed_point,
    upstream,
    norm_gain,
    query_weight,
    keyval_weight,
    output_weight,
    log_norm,
    attention_out,
):
    rows, width = fixed_point.shape
    wide = query_weight.shape[1]
    narrow = keyval_weight.shape[1]
    size = wide + narrow
    e = narrow // 2
    heads = log_norm.shape[0]
    seq_count = lax.axis_size("seq")
    parts = lax.axis_size("head")
    block = lax.axis_index("seq")
    head = lax.axis_index("head")
    scale = e ** (-0.5)
    gain = norm_gain.reshape(1, width)
    span = (WIN_DEVS + 1) * rows
    group = min(8, seq_count)

    cols = size // group
    spot = jnp.stack([head, lax.rem(block, group)])
    smem = pl.BlockSpec(memory_space=pltpu.SMEM)
    vmem = pl.BlockSpec(memory_space=pltpu.VMEM)
    hbm = pl.BlockSpec(memory_space=pltpu.HBM)

    def pinned(value):
        return pltpu.with_memory_space_constraint(value, pltpu.HBM)

    tile = 128 if wide % 128 == 0 and 128 % (wide // group) == 0 else wide
    own_cols, hidden, kv, kvf, inv = local_call(
        prep_body,
        [
            shape_of((cols, width), BF16),
            shape_of((rows, width), BF16),
            shape_of((rows, narrow), BF16),
            shape_of((rows, narrow), F32),
            shape_of((rows, rows), F32),
        ],
        2 * width * size * cols,
        2 * width * (tile + narrow + rows),
        10,
        in_specs=[smem] + [hbm] * 4,
        scratch_shapes=[
            pltpu.VMEM((width, tile), BF16),
            pltpu.VMEM((width, narrow), BF16),
            pltpu.VMEM((rows, width), BF16),
            pltpu.VMEM((1, width), F32),
            pltpu.SemaphoreType.DMA((4,)),
        ],
    )(
        block.reshape(1),
        pinned(query_weight),
        pinned(keyval_weight),
        pinned(fixed_point),
        pinned(gain),
    )
    every_cols = jnp.stack(rotated(own_cols, "head"))
    earlier = [shifted(kv, "seq", offset) for offset in range(WIN_DEVS, 0, -1)]

    qf, qt, go, nt, aot, scaled, norms = local_call(
        functools.partial(start_body, heads),
        [
            shape_of((rows, wide), F32),
            shape_of((e, heads * rows), BF16),
            shape_of((e, heads * rows), F32),
            shape_of((e, heads * rows), F32),
            shape_of((e, heads * rows), F32),
            shape_of((wide, width), BF16),
            shape_of((heads, rows), F32),
        ],
        6 * rows * width * wide,
        4 * width * (2 * rows + wide),
        14,
        in_specs=[vmem] * 2 + [hbm] * 7,
        scratch_shapes=[
            pltpu.VMEM((width, wide), BF16),
            pltpu.VMEM((wide, width), BF16),
            pltpu.VMEM((rows, width), BF16),
            pltpu.VMEM((rows, width), BF16),
            pltpu.VMEM((rows, wide), BF16),
            pltpu.VMEM((1, width), F32),
            pltpu.SemaphoreType.DMA((7,)),
        ],
    )(
        hidden,
        inv,
        pinned(query_weight),
        pinned(output_weight),
        pinned(upstream),
        pinned(fixed_point),
        pinned(attention_out),
        pinned(gain),
        pinned(log_norm),
    )

    pull_outs = [shape_of((span, heads * rows), BF16), shape_of((rows, narrow), F32)]
    pull_outs += [shape_of((rows, narrow), BF16)] * WIN_DEVS
    pull_flops = 6 * span * e * heads * rows

    def exchange(score, own, terms, split):
        arrived = [shifted(term, "seq", -offset - 1) for offset, term in enumerate(terms)]
        gq = local_call(
            functools.partial(query_body, heads, scale),
            shape_of((rows, wide), BF16),
            2 * span * e * heads * rows,
            span * heads * rows * 2,
            4,
        )(kt, score)
        ahead = rotated(gq, "head") if split else []
        if not split:
            arrived = list(lax.optimization_barrier((tuple(arrived), near[1]))[0])
        msg = local_call(
            functools.partial(collect_body, width),
            shape_of((rows + EXTRA, narrow if split else size), BF16),
            COLLECT * rows * size,
            rows * size * 4,
            4,
        )(own, gq, qf, kvf, *arrived)
        return rotated(msg, "head"), msg, ahead

    kvw, kt, probs, score, own, *terms = local_call(
        functools.partial(first_body, heads, scale),
        [
            shape_of((span, narrow), BF16),
            shape_of((e, span), BF16),
            shape_of((span, heads * rows), BF16),
        ]
        + pull_outs,
        pull_flops * 5 // 4,
        span * heads * rows * 2,
        16,
        in_specs=[smem] + [vmem] * (WIN_DEVS + 5),
    )(block.reshape(1), *earlier, kv, qt, go, aot, norms)
    packed, marks = [], []
    chain_shape = shape_of((parts, size, wide), BF16)
    for step in range(3):
        if step:
            score, own, lhs, row, *terms = local_call(
                functools.partial(next_body, heads, parts, scale, step == 1),
                pull_outs[:2]
                + [shape_of((parts, rows, size), BF16), shape_of((EXTRA, rows), F32)]
                + [chain_shape] * (step == 1)
                + pull_outs[2:],
                pull_flops + 2 * rows * parts * size * wide,
                span * heads * rows * 2 + parts * size * wide * 2,
                16,
                in_specs=[smem] + [vmem] * (len(ahead) + parts + 6 + len(chain)),
            )(spot, *ahead, *every_msg, inv, nt, qt, aot, kvw, probs, *chain)
            packed += [lhs, row]
            if step == 1:
                chain, *terms = terms
                chain = [chain]
        if step == 0:
            every_cols, _ = lax.optimization_barrier((every_cols, score))
            share = local_call(
                chain_body,
                shape_of((parts * cols, wide), BF16),
                2 * parts * cols * width * wide,
                2 * width * (wide + parts * cols),
                8,
            )(every_cols.reshape(parts * cols, width), scaled)
            share = share.reshape(parts, cols, wide)
            *terms, share = lax.optimization_barrier((*terms, share))
            pairs = [(i, i ^ (group // 2)) for i in range(seq_count)]
            near = [share[None], lax.ppermute(share[None], "seq", pairs)]
        every_msg, msg, ahead = exchange(score, own, terms, step > 0)
        if step == 0:
            chain = doubled(near, "seq", group // 2, (msg, every_msg[1:]))
        marks.append(dict(msg=msg, sent=(ahead[1:], every_msg[1:])))

    part = width // parts
    mine = lax.dynamic_slice_in_dim(every_cols, head * part, part, 2)
    weight = doubled([mine[None]], "seq", group, (marks[0]["msg"], marks[0]["sent"], marks[1]["sent"]))
    small = seq_count * parts <= 64
    fields, totals = local_call(
        functools.partial(field_body, parts, wide),
        [
            shape_of((3, rows, part), F32),
            shape_of((seq_count * parts if small else 1, 8, 128), F32),
        ],
        6 * rows * parts * size * part,
        2 * parts * size * part,
        20,
        in_specs=[smem] + [vmem] * (2 * parts + 8 + len(weight)),
        scratch_shapes=[
            pltpu.VMEM((parts, rows, size), BF16),
            pltpu.VMEM((parts, size, part), BF16),
        ],
    )(spot, *ahead, *every_msg, *packed, *weight, fixed_point, upstream, gain, inv)
    if small:
        totals = lax.all_to_all(totals, ("seq", "head"), 0, 0)
    else:
        totals = lax.psum(totals, ("seq", "head"))
    mixed = local_call(
        functools.partial(mix_body, rows * seq_count * width),
        shape_of((rows, part), BF16),
        8 * rows * part,
        18 * rows * part,
        6,
        in_specs=[smem] + [vmem] * 3,
    )(spot, totals, upstream, fields)
    every_mixed = rotated(mixed, "head")
    return local_call(
        join_body,
        shape_of((rows, width), F32),
        0,
        6 * rows * width,
        6,
        in_specs=[smem] + [vmem] * parts,
    )(spot, *every_mixed)


def solution(mesh):
    in_specs = (
        P("seq", None),
        P("seq", None),
        P(),
        P(None, "head"),
        P(None, "head"),
        P("head", None),
        P("head", "seq"),
        P("seq", "head"),
    )
    out_specs = P("seq", None)
    return jax.shard_map(shards, mesh=mesh, in_specs=in_specs, out_specs=out_specs, check_vma=False)
```

```python
import functools

import jax
import jax.numpy as jnp
from jax import lax
from jax.experimental import pallas as pl
from jax.experimental.pallas import tpu as pltpu
from jax.sharding import PartitionSpec as P

WIN_DEVS = 4
norm_eps = 1e-05
mix_eps = 1e-06
F32 = jnp.float32
BF16 = jnp.bfloat16
COLLECT = 50000
EXTRA = 16
NT = (((1,), (1,)), ((), ()))


def shape_of(shape, dtype):
    return jax.ShapeDtypeStruct(shape, dtype)


def local_call(body, outs, flops, moved, room, **more):
    return pl.pallas_call(
        body,
        out_shape=outs,
        compiler_params=pltpu.CompilerParams(vmem_limit_bytes=room * 1024 * 1024),
        cost_estimate=pl.CostEstimate(flops=flops, bytes_accessed=moved, transcendentals=0),
        **more,
    )


def shifted(value, axis, steps):
    count = lax.axis_size(axis)
    initial, last = (max(0, -steps), min(count, count - steps))
    return lax.ppermute(value, axis, [(source, source + steps) for source in range(initial, last)])


def rotated(value, axis):
    count = lax.axis_size(axis)
    parts = [value]
    for step in range(1, count):
        parts.append(lax.ppermute(value, axis, [(i, (i - step) % count) for i in range(count)]))
    return parts


def doubled(value, axis, group, gates):
    count = lax.axis_size(axis)
    near, bit = list(value), group // 2
    for gate in gates:
        near = list(lax.optimization_barrier((tuple(near), gate))[0])
        pairs = [(i, i ^ bit) for i in range(count)]
        if len(near) > 1:
            near = [jnp.concatenate(near)]
        if bit == 1:
            return near + [lax.ppermute(near[0], axis, pairs)]
        near.append(lax.ppermute(near[0], axis, pairs))
        bit //= 2


def assemble(place, wide, out_ref, refs):
    group = sum(ref.shape[0] for ref in refs)
    cut = wide // group
    rest_cut = refs[0].shape[2] - cut
    entries = [(ref, j) for ref in refs for j in range(ref.shape[0])]
    for j, (ref, at) in enumerate(entries):
        distance, bit, rest = 0, group // 2, j
        while rest:
            distance += bit * (rest & 1)
            rest >>= 1
            bit //= 2
        index = lax.bitwise_xor(place, jnp.int32(distance))
        first = pl.multiple_of(index * cut, cut)
        second = pl.multiple_of(wide + index * rest_cut, rest_cut)
        for k in range(out_ref.shape[0]):
            out_ref[k, pl.ds(first, cut), :] = ref[at, k, :cut, :]
            out_ref[k, pl.ds(second, rest_cut), :] = ref[at, k, cut:, :]


def prep_body(block_ref, qw_ref, kvw_ref, z_ref, gain_ref, cols_ref, hidden_ref, kv_ref, kvf_ref,
              inv_ref, q_tile, kv_tile, z_tile, gain_tile, sems):
    tile = q_tile.shape[1]
    wide, narrow = qw_ref.shape[1], kvw_ref.shape[1]
    group = (wide + narrow) // cols_ref.shape[0]
    place = lax.rem(block_ref[0], group)
    q_take, kv_take = wide // group, narrow // group
    q_at = place * q_take
    q_first = pl.multiple_of(q_at // tile * tile, tile)
    copies = [
        pltpu.make_async_copy(qw_ref.at[:, pl.ds(q_first, tile)], q_tile, sems.at[0]),
        pltpu.make_async_copy(kvw_ref, kv_tile, sems.at[1]),
        pltpu.make_async_copy(z_ref, z_tile, sems.at[2]),
        pltpu.make_async_copy(gain_ref, gain_tile, sems.at[3]),
    ]
    for copy in copies:
        copy.start()
    first = 0
    for copy, ref, at, take in (
        (copies[0], q_tile, q_at - q_first, q_take),
        (copies[1], kv_tile, place * kv_take, kv_take),
    ):
        copy.wait()
        total = ref.shape[1]
        row = lax.broadcasted_iota(jnp.int32, (take, total), 0) + at
        pick = (row == lax.broadcasted_iota(jnp.int32, (take, total), 1)).astype(BF16)
        cols = lax.dot_general(pick, ref[...], NT, preferred_element_type=F32)
        cols_ref[first : first + take, :] = cols.astype(BF16)
        first += take
    copies[2].wait()
    copies[3].wait()
    z = z_tile[...].astype(F32)
    inverse = lax.rsqrt(jnp.mean(z * z, axis=1, keepdims=True) + norm_eps)
    hidden = (z * inverse * gain_tile[...]).astype(BF16)
    hidden_ref[...] = hidden
    kvf = jnp.dot(hidden, kv_tile[...], preferred_element_type=F32)
    kvf_ref[...] = kvf
    kv_ref[...] = kvf.astype(BF16)
    inv_ref[...] = jnp.broadcast_to(inverse, inv_ref.shape)


def chain_body(cols_ref, scaled_ref, out_ref):
    share = lax.dot_general(cols_ref[...], scaled_ref[...], NT, preferred_element_type=F32)
    out_ref[...] = share.astype(BF16)


def lanes_of(value, heads):
    size = value.shape[0] // heads
    return jnp.concatenate([value[i * size : (i + 1) * size] for i in range(heads)], axis=1)


def start_body(heads, hidden_ref, inv_ref, qw_ref, ow_ref, up_ref, z_ref, ao_ref, gain_ref, ln_ref,
               qf_ref, qt_ref, go_ref, nt_ref, aot_ref, scaled_ref, norms_ref,
               qw_tile, ow_tile, up_tile, z_tile, ao_tile, gain_tile, sems):
    copies = [
        pltpu.make_async_copy(source, target, sems.at[i])
        for i, (source, target) in enumerate(
            ((ow_ref, ow_tile), (up_ref, up_tile), (z_ref, z_tile), (qw_ref, qw_tile),
             (ao_ref, ao_tile), (gain_ref, gain_tile), (ln_ref, norms_ref))
        )
    ]
    for copy in copies:
        copy.start()
    for copy in copies[:3]:
        copy.wait()
    out = lax.dot_general(up_tile[...], ow_tile[...], NT, preferred_element_type=F32)
    go_ref[...] = lanes_of(out.T, heads)
    base = lax.dot_general(z_tile[...], ow_tile[...], NT, preferred_element_type=F32)
    nt_ref[...] = lanes_of((base * inv_ref[:, :1]).T, heads)
    copies[3].wait()
    qf = jnp.dot(hidden_ref[...], qw_tile[...], preferred_element_type=F32)
    qf_ref[...] = qf
    qt_ref[...] = lanes_of(qf.T, heads).astype(BF16)
    for copy in copies[4:]:
        copy.wait()
    scaled_ref[...] = (ow_tile[...].astype(F32) * gain_tile[...]).astype(BF16)
    aot_ref[...] = lanes_of(ao_tile[...].astype(F32).T, heads)


def pull(heads, scale, go, aot, qt, kvw_ref, probs, score_ref, own_ref, term_refs):
    e = go.shape[0]
    rows = go.shape[1] // heads
    row_terms = jnp.sum(go * aot, axis=0, keepdims=True)
    gob = go.astype(BF16)
    grad_prob = jnp.dot(kvw_ref[:, e:], gob, preferred_element_type=F32)
    grad_score = (probs.astype(F32) * (grad_prob - row_terms)).astype(BF16)
    score_ref[...] = grad_score
    grad_key = lax.dot_general(grad_score, qt, NT, preferred_element_type=F32) * scale
    grad_value = lax.dot_general(probs, gob, NT, preferred_element_type=F32)
    terms = jnp.concatenate([grad_key, grad_value], axis=1)
    for offset in range(1, len(term_refs) + 1):
        first = (len(term_refs) - offset) * rows
        term_refs[offset - 1][...] = terms[first : first + rows].astype(BF16)
    own_ref[...] = terms[len(term_refs) * rows :]


def query_body(heads, scale, kt_ref, score_ref, gq_ref):
    rows = gq_ref.shape[0]
    grad_query = jnp.dot(kt_ref[...], score_ref[...], preferred_element_type=F32) * scale
    parts = [grad_query[:, i * rows : (i + 1) * rows] for i in range(heads)]
    gq_ref[...] = jnp.concatenate(parts, axis=0).T.astype(BF16)


def first_body(heads, scale, block_ref, *refs):
    windows = refs[: WIN_DEVS + 1]
    qt_ref, go_ref, aot_ref, ln_ref = refs[WIN_DEVS + 1 : WIN_DEVS + 5]
    kvw_ref, kt_ref, probs_ref, score_ref, own_ref = refs[WIN_DEVS + 5 : WIN_DEVS + 10]
    term_refs = refs[WIN_DEVS + 10 :]
    rows = windows[0].shape[0]
    for place, ref in enumerate(windows):
        kvw_ref[place * rows : (place + 1) * rows, :] = ref[...]
    kvw = kvw_ref[...]
    e = kvw.shape[1] // 2
    kt_ref[...] = kvw.astype(F32).T[:e].astype(BF16)
    scores = jnp.dot(kvw[:, :e], qt_ref[...], preferred_element_type=F32) * scale
    norms = jnp.concatenate([ln_ref[i : i + 1, :] for i in range(heads)], axis=1)
    key_pos = lax.broadcasted_iota(jnp.int32, scores.shape, 0)
    query_pos = lax.broadcasted_iota(jnp.int32, scores.shape, 1) & (rows - 1)
    allowed = (key_pos > query_pos) & (key_pos <= query_pos + WIN_DEVS * rows)
    allowed = allowed & (key_pos >= (WIN_DEVS - block_ref[0]) * rows)
    probs = jnp.where(allowed, jnp.exp(scores - norms), 0.0).astype(BF16)
    probs_ref[...] = probs
    pull(heads, scale, go_ref[...], aot_ref[...], qt_ref[...], kvw_ref, probs,
         score_ref, own_ref, term_refs)


def next_body(heads, parts, scale, fresh, spot_ref, *refs):
    gq_refs, refs = ([], refs) if fresh else (refs[:parts], refs[parts:])
    msg_refs, refs = refs[:parts], refs[parts:]
    inv_ref, nt_ref, qt_ref, aot_ref, kvw_ref, probs_ref, *refs = refs
    if fresh:
        *parts_refs, score_ref, own_ref, lhs_ref, row_ref, chain_ref = refs[:7]
        term_refs = refs[7:]
        assemble(spot_ref[1], chain_ref.shape[2], chain_ref, parts_refs)
    else:
        chain_ref, score_ref, own_ref, lhs_ref, row_ref = refs[:5]
        term_refs = refs[5:]
    rows, wide = lhs_ref.shape[1], chain_ref.shape[2]
    out = jnp.zeros((rows, wide), F32)
    along = jnp.zeros((EXTRA, rows), F32)
    for k in range(parts):
        index = lax.rem(spot_ref[0] + k, parts)
        msg = msg_refs[k][...]
        chain = chain_ref[k]
        lhs = msg[:rows]
        if gq_refs:
            lhs = jnp.concatenate([gq_refs[k][...], lhs], axis=1)
        out += jnp.dot(lhs, chain, preferred_element_type=F32)
        lhs_ref[index] = lhs
        along += msg[rows:, :rows].astype(F32)
    row_ref[...] = along
    along = jnp.sum(along, axis=0, keepdims=True)
    along = jnp.concatenate([along] * heads, axis=1)
    go = lanes_of((out * inv_ref[:, :1]).T, heads)
    inv_row = jnp.concatenate([inv_ref[...].T[:1, :]] * heads, axis=1)
    go = go - inv_row * along * nt_ref[...]
    pull(heads, scale, go, aot_ref[...], qt_ref[...], kvw_ref, probs_ref[...],
         score_ref, own_ref, term_refs)


def collect_body(width, own_ref, gq_ref, qf_ref, kvf_ref, *refs):
    msg_ref = refs[-1]
    rows = own_ref.shape[0]
    total = own_ref[...]
    for ref in refs[:-1]:
        total += ref[...].astype(F32)
    total = total.astype(BF16)
    ahead = msg_ref.shape[1] - total.shape[1]
    if ahead:
        msg_ref[:rows, :ahead] = gq_ref[...]
        msg_ref[rows:, :] = jnp.zeros((EXTRA, msg_ref.shape[1]), BF16)
    msg_ref[:rows, ahead:] = total
    prods = gq_ref[...].astype(F32) * qf_ref[...]
    partial = total.astype(F32) * kvf_ref[...]
    lanes = partial.shape[1]
    for first in range(0, prods.shape[1], lanes):
        partial += prods[:, first : first + lanes]
    along = jnp.sum(partial.T, axis=0, keepdims=True) * (1.0 / width)
    high = along.astype(BF16).astype(F32)
    place = lax.broadcasted_iota(jnp.int32, (EXTRA, rows), 0)
    extra = jnp.where(place == 0, high, jnp.where(place == 1, along - high, 0.0))
    msg_ref[rows:, :rows] = extra.astype(BF16)


def field_body(parts, wide, spot_ref, *refs):
    gq_refs, msg_refs, refs = refs[:parts], refs[parts : 2 * parts], refs[2 * parts :]
    lhs1_ref, row1_ref, lhs2_ref, row2_ref, *refs = refs
    *w_refs, z_ref, up_ref, gain_ref, inv_ref, v_ref, tot_ref, lhs3_ref, w_ref = refs
    rows, part = v_ref.shape[1:]
    head = spot_ref[0]
    row3 = jnp.zeros((EXTRA, rows), F32)
    for k in range(parts):
        msg = msg_refs[k][...]
        lhs3_ref[lax.rem(head + k, parts)] = jnp.concatenate(
            [gq_refs[k][...], msg[:rows]], axis=1
        )
        row3 += msg[rows:].astype(F32)
    assemble(spot_ref[1], wide, w_ref, w_refs)
    y = jnp.zeros((3 * rows, part), F32)
    for k in range(parts):
        lhs = jnp.concatenate([lhs1_ref[k], lhs2_ref[k], lhs3_ref[k]], axis=0)
        weight = w_ref[lax.rem(k - head + parts, parts)]
        y += jnp.dot(lhs, weight, preferred_element_type=F32)
    at = pl.ds(pl.multiple_of(head * part, part), part)
    inverse = inv_ref[:, :1]
    normed = z_ref[:, at].astype(F32) * inverse
    gain = gain_ref[:, at]
    fields = []
    for step, row in enumerate((row1_ref[...], row2_ref[...], row3)):
        along = jnp.broadcast_to(jnp.sum(row, axis=0, keepdims=True), (rows, rows)).T[:, :1]
        y_step = y[step * rows : (step + 1) * rows]
        fields.append(inverse * (y_step * gain - normed * along))
        v_ref[step] = fields[step]
    first, second, third = fields
    change1 = first - up_ref[:, at].astype(F32)
    change2 = second - first
    change3 = third - second
    pairs = [
        (change1, first), (change1, change1), (change2, first), (change2, change2),
        (change2, second), (change2, change3), (change3, second), (change3, change3),
    ]
    lanes = tot_ref.shape[2]
    sums = []
    for a, b in pairs:
        total = jnp.sum(a * b, axis=0, keepdims=True)
        sums.append(sum(total[:, i : i + lanes] for i in range(0, part, lanes)))
    totals = jnp.concatenate(sums, axis=0)
    for k in range(tot_ref.shape[0]):
        tot_ref[k] = totals


def mix_body(entries, spot_ref, tot_ref, up_ref, v_ref, out_ref):
    totals = jnp.sum(jnp.sum(tot_ref[...], axis=0), axis=1, keepdims=True) / entries
    s_r1, s_s, d2_v1, d2_d2, d2_v2, d2_d3, d3_v2, d3_d3 = [totals[i : i + 1] for i in range(8)]
    mix1 = s_r1 / (s_s + mix_eps)
    keep1 = 1.0 - mix1
    mix2 = keep1 * (d2_v1 + keep1 * d2_d2) / (keep1 * keep1 * d2_d2 + mix_eps)
    keep2 = keep1 * (1.0 - mix2)
    cross = mix1 * (d2_v2 + keep2 * d2_d3) + keep2 * (d3_v2 + keep2 * d3_d3)
    square = mix1 * mix1 * d2_d2 + 2.0 * mix1 * keep2 * d2_d3 + keep2 * keep2 * d3_d3
    mix3 = cross / (square + mix_eps)
    part = out_ref.shape[1]
    at = pl.ds(pl.multiple_of(spot_ref[0] * part, part), part)
    mixed = (
        up_ref[:, at].astype(F32)
        + v_ref[0]
        + (1.0 - mix3 * mix1) * v_ref[1]
        + keep2 * (1.0 - mix3) * v_ref[2]
    )
    out_ref[...] = mixed.astype(BF16)


def join_body(spot_ref, *refs):
    *part_refs, out_ref, tile, sems = refs
    parts = len(part_refs)
    part = part_refs[0].shape[1]
    copies = []
    for k in range(parts):
        tile[k] = part_refs[k][...].astype(F32)
        first = pl.multiple_of(lax.rem(spot_ref[0] + k, parts) * part, part)
        copies.append(
            pltpu.make_async_copy(tile.at[k], out_ref.at[:, pl.ds(first, part)], sems.at[k])
        )
        copies[k].start()
    for copy in copies:
        copy.wait()


def shards(
    fixed_point,
    upstream,
    norm_gain,
    query_weight,
    keyval_weight,
    output_weight,
    log_norm,
    attention_out,
):
    rows, width = fixed_point.shape
    wide = query_weight.shape[1]
    narrow = keyval_weight.shape[1]
    size = wide + narrow
    e = narrow // 2
    heads = log_norm.shape[0]
    seq_count = lax.axis_size("seq")
    parts = lax.axis_size("head")
    block = lax.axis_index("seq")
    head = lax.axis_index("head")
    scale = e ** (-0.5)
    gain = norm_gain.reshape(1, width)
    span = (WIN_DEVS + 1) * rows
    group = min(8, seq_count)

    cols = size // group
    spot = jnp.stack([head, lax.rem(block, group)])
    smem = pl.BlockSpec(memory_space=pltpu.SMEM)
    vmem = pl.BlockSpec(memory_space=pltpu.VMEM)
    hbm = pl.BlockSpec(memory_space=pltpu.HBM)

    def pinned(value):
        return pltpu.with_memory_space_constraint(value, pltpu.HBM)

    tile = 128 if wide % 128 == 0 and 128 % (wide // group) == 0 else wide
    own_cols, hidden, kv, kvf, inv = local_call(
        prep_body,
        [
            shape_of((cols, width), BF16),
            shape_of((rows, width), BF16),
            shape_of((rows, narrow), BF16),
            shape_of((rows, narrow), F32),
            shape_of((rows, rows), F32),
        ],
        2 * width * size * cols,
        2 * width * (tile + narrow + rows),
        10,
        in_specs=[smem] + [hbm] * 4,
        scratch_shapes=[
            pltpu.VMEM((width, tile), BF16),
            pltpu.VMEM((width, narrow), BF16),
            pltpu.VMEM((rows, width), BF16),
            pltpu.VMEM((1, width), F32),
            pltpu.SemaphoreType.DMA((4,)),
        ],
    )(
        block.reshape(1),
        pinned(query_weight),
        pinned(keyval_weight),
        pinned(fixed_point),
        pinned(gain),
    )
    every_cols = jnp.stack(rotated(own_cols, "head"))
    earlier = [shifted(kv, "seq", offset) for offset in range(WIN_DEVS, 0, -1)]

    qf, qt, go, nt, aot, scaled, norms = local_call(
        functools.partial(start_body, heads),
        [
            shape_of((rows, wide), F32),
            shape_of((e, heads * rows), BF16),
            shape_of((e, heads * rows), F32),
            shape_of((e, heads * rows), F32),
            shape_of((e, heads * rows), F32),
            shape_of((wide, width), BF16),
            shape_of((heads, rows), F32),
        ],
        6 * rows * width * wide,
        4 * width * (2 * rows + wide),
        14,
        in_specs=[vmem] * 2 + [hbm] * 7,
        scratch_shapes=[
            pltpu.VMEM((width, wide), BF16),
            pltpu.VMEM((wide, width), BF16),
            pltpu.VMEM((rows, width), BF16),
            pltpu.VMEM((rows, width), BF16),
            pltpu.VMEM((rows, wide), BF16),
            pltpu.VMEM((1, width), F32),
            pltpu.SemaphoreType.DMA((7,)),
        ],
    )(
        hidden,
        inv,
        pinned(query_weight),
        pinned(output_weight),
        pinned(upstream),
        pinned(fixed_point),
        pinned(attention_out),
        pinned(gain),
        pinned(log_norm),
    )

    pull_outs = [shape_of((span, heads * rows), BF16), shape_of((rows, narrow), F32)]
    pull_outs += [shape_of((rows, narrow), BF16)] * WIN_DEVS
    pull_flops = 6 * span * e * heads * rows

    def exchange(score, own, terms, split):
        arrived = [shifted(term, "seq", -offset - 1) for offset, term in enumerate(terms)]
        gq = local_call(
            functools.partial(query_body, heads, scale),
            shape_of((rows, wide), BF16),
            2 * span * e * heads * rows,
            span * heads * rows * 2,
            4,
        )(kt, score)
        ahead = rotated(gq, "head") if split else []
        if not split:
            arrived = list(lax.optimization_barrier((tuple(arrived), near[1]))[0])
        msg = local_call(
            functools.partial(collect_body, width),
            shape_of((rows + EXTRA, narrow if split else size), BF16),
            COLLECT * rows * size,
            rows * size * 4,
            4,
        )(own, gq, qf, kvf, *arrived)
        return rotated(msg, "head"), msg, ahead

    kvw, kt, probs, score, own, *terms = local_call(
        functools.partial(first_body, heads, scale),
        [
            shape_of((span, narrow), BF16),
            shape_of((e, span), BF16),
            shape_of((span, heads * rows), BF16),
        ]
        + pull_outs,
        pull_flops * 5 // 4,
        span * heads * rows * 2,
        16,
        in_specs=[smem] + [vmem] * (WIN_DEVS + 5),
    )(block.reshape(1), *earlier, kv, qt, go, aot, norms)
    packed, marks = [], []
    chain_shape = shape_of((parts, size, wide), BF16)
    for step in range(3):
        if step:
            score, own, lhs, row, *terms = local_call(
                functools.partial(next_body, heads, parts, scale, step == 1),
                pull_outs[:2]
                + [shape_of((parts, rows, size), BF16), shape_of((EXTRA, rows), F32)]
                + [chain_shape] * (step == 1)
                + pull_outs[2:],
                pull_flops + 2 * rows * parts * size * wide,
                span * heads * rows * 2 + parts * size * wide * 2,
                16,
                in_specs=[smem] + [vmem] * (len(ahead) + parts + 6 + len(chain)),
            )(spot, *ahead, *every_msg, inv, nt, qt, aot, kvw, probs, *chain)
            packed += [lhs, row]
            if step == 1:
                chain, *terms = terms
                chain = [chain]
        if step == 0:
            every_cols, _ = lax.optimization_barrier((every_cols, score))
            share = local_call(
                chain_body,
                shape_of((parts * cols, wide), BF16),
                2 * parts * cols * width * wide,
                2 * width * (wide + parts * cols),
                8,
            )(every_cols.reshape(parts * cols, width), scaled)
            share = share.reshape(parts, cols, wide)
            *terms, share = lax.optimization_barrier((*terms, share))
            pairs = [(i, i ^ (group // 2)) for i in range(seq_count)]
            near = [share[None], lax.ppermute(share[None], "seq", pairs)]
        every_msg, msg, ahead = exchange(score, own, terms, step > 0)
        if step == 0:
            chain = doubled(near, "seq", group // 2, (msg, every_msg[1:2]))
        marks.append(dict(msg=msg, sent=(ahead[1:], every_msg[1:])))

    part = width // parts
    mine = lax.dynamic_slice_in_dim(every_cols, head * part, part, 2)
    weight = doubled([mine[None]], "seq", group, (marks[0]["msg"], marks[0]["sent"], marks[1]["sent"]))
    small = seq_count * parts <= 64
    fields, totals = local_call(
        functools.partial(field_body, parts, wide),
        [
            shape_of((3, rows, part), F32),
            shape_of((seq_count * parts if small else 1, 8, 128), F32),
        ],
        6 * rows * parts * size * part,
        2 * parts * size * part,
        20,
        in_specs=[smem] + [vmem] * (2 * parts + 8 + len(weight)),
        scratch_shapes=[
            pltpu.VMEM((parts, rows, size), BF16),
            pltpu.VMEM((parts, size, part), BF16),
        ],
    )(spot, *ahead, *every_msg, *packed, *weight, fixed_point, upstream, gain, inv)
    if small:
        totals = lax.all_to_all(totals, ("seq", "head"), 0, 0)
    else:
        totals = lax.psum(totals, ("seq", "head"))
    mixed = local_call(
        functools.partial(mix_body, rows * seq_count * width),
        shape_of((rows, part), BF16),
        8 * rows * part,
        18 * rows * part,
        6,
        in_specs=[smem] + [vmem] * 3,
    )(spot, totals, upstream, fields)
    every_mixed = rotated(mixed, "head")
    return local_call(
        join_body,
        shape_of((rows, width), F32),
        0,
        6 * rows * width,
        6,
        in_specs=[smem] + [vmem] * parts,
        out_specs=hbm,
        scratch_shapes=[
            pltpu.VMEM((parts, rows, part), F32),
            pltpu.SemaphoreType.DMA((parts,)),
        ],
    )(spot, *every_mixed)


def solution(mesh):
    in_specs = (
        P("seq", None),
        P("seq", None),
        P(),
        P(None, "head"),
        P(None, "head"),
        P("head", None),
        P("head", "seq"),
        P("seq", "head"),
    )
    out_specs = P("seq", None)
    return jax.shard_map(shards, mesh=mesh, in_specs=in_specs, out_specs=out_specs, check_vma=False)
```

```python
import functools

import jax
import jax.numpy as jnp
from jax import lax
from jax.experimental import pallas as pl
from jax.experimental.pallas import tpu as pltpu
from jax.sharding import PartitionSpec as P

WIN_DEVS = 4
norm_eps = 1e-05
mix_eps = 1e-06
F32 = jnp.float32
BF16 = jnp.bfloat16
COLLECT = 50000
EXTRA = 16
NT = (((1,), (1,)), ((), ()))


def shape_of(shape, dtype):
    return jax.ShapeDtypeStruct(shape, dtype)


def local_call(body, outs, flops, moved, room, **more):
    return pl.pallas_call(
        body,
        out_shape=outs,
        compiler_params=pltpu.CompilerParams(vmem_limit_bytes=room * 1024 * 1024),
        cost_estimate=pl.CostEstimate(flops=flops, bytes_accessed=moved, transcendentals=0),
        **more,
    )


def shifted(value, axis, steps):
    count = lax.axis_size(axis)
    initial, last = (max(0, -steps), min(count, count - steps))
    return lax.ppermute(value, axis, [(source, source + steps) for source in range(initial, last)])


def rotated(value, axis):
    count = lax.axis_size(axis)
    parts = [value]
    for step in range(1, count):
        parts.append(lax.ppermute(value, axis, [(i, (i - step) % count) for i in range(count)]))
    return parts


def doubled(value, axis, group, gates):
    count = lax.axis_size(axis)
    near, bit = list(value), group // 2
    for gate in gates:
        near = list(lax.optimization_barrier((tuple(near), gate))[0])
        pairs = [(i, i ^ bit) for i in range(count)]
        if len(near) > 1:
            near = [jnp.concatenate(near)]
        if bit == 1:
            return near + [lax.ppermute(near[0], axis, pairs)]
        near.append(lax.ppermute(near[0], axis, pairs))
        bit //= 2


def assemble(place, wide, out_ref, refs):
    group = sum(ref.shape[0] for ref in refs)
    cut = wide // group
    rest_cut = refs[0].shape[2] - cut
    entries = [(ref, j) for ref in refs for j in range(ref.shape[0])]
    for j, (ref, at) in enumerate(entries):
        distance, bit, rest = 0, group // 2, j
        while rest:
            distance += bit * (rest & 1)
            rest >>= 1
            bit //= 2
        index = lax.bitwise_xor(place, jnp.int32(distance))
        first = pl.multiple_of(index * cut, cut)
        second = pl.multiple_of(wide + index * rest_cut, rest_cut)
        for k in range(out_ref.shape[0]):
            out_ref[k, pl.ds(first, cut), :] = ref[at, k, :cut, :]
            out_ref[k, pl.ds(second, rest_cut), :] = ref[at, k, cut:, :]


def prep_body(block_ref, qw_ref, kvw_ref, z_ref, gain_ref, cols_ref, hidden_ref, kv_ref, kvf_ref,
              inv_ref, q_tile, kv_tile, z_tile, gain_tile, sems):
    tile = q_tile.shape[1]
    wide, narrow = qw_ref.shape[1], kvw_ref.shape[1]
    group = (wide + narrow) // cols_ref.shape[0]
    place = lax.rem(block_ref[0], group)
    q_take, kv_take = wide // group, narrow // group
    q_at = place * q_take
    q_first = pl.multiple_of(q_at // tile * tile, tile)
    copies = [
        pltpu.make_async_copy(qw_ref.at[:, pl.ds(q_first, tile)], q_tile, sems.at[0]),
        pltpu.make_async_copy(kvw_ref, kv_tile, sems.at[1]),
        pltpu.make_async_copy(z_ref, z_tile, sems.at[2]),
        pltpu.make_async_copy(gain_ref, gain_tile, sems.at[3]),
    ]
    for copy in copies:
        copy.start()
    first = 0
    for copy, ref, at, take in (
        (copies[0], q_tile, q_at - q_first, q_take),
        (copies[1], kv_tile, place * kv_take, kv_take),
    ):
        copy.wait()
        total = ref.shape[1]
        row = lax.broadcasted_iota(jnp.int32, (take, total), 0) + at
        pick = (row == lax.broadcasted_iota(jnp.int32, (take, total), 1)).astype(BF16)
        cols = lax.dot_general(pick, ref[...], NT, preferred_element_type=F32)
        cols_ref[first : first + take, :] = cols.astype(BF16)
        first += take
    copies[2].wait()
    copies[3].wait()
    z = z_tile[...].astype(F32)
    inverse = lax.rsqrt(jnp.mean(z * z, axis=1, keepdims=True) + norm_eps)
    hidden = (z * inverse * gain_tile[...]).astype(BF16)
    hidden_ref[...] = hidden
    kvf = jnp.dot(hidden, kv_tile[...], preferred_element_type=F32)
    kvf_ref[...] = kvf
    kv_ref[...] = kvf.astype(BF16)
    inv_ref[...] = jnp.broadcast_to(inverse, inv_ref.shape)


def chain_body(cols_ref, scaled_ref, out_ref):
    share = lax.dot_general(cols_ref[...], scaled_ref[...], NT, preferred_element_type=F32)
    out_ref[...] = share.astype(BF16)


def lanes_of(value, heads):
    size = value.shape[0] // heads
    return jnp.concatenate([value[i * size : (i + 1) * size] for i in range(heads)], axis=1)


def start_body(heads, hidden_ref, inv_ref, qw_ref, ow_ref, up_ref, z_ref, ao_ref, gain_ref, ln_ref,
               qf_ref, qt_ref, go_ref, nt_ref, aot_ref, scaled_ref, norms_ref,
               qw_tile, ow_tile, up_tile, z_tile, ao_tile, gain_tile, sems):
    copies = [
        pltpu.make_async_copy(source, target, sems.at[i])
        for i, (source, target) in enumerate(
            ((ow_ref, ow_tile), (up_ref, up_tile), (z_ref, z_tile), (qw_ref, qw_tile),
             (ao_ref, ao_tile), (gain_ref, gain_tile), (ln_ref, norms_ref))
        )
    ]
    for copy in copies:
        copy.start()
    for copy in copies[:3]:
        copy.wait()
    out = lax.dot_general(up_tile[...], ow_tile[...], NT, preferred_element_type=F32)
    go_ref[...] = lanes_of(out.T, heads)
    base = lax.dot_general(z_tile[...], ow_tile[...], NT, preferred_element_type=F32)
    nt_ref[...] = lanes_of((base * inv_ref[:, :1]).T, heads)
    copies[3].wait()
    qf = jnp.dot(hidden_ref[...], qw_tile[...], preferred_element_type=F32)
    qf_ref[...] = qf
    qt_ref[...] = lanes_of(qf.T, heads).astype(BF16)
    for copy in copies[4:]:
        copy.wait()
    scaled_ref[...] = (ow_tile[...].astype(F32) * gain_tile[...]).astype(BF16)
    aot_ref[...] = lanes_of(ao_tile[...].astype(F32).T, heads)


def pull(heads, scale, go, aot, qt, kvw_ref, probs, score_ref, own_ref, term_refs):
    e = go.shape[0]
    rows = go.shape[1] // heads
    row_terms = jnp.sum(go * aot, axis=0, keepdims=True)
    gob = go.astype(BF16)
    grad_prob = jnp.dot(kvw_ref[:, e:], gob, preferred_element_type=F32)
    grad_score = (probs.astype(F32) * (grad_prob - row_terms)).astype(BF16)
    score_ref[...] = grad_score
    grad_key = lax.dot_general(grad_score, qt, NT, preferred_element_type=F32) * scale
    grad_value = lax.dot_general(probs, gob, NT, preferred_element_type=F32)
    terms = jnp.concatenate([grad_key, grad_value], axis=1)
    for offset in range(1, len(term_refs) + 1):
        first = (len(term_refs) - offset) * rows
        term_refs[offset - 1][...] = terms[first : first + rows].astype(BF16)
    own_ref[...] = terms[len(term_refs) * rows :]


def query_body(heads, scale, kt_ref, score_ref, gq_ref):
    rows = gq_ref.shape[0]
    grad_query = jnp.dot(kt_ref[...], score_ref[...], preferred_element_type=F32) * scale
    parts = [grad_query[:, i * rows : (i + 1) * rows] for i in range(heads)]
    gq_ref[...] = jnp.concatenate(parts, axis=0).T.astype(BF16)


def first_body(heads, scale, block_ref, *refs):
    windows = refs[: WIN_DEVS + 1]
    qt_ref, go_ref, aot_ref, ln_ref = refs[WIN_DEVS + 1 : WIN_DEVS + 5]
    kvw_ref, kt_ref, probs_ref, score_ref, own_ref = refs[WIN_DEVS + 5 : WIN_DEVS + 10]
    term_refs = refs[WIN_DEVS + 10 :]
    rows = windows[0].shape[0]
    for place, ref in enumerate(windows):
        kvw_ref[place * rows : (place + 1) * rows, :] = ref[...]
    kvw = kvw_ref[...]
    e = kvw.shape[1] // 2
    kt_ref[...] = kvw.astype(F32).T[:e].astype(BF16)
    scores = jnp.dot(kvw[:, :e], qt_ref[...], preferred_element_type=F32) * scale
    norms = jnp.concatenate([ln_ref[i : i + 1, :] for i in range(heads)], axis=1)
    key_pos = lax.broadcasted_iota(jnp.int32, scores.shape, 0)
    query_pos = lax.broadcasted_iota(jnp.int32, scores.shape, 1) & (rows - 1)
    allowed = (key_pos > query_pos) & (key_pos <= query_pos + WIN_DEVS * rows)
    allowed = allowed & (key_pos >= (WIN_DEVS - block_ref[0]) * rows)
    probs = jnp.where(allowed, jnp.exp(scores - norms), 0.0).astype(BF16)
    probs_ref[...] = probs
    pull(heads, scale, go_ref[...], aot_ref[...], qt_ref[...], kvw_ref, probs,
         score_ref, own_ref, term_refs)


def next_body(heads, parts, scale, fresh, spot_ref, *refs):
    gq_refs, refs = ([], refs) if fresh else (refs[:parts], refs[parts:])
    msg_refs, refs = refs[:parts], refs[parts:]
    inv_ref, nt_ref, qt_ref, aot_ref, kvw_ref, probs_ref, *refs = refs
    if fresh:
        *parts_refs, score_ref, own_ref, lhs_ref, row_ref, chain_ref = refs[:7]
        term_refs = refs[7:]
        assemble(spot_ref[1], chain_ref.shape[2], chain_ref, parts_refs)
    else:
        chain_ref, score_ref, own_ref, lhs_ref, row_ref = refs[:5]
        term_refs = refs[5:]
    rows, wide = lhs_ref.shape[1], chain_ref.shape[2]
    out = jnp.zeros((rows, wide), F32)
    along = jnp.zeros((EXTRA, rows), F32)
    for k in range(parts):
        index = lax.rem(spot_ref[0] + k, parts)
        msg = msg_refs[k][...]
        chain = chain_ref[k]
        lhs = msg[:rows]
        if gq_refs:
            lhs = jnp.concatenate([gq_refs[k][...], lhs], axis=1)
        out += jnp.dot(lhs, chain, preferred_element_type=F32)
        lhs_ref[index] = lhs
        along += msg[rows:, :rows].astype(F32)
    row_ref[...] = along
    along = jnp.sum(along, axis=0, keepdims=True)
    along = jnp.concatenate([along] * heads, axis=1)
    go = lanes_of((out * inv_ref[:, :1]).T, heads)
    inv_row = jnp.concatenate([inv_ref[...].T[:1, :]] * heads, axis=1)
    go = go - inv_row * along * nt_ref[...]
    pull(heads, scale, go, aot_ref[...], qt_ref[...], kvw_ref, probs_ref[...],
         score_ref, own_ref, term_refs)


def collect_body(width, own_ref, gq_ref, qf_ref, kvf_ref, *refs):
    msg_ref = refs[-1]
    rows = own_ref.shape[0]
    total = own_ref[...]
    for ref in refs[:-1]:
        total += ref[...].astype(F32)
    total = total.astype(BF16)
    ahead = msg_ref.shape[1] - total.shape[1]
    if ahead:
        msg_ref[:rows, :ahead] = gq_ref[...]
        msg_ref[rows:, :] = jnp.zeros((EXTRA, msg_ref.shape[1]), BF16)
    msg_ref[:rows, ahead:] = total
    prods = gq_ref[...].astype(F32) * qf_ref[...]
    partial = total.astype(F32) * kvf_ref[...]
    lanes = partial.shape[1]
    for first in range(0, prods.shape[1], lanes):
        partial += prods[:, first : first + lanes]
    along = jnp.sum(partial.T, axis=0, keepdims=True) * (1.0 / width)
    high = along.astype(BF16).astype(F32)
    place = lax.broadcasted_iota(jnp.int32, (EXTRA, rows), 0)
    extra = jnp.where(place == 0, high, jnp.where(place == 1, along - high, 0.0))
    msg_ref[rows:, :rows] = extra.astype(BF16)


def field_body(parts, wide, spot_ref, *refs):
    gq_refs, msg_refs, refs = refs[:parts], refs[parts : 2 * parts], refs[2 * parts :]
    lhs1_ref, row1_ref, lhs2_ref, row2_ref, *refs = refs
    *w_refs, z_ref, up_ref, gain_ref, inv_ref, v_ref, tot_ref, lhs3_ref, w_ref = refs
    rows, part = v_ref.shape[1:]
    head = spot_ref[0]
    row3 = jnp.zeros((EXTRA, rows), F32)
    for k in range(parts):
        msg = msg_refs[k][...]
        lhs3_ref[lax.rem(head + k, parts)] = jnp.concatenate(
            [gq_refs[k][...], msg[:rows]], axis=1
        )
        row3 += msg[rows:].astype(F32)
    assemble(spot_ref[1], wide, w_ref, w_refs)
    y = jnp.zeros((3 * rows, part), F32)
    for k in range(parts):
        lhs = jnp.concatenate([lhs1_ref[k], lhs2_ref[k], lhs3_ref[k]], axis=0)
        weight = w_ref[lax.rem(k - head + parts, parts)]
        y += jnp.dot(lhs, weight, preferred_element_type=F32)
    at = pl.ds(pl.multiple_of(head * part, part), part)
    inverse = inv_ref[:, :1]
    normed = z_ref[:, at].astype(F32) * inverse
    gain = gain_ref[:, at]
    fields = []
    for step, row in enumerate((row1_ref[...], row2_ref[...], row3)):
        along = jnp.broadcast_to(jnp.sum(row, axis=0, keepdims=True), (rows, rows)).T[:, :1]
        y_step = y[step * rows : (step + 1) * rows]
        fields.append(inverse * (y_step * gain - normed * along))
        v_ref[step] = fields[step]
    first, second, third = fields
    change1 = first - up_ref[:, at].astype(F32)
    change2 = second - first
    change3 = third - second
    pairs = [
        (change1, first), (change1, change1), (change2, first), (change2, change2),
        (change2, second), (change2, change3), (change3, second), (change3, change3),
    ]
    lanes = tot_ref.shape[2]
    sums = []
    for a, b in pairs:
        total = jnp.sum(a * b, axis=0, keepdims=True)
        sums.append(sum(total[:, i : i + lanes] for i in range(0, part, lanes)))
    totals = jnp.concatenate(sums, axis=0)
    for k in range(tot_ref.shape[0]):
        tot_ref[k] = totals


def mix_body(entries, spot_ref, tot_ref, up_ref, v_ref, out_ref):
    totals = jnp.sum(jnp.sum(tot_ref[...], axis=0), axis=1, keepdims=True) / entries
    s_r1, s_s, d2_v1, d2_d2, d2_v2, d2_d3, d3_v2, d3_d3 = [totals[i : i + 1] for i in range(8)]
    mix1 = s_r1 / (s_s + mix_eps)
    keep1 = 1.0 - mix1
    mix2 = keep1 * (d2_v1 + keep1 * d2_d2) / (keep1 * keep1 * d2_d2 + mix_eps)
    keep2 = keep1 * (1.0 - mix2)
    cross = mix1 * (d2_v2 + keep2 * d2_d3) + keep2 * (d3_v2 + keep2 * d3_d3)
    square = mix1 * mix1 * d2_d2 + 2.0 * mix1 * keep2 * d2_d3 + keep2 * keep2 * d3_d3
    mix3 = cross / (square + mix_eps)
    part = out_ref.shape[1]
    at = pl.ds(pl.multiple_of(spot_ref[0] * part, part), part)
    mixed = (
        up_ref[:, at].astype(F32)
        + v_ref[0]
        + (1.0 - mix3 * mix1) * v_ref[1]
        + keep2 * (1.0 - mix3) * v_ref[2]
    )
    out_ref[...] = mixed.astype(BF16)


def join_body(spot_ref, *refs):
    *part_refs, out_ref, tile, sems = refs
    parts = len(part_refs)
    part = part_refs[0].shape[1]
    copies = []
    for k in range(parts):
        tile[k] = part_refs[k][...].astype(F32)
        first = pl.multiple_of(lax.rem(spot_ref[0] + k, parts) * part, part)
        copies.append(
            pltpu.make_async_copy(tile.at[k], out_ref.at[:, pl.ds(first, part)], sems.at[k])
        )
        copies[k].start()
    for copy in copies:
        copy.wait()


def shards(
    fixed_point,
    upstream,
    norm_gain,
    query_weight,
    keyval_weight,
    output_weight,
    log_norm,
    attention_out,
):
    rows, width = fixed_point.shape
    wide = query_weight.shape[1]
    narrow = keyval_weight.shape[1]
    size = wide + narrow
    e = narrow // 2
    heads = log_norm.shape[0]
    seq_count = lax.axis_size("seq")
    parts = lax.axis_size("head")
    block = lax.axis_index("seq")
    head = lax.axis_index("head")
    scale = e ** (-0.5)
    gain = norm_gain.reshape(1, width)
    span = (WIN_DEVS + 1) * rows
    group = min(8, seq_count)

    cols = size // group
    spot = jnp.stack([head, lax.rem(block, group)])
    smem = pl.BlockSpec(memory_space=pltpu.SMEM)
    vmem = pl.BlockSpec(memory_space=pltpu.VMEM)
    hbm = pl.BlockSpec(memory_space=pltpu.HBM)

    def pinned(value):
        return pltpu.with_memory_space_constraint(value, pltpu.HBM)

    tile = 128 if wide % 128 == 0 and 128 % (wide // group) == 0 else wide
    own_cols, hidden, kv, kvf, inv = local_call(
        prep_body,
        [
            shape_of((cols, width), BF16),
            shape_of((rows, width), BF16),
            shape_of((rows, narrow), BF16),
            shape_of((rows, narrow), F32),
            shape_of((rows, rows), F32),
        ],
        2 * width * size * cols,
        2 * width * (tile + narrow + rows),
        10,
        in_specs=[smem] + [hbm] * 4,
        scratch_shapes=[
            pltpu.VMEM((width, tile), BF16),
            pltpu.VMEM((width, narrow), BF16),
            pltpu.VMEM((rows, width), BF16),
            pltpu.VMEM((1, width), F32),
            pltpu.SemaphoreType.DMA((4,)),
        ],
    )(
        block.reshape(1),
        pinned(query_weight),
        pinned(keyval_weight),
        pinned(fixed_point),
        pinned(gain),
    )
    every_cols = jnp.stack(rotated(own_cols, "head"))
    earlier = [shifted(kv, "seq", offset) for offset in range(WIN_DEVS, 0, -1)]

    qf, qt, go, nt, aot, scaled, norms = local_call(
        functools.partial(start_body, heads),
        [
            shape_of((rows, wide), F32),
            shape_of((e, heads * rows), BF16),
            shape_of((e, heads * rows), F32),
            shape_of((e, heads * rows), F32),
            shape_of((e, heads * rows), F32),
            shape_of((wide, width), BF16),
            shape_of((heads, rows), F32),
        ],
        6 * rows * width * wide,
        4 * width * (2 * rows + wide),
        14,
        in_specs=[vmem] * 2 + [hbm] * 7,
        scratch_shapes=[
            pltpu.VMEM((width, wide), BF16),
            pltpu.VMEM((wide, width), BF16),
            pltpu.VMEM((rows, width), BF16),
            pltpu.VMEM((rows, width), BF16),
            pltpu.VMEM((rows, wide), BF16),
            pltpu.VMEM((1, width), F32),
            pltpu.SemaphoreType.DMA((7,)),
        ],
    )(
        hidden,
        inv,
        pinned(query_weight),
        pinned(output_weight),
        pinned(upstream),
        pinned(fixed_point),
        pinned(attention_out),
        pinned(gain),
        pinned(log_norm),
    )

    pull_outs = [shape_of((span, heads * rows), BF16), shape_of((rows, narrow), F32)]
    pull_outs += [shape_of((rows, narrow), BF16)] * WIN_DEVS
    pull_flops = 6 * span * e * heads * rows

    def exchange(score, own, terms, split, step):
        if step == 2:
            score, weight[:] = (lambda a, *b: (a, list(b)))(
                *lax.optimization_barrier((score, *weight))
            )
        gq = local_call(
            functools.partial(query_body, heads, scale),
            shape_of((rows, wide), BF16),
            2 * span * e * heads * rows,
            span * heads * rows * 2,
            4,
        )(kt, score)
        arrived = [shifted(term, "seq", -offset - 1) for offset, term in enumerate(terms)]
        ahead = rotated(gq, "head") if split else []
        if step in (2,):
            arrived = list(lax.optimization_barrier((tuple(arrived), tuple(ahead[1:1+3])))[0])
        if not split:
            arrived = list(lax.optimization_barrier((tuple(arrived), near[1]))[0])
        msg = local_call(
            functools.partial(collect_body, width),
            shape_of((rows + EXTRA, narrow if split else size), BF16),
            COLLECT * rows * size,
            rows * size * 4,
            4,
        )(own, gq, qf, kvf, *arrived)
        return rotated(msg, "head"), msg, ahead

    kvw, kt, probs, score, own, *terms = local_call(
        functools.partial(first_body, heads, scale),
        [
            shape_of((span, narrow), BF16),
            shape_of((e, span), BF16),
            shape_of((span, heads * rows), BF16),
        ]
        + pull_outs,
        pull_flops * 5 // 4,
        span * heads * rows * 2,
        16,
        in_specs=[smem] + [vmem] * (WIN_DEVS + 5),
    )(block.reshape(1), *earlier, kv, qt, go, aot, norms)
    packed, marks = [], []
    chain_shape = shape_of((parts, size, wide), BF16)
    for step in range(3):
        if step:
            score, own, lhs, row, *terms = local_call(
                functools.partial(next_body, heads, parts, scale, step == 1),
                pull_outs[:2]
                + [shape_of((parts, rows, size), BF16), shape_of((EXTRA, rows), F32)]
                + [chain_shape] * (step == 1)
                + pull_outs[2:],
                pull_flops + 2 * rows * parts * size * wide,
                span * heads * rows * 2 + parts * size * wide * 2,
                16,
                in_specs=[smem] + [vmem] * (len(ahead) + parts + 6 + len(chain)),
            )(spot, *ahead, *every_msg, inv, nt, qt, aot, kvw, probs, *chain)
            packed += [lhs, row]
            if step == 1:
                chain, *terms = terms
                chain = [chain]
        if step == 0:
            every_cols, _ = lax.optimization_barrier((every_cols, score))
            share = local_call(
                chain_body,
                shape_of((parts * cols, wide), BF16),
                2 * parts * cols * width * wide,
                2 * width * (wide + parts * cols),
                8,
            )(every_cols.reshape(parts * cols, width), scaled)
            share = share.reshape(parts, cols, wide)
            *terms, share = lax.optimization_barrier((*terms, share))
            pairs = [(i, i ^ (group // 2)) for i in range(seq_count)]
            near = [share[None], lax.ppermute(share[None], "seq", pairs)]
        every_msg, msg, ahead = exchange(score, own, terms, step > 0, step)
        if step == 0:
            chain = doubled(near, "seq", group // 2, (msg, every_msg[1:2]))
        marks.append(dict(msg=msg, sent=(ahead[1:], every_msg[1:])))
        if step == 1:
            gates = (marks[0]["msg"], marks[0]["sent"], marks[1]["sent"])
            part = width // parts
            mine = lax.dynamic_slice_in_dim(every_cols, head * part, part, 2)
            weight = doubled([mine[None]], "seq", group, gates)

    small = seq_count * parts <= 64
    fields, totals = local_call(
        functools.partial(field_body, parts, wide),
        [
            shape_of((3, rows, part), F32),
            shape_of((seq_count * parts if small else 1, 8, 128), F32),
        ],
        6 * rows * parts * size * part,
        2 * parts * size * part,
        20,
        in_specs=[smem] + [vmem] * (2 * parts + 8 + len(weight)),
        scratch_shapes=[
            pltpu.VMEM((parts, rows, size), BF16),
            pltpu.VMEM((parts, size, part), BF16),
        ],
    )(spot, *ahead, *every_msg, *packed, *weight, fixed_point, upstream, gain, inv)
    if small:
        totals = lax.all_to_all(totals, ("seq", "head"), 0, 0)
    else:
        totals = lax.psum(totals, ("seq", "head"))
    mixed = local_call(
        functools.partial(mix_body, rows * seq_count * width),
        shape_of((rows, part), BF16),
        8 * rows * part,
        18 * rows * part,
        6,
        in_specs=[smem] + [vmem] * 3,
    )(spot, totals, upstream, fields)
    every_mixed = rotated(mixed, "head")
    return local_call(
        join_body,
        shape_of((rows, width), F32),
        0,
        6 * rows * width,
        6,
        in_specs=[smem] + [vmem] * parts,
        out_specs=hbm,
        scratch_shapes=[
            pltpu.VMEM((parts, rows, part), F32),
            pltpu.SemaphoreType.DMA((parts,)),
        ],
    )(spot, *every_mixed)


def solution(mesh):
    in_specs = (
        P("seq", None),
        P("seq", None),
        P(),
        P(None, "head"),
        P(None, "head"),
        P("head", None),
        P("head", "seq"),
        P("seq", "head"),
    )
    out_specs = P("seq", None)
    return jax.shard_map(shards, mesh=mesh, in_specs=in_specs, out_specs=out_specs, check_vma=False)
```

```python
import functools

import jax
import jax.numpy as jnp
from jax import lax
from jax.experimental import pallas as pl
from jax.experimental.pallas import tpu as pltpu
from jax.sharding import PartitionSpec as P

WIN_DEVS = 4
norm_eps = 1e-05
mix_eps = 1e-06
F32 = jnp.float32
BF16 = jnp.bfloat16
COLLECT = 50000
EXTRA = 16
NT = (((1,), (1,)), ((), ()))


def shape_of(shape, dtype):
    return jax.ShapeDtypeStruct(shape, dtype)


def local_call(body, outs, flops, moved, room, **more):
    return pl.pallas_call(
        body,
        out_shape=outs,
        compiler_params=pltpu.CompilerParams(vmem_limit_bytes=room * 1024 * 1024),
        cost_estimate=pl.CostEstimate(flops=flops, bytes_accessed=moved, transcendentals=0),
        **more,
    )


def shifted(value, axis, steps):
    count = lax.axis_size(axis)
    initial, last = (max(0, -steps), min(count, count - steps))
    return lax.ppermute(value, axis, [(source, source + steps) for source in range(initial, last)])


def rotated(value, axis):
    count = lax.axis_size(axis)
    parts = [value]
    for step in range(1, count):
        parts.append(lax.ppermute(value, axis, [(i, (i - step) % count) for i in range(count)]))
    return parts


def doubled(value, axis, group, gates):
    count = lax.axis_size(axis)
    near, bit = list(value), group // 2
    for gate in gates:
        near = list(lax.optimization_barrier((tuple(near), gate))[0])
        pairs = [(i, i ^ bit) for i in range(count)]
        if len(near) > 1:
            near = [jnp.concatenate(near)]
        if bit == 1:
            return near + [lax.ppermute(near[0], axis, pairs)]
        near.append(lax.ppermute(near[0], axis, pairs))
        bit //= 2


def assemble(place, wide, out_ref, refs):
    group = sum(ref.shape[0] for ref in refs)
    cut = wide // group
    rest_cut = refs[0].shape[2] - cut
    entries = [(ref, j) for ref in refs for j in range(ref.shape[0])]
    for j, (ref, at) in enumerate(entries):
        distance, bit, rest = 0, group // 2, j
        while rest:
            distance += bit * (rest & 1)
            rest >>= 1
            bit //= 2
        index = lax.bitwise_xor(place, jnp.int32(distance))
        first = pl.multiple_of(index * cut, cut)
        second = pl.multiple_of(wide + index * rest_cut, rest_cut)
        for k in range(out_ref.shape[0]):
            out_ref[k, pl.ds(first, cut), :] = ref[at, k, :cut, :]
            out_ref[k, pl.ds(second, rest_cut), :] = ref[at, k, cut:, :]


def prep_body(block_ref, qw_ref, kvw_ref, z_ref, gain_ref, cols_ref, hidden_ref, kv_ref, kvf_ref,
              inv_ref, q_tile, kv_tile, z_tile, gain_tile, sems):
    tile = q_tile.shape[1]
    wide, narrow = qw_ref.shape[1], kvw_ref.shape[1]
    group = (wide + narrow) // cols_ref.shape[0]
    place = lax.rem(block_ref[0], group)
    q_take, kv_take = wide // group, narrow // group
    q_at = place * q_take
    q_first = pl.multiple_of(q_at // tile * tile, tile)
    copies = [
        pltpu.make_async_copy(qw_ref.at[:, pl.ds(q_first, tile)], q_tile, sems.at[0]),
        pltpu.make_async_copy(kvw_ref, kv_tile, sems.at[1]),
        pltpu.make_async_copy(z_ref, z_tile, sems.at[2]),
        pltpu.make_async_copy(gain_ref, gain_tile, sems.at[3]),
    ]
    for copy in copies:
        copy.start()
    first = 0
    for copy, ref, at, take in (
        (copies[0], q_tile, q_at - q_first, q_take),
        (copies[1], kv_tile, place * kv_take, kv_take),
    ):
        copy.wait()
        total = ref.shape[1]
        row = lax.broadcasted_iota(jnp.int32, (take, total), 0) + at
        pick = (row == lax.broadcasted_iota(jnp.int32, (take, total), 1)).astype(BF16)
        cols = lax.dot_general(pick, ref[...], NT, preferred_element_type=F32)
        cols_ref[first : first + take, :] = cols.astype(BF16)
        first += take
    copies[2].wait()
    copies[3].wait()
    z = z_tile[...].astype(F32)
    inverse = lax.rsqrt(jnp.mean(z * z, axis=1, keepdims=True) + norm_eps)
    hidden = (z * inverse * gain_tile[...]).astype(BF16)
    hidden_ref[...] = hidden
    kvf = jnp.dot(hidden, kv_tile[...], preferred_element_type=F32)
    kvf_ref[...] = kvf
    kv_ref[...] = kvf.astype(BF16)
    inv_ref[...] = jnp.broadcast_to(inverse, inv_ref.shape)


def chain_body(cols_ref, scaled_ref, out_ref):
    share = lax.dot_general(cols_ref[...], scaled_ref[...], NT, preferred_element_type=F32)
    out_ref[...] = share.astype(BF16)


def lanes_of(value, heads):
    size = value.shape[0] // heads
    return jnp.concatenate([value[i * size : (i + 1) * size] for i in range(heads)], axis=1)


def start_body(heads, hidden_ref, inv_ref, qw_ref, ow_ref, up_ref, z_ref, ao_ref, gain_ref, ln_ref,
               qf_ref, qt_ref, go_ref, nt_ref, aot_ref, scaled_ref, norms_ref,
               qw_tile, ow_tile, up_tile, z_tile, ao_tile, gain_tile, sems):
    copies = [
        pltpu.make_async_copy(source, target, sems.at[i])
        for i, (source, target) in enumerate(
            ((ow_ref, ow_tile), (up_ref, up_tile), (z_ref, z_tile), (qw_ref, qw_tile),
             (ao_ref, ao_tile), (gain_ref, gain_tile), (ln_ref, norms_ref))
        )
    ]
    for copy in copies:
        copy.start()
    for copy in copies[:3]:
        copy.wait()
    out = lax.dot_general(up_tile[...], ow_tile[...], NT, preferred_element_type=F32)
    go_ref[...] = lanes_of(out.T, heads)
    base = lax.dot_general(z_tile[...], ow_tile[...], NT, preferred_element_type=F32)
    nt_ref[...] = lanes_of((base * inv_ref[:, :1]).T, heads)
    copies[3].wait()
    qf = jnp.dot(hidden_ref[...], qw_tile[...], preferred_element_type=F32)
    qf_ref[...] = qf
    qt_ref[...] = lanes_of(qf.T, heads).astype(BF16)
    for copy in copies[4:]:
        copy.wait()
    scaled_ref[...] = (ow_tile[...].astype(F32) * gain_tile[...]).astype(BF16)
    aot_ref[...] = lanes_of(ao_tile[...].astype(F32).T, heads)


def pull(heads, scale, go, aot, qt, kvw_ref, probs, score_ref, own_ref, term_refs):
    e = go.shape[0]
    rows = go.shape[1] // heads
    row_terms = jnp.sum(go * aot, axis=0, keepdims=True)
    gob = go.astype(BF16)
    grad_prob = jnp.dot(kvw_ref[:, e:], gob, preferred_element_type=F32)
    grad_score = (probs.astype(F32) * (grad_prob - row_terms)).astype(BF16)
    score_ref[...] = grad_score
    grad_key = lax.dot_general(grad_score, qt, NT, preferred_element_type=F32) * scale
    grad_value = lax.dot_general(probs, gob, NT, preferred_element_type=F32)
    terms = jnp.concatenate([grad_key, grad_value], axis=1)
    for offset in range(1, len(term_refs) + 1):
        first = (len(term_refs) - offset) * rows
        term_refs[offset - 1][...] = terms[first : first + rows].astype(BF16)
    own_ref[...] = terms[len(term_refs) * rows :]


def query_body(heads, scale, kt_ref, score_ref, gq_ref):
    rows = gq_ref.shape[0]
    grad_query = jnp.dot(kt_ref[...], score_ref[...], preferred_element_type=F32) * scale
    parts = [grad_query[:, i * rows : (i + 1) * rows] for i in range(heads)]
    gq_ref[...] = jnp.concatenate(parts, axis=0).T.astype(BF16)


def first_body(heads, scale, block_ref, *refs):
    windows = refs[: WIN_DEVS + 1]
    qt_ref, go_ref, aot_ref, ln_ref = refs[WIN_DEVS + 1 : WIN_DEVS + 5]
    kvw_ref, kt_ref, probs_ref, score_ref, own_ref = refs[WIN_DEVS + 5 : WIN_DEVS + 10]
    term_refs = refs[WIN_DEVS + 10 :]
    rows = windows[0].shape[0]
    for place, ref in enumerate(windows):
        kvw_ref[place * rows : (place + 1) * rows, :] = ref[...]
    kvw = kvw_ref[...]
    e = kvw.shape[1] // 2
    kt_ref[...] = kvw.astype(F32).T[:e].astype(BF16)
    scores = jnp.dot(kvw[:, :e], qt_ref[...], preferred_element_type=F32) * scale
    norms = jnp.concatenate([ln_ref[i : i + 1, :] for i in range(heads)], axis=1)
    key_pos = lax.broadcasted_iota(jnp.int32, scores.shape, 0)
    query_pos = lax.broadcasted_iota(jnp.int32, scores.shape, 1) & (rows - 1)
    allowed = (key_pos > query_pos) & (key_pos <= query_pos + WIN_DEVS * rows)
    allowed = allowed & (key_pos >= (WIN_DEVS - block_ref[0]) * rows)
    probs = jnp.where(allowed, jnp.exp(scores - norms), 0.0).astype(BF16)
    probs_ref[...] = probs
    pull(heads, scale, go_ref[...], aot_ref[...], qt_ref[...], kvw_ref, probs,
         score_ref, own_ref, term_refs)


def next_body(heads, parts, scale, fresh, spot_ref, *refs):
    gq_refs, refs = ([], refs) if fresh else (refs[:parts], refs[parts:])
    msg_refs, refs = refs[:parts], refs[parts:]
    inv_ref, nt_ref, qt_ref, aot_ref, kvw_ref, probs_ref, *refs = refs
    if fresh:
        *parts_refs, score_ref, own_ref, lhs_ref, row_ref, chain_ref = refs[:7]
        term_refs = refs[7:]
        assemble(spot_ref[1], chain_ref.shape[2], chain_ref, parts_refs)
    else:
        chain_ref, score_ref, own_ref, lhs_ref, row_ref = refs[:5]
        term_refs = refs[5:]
    rows, wide = lhs_ref.shape[1], chain_ref.shape[2]
    out = jnp.zeros((rows, wide), F32)
    along = jnp.zeros((EXTRA, rows), F32)
    for k in range(parts):
        index = lax.rem(spot_ref[0] + k, parts)
        msg = msg_refs[k][...]
        chain = chain_ref[k]
        lhs = msg[:rows]
        if gq_refs:
            lhs = jnp.concatenate([gq_refs[k][...], lhs], axis=1)
        out += jnp.dot(lhs, chain, preferred_element_type=F32)
        lhs_ref[index] = lhs
        along += msg[rows:, :rows].astype(F32)
    row_ref[...] = along
    along = jnp.sum(along, axis=0, keepdims=True)
    along = jnp.concatenate([along] * heads, axis=1)
    go = lanes_of((out * inv_ref[:, :1]).T, heads)
    inv_row = jnp.concatenate([inv_ref[...].T[:1, :]] * heads, axis=1)
    go = go - inv_row * along * nt_ref[...]
    pull(heads, scale, go, aot_ref[...], qt_ref[...], kvw_ref, probs_ref[...],
         score_ref, own_ref, term_refs)


def collect_body(width, own_ref, gq_ref, qf_ref, kvf_ref, *refs):
    msg_ref = refs[-1]
    rows = own_ref.shape[0]
    total = own_ref[...]
    for ref in refs[:-1]:
        total += ref[...].astype(F32)
    total = total.astype(BF16)
    ahead = msg_ref.shape[1] - total.shape[1]
    if ahead:
        msg_ref[:rows, :ahead] = gq_ref[...]
        msg_ref[rows:, :] = jnp.zeros((EXTRA, msg_ref.shape[1]), BF16)
    msg_ref[:rows, ahead:] = total
    prods = gq_ref[...].astype(F32) * qf_ref[...]
    partial = total.astype(F32) * kvf_ref[...]
    lanes = partial.shape[1]
    for first in range(0, prods.shape[1], lanes):
        partial += prods[:, first : first + lanes]
    along = jnp.sum(partial.T, axis=0, keepdims=True) * (1.0 / width)
    high = along.astype(BF16).astype(F32)
    place = lax.broadcasted_iota(jnp.int32, (EXTRA, rows), 0)
    extra = jnp.where(place == 0, high, jnp.where(place == 1, along - high, 0.0))
    msg_ref[rows:, :rows] = extra.astype(BF16)


def field_body(parts, wide, spot_ref, *refs):
    gq_refs, msg_refs, refs = refs[:parts], refs[parts : 2 * parts], refs[2 * parts :]
    lhs1_ref, row1_ref, lhs2_ref, row2_ref, *refs = refs
    *w_refs, z_ref, up_ref, gain_ref, inv_ref, v_ref, tot_ref, lhs3_ref, w_ref = refs
    rows, part = v_ref.shape[1:]
    head = spot_ref[0]
    row3 = jnp.zeros((EXTRA, rows), F32)
    for k in range(parts):
        msg = msg_refs[k][...]
        lhs3_ref[lax.rem(head + k, parts)] = jnp.concatenate(
            [gq_refs[k][...], msg[:rows]], axis=1
        )
        row3 += msg[rows:].astype(F32)
    assemble(spot_ref[1], wide, w_ref, w_refs)
    y = jnp.zeros((3 * rows, part), F32)
    for k in range(parts):
        lhs = jnp.concatenate([lhs1_ref[k], lhs2_ref[k], lhs3_ref[k]], axis=0)
        weight = w_ref[lax.rem(k - head + parts, parts)]
        y += jnp.dot(lhs, weight, preferred_element_type=F32)
    at = pl.ds(pl.multiple_of(head * part, part), part)
    inverse = inv_ref[:, :1]
    normed = z_ref[:, at].astype(F32) * inverse
    gain = gain_ref[:, at]
    fields = []
    for step, row in enumerate((row1_ref[...], row2_ref[...], row3)):
        along = jnp.broadcast_to(jnp.sum(row, axis=0, keepdims=True), (rows, rows)).T[:, :1]
        y_step = y[step * rows : (step + 1) * rows]
        fields.append(inverse * (y_step * gain - normed * along))
        v_ref[step] = fields[step]
    first, second, third = fields
    change1 = first - up_ref[:, at].astype(F32)
    change2 = second - first
    change3 = third - second
    pairs = [
        (change1, first), (change1, change1), (change2, first), (change2, change2),
        (change2, second), (change2, change3), (change3, second), (change3, change3),
    ]
    lanes = tot_ref.shape[2]
    sums = []
    for a, b in pairs:
        total = jnp.sum(a * b, axis=0, keepdims=True)
        sums.append(sum(total[:, i : i + lanes] for i in range(0, part, lanes)))
    totals = jnp.concatenate(sums, axis=0)
    for k in range(tot_ref.shape[0]):
        tot_ref[k] = totals


def mix_body(entries, spot_ref, tot_ref, up_ref, v_ref, out_ref):
    totals = jnp.sum(jnp.sum(tot_ref[...], axis=0), axis=1, keepdims=True) / entries
    s_r1, s_s, d2_v1, d2_d2, d2_v2, d2_d3, d3_v2, d3_d3 = [totals[i : i + 1] for i in range(8)]
    mix1 = s_r1 / (s_s + mix_eps)
    keep1 = 1.0 - mix1
    mix2 = keep1 * (d2_v1 + keep1 * d2_d2) / (keep1 * keep1 * d2_d2 + mix_eps)
    keep2 = keep1 * (1.0 - mix2)
    cross = mix1 * (d2_v2 + keep2 * d2_d3) + keep2 * (d3_v2 + keep2 * d3_d3)
    square = mix1 * mix1 * d2_d2 + 2.0 * mix1 * keep2 * d2_d3 + keep2 * keep2 * d3_d3
    mix3 = cross / (square + mix_eps)
    part = out_ref.shape[1]
    at = pl.ds(pl.multiple_of(spot_ref[0] * part, part), part)
    mixed = (
        up_ref[:, at].astype(F32)
        + v_ref[0]
        + (1.0 - mix3 * mix1) * v_ref[1]
        + keep2 * (1.0 - mix3) * v_ref[2]
    )
    out_ref[...] = mixed.astype(BF16)


def join_body(spot_ref, *refs):
    *part_refs, out_ref, tile, sems = refs
    parts = len(part_refs)
    part = part_refs[0].shape[1]
    copies = []
    for k in range(parts):
        tile[k] = part_refs[k][...].astype(F32)
        first = pl.multiple_of(lax.rem(spot_ref[0] + k, parts) * part, part)
        copies.append(
            pltpu.make_async_copy(tile.at[k], out_ref.at[:, pl.ds(first, part)], sems.at[k])
        )
        copies[k].start()
    for copy in copies:
        copy.wait()


def shards(
    fixed_point,
    upstream,
    norm_gain,
    query_weight,
    keyval_weight,
    output_weight,
    log_norm,
    attention_out,
):
    rows, width = fixed_point.shape
    wide = query_weight.shape[1]
    narrow = keyval_weight.shape[1]
    size = wide + narrow
    e = narrow // 2
    heads = log_norm.shape[0]
    seq_count = lax.axis_size("seq")
    parts = lax.axis_size("head")
    block = lax.axis_index("seq")
    head = lax.axis_index("head")
    scale = e ** (-0.5)
    gain = norm_gain.reshape(1, width)
    span = (WIN_DEVS + 1) * rows
    group = min(8, seq_count)

    cols = size // group
    spot = jnp.stack([head, lax.rem(block, group)])
    smem = pl.BlockSpec(memory_space=pltpu.SMEM)
    vmem = pl.BlockSpec(memory_space=pltpu.VMEM)
    hbm = pl.BlockSpec(memory_space=pltpu.HBM)

    def pinned(value):
        return pltpu.with_memory_space_constraint(value, pltpu.HBM)

    tile = 128 if wide % 128 == 0 and 128 % (wide // group) == 0 else wide
    own_cols, hidden, kv, kvf, inv = local_call(
        prep_body,
        [
            shape_of((cols, width), BF16),
            shape_of((rows, width), BF16),
            shape_of((rows, narrow), BF16),
            shape_of((rows, narrow), F32),
            shape_of((rows, rows), F32),
        ],
        2 * width * size * cols,
        2 * width * (tile + narrow + rows),
        10,
        in_specs=[smem] + [hbm] * 4,
        scratch_shapes=[
            pltpu.VMEM((width, tile), BF16),
            pltpu.VMEM((width, narrow), BF16),
            pltpu.VMEM((rows, width), BF16),
            pltpu.VMEM((1, width), F32),
            pltpu.SemaphoreType.DMA((4,)),
        ],
    )(
        block.reshape(1),
        pinned(query_weight),
        pinned(keyval_weight),
        pinned(fixed_point),
        pinned(gain),
    )
    every_cols = jnp.stack(rotated(own_cols, "head"))
    earlier = [shifted(kv, "seq", offset) for offset in range(WIN_DEVS, 0, -1)]

    qf, qt, go, nt, aot, scaled, norms = local_call(
        functools.partial(start_body, heads),
        [
            shape_of((rows, wide), F32),
            shape_of((e, heads * rows), BF16),
            shape_of((e, heads * rows), F32),
            shape_of((e, heads * rows), F32),
            shape_of((e, heads * rows), F32),
            shape_of((wide, width), BF16),
            shape_of((heads, rows), F32),
        ],
        6 * rows * width * wide,
        4 * width * (2 * rows + wide),
        14,
        in_specs=[vmem] * 2 + [hbm] * 7,
        scratch_shapes=[
            pltpu.VMEM((width, wide), BF16),
            pltpu.VMEM((wide, width), BF16),
            pltpu.VMEM((rows, width), BF16),
            pltpu.VMEM((rows, width), BF16),
            pltpu.VMEM((rows, wide), BF16),
            pltpu.VMEM((1, width), F32),
            pltpu.SemaphoreType.DMA((7,)),
        ],
    )(
        hidden,
        inv,
        pinned(query_weight),
        pinned(output_weight),
        pinned(upstream),
        pinned(fixed_point),
        pinned(attention_out),
        pinned(gain),
        pinned(log_norm),
    )

    pull_outs = [shape_of((span, heads * rows), BF16), shape_of((rows, narrow), F32)]
    pull_outs += [shape_of((rows, narrow), BF16)] * WIN_DEVS
    pull_flops = 6 * span * e * heads * rows

    def exchange(score, own, terms, split, step):
        if step:
            score, weight[:] = (lambda a, *b: (a, list(b)))(
                *lax.optimization_barrier((score, *weight))
            )
        gq = local_call(
            functools.partial(query_body, heads, scale),
            shape_of((rows, wide), BF16),
            2 * span * e * heads * rows,
            span * heads * rows * 2,
            4,
        )(kt, score)
        arrived = [shifted(term, "seq", -offset - 1) for offset, term in enumerate(terms)]
        ahead = rotated(gq, "head") if split else []
        if step in (1, 2):
            arrived = list(lax.optimization_barrier((tuple(arrived), tuple(ahead[1:1+3])))[0])
        if not split:
            arrived = list(lax.optimization_barrier((tuple(arrived), near[1]))[0])
        msg = local_call(
            functools.partial(collect_body, width),
            shape_of((rows + EXTRA, narrow if split else size), BF16),
            COLLECT * rows * size,
            rows * size * 4,
            4,
        )(own, gq, qf, kvf, *arrived)
        return rotated(msg, "head"), msg, ahead

    kvw, kt, probs, score, own, *terms = local_call(
        functools.partial(first_body, heads, scale),
        [
            shape_of((span, narrow), BF16),
            shape_of((e, span), BF16),
            shape_of((span, heads * rows), BF16),
        ]
        + pull_outs,
        pull_flops * 5 // 4,
        span * heads * rows * 2,
        16,
        in_specs=[smem] + [vmem] * (WIN_DEVS + 5),
    )(block.reshape(1), *earlier, kv, qt, go, aot, norms)
    packed, marks = [], []
    chain_shape = shape_of((parts, size, wide), BF16)
    for step in range(3):
        if step:
            score, own, lhs, row, *terms = local_call(
                functools.partial(next_body, heads, parts, scale, step == 1),
                pull_outs[:2]
                + [shape_of((parts, rows, size), BF16), shape_of((EXTRA, rows), F32)]
                + [chain_shape] * (step == 1)
                + pull_outs[2:],
                pull_flops + 2 * rows * parts * size * wide,
                span * heads * rows * 2 + parts * size * wide * 2,
                16,
                in_specs=[smem] + [vmem] * (len(ahead) + parts + 6 + len(chain)),
            )(spot, *ahead, *every_msg, inv, nt, qt, aot, kvw, probs, *chain)
            packed += [lhs, row]
            if step == 1:
                chain, *terms = terms
                chain = [chain]
        if step == 0:
            every_cols, _ = lax.optimization_barrier((every_cols, score))
            share = local_call(
                chain_body,
                shape_of((parts * cols, wide), BF16),
                2 * parts * cols * width * wide,
                2 * width * (wide + parts * cols),
                8,
            )(every_cols.reshape(parts * cols, width), scaled)
            share = share.reshape(parts, cols, wide)
            *terms, share = lax.optimization_barrier((*terms, share))
            pairs = [(i, i ^ (group // 2)) for i in range(seq_count)]
            near = [share[None], lax.ppermute(share[None], "seq", pairs)]
        every_msg, msg, ahead = exchange(score, own, terms, step > 0, step)
        if step == 0:
            part = width // parts
            mine = lax.dynamic_slice_in_dim(every_cols, head * part, part, 2)
            mine, _ = lax.optimization_barrier((mine[None], msg))
            weight = [mine, lax.ppermute(mine, "seq", pairs)]
            chain = doubled(near, "seq", group // 2, (msg, (every_msg[1:], weight[1])))
        marks.append(dict(msg=msg, sent=(ahead[1:], every_msg[1:])))
        if step == 1:
            weight = doubled(weight, "seq", group // 2, (msg, (ahead[1:], every_msg[1:])))

    small = seq_count * parts <= 64
    fields, totals = local_call(
        functools.partial(field_body, parts, wide),
        [
            shape_of((3, rows, part), F32),
            shape_of((seq_count * parts if small else 1, 8, 128), F32),
        ],
        6 * rows * parts * size * part,
        2 * parts * size * part,
        20,
        in_specs=[smem] + [vmem] * (2 * parts + 8 + len(weight)),
        scratch_shapes=[
            pltpu.VMEM((parts, rows, size), BF16),
            pltpu.VMEM((parts, size, part), BF16),
        ],
    )(spot, *ahead, *every_msg, *packed, *weight, fixed_point, upstream, gain, inv)
    if small:
        totals = lax.all_to_all(totals, ("seq", "head"), 0, 0)
    else:
        totals = lax.psum(totals, ("seq", "head"))
    mixed = local_call(
        functools.partial(mix_body, rows * seq_count * width),
        shape_of((rows, part), BF16),
        8 * rows * part,
        18 * rows * part,
        6,
        in_specs=[smem] + [vmem] * 3,
    )(spot, totals, upstream, fields)
    every_mixed = rotated(mixed, "head")
    return local_call(
        join_body,
        shape_of((rows, width), F32),
        0,
        6 * rows * width,
        6,
        in_specs=[smem] + [vmem] * parts,
        out_specs=hbm,
        scratch_shapes=[
            pltpu.VMEM((parts, rows, part), F32),
            pltpu.SemaphoreType.DMA((parts,)),
        ],
    )(spot, *every_mixed)


def solution(mesh):
    in_specs = (
        P("seq", None),
        P("seq", None),
        P(),
        P(None, "head"),
        P(None, "head"),
        P("head", None),
        P("head", "seq"),
        P("seq", "head"),
    )
    out_specs = P("seq", None)
    return jax.shard_map(shards, mesh=mesh, in_specs=in_specs, out_specs=out_specs, check_vma=False)
```

```python
import functools

import jax
import jax.numpy as jnp
from jax import lax
from jax.experimental import pallas as pl
from jax.experimental.pallas import tpu as pltpu
from jax.sharding import PartitionSpec as P

WIN_DEVS = 4
norm_eps = 1e-05
mix_eps = 1e-06
F32 = jnp.float32
BF16 = jnp.bfloat16
COLLECT = 50000
EXTRA = 16
NT = (((1,), (1,)), ((), ()))


def shape_of(shape, dtype):
    return jax.ShapeDtypeStruct(shape, dtype)


def local_call(body, outs, flops, moved, room, **more):
    return pl.pallas_call(
        body,
        out_shape=outs,
        compiler_params=pltpu.CompilerParams(vmem_limit_bytes=room * 1024 * 1024),
        cost_estimate=pl.CostEstimate(flops=flops, bytes_accessed=moved, transcendentals=0),
        **more,
    )


def shifted(value, axis, steps):
    count = lax.axis_size(axis)
    initial, last = (max(0, -steps), min(count, count - steps))
    return lax.ppermute(value, axis, [(source, source + steps) for source in range(initial, last)])


def rotated(value, axis):
    count = lax.axis_size(axis)
    parts = [value]
    for step in range(1, count):
        parts.append(lax.ppermute(value, axis, [(i, (i - step) % count) for i in range(count)]))
    return parts


def doubled(value, axis, group, gates):
    count = lax.axis_size(axis)
    near, bit = list(value), group // 2
    for gate in gates:
        near = list(lax.optimization_barrier((tuple(near), gate))[0])
        pairs = [(i, i ^ bit) for i in range(count)]
        if len(near) > 1:
            near = [jnp.concatenate(near)]
        if bit == 1:
            return near + [lax.ppermute(near[0], axis, pairs)]
        near.append(lax.ppermute(near[0], axis, pairs))
        bit //= 2


def assemble(place, wide, out_ref, refs):
    group = sum(ref.shape[0] for ref in refs)
    cut = wide // group
    rest_cut = refs[0].shape[2] - cut
    entries = [(ref, j) for ref in refs for j in range(ref.shape[0])]
    for j, (ref, at) in enumerate(entries):
        distance, bit, rest = 0, group // 2, j
        while rest:
            distance += bit * (rest & 1)
            rest >>= 1
            bit //= 2
        index = lax.bitwise_xor(place, jnp.int32(distance))
        first = pl.multiple_of(index * cut, cut)
        second = pl.multiple_of(wide + index * rest_cut, rest_cut)
        for k in range(out_ref.shape[0]):
            out_ref[k, pl.ds(first, cut), :] = ref[at, k, :cut, :]
            out_ref[k, pl.ds(second, rest_cut), :] = ref[at, k, cut:, :]


def prep_body(block_ref, qw_ref, kvw_ref, z_ref, gain_ref, cols_ref, hidden_ref, kv_ref, kvf_ref,
              inv_ref, q_tile, kv_tile, z_tile, gain_tile, sems):
    tile = q_tile.shape[1]
    wide, narrow = qw_ref.shape[1], kvw_ref.shape[1]
    group = (wide + narrow) // cols_ref.shape[0]
    place = lax.rem(block_ref[0], group)
    q_take, kv_take = wide // group, narrow // group
    q_at = place * q_take
    q_first = pl.multiple_of(q_at // tile * tile, tile)
    copies = [
        pltpu.make_async_copy(qw_ref.at[:, pl.ds(q_first, tile)], q_tile, sems.at[0]),
        pltpu.make_async_copy(kvw_ref, kv_tile, sems.at[1]),
        pltpu.make_async_copy(z_ref, z_tile, sems.at[2]),
        pltpu.make_async_copy(gain_ref, gain_tile, sems.at[3]),
    ]
    for copy in copies:
        copy.start()
    first = 0
    for copy, ref, at, take in (
        (copies[0], q_tile, q_at - q_first, q_take),
        (copies[1], kv_tile, place * kv_take, kv_take),
    ):
        copy.wait()
        total = ref.shape[1]
        row = lax.broadcasted_iota(jnp.int32, (take, total), 0) + at
        pick = (row == lax.broadcasted_iota(jnp.int32, (take, total), 1)).astype(BF16)
        cols = lax.dot_general(pick, ref[...], NT, preferred_element_type=F32)
        cols_ref[first : first + take, :] = cols.astype(BF16)
        first += take
    copies[2].wait()
    copies[3].wait()
    z = z_tile[...].astype(F32)
    inverse = lax.rsqrt(jnp.mean(z * z, axis=1, keepdims=True) + norm_eps)
    hidden = (z * inverse * gain_tile[...]).astype(BF16)
    hidden_ref[...] = hidden
    kvf = jnp.dot(hidden, kv_tile[...], preferred_element_type=F32)
    kvf_ref[...] = kvf
    kv_ref[...] = kvf.astype(BF16)
    inv_ref[...] = jnp.broadcast_to(inverse, inv_ref.shape)


def chain_body(cols_ref, scaled_ref, out_ref):
    share = lax.dot_general(cols_ref[...], scaled_ref[...], NT, preferred_element_type=F32)
    out_ref[...] = share.astype(BF16)


def lanes_of(value, heads):
    size = value.shape[0] // heads
    return jnp.concatenate([value[i * size : (i + 1) * size] for i in range(heads)], axis=1)


def start_body(heads, hidden_ref, inv_ref, qw_ref, ow_ref, up_ref, z_ref, ao_ref, gain_ref, ln_ref,
               qf_ref, qt_ref, go_ref, nt_ref, aot_ref, scaled_ref, norms_ref,
               ow_tile, up_tile, z_tile, ao_tile, gain_tile, sems):
    copies = [
        pltpu.make_async_copy(source, target, sems.at[i])
        for i, (source, target) in enumerate(
            ((ow_ref, ow_tile), (up_ref, up_tile), (z_ref, z_tile), (ao_ref, ao_tile),
             (gain_ref, gain_tile), (ln_ref, norms_ref))
        )
    ]
    for copy in copies:
        copy.start()
    qf = jnp.dot(hidden_ref[...], qw_ref[...], preferred_element_type=F32)
    qf_ref[...] = qf
    qt_ref[...] = lanes_of(qf.T, heads).astype(BF16)
    for copy in copies:
        copy.wait()
    weight = ow_tile[...]
    out = lax.dot_general(up_tile[...], weight, NT, preferred_element_type=F32)
    go_ref[...] = lanes_of(out.T, heads)
    base = lax.dot_general(z_tile[...], weight, NT, preferred_element_type=F32)
    nt_ref[...] = lanes_of((base * inv_ref[:, :1]).T, heads)
    scaled_ref[...] = (weight.astype(F32) * gain_tile[...]).astype(BF16)
    aot_ref[...] = lanes_of(ao_tile[...].astype(F32).T, heads)


def pull(heads, scale, go, aot, qt, kvw_ref, probs, score_ref, own_ref, term_refs):
    e = go.shape[0]
    rows = go.shape[1] // heads
    row_terms = jnp.sum(go * aot, axis=0, keepdims=True)
    gob = go.astype(BF16)
    grad_prob = jnp.dot(kvw_ref[:, e:], gob, preferred_element_type=F32)
    grad_score = (probs.astype(F32) * (grad_prob - row_terms)).astype(BF16)
    score_ref[...] = grad_score
    grad_key = lax.dot_general(grad_score, qt, NT, preferred_element_type=F32) * scale
    grad_value = lax.dot_general(probs, gob, NT, preferred_element_type=F32)
    terms = jnp.concatenate([grad_key, grad_value], axis=1)
    for offset in range(1, len(term_refs) + 1):
        first = (len(term_refs) - offset) * rows
        term_refs[offset - 1][...] = terms[first : first + rows].astype(BF16)
    own_ref[...] = terms[len(term_refs) * rows :]


def query_body(heads, scale, kt_ref, score_ref, gq_ref):
    rows = gq_ref.shape[0]
    grad_query = jnp.dot(kt_ref[...], score_ref[...], preferred_element_type=F32) * scale
    parts = [grad_query[:, i * rows : (i + 1) * rows] for i in range(heads)]
    gq_ref[...] = jnp.concatenate(parts, axis=0).T.astype(BF16)


def first_body(heads, scale, block_ref, *refs):
    windows = refs[: WIN_DEVS + 1]
    qt_ref, go_ref, aot_ref, ln_ref = refs[WIN_DEVS + 1 : WIN_DEVS + 5]
    kvw_ref, kt_ref, probs_ref, score_ref, own_ref = refs[WIN_DEVS + 5 : WIN_DEVS + 10]
    term_refs = refs[WIN_DEVS + 10 :]
    rows = windows[0].shape[0]
    for place, ref in enumerate(windows):
        kvw_ref[place * rows : (place + 1) * rows, :] = ref[...]
    kvw = kvw_ref[...]
    e = kvw.shape[1] // 2
    kt_ref[...] = kvw.astype(F32).T[:e].astype(BF16)
    scores = jnp.dot(kvw[:, :e], qt_ref[...], preferred_element_type=F32) * scale
    norms = jnp.concatenate([ln_ref[i : i + 1, :] for i in range(heads)], axis=1)
    key_pos = lax.broadcasted_iota(jnp.int32, scores.shape, 0)
    query_pos = lax.broadcasted_iota(jnp.int32, scores.shape, 1) & (rows - 1)
    allowed = (key_pos > query_pos) & (key_pos <= query_pos + WIN_DEVS * rows)
    allowed = allowed & (key_pos >= (WIN_DEVS - block_ref[0]) * rows)
    probs = jnp.where(allowed, jnp.exp(scores - norms), 0.0).astype(BF16)
    probs_ref[...] = probs
    pull(heads, scale, go_ref[...], aot_ref[...], qt_ref[...], kvw_ref, probs,
         score_ref, own_ref, term_refs)


def next_body(heads, parts, scale, fresh, spot_ref, *refs):
    gq_refs, refs = ([], refs) if fresh else (refs[:parts], refs[parts:])
    msg_refs, refs = refs[:parts], refs[parts:]
    inv_ref, nt_ref, qt_ref, aot_ref, kvw_ref, probs_ref, *refs = refs
    if fresh:
        *parts_refs, score_ref, own_ref, lhs_ref, row_ref, chain_ref = refs[:7]
        term_refs = refs[7:]
        assemble(spot_ref[1], chain_ref.shape[2], chain_ref, parts_refs)
    else:
        chain_ref, score_ref, own_ref, lhs_ref, row_ref = refs[:5]
        term_refs = refs[5:]
    rows, wide = lhs_ref.shape[1], chain_ref.shape[2]
    out = jnp.zeros((rows, wide), F32)
    along = jnp.zeros((EXTRA, rows), F32)
    for k in range(parts):
        index = lax.rem(spot_ref[0] + k, parts)
        msg = msg_refs[k][...]
        chain = chain_ref[k]
        lhs = msg[:rows]
        if gq_refs:
            lhs = jnp.concatenate([gq_refs[k][...], lhs], axis=1)
        out += jnp.dot(lhs, chain, preferred_element_type=F32)
        lhs_ref[index] = lhs
        along += msg[rows:, :rows].astype(F32)
    row_ref[...] = along
    along = jnp.sum(along, axis=0, keepdims=True)
    along = jnp.concatenate([along] * heads, axis=1)
    go = lanes_of((out * inv_ref[:, :1]).T, heads)
    inv_row = jnp.concatenate([inv_ref[...].T[:1, :]] * heads, axis=1)
    go = go - inv_row * along * nt_ref[...]
    pull(heads, scale, go, aot_ref[...], qt_ref[...], kvw_ref, probs_ref[...],
         score_ref, own_ref, term_refs)


def collect_body(width, own_ref, gq_ref, qf_ref, kvf_ref, *refs):
    msg_ref = refs[-1]
    rows = own_ref.shape[0]
    total = own_ref[...]
    for ref in refs[:-1]:
        total += ref[...].astype(F32)
    total = total.astype(BF16)
    ahead = msg_ref.shape[1] - total.shape[1]
    if ahead:
        msg_ref[:rows, :ahead] = gq_ref[...]
        msg_ref[rows:, :] = jnp.zeros((EXTRA, msg_ref.shape[1]), BF16)
    msg_ref[:rows, ahead:] = total
    prods = gq_ref[...].astype(F32) * qf_ref[...]
    partial = total.astype(F32) * kvf_ref[...]
    lanes = partial.shape[1]
    for first in range(0, prods.shape[1], lanes):
        partial += prods[:, first : first + lanes]
    along = jnp.sum(partial.T, axis=0, keepdims=True) * (1.0 / width)
    high = along.astype(BF16).astype(F32)
    place = lax.broadcasted_iota(jnp.int32, (EXTRA, rows), 0)
    extra = jnp.where(place == 0, high, jnp.where(place == 1, along - high, 0.0))
    msg_ref[rows:, :rows] = extra.astype(BF16)


def field_body(parts, wide, spot_ref, *refs):
    gq_refs, msg_refs, refs = refs[:parts], refs[parts : 2 * parts], refs[2 * parts :]
    lhs1_ref, row1_ref, lhs2_ref, row2_ref, *refs = refs
    *w_refs, z_ref, up_ref, gain_ref, inv_ref, v_ref, tot_ref, lhs3_ref, w_ref = refs
    rows, part = v_ref.shape[1:]
    head = spot_ref[0]
    row3 = jnp.zeros((EXTRA, rows), F32)
    for k in range(parts):
        msg = msg_refs[k][...]
        lhs3_ref[lax.rem(head + k, parts)] = jnp.concatenate(
            [gq_refs[k][...], msg[:rows]], axis=1
        )
        row3 += msg[rows:].astype(F32)
    assemble(spot_ref[1], wide, w_ref, w_refs)
    y = jnp.zeros((3 * rows, part), F32)
    for k in range(parts):
        lhs = jnp.concatenate([lhs1_ref[k], lhs2_ref[k], lhs3_ref[k]], axis=0)
        weight = w_ref[lax.rem(k - head + parts, parts)]
        y += jnp.dot(lhs, weight, preferred_element_type=F32)
    at = pl.ds(pl.multiple_of(head * part, part), part)
    inverse = inv_ref[:, :1]
    normed = z_ref[:, at].astype(F32) * inverse
    gain = gain_ref[:, at]
    fields = []
    for step, row in enumerate((row1_ref[...], row2_ref[...], row3)):
        along = jnp.broadcast_to(jnp.sum(row, axis=0, keepdims=True), (rows, rows)).T[:, :1]
        y_step = y[step * rows : (step + 1) * rows]
        fields.append(inverse * (y_step * gain - normed * along))
        v_ref[step] = fields[step]
    first, second, third = fields
    change1 = first - up_ref[:, at].astype(F32)
    change2 = second - first
    change3 = third - second
    pairs = [
        (change1, first), (change1, change1), (change2, first), (change2, change2),
        (change2, second), (change2, change3), (change3, second), (change3, change3),
    ]
    lanes = tot_ref.shape[2]
    sums = []
    for a, b in pairs:
        total = jnp.sum(a * b, axis=0, keepdims=True)
        sums.append(sum(total[:, i : i + lanes] for i in range(0, part, lanes)))
    totals = jnp.concatenate(sums, axis=0)
    for k in range(tot_ref.shape[0]):
        tot_ref[k] = totals


def mix_body(entries, spot_ref, tot_ref, up_ref, v_ref, out_ref):
    totals = jnp.sum(jnp.sum(tot_ref[...], axis=0), axis=1, keepdims=True) / entries
    s_r1, s_s, d2_v1, d2_d2, d2_v2, d2_d3, d3_v2, d3_d3 = [totals[i : i + 1] for i in range(8)]
    mix1 = s_r1 / (s_s + mix_eps)
    keep1 = 1.0 - mix1
    mix2 = keep1 * (d2_v1 + keep1 * d2_d2) / (keep1 * keep1 * d2_d2 + mix_eps)
    keep2 = keep1 * (1.0 - mix2)
    cross = mix1 * (d2_v2 + keep2 * d2_d3) + keep2 * (d3_v2 + keep2 * d3_d3)
    square = mix1 * mix1 * d2_d2 + 2.0 * mix1 * keep2 * d2_d3 + keep2 * keep2 * d3_d3
    mix3 = cross / (square + mix_eps)
    part = out_ref.shape[1]
    at = pl.ds(pl.multiple_of(spot_ref[0] * part, part), part)
    mixed = (
        up_ref[:, at].astype(F32)
        + v_ref[0]
        + (1.0 - mix3 * mix1) * v_ref[1]
        + keep2 * (1.0 - mix3) * v_ref[2]
    )
    out_ref[...] = mixed.astype(BF16)


def join_body(spot_ref, *refs):
    *part_refs, out_ref, tile, sems = refs
    parts = len(part_refs)
    part = part_refs[0].shape[1]
    copies = []
    for k in range(parts):
        tile[k] = part_refs[k][...].astype(F32)
        first = pl.multiple_of(lax.rem(spot_ref[0] + k, parts) * part, part)
        copies.append(
            pltpu.make_async_copy(tile.at[k], out_ref.at[:, pl.ds(first, part)], sems.at[k])
        )
        copies[k].start()
    for copy in copies:
        copy.wait()


def shards(
    fixed_point,
    upstream,
    norm_gain,
    query_weight,
    keyval_weight,
    output_weight,
    log_norm,
    attention_out,
):
    rows, width = fixed_point.shape
    wide = query_weight.shape[1]
    narrow = keyval_weight.shape[1]
    size = wide + narrow
    e = narrow // 2
    heads = log_norm.shape[0]
    seq_count = lax.axis_size("seq")
    parts = lax.axis_size("head")
    block = lax.axis_index("seq")
    head = lax.axis_index("head")
    scale = e ** (-0.5)
    gain = norm_gain.reshape(1, width)
    span = (WIN_DEVS + 1) * rows
    group = min(8, seq_count)

    cols = size // group
    spot = jnp.stack([head, lax.rem(block, group)])
    smem = pl.BlockSpec(memory_space=pltpu.SMEM)
    vmem = pl.BlockSpec(memory_space=pltpu.VMEM)
    hbm = pl.BlockSpec(memory_space=pltpu.HBM)

    def pinned(value):
        return pltpu.with_memory_space_constraint(value, pltpu.HBM)

    tile = 128 if wide % 128 == 0 and 128 % (wide // group) == 0 else wide
    own_cols, hidden, kv, kvf, inv = local_call(
        prep_body,
        [
            shape_of((cols, width), BF16),
            shape_of((rows, width), BF16),
            shape_of((rows, narrow), BF16),
            shape_of((rows, narrow), F32),
            shape_of((rows, rows), F32),
        ],
        2 * width * size * cols,
        2 * width * (tile + narrow + rows),
        10,
        in_specs=[smem] + [hbm] * 4,
        scratch_shapes=[
            pltpu.VMEM((width, tile), BF16),
            pltpu.VMEM((width, narrow), BF16),
            pltpu.VMEM((rows, width), BF16),
            pltpu.VMEM((1, width), F32),
            pltpu.SemaphoreType.DMA((4,)),
        ],
    )(
        block.reshape(1),
        pinned(query_weight),
        pinned(keyval_weight),
        pinned(fixed_point),
        pinned(gain),
    )
    every_cols = jnp.stack(rotated(own_cols, "head"))
    earlier = [shifted(kv, "seq", offset) for offset in range(WIN_DEVS, 0, -1)]

    qf, qt, go, nt, aot, scaled, norms = local_call(
        functools.partial(start_body, heads),
        [
            shape_of((rows, wide), F32),
            shape_of((e, heads * rows), BF16),
            shape_of((e, heads * rows), F32),
            shape_of((e, heads * rows), F32),
            shape_of((e, heads * rows), F32),
            shape_of((wide, width), BF16),
            shape_of((heads, rows), F32),
        ],
        6 * rows * width * wide,
        4 * width * (2 * rows + wide),
        14,
        in_specs=[vmem] * 3 + [hbm] * 6,
        scratch_shapes=[
            pltpu.VMEM((wide, width), BF16),
            pltpu.VMEM((rows, width), BF16),
            pltpu.VMEM((rows, width), BF16),
            pltpu.VMEM((rows, wide), BF16),
            pltpu.VMEM((1, width), F32),
            pltpu.SemaphoreType.DMA((6,)),
        ],
    )(
        hidden,
        inv,
        query_weight,
        pinned(output_weight),
        pinned(upstream),
        pinned(fixed_point),
        pinned(attention_out),
        pinned(gain),
        pinned(log_norm),
    )

    pull_outs = [shape_of((span, heads * rows), BF16), shape_of((rows, narrow), F32)]
    pull_outs += [shape_of((rows, narrow), BF16)] * WIN_DEVS
    pull_flops = 6 * span * e * heads * rows

    def exchange(score, own, terms, split, step):
        if step == 2:
            score, weight[:] = (lambda a, *b: (a, list(b)))(
                *lax.optimization_barrier((score, *weight))
            )
        gq = local_call(
            functools.partial(query_body, heads, scale),
            shape_of((rows, wide), BF16),
            2 * span * e * heads * rows,
            span * heads * rows * 2,
            4,
        )(kt, score)
        arrived = [shifted(term, "seq", -offset - 1) for offset, term in enumerate(terms)]
        ahead = rotated(gq, "head") if split else []
        if step in (2,):
            arrived = list(lax.optimization_barrier((tuple(arrived), tuple(ahead[1:1+3])))[0])
        if not split:
            arrived = list(lax.optimization_barrier((tuple(arrived), near[1]))[0])
        msg = local_call(
            functools.partial(collect_body, width),
            shape_of((rows + EXTRA, narrow if split else size), BF16),
            COLLECT * rows * size,
            rows * size * 4,
            4,
        )(own, gq, qf, kvf, *arrived)
        return rotated(msg, "head"), msg, ahead

    kvw, kt, probs, score, own, *terms = local_call(
        functools.partial(first_body, heads, scale),
        [
            shape_of((span, narrow), BF16),
            shape_of((e, span), BF16),
            shape_of((span, heads * rows), BF16),
        ]
        + pull_outs,
        pull_flops * 5 // 4,
        span * heads * rows * 2,
        16,
        in_specs=[smem] + [vmem] * (WIN_DEVS + 5),
    )(block.reshape(1), *earlier, kv, qt, go, aot, norms)
    packed, marks = [], []
    chain_shape = shape_of((parts, size, wide), BF16)
    for step in range(3):
        if step:
            score, own, lhs, row, *terms = local_call(
                functools.partial(next_body, heads, parts, scale, step == 1),
                pull_outs[:2]
                + [shape_of((parts, rows, size), BF16), shape_of((EXTRA, rows), F32)]
                + [chain_shape] * (step == 1)
                + pull_outs[2:],
                pull_flops + 2 * rows * parts * size * wide,
                span * heads * rows * 2 + parts * size * wide * 2,
                16,
                in_specs=[smem] + [vmem] * (len(ahead) + parts + 6 + len(chain)),
            )(spot, *ahead, *every_msg, inv, nt, qt, aot, kvw, probs, *chain)
            packed += [lhs, row]
            if step == 1:
                chain, *terms = terms
                chain = [chain]
        if step == 0:
            every_cols, _ = lax.optimization_barrier((every_cols, score))
            share = local_call(
                chain_body,
                shape_of((parts * cols, wide), BF16),
                2 * parts * cols * width * wide,
                2 * width * (wide + parts * cols),
                8,
            )(every_cols.reshape(parts * cols, width), scaled)
            share = share.reshape(parts, cols, wide)
            *terms, share = lax.optimization_barrier((*terms, share))
            pairs = [(i, i ^ (group // 2)) for i in range(seq_count)]
            near = [share[None], lax.ppermute(share[None], "seq", pairs)]
        every_msg, msg, ahead = exchange(score, own, terms, step > 0, step)
        if step == 0:
            chain = doubled(near, "seq", group // 2, (msg, every_msg[1:2]))
        marks.append(dict(msg=msg, sent=(ahead[1:], every_msg[1:])))
        if step == 1:
            gates = (marks[0]["msg"], marks[0]["sent"], marks[1]["sent"])
            part = width // parts
            mine = lax.dynamic_slice_in_dim(every_cols, head * part, part, 2)
            weight = doubled([mine[None]], "seq", group, gates)

    small = seq_count * parts <= 64
    fields, totals = local_call(
        functools.partial(field_body, parts, wide),
        [
            shape_of((3, rows, part), F32),
            shape_of((seq_count * parts if small else 1, 8, 128), F32),
        ],
        6 * rows * parts * size * part,
        2 * parts * size * part,
        20,
        in_specs=[smem] + [vmem] * (2 * parts + 8 + len(weight)),
        scratch_shapes=[
            pltpu.VMEM((parts, rows, size), BF16),
            pltpu.VMEM((parts, size, part), BF16),
        ],
    )(spot, *ahead, *every_msg, *packed, *weight, fixed_point, upstream, gain, inv)
    if small:
        totals = lax.all_to_all(totals, ("seq", "head"), 0, 0)
    else:
        totals = lax.psum(totals, ("seq", "head"))
    mixed = local_call(
        functools.partial(mix_body, rows * seq_count * width),
        shape_of((rows, part), BF16),
        8 * rows * part,
        18 * rows * part,
        6,
        in_specs=[smem] + [vmem] * 3,
    )(spot, totals, upstream, fields)
    every_mixed = rotated(mixed, "head")
    return local_call(
        join_body,
        shape_of((rows, width), F32),
        0,
        6 * rows * width,
        6,
        in_specs=[smem] + [vmem] * parts,
        out_specs=hbm,
        scratch_shapes=[
            pltpu.VMEM((parts, rows, part), F32),
            pltpu.SemaphoreType.DMA((parts,)),
        ],
    )(spot, *every_mixed)


def solution(mesh):
    in_specs = (
        P("seq", None),
        P("seq", None),
        P(),
        P(None, "head"),
        P(None, "head"),
        P("head", None),
        P("head", "seq"),
        P("seq", "head"),
    )
    out_specs = P("seq", None)
    return jax.shard_map(shards, mesh=mesh, in_specs=in_specs, out_specs=out_specs, check_vma=False)
```

```python
import functools

import jax
import jax.numpy as jnp
from jax import lax
from jax.experimental import pallas as pl
from jax.experimental.pallas import tpu as pltpu
from jax.sharding import PartitionSpec as P

WIN_DEVS = 4
norm_eps = 1e-05
mix_eps = 1e-06
F32 = jnp.float32
BF16 = jnp.bfloat16
COLLECT = 50000
EXTRA = 16
NT = (((1,), (1,)), ((), ()))


def shape_of(shape, dtype):
    return jax.ShapeDtypeStruct(shape, dtype)


def local_call(body, outs, flops, moved, room, **more):
    return pl.pallas_call(
        body,
        out_shape=outs,
        compiler_params=pltpu.CompilerParams(vmem_limit_bytes=room * 1024 * 1024),
        cost_estimate=pl.CostEstimate(flops=flops, bytes_accessed=moved, transcendentals=0),
        **more,
    )


def shifted(value, axis, steps):
    count = lax.axis_size(axis)
    initial, last = (max(0, -steps), min(count, count - steps))
    return lax.ppermute(value, axis, [(source, source + steps) for source in range(initial, last)])


def rotated(value, axis):
    count = lax.axis_size(axis)
    parts = [value]
    for step in range(1, count):
        parts.append(lax.ppermute(value, axis, [(i, (i - step) % count) for i in range(count)]))
    return parts


def doubled(value, axis, group, gates):
    count = lax.axis_size(axis)
    near, bit = list(value), group // 2
    for gate in gates:
        near = list(lax.optimization_barrier((tuple(near), gate))[0])
        pairs = [(i, i ^ bit) for i in range(count)]
        if len(near) > 1:
            near = [jnp.concatenate(near)]
        if bit == 1:
            return near + [lax.ppermute(near[0], axis, pairs)]
        near.append(lax.ppermute(near[0], axis, pairs))
        bit //= 2


def assemble(place, wide, out_ref, refs):
    group = sum(ref.shape[0] for ref in refs)
    cut = wide // group
    rest_cut = refs[0].shape[2] - cut
    entries = [(ref, j) for ref in refs for j in range(ref.shape[0])]
    for j, (ref, at) in enumerate(entries):
        distance, bit, rest = 0, group // 2, j
        while rest:
            distance += bit * (rest & 1)
            rest >>= 1
            bit //= 2
        index = lax.bitwise_xor(place, jnp.int32(distance))
        first = pl.multiple_of(index * cut, cut)
        second = pl.multiple_of(wide + index * rest_cut, rest_cut)
        for k in range(out_ref.shape[0]):
            out_ref[k, pl.ds(first, cut), :] = ref[at, k, :cut, :]
            out_ref[k, pl.ds(second, rest_cut), :] = ref[at, k, cut:, :]


def prep_body(block_ref, qw_ref, kvw_ref, z_ref, gain_ref, cols_ref, hidden_ref, kv_ref, kvf_ref,
              inv_ref, q_tile, kv_tile, z_tile, gain_tile, sems):
    tile = q_tile.shape[1]
    wide, narrow = qw_ref.shape[1], kvw_ref.shape[1]
    group = (wide + narrow) // cols_ref.shape[0]
    place = lax.rem(block_ref[0], group)
    q_take, kv_take = wide // group, narrow // group
    q_at = place * q_take
    q_first = pl.multiple_of(q_at // tile * tile, tile)
    copies = [
        pltpu.make_async_copy(qw_ref.at[:, pl.ds(q_first, tile)], q_tile, sems.at[0]),
        pltpu.make_async_copy(kvw_ref, kv_tile, sems.at[1]),
        pltpu.make_async_copy(z_ref, z_tile, sems.at[2]),
        pltpu.make_async_copy(gain_ref, gain_tile, sems.at[3]),
    ]
    for copy in copies:
        copy.start()
    first = 0
    for copy, ref, at, take in (
        (copies[0], q_tile, q_at - q_first, q_take),
        (copies[1], kv_tile, place * kv_take, kv_take),
    ):
        copy.wait()
        total = ref.shape[1]
        row = lax.broadcasted_iota(jnp.int32, (take, total), 0) + at
        pick = (row == lax.broadcasted_iota(jnp.int32, (take, total), 1)).astype(BF16)
        cols = lax.dot_general(pick, ref[...], NT, preferred_element_type=F32)
        cols_ref[first : first + take, :] = cols.astype(BF16)
        first += take
    copies[2].wait()
    copies[3].wait()
    z = z_tile[...].astype(F32)
    inverse = lax.rsqrt(jnp.mean(z * z, axis=1, keepdims=True) + norm_eps)
    hidden = (z * inverse * gain_tile[...]).astype(BF16)
    hidden_ref[...] = hidden
    kvf = jnp.dot(hidden, kv_tile[...], preferred_element_type=F32)
    kvf_ref[...] = kvf
    kv_ref[...] = kvf.astype(BF16)
    inv_ref[...] = jnp.broadcast_to(inverse, inv_ref.shape)


def chain_body(cols_ref, scaled_ref, out_ref):
    share = lax.dot_general(cols_ref[...], scaled_ref[...], NT, preferred_element_type=F32)
    out_ref[...] = share.astype(BF16)


def lanes_of(value, heads):
    size = value.shape[0] // heads
    return jnp.concatenate([value[i * size : (i + 1) * size] for i in range(heads)], axis=1)


def start_body(heads, hidden_ref, inv_ref, qw_ref, ow_ref, up_ref, z_ref, ao_ref, gain_ref, ln_ref,
               qf_ref, qt_ref, go_ref, nt_ref, aot_ref, scaled_ref, norms_ref,
               ow_tile, up_tile, z_tile, ao_tile, gain_tile, sems):
    copies = [
        pltpu.make_async_copy(source, target, sems.at[i])
        for i, (source, target) in enumerate(
            ((ow_ref, ow_tile), (up_ref, up_tile), (z_ref, z_tile), (ao_ref, ao_tile),
             (gain_ref, gain_tile), (ln_ref, norms_ref))
        )
    ]
    for copy in copies:
        copy.start()
    qf = jnp.dot(hidden_ref[...], qw_ref[...], preferred_element_type=F32)
    qf_ref[...] = qf
    qt_ref[...] = lanes_of(qf.T, heads).astype(BF16)
    for copy in copies:
        copy.wait()
    weight = ow_tile[...]
    out = lax.dot_general(up_tile[...], weight, NT, preferred_element_type=F32)
    go_ref[...] = lanes_of(out.T, heads)
    base = lax.dot_general(z_tile[...], weight, NT, preferred_element_type=F32)
    nt_ref[...] = lanes_of((base * inv_ref[:, :1]).T, heads)
    scaled_ref[...] = (weight.astype(F32) * gain_tile[...]).astype(BF16)
    aot_ref[...] = lanes_of(ao_tile[...].astype(F32).T, heads)


def pull(heads, scale, go, aot, qt, kvw_ref, probs, score_ref, own_ref, term_refs):
    e = go.shape[0]
    rows = go.shape[1] // heads
    row_terms = jnp.sum(go * aot, axis=0, keepdims=True)
    gob = go.astype(BF16)
    grad_prob = jnp.dot(kvw_ref[:, e:], gob, preferred_element_type=F32)
    grad_score = (probs.astype(F32) * (grad_prob - row_terms)).astype(BF16)
    score_ref[...] = grad_score
    grad_key = lax.dot_general(grad_score, qt, NT, preferred_element_type=F32) * scale
    grad_value = lax.dot_general(probs, gob, NT, preferred_element_type=F32)
    terms = jnp.concatenate([grad_key, grad_value], axis=1)
    for offset in range(1, len(term_refs) + 1):
        first = (len(term_refs) - offset) * rows
        term_refs[offset - 1][...] = terms[first : first + rows].astype(BF16)
    own_ref[...] = terms[len(term_refs) * rows :]


def query_body(heads, scale, kt_ref, score_ref, gq_ref):
    rows = gq_ref.shape[0]
    grad_query = jnp.dot(kt_ref[...], score_ref[...], preferred_element_type=F32) * scale
    parts = [grad_query[:, i * rows : (i + 1) * rows] for i in range(heads)]
    gq_ref[...] = jnp.concatenate(parts, axis=0).T.astype(BF16)


def first_body(heads, scale, block_ref, *refs):
    windows = refs[: WIN_DEVS + 1]
    qt_ref, go_ref, aot_ref, ln_ref = refs[WIN_DEVS + 1 : WIN_DEVS + 5]
    kvw_ref, kt_ref, probs_ref, score_ref, own_ref = refs[WIN_DEVS + 5 : WIN_DEVS + 10]
    term_refs = refs[WIN_DEVS + 10 :]
    rows = windows[0].shape[0]
    for place, ref in enumerate(windows):
        kvw_ref[place * rows : (place + 1) * rows, :] = ref[...]
    kvw = kvw_ref[...]
    e = kvw.shape[1] // 2
    kt_ref[...] = kvw.astype(F32).T[:e].astype(BF16)
    scores = jnp.dot(kvw[:, :e], qt_ref[...], preferred_element_type=F32) * scale
    norms = jnp.concatenate([ln_ref[i : i + 1, :] for i in range(heads)], axis=1)
    key_pos = lax.broadcasted_iota(jnp.int32, scores.shape, 0)
    query_pos = lax.broadcasted_iota(jnp.int32, scores.shape, 1) & (rows - 1)
    allowed = (key_pos > query_pos) & (key_pos <= query_pos + WIN_DEVS * rows)
    allowed = allowed & (key_pos >= (WIN_DEVS - block_ref[0]) * rows)
    probs = jnp.where(allowed, jnp.exp(scores - norms), 0.0).astype(BF16)
    probs_ref[...] = probs
    pull(heads, scale, go_ref[...], aot_ref[...], qt_ref[...], kvw_ref, probs,
         score_ref, own_ref, term_refs)


def next_body(heads, parts, scale, fresh, spot_ref, *refs):
    gq_refs, refs = ([], refs) if fresh else (refs[:parts], refs[parts:])
    msg_refs, refs = refs[:parts], refs[parts:]
    inv_ref, nt_ref, qt_ref, aot_ref, kvw_ref, probs_ref, *refs = refs
    if fresh:
        *parts_refs, score_ref, own_ref, lhs_ref, row_ref, chain_ref = refs[:7]
        term_refs = refs[7:]
        assemble(spot_ref[1], chain_ref.shape[2], chain_ref, parts_refs)
    else:
        chain_ref, score_ref, own_ref, lhs_ref, row_ref = refs[:5]
        term_refs = refs[5:]
    rows, wide = lhs_ref.shape[1], chain_ref.shape[2]
    out = jnp.zeros((rows, wide), F32)
    along = jnp.zeros((EXTRA, rows), F32)
    for k in range(parts):
        index = lax.rem(spot_ref[0] + k, parts)
        msg = msg_refs[k][...]
        chain = chain_ref[k]
        lhs = msg[:rows]
        if gq_refs:
            lhs = jnp.concatenate([gq_refs[k][...], lhs], axis=1)
        out += jnp.dot(lhs, chain, preferred_element_type=F32)
        lhs_ref[index] = lhs
        along += msg[rows:, :rows].astype(F32)
    row_ref[...] = along
    along = jnp.sum(along, axis=0, keepdims=True)
    along = jnp.concatenate([along] * heads, axis=1)
    go = lanes_of((out * inv_ref[:, :1]).T, heads)
    inv_row = jnp.concatenate([inv_ref[...].T[:1, :]] * heads, axis=1)
    go = go - inv_row * along * nt_ref[...]
    pull(heads, scale, go, aot_ref[...], qt_ref[...], kvw_ref, probs_ref[...],
         score_ref, own_ref, term_refs)


def collect_body(width, own_ref, gq_ref, qf_ref, kvf_ref, *refs):
    msg_ref = refs[-1]
    rows = own_ref.shape[0]
    total = own_ref[...]
    for ref in refs[:-1]:
        total += ref[...].astype(F32)
    total = total.astype(BF16)
    ahead = msg_ref.shape[1] - total.shape[1]
    if ahead:
        msg_ref[:rows, :ahead] = gq_ref[...]
        msg_ref[rows:, :] = jnp.zeros((EXTRA, msg_ref.shape[1]), BF16)
    msg_ref[:rows, ahead:] = total
    prods = gq_ref[...].astype(F32) * qf_ref[...]
    partial = total.astype(F32) * kvf_ref[...]
    lanes = partial.shape[1]
    for first in range(0, prods.shape[1], lanes):
        partial += prods[:, first : first + lanes]
    along = jnp.sum(partial.T, axis=0, keepdims=True) * (1.0 / width)
    high = along.astype(BF16).astype(F32)
    place = lax.broadcasted_iota(jnp.int32, (EXTRA, rows), 0)
    extra = jnp.where(place == 0, high, jnp.where(place == 1, along - high, 0.0))
    msg_ref[rows:, :rows] = extra.astype(BF16)


def field_body(parts, wide, spot_ref, *refs):
    gq_refs, msg_refs, refs = refs[:parts], refs[parts : 2 * parts], refs[2 * parts :]
    lhs1_ref, row1_ref, lhs2_ref, row2_ref, *refs = refs
    *w_refs, z_ref, up_ref, gain_ref, inv_ref, v_ref, tot_ref, lhs3_ref, w_ref = refs
    rows, part = v_ref.shape[1:]
    head = spot_ref[0]
    row3 = jnp.zeros((EXTRA, rows), F32)
    for k in range(parts):
        msg = msg_refs[k][...]
        lhs3_ref[lax.rem(head + k, parts)] = jnp.concatenate(
            [gq_refs[k][...], msg[:rows]], axis=1
        )
        row3 += msg[rows:].astype(F32)
    assemble(spot_ref[1], wide, w_ref, w_refs)
    y = jnp.zeros((3 * rows, part), F32)
    for k in range(parts):
        lhs = jnp.concatenate([lhs1_ref[k], lhs2_ref[k], lhs3_ref[k]], axis=0)
        weight = w_ref[lax.rem(k - head + parts, parts)]
        y += jnp.dot(lhs, weight, preferred_element_type=F32)
    at = pl.ds(pl.multiple_of(head * part, part), part)
    inverse = inv_ref[:, :1]
    normed = z_ref[:, at].astype(F32) * inverse
    gain = gain_ref[:, at]
    fields = []
    for step, row in enumerate((row1_ref[...], row2_ref[...], row3)):
        along = jnp.broadcast_to(jnp.sum(row, axis=0, keepdims=True), (rows, rows)).T[:, :1]
        y_step = y[step * rows : (step + 1) * rows]
        fields.append(inverse * (y_step * gain - normed * along))
        v_ref[step] = fields[step]
    first, second, third = fields
    change1 = first - up_ref[:, at].astype(F32)
    change2 = second - first
    change3 = third - second
    pairs = [
        (change1, first), (change1, change1), (change2, first), (change2, change2),
        (change2, second), (change2, change3), (change3, second), (change3, change3),
    ]
    lanes = tot_ref.shape[2]
    sums = []
    for a, b in pairs:
        total = jnp.sum(a * b, axis=0, keepdims=True)
        sums.append(sum(total[:, i : i + lanes] for i in range(0, part, lanes)))
    totals = jnp.concatenate(sums, axis=0)
    for k in range(tot_ref.shape[0]):
        tot_ref[k] = totals


def mix_body(entries, spot_ref, tot_ref, up_ref, v_ref, out_ref):
    totals = jnp.sum(jnp.sum(tot_ref[...], axis=0), axis=1, keepdims=True) / entries
    s_r1, s_s, d2_v1, d2_d2, d2_v2, d2_d3, d3_v2, d3_d3 = [totals[i : i + 1] for i in range(8)]
    mix1 = s_r1 / (s_s + mix_eps)
    keep1 = 1.0 - mix1
    mix2 = keep1 * (d2_v1 + keep1 * d2_d2) / (keep1 * keep1 * d2_d2 + mix_eps)
    keep2 = keep1 * (1.0 - mix2)
    cross = mix1 * (d2_v2 + keep2 * d2_d3) + keep2 * (d3_v2 + keep2 * d3_d3)
    square = mix1 * mix1 * d2_d2 + 2.0 * mix1 * keep2 * d2_d3 + keep2 * keep2 * d3_d3
    mix3 = cross / (square + mix_eps)
    part = out_ref.shape[1]
    at = pl.ds(pl.multiple_of(spot_ref[0] * part, part), part)
    mixed = (
        up_ref[:, at].astype(F32)
        + v_ref[0]
        + (1.0 - mix3 * mix1) * v_ref[1]
        + keep2 * (1.0 - mix3) * v_ref[2]
    )
    out_ref[...] = mixed.astype(BF16)


def join_body(spot_ref, *refs):
    *part_refs, out_ref, tile, sems = refs
    parts = len(part_refs)
    part = part_refs[0].shape[1]
    copies = []
    for k in range(parts):
        tile[k] = part_refs[k][...].astype(F32)
        first = pl.multiple_of(lax.rem(spot_ref[0] + k, parts) * part, part)
        copies.append(
            pltpu.make_async_copy(tile.at[k], out_ref.at[:, pl.ds(first, part)], sems.at[k])
        )
        copies[k].start()
    for copy in copies:
        copy.wait()


def shards(
    fixed_point,
    upstream,
    norm_gain,
    query_weight,
    keyval_weight,
    output_weight,
    log_norm,
    attention_out,
):
    rows, width = fixed_point.shape
    wide = query_weight.shape[1]
    narrow = keyval_weight.shape[1]
    size = wide + narrow
    e = narrow // 2
    heads = log_norm.shape[0]
    seq_count = lax.axis_size("seq")
    parts = lax.axis_size("head")
    block = lax.axis_index("seq")
    head = lax.axis_index("head")
    scale = e ** (-0.5)
    gain = norm_gain.reshape(1, width)
    span = (WIN_DEVS + 1) * rows
    group = min(8, seq_count)

    cols = size // group
    spot = jnp.stack([head, lax.rem(block, group)])
    smem = pl.BlockSpec(memory_space=pltpu.SMEM)
    vmem = pl.BlockSpec(memory_space=pltpu.VMEM)
    hbm = pl.BlockSpec(memory_space=pltpu.HBM)

    def pinned(value):
        return pltpu.with_memory_space_constraint(value, pltpu.HBM)

    tile = 128 if wide % 128 == 0 and 128 % (wide // group) == 0 else wide
    own_cols, hidden, kv, kvf, inv = local_call(
        prep_body,
        [
            shape_of((cols, width), BF16),
            shape_of((rows, width), BF16),
            shape_of((rows, narrow), BF16),
            shape_of((rows, narrow), F32),
            shape_of((rows, rows), F32),
        ],
        2 * width * size * cols,
        2 * width * (tile + narrow + rows),
        10,
        in_specs=[smem] + [hbm] * 4,
        scratch_shapes=[
            pltpu.VMEM((width, tile), BF16),
            pltpu.VMEM((width, narrow), BF16),
            pltpu.VMEM((rows, width), BF16),
            pltpu.VMEM((1, width), F32),
            pltpu.SemaphoreType.DMA((4,)),
        ],
    )(
        block.reshape(1),
        pinned(query_weight),
        pinned(keyval_weight),
        pinned(fixed_point),
        pinned(gain),
    )
    every_cols = jnp.stack(rotated(own_cols, "head"))
    earlier = [shifted(kv, "seq", offset) for offset in range(WIN_DEVS, 0, -1)]

    qf, qt, go, nt, aot, scaled, norms = local_call(
        functools.partial(start_body, heads),
        [
            shape_of((rows, wide), F32),
            shape_of((e, heads * rows), BF16),
            shape_of((e, heads * rows), F32),
            shape_of((e, heads * rows), F32),
            shape_of((e, heads * rows), F32),
            shape_of((wide, width), BF16),
            shape_of((heads, rows), F32),
        ],
        6 * rows * width * wide,
        4 * width * (2 * rows + wide),
        14,
        in_specs=[vmem] * 3 + [hbm] * 6,
        scratch_shapes=[
            pltpu.VMEM((wide, width), BF16),
            pltpu.VMEM((rows, width), BF16),
            pltpu.VMEM((rows, width), BF16),
            pltpu.VMEM((rows, wide), BF16),
            pltpu.VMEM((1, width), F32),
            pltpu.SemaphoreType.DMA((6,)),
        ],
    )(
        hidden,
        inv,
        query_weight,
        pinned(output_weight),
        pinned(upstream),
        pinned(fixed_point),
        pinned(attention_out),
        pinned(gain),
        pinned(log_norm),
    )

    pull_outs = [shape_of((span, heads * rows), BF16), shape_of((rows, narrow), F32)]
    pull_outs += [shape_of((rows, narrow), BF16)] * WIN_DEVS
    pull_flops = 6 * span * e * heads * rows

    def exchange(score, own, terms, split, step):
        if step == 2:
            score, weight[:] = (lambda a, *b: (a, list(b)))(
                *lax.optimization_barrier((score, *weight))
            )
        gq = local_call(
            functools.partial(query_body, heads, scale),
            shape_of((rows, wide), BF16),
            2 * span * e * heads * rows,
            span * heads * rows * 2,
            4,
        )(kt, score)
        arrived = [shifted(term, "seq", -offset - 1) for offset, term in enumerate(terms)]
        ahead = rotated(gq, "head") if split else []
        if step in (2,):
            arrived = list(lax.optimization_barrier((tuple(arrived), tuple(ahead[1:1+2])))[0])
        if not split:
            arrived = list(lax.optimization_barrier((tuple(arrived), near[1]))[0])
        msg = local_call(
            functools.partial(collect_body, width),
            shape_of((rows + EXTRA, narrow if split else size), BF16),
            COLLECT * rows * size,
            rows * size * 4,
            4,
        )(own, gq, qf, kvf, *arrived)
        return rotated(msg, "head"), msg, ahead

    kvw, kt, probs, score, own, *terms = local_call(
        functools.partial(first_body, heads, scale),
        [
            shape_of((span, narrow), BF16),
            shape_of((e, span), BF16),
            shape_of((span, heads * rows), BF16),
        ]
        + pull_outs,
        pull_flops * 5 // 4,
        span * heads * rows * 2,
        16,
        in_specs=[smem] + [vmem] * (WIN_DEVS + 5),
    )(block.reshape(1), *earlier, kv, qt, go, aot, norms)
    packed, marks = [], []
    chain_shape = shape_of((parts, size, wide), BF16)
    for step in range(3):
        if step:
            score, own, lhs, row, *terms = local_call(
                functools.partial(next_body, heads, parts, scale, step == 1),
                pull_outs[:2]
                + [shape_of((parts, rows, size), BF16), shape_of((EXTRA, rows), F32)]
                + [chain_shape] * (step == 1)
                + pull_outs[2:],
                pull_flops + 2 * rows * parts * size * wide,
                span * heads * rows * 2 + parts * size * wide * 2,
                16,
                in_specs=[smem] + [vmem] * (len(ahead) + parts + 6 + len(chain)),
            )(spot, *ahead, *every_msg, inv, nt, qt, aot, kvw, probs, *chain)
            packed += [lhs, row]
            if step == 1:
                chain, *terms = terms
                chain = [chain]
        if step == 0:
            every_cols, _ = lax.optimization_barrier((every_cols, score))
            share = local_call(
                chain_body,
                shape_of((parts * cols, wide), BF16),
                2 * parts * cols * width * wide,
                2 * width * (wide + parts * cols),
                8,
            )(every_cols.reshape(parts * cols, width), scaled)
            share = share.reshape(parts, cols, wide)
            *terms, share = lax.optimization_barrier((*terms, share))
            pairs = [(i, i ^ (group // 2)) for i in range(seq_count)]
            near = [share[None], lax.ppermute(share[None], "seq", pairs)]
        every_msg, msg, ahead = exchange(score, own, terms, step > 0, step)
        if step == 0:
            chain = doubled(near, "seq", group // 2, (msg, every_msg[1:2]))
        marks.append(dict(msg=msg, sent=(ahead[1:], every_msg[1:])))
        if step == 1:
            gates = (marks[0]["msg"], marks[0]["sent"], marks[1]["sent"])
            part = width // parts
            mine = lax.dynamic_slice_in_dim(every_cols, head * part, part, 2)
            weight = doubled([mine[None]], "seq", group, gates)

    small = seq_count * parts <= 64
    fields, totals = local_call(
        functools.partial(field_body, parts, wide),
        [
            shape_of((3, rows, part), F32),
            shape_of((seq_count * parts if small else 1, 8, 128), F32),
        ],
        6 * rows * parts * size * part,
        2 * parts * size * part,
        20,
        in_specs=[smem] + [vmem] * (2 * parts + 8 + len(weight)),
        scratch_shapes=[
            pltpu.VMEM((parts, rows, size), BF16),
            pltpu.VMEM((parts, size, part), BF16),
        ],
    )(spot, *ahead, *every_msg, *packed, *weight, fixed_point, upstream, gain, inv)
    if small:
        totals = lax.all_to_all(totals, ("seq", "head"), 0, 0)
    else:
        totals = lax.psum(totals, ("seq", "head"))
    mixed = local_call(
        functools.partial(mix_body, rows * seq_count * width),
        shape_of((rows, part), BF16),
        8 * rows * part,
        18 * rows * part,
        6,
        in_specs=[smem] + [vmem] * 3,
    )(spot, totals, upstream, fields)
    every_mixed = rotated(mixed, "head")
    return local_call(
        join_body,
        shape_of((rows, width), F32),
        0,
        6 * rows * width,
        6,
        in_specs=[smem] + [vmem] * parts,
        out_specs=hbm,
        scratch_shapes=[
            pltpu.VMEM((parts, rows, part), F32),
            pltpu.SemaphoreType.DMA((parts,)),
        ],
    )(spot, *every_mixed)


def solution(mesh):
    in_specs = (
        P("seq", None),
        P("seq", None),
        P(),
        P(None, "head"),
        P(None, "head"),
        P("head", None),
        P("head", "seq"),
        P("seq", "head"),
    )
    out_specs = P("seq", None)
    return jax.shard_map(shards, mesh=mesh, in_specs=in_specs, out_specs=out_specs, check_vma=False)
```

```python
import functools

import jax
import jax.numpy as jnp
from jax import lax
from jax.experimental import pallas as pl
from jax.experimental.pallas import tpu as pltpu
from jax.sharding import PartitionSpec as P

WIN_DEVS = 4
norm_eps = 1e-05
mix_eps = 1e-06
F32 = jnp.float32
BF16 = jnp.bfloat16
COLLECT = 50000
EXTRA = 16
NT = (((1,), (1,)), ((), ()))


def shape_of(shape, dtype):
    return jax.ShapeDtypeStruct(shape, dtype)


def local_call(body, outs, flops, moved, room, **more):
    return pl.pallas_call(
        body,
        out_shape=outs,
        compiler_params=pltpu.CompilerParams(vmem_limit_bytes=room * 1024 * 1024),
        cost_estimate=pl.CostEstimate(flops=flops, bytes_accessed=moved, transcendentals=0),
        **more,
    )


def shifted(value, axis, steps):
    count = lax.axis_size(axis)
    initial, last = (max(0, -steps), min(count, count - steps))
    return lax.ppermute(value, axis, [(source, source + steps) for source in range(initial, last)])


def rotated(value, axis):
    count = lax.axis_size(axis)
    parts = [value]
    for step in range(1, count):
        parts.append(lax.ppermute(value, axis, [(i, (i - step) % count) for i in range(count)]))
    return parts


def doubled(value, axis, group, gates):
    count = lax.axis_size(axis)
    near, bit = list(value), group // 2
    for gate in gates:
        near = list(lax.optimization_barrier((tuple(near), gate))[0])
        pairs = [(i, i ^ bit) for i in range(count)]
        if len(near) > 1:
            near = [jnp.concatenate(near)]
        if bit == 1:
            return near + [lax.ppermute(near[0], axis, pairs)]
        near.append(lax.ppermute(near[0], axis, pairs))
        bit //= 2


def assemble(place, wide, out_ref, refs):
    group = sum(ref.shape[0] for ref in refs)
    cut = wide // group
    rest_cut = refs[0].shape[2] - cut
    entries = [(ref, j) for ref in refs for j in range(ref.shape[0])]
    for j, (ref, at) in enumerate(entries):
        distance, bit, rest = 0, group // 2, j
        while rest:
            distance += bit * (rest & 1)
            rest >>= 1
            bit //= 2
        index = lax.bitwise_xor(place, jnp.int32(distance))
        first = pl.multiple_of(index * cut, cut)
        second = pl.multiple_of(wide + index * rest_cut, rest_cut)
        for k in range(out_ref.shape[0]):
            out_ref[k, pl.ds(first, cut), :] = ref[at, k, :cut, :]
            out_ref[k, pl.ds(second, rest_cut), :] = ref[at, k, cut:, :]


def prep_body(block_ref, qw_ref, kvw_ref, z_ref, gain_ref, cols_ref, hidden_ref, kv_ref, kvf_ref,
              inv_ref, q_tile, kv_tile, z_tile, gain_tile, sems):
    tile = q_tile.shape[1]
    wide, narrow = qw_ref.shape[1], kvw_ref.shape[1]
    group = (wide + narrow) // cols_ref.shape[0]
    place = lax.rem(block_ref[0], group)
    q_take, kv_take = wide // group, narrow // group
    q_at = place * q_take
    q_first = pl.multiple_of(q_at // tile * tile, tile)
    copies = [
        pltpu.make_async_copy(qw_ref.at[:, pl.ds(q_first, tile)], q_tile, sems.at[0]),
        pltpu.make_async_copy(kvw_ref, kv_tile, sems.at[1]),
        pltpu.make_async_copy(z_ref, z_tile, sems.at[2]),
        pltpu.make_async_copy(gain_ref, gain_tile, sems.at[3]),
    ]
    for copy in copies:
        copy.start()
    first = 0
    for copy, ref, at, take in (
        (copies[0], q_tile, q_at - q_first, q_take),
        (copies[1], kv_tile, place * kv_take, kv_take),
    ):
        copy.wait()
        total = ref.shape[1]
        row = lax.broadcasted_iota(jnp.int32, (take, total), 0) + at
        pick = (row == lax.broadcasted_iota(jnp.int32, (take, total), 1)).astype(BF16)
        cols = lax.dot_general(pick, ref[...], NT, preferred_element_type=F32)
        cols_ref[first : first + take, :] = cols.astype(BF16)
        first += take
    copies[2].wait()
    copies[3].wait()
    z = z_tile[...].astype(F32)
    inverse = lax.rsqrt(jnp.mean(z * z, axis=1, keepdims=True) + norm_eps)
    hidden = (z * inverse * gain_tile[...]).astype(BF16)
    hidden_ref[...] = hidden
    kvf = jnp.dot(hidden, kv_tile[...], preferred_element_type=F32)
    kvf_ref[...] = kvf
    kv_ref[...] = kvf.astype(BF16)
    inv_ref[...] = jnp.broadcast_to(inverse, inv_ref.shape)


def chain_body(cols_ref, scaled_ref, out_ref):
    share = lax.dot_general(cols_ref[...], scaled_ref[...], NT, preferred_element_type=F32)
    out_ref[...] = share.astype(BF16)


def lanes_of(value, heads):
    size = value.shape[0] // heads
    return jnp.concatenate([value[i * size : (i + 1) * size] for i in range(heads)], axis=1)


def start_body(heads, hidden_ref, inv_ref, qw_ref, ow_ref, up_ref, z_ref, ao_ref, gain_ref, ln_ref,
               qf_ref, qt_ref, go_ref, nt_ref, aot_ref, scaled_ref, norms_ref,
               ow_tile, up_tile, z_tile, ao_tile, gain_tile, sems):
    copies = [
        pltpu.make_async_copy(source, target, sems.at[i])
        for i, (source, target) in enumerate(
            ((ow_ref, ow_tile), (up_ref, up_tile), (z_ref, z_tile), (ao_ref, ao_tile),
             (gain_ref, gain_tile), (ln_ref, norms_ref))
        )
    ]
    for copy in copies:
        copy.start()
    qf = jnp.dot(hidden_ref[...], qw_ref[...], preferred_element_type=F32)
    qf_ref[...] = qf
    qt_ref[...] = lanes_of(qf.T, heads).astype(BF16)
    for copy in copies:
        copy.wait()
    weight = ow_tile[...]
    out = lax.dot_general(up_tile[...], weight, NT, preferred_element_type=F32)
    go_ref[...] = lanes_of(out.T, heads)
    base = lax.dot_general(z_tile[...], weight, NT, preferred_element_type=F32)
    nt_ref[...] = lanes_of((base * inv_ref[:, :1]).T, heads)
    scaled_ref[...] = (weight.astype(F32) * gain_tile[...]).astype(BF16)
    aot_ref[...] = lanes_of(ao_tile[...].astype(F32).T, heads)


def pull(heads, scale, go, aot, qt, kvw_ref, probs, score_ref, own_ref, term_refs):
    e = go.shape[0]
    rows = go.shape[1] // heads
    row_terms = jnp.sum(go * aot, axis=0, keepdims=True)
    gob = go.astype(BF16)
    grad_prob = jnp.dot(kvw_ref[:, e:], gob, preferred_element_type=F32)
    grad_score = (probs.astype(F32) * (grad_prob - row_terms)).astype(BF16)
    score_ref[...] = grad_score
    grad_key = lax.dot_general(grad_score, qt, NT, preferred_element_type=F32) * scale
    grad_value = lax.dot_general(probs, gob, NT, preferred_element_type=F32)
    terms = jnp.concatenate([grad_key, grad_value], axis=1)
    for offset in range(1, len(term_refs) + 1):
        first = (len(term_refs) - offset) * rows
        term_refs[offset - 1][...] = terms[first : first + rows].astype(BF16)
    own_ref[...] = terms[len(term_refs) * rows :]


def query_body(heads, scale, kt_ref, score_ref, gq_ref):
    rows = gq_ref.shape[0]
    grad_query = jnp.dot(kt_ref[...], score_ref[...], preferred_element_type=F32) * scale
    parts = [grad_query[:, i * rows : (i + 1) * rows] for i in range(heads)]
    gq_ref[...] = jnp.concatenate(parts, axis=0).T.astype(BF16)


def first_body(heads, scale, block_ref, *refs):
    windows = refs[: WIN_DEVS + 1]
    qt_ref, go_ref, aot_ref, ln_ref = refs[WIN_DEVS + 1 : WIN_DEVS + 5]
    kvw_ref, kt_ref, probs_ref, score_ref, own_ref = refs[WIN_DEVS + 5 : WIN_DEVS + 10]
    term_refs = refs[WIN_DEVS + 10 :]
    rows = windows[0].shape[0]
    for place, ref in enumerate(windows):
        kvw_ref[place * rows : (place + 1) * rows, :] = ref[...]
    kvw = kvw_ref[...]
    e = kvw.shape[1] // 2
    kt_ref[...] = kvw.astype(F32).T[:e].astype(BF16)
    scores = jnp.dot(kvw[:, :e], qt_ref[...], preferred_element_type=F32) * scale
    norms = jnp.concatenate([ln_ref[i : i + 1, :] for i in range(heads)], axis=1)
    key_pos = lax.broadcasted_iota(jnp.int32, scores.shape, 0)
    query_pos = lax.broadcasted_iota(jnp.int32, scores.shape, 1) & (rows - 1)
    allowed = (key_pos > query_pos) & (key_pos <= query_pos + WIN_DEVS * rows)
    allowed = allowed & (key_pos >= (WIN_DEVS - block_ref[0]) * rows)
    probs = jnp.where(allowed, jnp.exp(scores - norms), 0.0).astype(BF16)
    probs_ref[...] = probs
    pull(heads, scale, go_ref[...], aot_ref[...], qt_ref[...], kvw_ref, probs,
         score_ref, own_ref, term_refs)


def next_body(heads, parts, scale, fresh, spot_ref, *refs):
    gq_refs, refs = ([], refs) if fresh else (refs[:parts], refs[parts:])
    msg_refs, refs = refs[:parts], refs[parts:]
    inv_ref, nt_ref, qt_ref, aot_ref, kvw_ref, probs_ref, *refs = refs
    if fresh:
        *parts_refs, score_ref, own_ref, lhs_ref, row_ref, chain_ref = refs[:7]
        term_refs = refs[7:]
        assemble(spot_ref[1], chain_ref.shape[2], chain_ref, parts_refs)
    else:
        chain_ref, score_ref, own_ref, lhs_ref, row_ref = refs[:5]
        term_refs = refs[5:]
    rows, wide = lhs_ref.shape[1], chain_ref.shape[2]
    out = jnp.zeros((rows, wide), F32)
    along = jnp.zeros((EXTRA, rows), F32)
    for k in range(parts):
        index = lax.rem(spot_ref[0] + k, parts)
        msg = msg_refs[k][...]
        chain = chain_ref[k]
        lhs = msg[:rows]
        if gq_refs:
            lhs = jnp.concatenate([gq_refs[k][...], lhs], axis=1)
        out += jnp.dot(lhs, chain, preferred_element_type=F32)
        lhs_ref[index] = lhs
        along += msg[rows:, :rows].astype(F32)
    row_ref[...] = along
    along = jnp.sum(along, axis=0, keepdims=True)
    along = jnp.concatenate([along] * heads, axis=1)
    go = lanes_of((out * inv_ref[:, :1]).T, heads)
    inv_row = jnp.concatenate([inv_ref[...].T[:1, :]] * heads, axis=1)
    go = go - inv_row * along * nt_ref[...]
    pull(heads, scale, go, aot_ref[...], qt_ref[...], kvw_ref, probs_ref[...],
         score_ref, own_ref, term_refs)


def collect_body(width, own_ref, gq_ref, qf_ref, kvf_ref, *refs):
    msg_ref = refs[-1]
    rows = own_ref.shape[0]
    total = own_ref[...]
    for ref in refs[:-1]:
        total += ref[...].astype(F32)
    total = total.astype(BF16)
    ahead = msg_ref.shape[1] - total.shape[1]
    if ahead:
        msg_ref[:rows, :ahead] = gq_ref[...]
        msg_ref[rows:, :] = jnp.zeros((EXTRA, msg_ref.shape[1]), BF16)
    msg_ref[:rows, ahead:] = total
    prods = gq_ref[...].astype(F32) * qf_ref[...]
    partial = total.astype(F32) * kvf_ref[...]
    lanes = partial.shape[1]
    for first in range(0, prods.shape[1], lanes):
        partial += prods[:, first : first + lanes]
    along = jnp.sum(partial.T, axis=0, keepdims=True) * (1.0 / width)
    high = along.astype(BF16).astype(F32)
    place = lax.broadcasted_iota(jnp.int32, (EXTRA, rows), 0)
    extra = jnp.where(place == 0, high, jnp.where(place == 1, along - high, 0.0))
    msg_ref[rows:, :rows] = extra.astype(BF16)


def field_body(parts, wide, spot_ref, *refs):
    gq_refs, msg_refs, refs = refs[:parts], refs[parts : 2 * parts], refs[2 * parts :]
    lhs1_ref, row1_ref, lhs2_ref, row2_ref, *refs = refs
    *w_refs, z_ref, up_ref, gain_ref, inv_ref, v_ref, tot_ref, lhs3_ref, w_ref = refs
    rows, part = v_ref.shape[1:]
    head = spot_ref[0]
    row3 = jnp.zeros((EXTRA, rows), F32)
    for k in range(parts):
        msg = msg_refs[k][...]
        lhs3_ref[lax.rem(head + k, parts)] = jnp.concatenate(
            [gq_refs[k][...], msg[:rows]], axis=1
        )
        row3 += msg[rows:].astype(F32)
    assemble(spot_ref[1], wide, w_ref, w_refs)
    y = jnp.zeros((3 * rows, part), F32)
    for k in range(parts):
        lhs = jnp.concatenate([lhs1_ref[k], lhs2_ref[k], lhs3_ref[k]], axis=0)
        weight = w_ref[lax.rem(k - head + parts, parts)]
        y += jnp.dot(lhs, weight, preferred_element_type=F32)
    at = pl.ds(pl.multiple_of(head * part, part), part)
    inverse = inv_ref[:, :1]
    normed = z_ref[:, at].astype(F32) * inverse
    gain = gain_ref[:, at]
    fields = []
    for step, row in enumerate((row1_ref[...], row2_ref[...], row3)):
        along = jnp.broadcast_to(jnp.sum(row, axis=0, keepdims=True), (rows, rows)).T[:, :1]
        y_step = y[step * rows : (step + 1) * rows]
        fields.append(inverse * (y_step * gain - normed * along))
        v_ref[step] = fields[step]
    first, second, third = fields
    change1 = first - up_ref[:, at].astype(F32)
    change2 = second - first
    change3 = third - second
    pairs = [
        (change1, first), (change1, change1), (change2, first), (change2, change2),
        (change2, second), (change2, change3), (change3, second), (change3, change3),
    ]
    lanes = tot_ref.shape[2]
    sums = []
    for a, b in pairs:
        total = jnp.sum(a * b, axis=0, keepdims=True)
        sums.append(sum(total[:, i : i + lanes] for i in range(0, part, lanes)))
    totals = jnp.concatenate(sums, axis=0)
    for k in range(tot_ref.shape[0]):
        tot_ref[k] = totals


def mix_body(entries, spot_ref, tot_ref, up_ref, v_ref, out_ref):
    totals = jnp.sum(jnp.sum(tot_ref[...], axis=0), axis=1, keepdims=True) / entries
    s_r1, s_s, d2_v1, d2_d2, d2_v2, d2_d3, d3_v2, d3_d3 = [totals[i : i + 1] for i in range(8)]
    mix1 = s_r1 / (s_s + mix_eps)
    keep1 = 1.0 - mix1
    mix2 = keep1 * (d2_v1 + keep1 * d2_d2) / (keep1 * keep1 * d2_d2 + mix_eps)
    keep2 = keep1 * (1.0 - mix2)
    cross = mix1 * (d2_v2 + keep2 * d2_d3) + keep2 * (d3_v2 + keep2 * d3_d3)
    square = mix1 * mix1 * d2_d2 + 2.0 * mix1 * keep2 * d2_d3 + keep2 * keep2 * d3_d3
    mix3 = cross / (square + mix_eps)
    part = out_ref.shape[1]
    at = pl.ds(pl.multiple_of(spot_ref[0] * part, part), part)
    mixed = (
        up_ref[:, at].astype(F32)
        + v_ref[0]
        + (1.0 - mix3 * mix1) * v_ref[1]
        + keep2 * (1.0 - mix3) * v_ref[2]
    )
    out_ref[...] = mixed.astype(BF16)


def join_body(spot_ref, *refs):
    *part_refs, out_ref, tile, sems = refs
    parts = len(part_refs)
    part = part_refs[0].shape[1]
    copies = []
    for k in range(parts):
        tile[k] = part_refs[k][...].astype(F32)
        first = pl.multiple_of(lax.rem(spot_ref[0] + k, parts) * part, part)
        copies.append(
            pltpu.make_async_copy(tile.at[k], out_ref.at[:, pl.ds(first, part)], sems.at[k])
        )
        copies[k].start()
    for copy in copies:
        copy.wait()


def shards(
    fixed_point,
    upstream,
    norm_gain,
    query_weight,
    keyval_weight,
    output_weight,
    log_norm,
    attention_out,
):
    rows, width = fixed_point.shape
    wide = query_weight.shape[1]
    narrow = keyval_weight.shape[1]
    size = wide + narrow
    e = narrow // 2
    heads = log_norm.shape[0]
    seq_count = lax.axis_size("seq")
    parts = lax.axis_size("head")
    block = lax.axis_index("seq")
    head = lax.axis_index("head")
    scale = e ** (-0.5)
    gain = norm_gain.reshape(1, width)
    span = (WIN_DEVS + 1) * rows
    group = min(8, seq_count)

    cols = size // group
    spot = jnp.stack([head, lax.rem(block, group)])
    smem = pl.BlockSpec(memory_space=pltpu.SMEM)
    vmem = pl.BlockSpec(memory_space=pltpu.VMEM)
    hbm = pl.BlockSpec(memory_space=pltpu.HBM)

    def pinned(value):
        return pltpu.with_memory_space_constraint(value, pltpu.HBM)

    tile = 128 if wide % 128 == 0 and 128 % (wide // group) == 0 else wide
    own_cols, hidden, kv, kvf, inv = local_call(
        prep_body,
        [
            shape_of((cols, width), BF16),
            shape_of((rows, width), BF16),
            shape_of((rows, narrow), BF16),
            shape_of((rows, narrow), F32),
            shape_of((rows, rows), F32),
        ],
        2 * width * size * cols,
        2 * width * (tile + narrow + rows),
        10,
        in_specs=[smem] + [hbm] * 4,
        scratch_shapes=[
            pltpu.VMEM((width, tile), BF16),
            pltpu.VMEM((width, narrow), BF16),
            pltpu.VMEM((rows, width), BF16),
            pltpu.VMEM((1, width), F32),
            pltpu.SemaphoreType.DMA((4,)),
        ],
    )(
        block.reshape(1),
        pinned(query_weight),
        pinned(keyval_weight),
        pinned(fixed_point),
        pinned(gain),
    )
    every_cols = jnp.stack(rotated(own_cols, "head"))
    earlier = [shifted(kv, "seq", offset) for offset in range(WIN_DEVS, 0, -1)]

    qf, qt, go, nt, aot, scaled, norms = local_call(
        functools.partial(start_body, heads),
        [
            shape_of((rows, wide), F32),
            shape_of((e, heads * rows), BF16),
            shape_of((e, heads * rows), F32),
            shape_of((e, heads * rows), F32),
            shape_of((e, heads * rows), F32),
            shape_of((wide, width), BF16),
            shape_of((heads, rows), F32),
        ],
        6 * rows * width * wide,
        4 * width * (2 * rows + wide),
        14,
        in_specs=[vmem] * 3 + [hbm] * 6,
        scratch_shapes=[
            pltpu.VMEM((wide, width), BF16),
            pltpu.VMEM((rows, width), BF16),
            pltpu.VMEM((rows, width), BF16),
            pltpu.VMEM((rows, wide), BF16),
            pltpu.VMEM((1, width), F32),
            pltpu.SemaphoreType.DMA((6,)),
        ],
    )(
        hidden,
        inv,
        query_weight,
        pinned(output_weight),
        pinned(upstream),
        pinned(fixed_point),
        pinned(attention_out),
        pinned(gain),
        pinned(log_norm),
    )

    pull_outs = [shape_of((span, heads * rows), BF16), shape_of((rows, narrow), F32)]
    pull_outs += [shape_of((rows, narrow), BF16)] * WIN_DEVS
    pull_flops = 6 * span * e * heads * rows

    def exchange(score, own, terms, split, step):
        if step == 2:
            score, weight[:] = (lambda a, *b: (a, list(b)))(
                *lax.optimization_barrier((score, *weight))
            )
        gq = local_call(
            functools.partial(query_body, heads, scale),
            shape_of((rows, wide), BF16),
            2 * span * e * heads * rows,
            span * heads * rows * 2,
            4,
        )(kt, score)
        arrived = [shifted(term, "seq", -offset - 1) for offset, term in enumerate(terms)]
        ahead = rotated(gq, "head") if split else []
        if step:
            arrived = list(lax.optimization_barrier((tuple(arrived), tuple(ahead[1 : 1 + (2 if step == 2 else 1)])))[0])
        if not split:
            arrived = list(lax.optimization_barrier((tuple(arrived), near[1]))[0])
        msg = local_call(
            functools.partial(collect_body, width),
            shape_of((rows + EXTRA, narrow if split else size), BF16),
            COLLECT * rows * size,
            rows * size * 4,
            4,
        )(own, gq, qf, kvf, *arrived)
        return rotated(msg, "head"), msg, ahead

    kvw, kt, probs, score, own, *terms = local_call(
        functools.partial(first_body, heads, scale),
        [
            shape_of((span, narrow), BF16),
            shape_of((e, span), BF16),
            shape_of((span, heads * rows), BF16),
        ]
        + pull_outs,
        pull_flops * 5 // 4,
        span * heads * rows * 2,
        16,
        in_specs=[smem] + [vmem] * (WIN_DEVS + 5),
    )(block.reshape(1), *earlier, kv, qt, go, aot, norms)
    packed, marks = [], []
    chain_shape = shape_of((parts, size, wide), BF16)
    for step in range(3):
        if step:
            score, own, lhs, row, *terms = local_call(
                functools.partial(next_body, heads, parts, scale, step == 1),
                pull_outs[:2]
                + [shape_of((parts, rows, size), BF16), shape_of((EXTRA, rows), F32)]
                + [chain_shape] * (step == 1)
                + pull_outs[2:],
                pull_flops + 2 * rows * parts * size * wide,
                span * heads * rows * 2 + parts * size * wide * 2,
                16,
                in_specs=[smem] + [vmem] * (len(ahead) + parts + 6 + len(chain)),
            )(spot, *ahead, *every_msg, inv, nt, qt, aot, kvw, probs, *chain)
            packed += [lhs, row]
            if step == 1:
                chain, *terms = terms
                chain = [chain]
        if step == 0:
            every_cols, _ = lax.optimization_barrier((every_cols, score))
            share = local_call(
                chain_body,
                shape_of((parts * cols, wide), BF16),
                2 * parts * cols * width * wide,
                2 * width * (wide + parts * cols),
                8,
            )(every_cols.reshape(parts * cols, width), scaled)
            share = share.reshape(parts, cols, wide)
            *terms, share = lax.optimization_barrier((*terms, share))
            pairs = [(i, i ^ (group // 2)) for i in range(seq_count)]
            near = [share[None], lax.ppermute(share[None], "seq", pairs)]
        every_msg, msg, ahead = exchange(score, own, terms, step > 0, step)
        if step == 0:
            chain = doubled(near, "seq", group // 2, (msg, every_msg[1:2]))
        marks.append(dict(msg=msg, sent=(ahead[1:], every_msg[1:])))
        if step == 1:
            gates = (marks[0]["msg"], marks[0]["sent"], marks[1]["sent"])
            part = width // parts
            mine = lax.dynamic_slice_in_dim(every_cols, head * part, part, 2)
            weight = doubled([mine[None]], "seq", group, gates)

    small = seq_count * parts <= 64
    fields, totals = local_call(
        functools.partial(field_body, parts, wide),
        [
            shape_of((3, rows, part), F32),
            shape_of((seq_count * parts if small else 1, 8, 128), F32),
        ],
        6 * rows * parts * size * part,
        2 * parts * size * part,
        20,
        in_specs=[smem] + [vmem] * (2 * parts + 8 + len(weight)),
        scratch_shapes=[
            pltpu.VMEM((parts, rows, size), BF16),
            pltpu.VMEM((parts, size, part), BF16),
        ],
    )(spot, *ahead, *every_msg, *packed, *weight, fixed_point, upstream, gain, inv)
    if small:
        totals = lax.all_to_all(totals, ("seq", "head"), 0, 0)
    else:
        totals = lax.psum(totals, ("seq", "head"))
    mixed = local_call(
        functools.partial(mix_body, rows * seq_count * width),
        shape_of((rows, part), BF16),
        8 * rows * part,
        18 * rows * part,
        6,
        in_specs=[smem] + [vmem] * 3,
    )(spot, totals, upstream, fields)
    every_mixed = rotated(mixed, "head")
    return local_call(
        join_body,
        shape_of((rows, width), F32),
        0,
        6 * rows * width,
        6,
        in_specs=[smem] + [vmem] * parts,
        out_specs=hbm,
        scratch_shapes=[
            pltpu.VMEM((parts, rows, part), F32),
            pltpu.SemaphoreType.DMA((parts,)),
        ],
    )(spot, *every_mixed)


def solution(mesh):
    in_specs = (
        P("seq", None),
        P("seq", None),
        P(),
        P(None, "head"),
        P(None, "head"),
        P("head", None),
        P("head", "seq"),
        P("seq", "head"),
    )
    out_specs = P("seq", None)
    return jax.shard_map(shards, mesh=mesh, in_specs=in_specs, out_specs=out_specs, check_vma=False)
```

```python
import functools

import jax
import jax.numpy as jnp
from jax import lax
from jax.experimental import pallas as pl
from jax.experimental.pallas import tpu as pltpu
from jax.sharding import PartitionSpec as P

WIN_DEVS = 4
norm_eps = 1e-05
mix_eps = 1e-06
F32 = jnp.float32
BF16 = jnp.bfloat16
COLLECT = 50000
EXTRA = 16
NT = (((1,), (1,)), ((), ()))


def shape_of(shape, dtype):
    return jax.ShapeDtypeStruct(shape, dtype)


def local_call(body, outs, flops, moved, room, **more):
    return pl.pallas_call(
        body,
        out_shape=outs,
        compiler_params=pltpu.CompilerParams(vmem_limit_bytes=room * 1024 * 1024),
        cost_estimate=pl.CostEstimate(flops=flops, bytes_accessed=moved, transcendentals=0),
        **more,
    )


def shifted(value, axis, steps):
    count = lax.axis_size(axis)
    initial, last = (max(0, -steps), min(count, count - steps))
    return lax.ppermute(value, axis, [(source, source + steps) for source in range(initial, last)])


def rotated(value, axis):
    count = lax.axis_size(axis)
    parts = [value]
    for step in range(1, count):
        parts.append(lax.ppermute(value, axis, [(i, (i - step) % count) for i in range(count)]))
    return parts


def doubled(value, axis, group, gates):
    count = lax.axis_size(axis)
    near, bit = list(value), group // 2
    for gate in gates:
        near = list(lax.optimization_barrier((tuple(near), gate))[0])
        pairs = [(i, i ^ bit) for i in range(count)]
        if len(near) > 1:
            near = [jnp.concatenate(near)]
        if bit == 1:
            return near + [lax.ppermute(near[0], axis, pairs)]
        near.append(lax.ppermute(near[0], axis, pairs))
        bit //= 2


def assemble(place, wide, out_ref, refs):
    group = sum(ref.shape[0] for ref in refs)
    cut = wide // group
    rest_cut = refs[0].shape[2] - cut
    entries = [(ref, j) for ref in refs for j in range(ref.shape[0])]
    for j, (ref, at) in enumerate(entries):
        distance, bit, rest = 0, group // 2, j
        while rest:
            distance += bit * (rest & 1)
            rest >>= 1
            bit //= 2
        index = lax.bitwise_xor(place, jnp.int32(distance))
        first = pl.multiple_of(index * cut, cut)
        second = pl.multiple_of(wide + index * rest_cut, rest_cut)
        for k in range(out_ref.shape[0]):
            out_ref[k, pl.ds(first, cut), :] = ref[at, k, :cut, :]
            out_ref[k, pl.ds(second, rest_cut), :] = ref[at, k, cut:, :]


def prep_body(block_ref, qw_ref, kvw_ref, z_ref, gain_ref, cols_ref, hidden_ref, kv_ref, kvf_ref,
              inv_ref, q_tile, kv_tile, z_tile, gain_tile, sems):
    tile = q_tile.shape[1]
    wide, narrow = qw_ref.shape[1], kvw_ref.shape[1]
    group = (wide + narrow) // cols_ref.shape[0]
    place = lax.rem(block_ref[0], group)
    q_take, kv_take = wide // group, narrow // group
    q_at = place * q_take
    q_first = pl.multiple_of(q_at // tile * tile, tile)
    copies = [
        pltpu.make_async_copy(qw_ref.at[:, pl.ds(q_first, tile)], q_tile, sems.at[0]),
        pltpu.make_async_copy(kvw_ref, kv_tile, sems.at[1]),
        pltpu.make_async_copy(z_ref, z_tile, sems.at[2]),
        pltpu.make_async_copy(gain_ref, gain_tile, sems.at[3]),
    ]
    for copy in copies:
        copy.start()
    first = 0
    for copy, ref, at, take in (
        (copies[0], q_tile, q_at - q_first, q_take),
        (copies[1], kv_tile, place * kv_take, kv_take),
    ):
        copy.wait()
        total = ref.shape[1]
        row = lax.broadcasted_iota(jnp.int32, (take, total), 0) + at
        pick = (row == lax.broadcasted_iota(jnp.int32, (take, total), 1)).astype(BF16)
        cols = lax.dot_general(pick, ref[...], NT, preferred_element_type=F32)
        cols_ref[first : first + take, :] = cols.astype(BF16)
        first += take
    copies[2].wait()
    copies[3].wait()
    z = z_tile[...].astype(F32)
    inverse = lax.rsqrt(jnp.mean(z * z, axis=1, keepdims=True) + norm_eps)
    hidden = (z * inverse * gain_tile[...]).astype(BF16)
    hidden_ref[...] = hidden
    kvf = jnp.dot(hidden, kv_tile[...], preferred_element_type=F32)
    kvf_ref[...] = kvf
    kv_ref[...] = kvf.astype(BF16)
    inv_ref[...] = jnp.broadcast_to(inverse, inv_ref.shape)


def chain_body(cols_ref, scaled_ref, out_ref):
    share = lax.dot_general(cols_ref[...], scaled_ref[...], NT, preferred_element_type=F32)
    out_ref[...] = share.astype(BF16)


def lanes_of(value, heads):
    size = value.shape[0] // heads
    return jnp.concatenate([value[i * size : (i + 1) * size] for i in range(heads)], axis=1)


def start_body(heads, hidden_ref, inv_ref, qw_ref, ow_ref, up_ref, z_ref, ao_ref, gain_ref, ln_ref,
               qf_ref, qt_ref, go_ref, nt_ref, aot_ref, scaled_ref, norms_ref,
               ow_tile, up_tile, z_tile, ao_tile, gain_tile, sems):
    copies = [
        pltpu.make_async_copy(source, target, sems.at[i])
        for i, (source, target) in enumerate(
            ((ow_ref, ow_tile), (up_ref, up_tile), (z_ref, z_tile), (ao_ref, ao_tile),
             (gain_ref, gain_tile), (ln_ref, norms_ref))
        )
    ]
    for copy in copies:
        copy.start()
    qf = jnp.dot(hidden_ref[...], qw_ref[...], preferred_element_type=F32)
    qf_ref[...] = qf
    qt_ref[...] = lanes_of(qf.T, heads).astype(BF16)
    for copy in copies:
        copy.wait()
    weight = ow_tile[...]
    out = lax.dot_general(up_tile[...], weight, NT, preferred_element_type=F32)
    go_ref[...] = lanes_of(out.T, heads)
    base = lax.dot_general(z_tile[...], weight, NT, preferred_element_type=F32)
    nt_ref[...] = lanes_of((base * inv_ref[:, :1]).T, heads)
    scaled_ref[...] = (weight.astype(F32) * gain_tile[...]).astype(BF16)
    aot_ref[...] = lanes_of(ao_tile[...].astype(F32).T, heads)


def pull(heads, scale, go, aot, qt, kvw_ref, probs, score_ref, own_ref, term_refs):
    e = go.shape[0]
    rows = go.shape[1] // heads
    row_terms = jnp.sum(go * aot, axis=0, keepdims=True)
    gob = go.astype(BF16)
    grad_prob = jnp.dot(kvw_ref[:, e:], gob, preferred_element_type=F32)
    grad_score = (probs.astype(F32) * (grad_prob - row_terms)).astype(BF16)
    score_ref[...] = grad_score
    grad_key = lax.dot_general(grad_score, qt, NT, preferred_element_type=F32) * scale
    grad_value = lax.dot_general(probs, gob, NT, preferred_element_type=F32)
    terms = jnp.concatenate([grad_key, grad_value], axis=1)
    for offset in range(1, len(term_refs) + 1):
        first = (len(term_refs) - offset) * rows
        term_refs[offset - 1][...] = terms[first : first + rows].astype(BF16)
    own_ref[...] = terms[len(term_refs) * rows :]


def query_body(heads, scale, kt_ref, score_ref, gq_ref):
    rows = gq_ref.shape[0]
    grad_query = jnp.dot(kt_ref[...], score_ref[...], preferred_element_type=F32) * scale
    parts = [grad_query[:, i * rows : (i + 1) * rows] for i in range(heads)]
    gq_ref[...] = jnp.concatenate(parts, axis=0).T.astype(BF16)


def first_body(heads, scale, block_ref, *refs):
    windows = refs[: WIN_DEVS + 1]
    qt_ref, go_ref, aot_ref, ln_ref = refs[WIN_DEVS + 1 : WIN_DEVS + 5]
    kvw_ref, kt_ref, probs_ref, score_ref, own_ref = refs[WIN_DEVS + 5 : WIN_DEVS + 10]
    term_refs = refs[WIN_DEVS + 10 :]
    rows = windows[0].shape[0]
    for place, ref in enumerate(windows):
        kvw_ref[place * rows : (place + 1) * rows, :] = ref[...]
    kvw = kvw_ref[...]
    e = kvw.shape[1] // 2
    kt_ref[...] = kvw.astype(F32).T[:e].astype(BF16)
    scores = jnp.dot(kvw[:, :e], qt_ref[...], preferred_element_type=F32) * scale
    norms = jnp.concatenate([ln_ref[i : i + 1, :] for i in range(heads)], axis=1)
    key_pos = lax.broadcasted_iota(jnp.int32, scores.shape, 0)
    query_pos = lax.broadcasted_iota(jnp.int32, scores.shape, 1) & (rows - 1)
    allowed = (key_pos > query_pos) & (key_pos <= query_pos + WIN_DEVS * rows)
    allowed = allowed & (key_pos >= (WIN_DEVS - block_ref[0]) * rows)
    probs = jnp.where(allowed, jnp.exp(scores - norms), 0.0).astype(BF16)
    probs_ref[...] = probs
    pull(heads, scale, go_ref[...], aot_ref[...], qt_ref[...], kvw_ref, probs,
         score_ref, own_ref, term_refs)


def next_body(heads, parts, scale, fresh, spot_ref, *refs):
    gq_refs, refs = ([], refs) if fresh else (refs[:parts], refs[parts:])
    msg_refs, refs = refs[:parts], refs[parts:]
    inv_ref, nt_ref, qt_ref, aot_ref, kvw_ref, probs_ref, *refs = refs
    if fresh:
        *parts_refs, score_ref, own_ref, lhs_ref, row_ref, chain_ref = refs[:7]
        term_refs = refs[7:]
        assemble(spot_ref[1], chain_ref.shape[2], chain_ref, parts_refs)
    else:
        chain_ref, score_ref, own_ref, lhs_ref, row_ref = refs[:5]
        term_refs = refs[5:]
    rows, wide = lhs_ref.shape[1], chain_ref.shape[2]
    out = jnp.zeros((rows, wide), F32)
    along = jnp.zeros((EXTRA, rows), F32)
    for k in range(parts):
        index = lax.rem(spot_ref[0] + k, parts)
        msg = msg_refs[k][...]
        chain = chain_ref[k]
        lhs = msg[:rows]
        if gq_refs:
            lhs = jnp.concatenate([gq_refs[k][...], lhs], axis=1)
        out += jnp.dot(lhs, chain, preferred_element_type=F32)
        lhs_ref[index] = lhs
        along += msg[rows:, :rows].astype(F32)
    row_ref[...] = along
    along = jnp.sum(along, axis=0, keepdims=True)
    along = jnp.concatenate([along] * heads, axis=1)
    go = lanes_of((out * inv_ref[:, :1]).T, heads)
    inv_row = jnp.concatenate([inv_ref[...].T[:1, :]] * heads, axis=1)
    go = go - inv_row * along * nt_ref[...]
    pull(heads, scale, go, aot_ref[...], qt_ref[...], kvw_ref, probs_ref[...],
         score_ref, own_ref, term_refs)


def collect_body(width, own_ref, gq_ref, qf_ref, kvf_ref, *refs):
    msg_ref = refs[-1]
    rows = own_ref.shape[0]
    total = own_ref[...]
    for ref in refs[:-1]:
        total += ref[...].astype(F32)
    total = total.astype(BF16)
    ahead = msg_ref.shape[1] - total.shape[1]
    if ahead:
        msg_ref[:rows, :ahead] = gq_ref[...]
        msg_ref[rows:, :] = jnp.zeros((EXTRA, msg_ref.shape[1]), BF16)
    msg_ref[:rows, ahead:] = total
    prods = gq_ref[...].astype(F32) * qf_ref[...]
    partial = total.astype(F32) * kvf_ref[...]
    lanes = partial.shape[1]
    for first in range(0, prods.shape[1], lanes):
        partial += prods[:, first : first + lanes]
    along = jnp.sum(partial.T, axis=0, keepdims=True) * (1.0 / width)
    high = along.astype(BF16).astype(F32)
    place = lax.broadcasted_iota(jnp.int32, (EXTRA, rows), 0)
    extra = jnp.where(place == 0, high, jnp.where(place == 1, along - high, 0.0))
    msg_ref[rows:, :rows] = extra.astype(BF16)


def field_body(parts, wide, spot_ref, *refs):
    gq_refs, msg_refs, refs = refs[:parts], refs[parts : 2 * parts], refs[2 * parts :]
    lhs1_ref, row1_ref, lhs2_ref, row2_ref, *refs = refs
    *w_refs, z_ref, up_ref, gain_ref, inv_ref, v_ref, tot_ref, lhs3_ref, w_ref = refs
    rows, part = v_ref.shape[1:]
    head = spot_ref[0]
    row3 = jnp.zeros((EXTRA, rows), F32)
    for k in range(parts):
        msg = msg_refs[k][...]
        lhs3_ref[lax.rem(head + k, parts)] = jnp.concatenate(
            [gq_refs[k][...], msg[:rows]], axis=1
        )
        row3 += msg[rows:].astype(F32)
    assemble(spot_ref[1], wide, w_ref, w_refs)
    y = jnp.zeros((3 * rows, part), F32)
    for k in range(parts):
        lhs = jnp.concatenate([lhs1_ref[k], lhs2_ref[k], lhs3_ref[k]], axis=0)
        weight = w_ref[lax.rem(k - head + parts, parts)]
        y += jnp.dot(lhs, weight, preferred_element_type=F32)
    at = pl.ds(pl.multiple_of(head * part, part), part)
    inverse = inv_ref[:, :1]
    normed = z_ref[:, at].astype(F32) * inverse
    gain = gain_ref[:, at]
    fields = []
    for step, row in enumerate((row1_ref[...], row2_ref[...], row3)):
        along = jnp.broadcast_to(jnp.sum(row, axis=0, keepdims=True), (rows, rows)).T[:, :1]
        y_step = y[step * rows : (step + 1) * rows]
        fields.append(inverse * (y_step * gain - normed * along))
        v_ref[step] = fields[step]
    first, second, third = fields
    change1 = first - up_ref[:, at].astype(F32)
    change2 = second - first
    change3 = third - second
    pairs = [
        (change1, first), (change1, change1), (change2, first), (change2, change2),
        (change2, second), (change2, change3), (change3, second), (change3, change3),
    ]
    lanes = tot_ref.shape[2]
    sums = []
    for a, b in pairs:
        total = jnp.sum(a * b, axis=0, keepdims=True)
        sums.append(sum(total[:, i : i + lanes] for i in range(0, part, lanes)))
    totals = jnp.concatenate(sums, axis=0)
    for k in range(tot_ref.shape[0]):
        tot_ref[k] = totals


def mix_body(entries, spot_ref, tot_ref, up_ref, v_ref, out_ref):
    totals = jnp.sum(jnp.sum(tot_ref[...], axis=0), axis=1, keepdims=True) / entries
    s_r1, s_s, d2_v1, d2_d2, d2_v2, d2_d3, d3_v2, d3_d3 = [totals[i : i + 1] for i in range(8)]
    mix1 = s_r1 / (s_s + mix_eps)
    keep1 = 1.0 - mix1
    mix2 = keep1 * (d2_v1 + keep1 * d2_d2) / (keep1 * keep1 * d2_d2 + mix_eps)
    keep2 = keep1 * (1.0 - mix2)
    cross = mix1 * (d2_v2 + keep2 * d2_d3) + keep2 * (d3_v2 + keep2 * d3_d3)
    square = mix1 * mix1 * d2_d2 + 2.0 * mix1 * keep2 * d2_d3 + keep2 * keep2 * d3_d3
    mix3 = cross / (square + mix_eps)
    part = out_ref.shape[1]
    at = pl.ds(pl.multiple_of(spot_ref[0] * part, part), part)
    mixed = (
        up_ref[:, at].astype(F32)
        + v_ref[0]
        + (1.0 - mix3 * mix1) * v_ref[1]
        + keep2 * (1.0 - mix3) * v_ref[2]
    )
    out_ref[...] = mixed.astype(BF16)


def join_body(spot_ref, *refs):
    *part_refs, out_ref, tile, sems = refs
    parts = len(part_refs)
    part = part_refs[0].shape[1]
    copies = []
    for k in range(parts):
        tile[k] = part_refs[k][...].astype(F32)
        first = pl.multiple_of(lax.rem(spot_ref[0] + k, parts) * part, part)
        copies.append(
            pltpu.make_async_copy(tile.at[k], out_ref.at[:, pl.ds(first, part)], sems.at[k])
        )
        copies[k].start()
    for copy in copies:
        copy.wait()


def shards(
    fixed_point,
    upstream,
    norm_gain,
    query_weight,
    keyval_weight,
    output_weight,
    log_norm,
    attention_out,
):
    rows, width = fixed_point.shape
    wide = query_weight.shape[1]
    narrow = keyval_weight.shape[1]
    size = wide + narrow
    e = narrow // 2
    heads = log_norm.shape[0]
    seq_count = lax.axis_size("seq")
    parts = lax.axis_size("head")
    block = lax.axis_index("seq")
    head = lax.axis_index("head")
    scale = e ** (-0.5)
    gain = norm_gain.reshape(1, width)
    span = (WIN_DEVS + 1) * rows
    group = min(8, seq_count)

    cols = size // group
    spot = jnp.stack([head, lax.rem(block, group)])
    smem = pl.BlockSpec(memory_space=pltpu.SMEM)
    vmem = pl.BlockSpec(memory_space=pltpu.VMEM)
    hbm = pl.BlockSpec(memory_space=pltpu.HBM)

    def pinned(value):
        return pltpu.with_memory_space_constraint(value, pltpu.HBM)

    tile = 128 if wide % 128 == 0 and 128 % (wide // group) == 0 else wide
    own_cols, hidden, kv, kvf, inv = local_call(
        prep_body,
        [
            shape_of((cols, width), BF16),
            shape_of((rows, width), BF16),
            shape_of((rows, narrow), BF16),
            shape_of((rows, narrow), F32),
            shape_of((rows, rows), F32),
        ],
        2 * width * size * cols,
        2 * width * (tile + narrow + rows),
        10,
        in_specs=[smem] + [hbm] * 4,
        scratch_shapes=[
            pltpu.VMEM((width, tile), BF16),
            pltpu.VMEM((width, narrow), BF16),
            pltpu.VMEM((rows, width), BF16),
            pltpu.VMEM((1, width), F32),
            pltpu.SemaphoreType.DMA((4,)),
        ],
    )(
        block.reshape(1),
        pinned(query_weight),
        pinned(keyval_weight),
        pinned(fixed_point),
        pinned(gain),
    )
    every_cols = jnp.stack(rotated(own_cols, "head"))
    earlier = [shifted(kv, "seq", offset) for offset in range(WIN_DEVS, 0, -1)]

    qf, qt, go, nt, aot, scaled, norms = local_call(
        functools.partial(start_body, heads),
        [
            shape_of((rows, wide), F32),
            shape_of((e, heads * rows), BF16),
            shape_of((e, heads * rows), F32),
            shape_of((e, heads * rows), F32),
            shape_of((e, heads * rows), F32),
            shape_of((wide, width), BF16),
            shape_of((heads, rows), F32),
        ],
        6 * rows * width * wide,
        4 * width * (2 * rows + wide),
        14,
        in_specs=[vmem] * 3 + [hbm] * 6,
        scratch_shapes=[
            pltpu.VMEM((wide, width), BF16),
            pltpu.VMEM((rows, width), BF16),
            pltpu.VMEM((rows, width), BF16),
            pltpu.VMEM((rows, wide), BF16),
            pltpu.VMEM((1, width), F32),
            pltpu.SemaphoreType.DMA((6,)),
        ],
    )(
        hidden,
        inv,
        query_weight,
        pinned(output_weight),
        pinned(upstream),
        pinned(fixed_point),
        pinned(attention_out),
        pinned(gain),
        pinned(log_norm),
    )

    pull_outs = [shape_of((span, heads * rows), BF16), shape_of((rows, narrow), F32)]
    pull_outs += [shape_of((rows, narrow), BF16)] * WIN_DEVS
    pull_flops = 6 * span * e * heads * rows

    def exchange(score, own, terms, split, step):
        if step == 2:
            score, weight[:] = (lambda a, *b: (a, list(b)))(
                *lax.optimization_barrier((score, *weight))
            )
        gq = local_call(
            functools.partial(query_body, heads, scale),
            shape_of((rows, wide), BF16),
            2 * span * e * heads * rows,
            span * heads * rows * 2,
            4,
        )(kt, score)
        arrived = [shifted(term, "seq", -offset - 1) for offset, term in enumerate(terms)]
        ahead = rotated(gq, "head") if split else []
        if step in (2,):
            arrived = list(lax.optimization_barrier((tuple(arrived), tuple(ahead[1:1+1])))[0])
        if not split:
            arrived = list(lax.optimization_barrier((tuple(arrived), near[1]))[0])
        msg = local_call(
            functools.partial(collect_body, width),
            shape_of((rows + EXTRA, narrow if split else size), BF16),
            COLLECT * rows * size,
            rows * size * 4,
            4,
        )(own, gq, qf, kvf, *arrived)
        return rotated(msg, "head"), msg, ahead

    kvw, kt, probs, score, own, *terms = local_call(
        functools.partial(first_body, heads, scale),
        [
            shape_of((span, narrow), BF16),
            shape_of((e, span), BF16),
            shape_of((span, heads * rows), BF16),
        ]
        + pull_outs,
        pull_flops * 5 // 4,
        span * heads * rows * 2,
        16,
        in_specs=[smem] + [vmem] * (WIN_DEVS + 5),
    )(block.reshape(1), *earlier, kv, qt, go, aot, norms)
    packed, marks = [], []
    chain_shape = shape_of((parts, size, wide), BF16)
    for step in range(3):
        if step:
            score, own, lhs, row, *terms = local_call(
                functools.partial(next_body, heads, parts, scale, step == 1),
                pull_outs[:2]
                + [shape_of((parts, rows, size), BF16), shape_of((EXTRA, rows), F32)]
                + [chain_shape] * (step == 1)
                + pull_outs[2:],
                pull_flops + 2 * rows * parts * size * wide,
                span * heads * rows * 2 + parts * size * wide * 2,
                16,
                in_specs=[smem] + [vmem] * (len(ahead) + parts + 6 + len(chain)),
            )(spot, *ahead, *every_msg, inv, nt, qt, aot, kvw, probs, *chain)
            packed += [lhs, row]
            if step == 1:
                chain, *terms = terms
                chain = [chain]
        if step == 0:
            every_cols, _ = lax.optimization_barrier((every_cols, score))
            share = local_call(
                chain_body,
                shape_of((parts * cols, wide), BF16),
                2 * parts * cols * width * wide,
                2 * width * (wide + parts * cols),
                8,
            )(every_cols.reshape(parts * cols, width), scaled)
            share = share.reshape(parts, cols, wide)
            *terms, share = lax.optimization_barrier((*terms, share))
            pairs = [(i, i ^ (group // 2)) for i in range(seq_count)]
            near = [share[None], lax.ppermute(share[None], "seq", pairs)]
        every_msg, msg, ahead = exchange(score, own, terms, step > 0, step)
        if step == 0:
            chain = doubled(near, "seq", group // 2, (msg, every_msg[1:2]))
        marks.append(dict(msg=msg, sent=(ahead[1:], every_msg[1:])))
        if step == 1:
            gates = (marks[0]["msg"], marks[0]["sent"], marks[1]["sent"])
            part = width // parts
            mine = lax.dynamic_slice_in_dim(every_cols, head * part, part, 2)
            weight = doubled([mine[None]], "seq", group, gates)

    small = seq_count * parts <= 64
    fields, totals = local_call(
        functools.partial(field_body, parts, wide),
        [
            shape_of((3, rows, part), F32),
            shape_of((seq_count * parts if small else 1, 8, 128), F32),
        ],
        6 * rows * parts * size * part,
        2 * parts * size * part,
        20,
        in_specs=[smem] + [vmem] * (2 * parts + 8 + len(weight)),
        scratch_shapes=[
            pltpu.VMEM((parts, rows, size), BF16),
            pltpu.VMEM((parts, size, part), BF16),
        ],
    )(spot, *ahead, *every_msg, *packed, *weight, fixed_point, upstream, gain, inv)
    if small:
        totals = lax.all_to_all(totals, ("seq", "head"), 0, 0)
    else:
        totals = lax.psum(totals, ("seq", "head"))
    mixed = local_call(
        functools.partial(mix_body, rows * seq_count * width),
        shape_of((rows, part), BF16),
        8 * rows * part,
        18 * rows * part,
        6,
        in_specs=[smem] + [vmem] * 3,
    )(spot, totals, upstream, fields)
    every_mixed = rotated(mixed, "head")
    return local_call(
        join_body,
        shape_of((rows, width), F32),
        0,
        6 * rows * width,
        6,
        in_specs=[smem] + [vmem] * parts,
        out_specs=hbm,
        scratch_shapes=[
            pltpu.VMEM((parts, rows, part), F32),
            pltpu.SemaphoreType.DMA((parts,)),
        ],
    )(spot, *every_mixed)


def solution(mesh):
    in_specs = (
        P("seq", None),
        P("seq", None),
        P(),
        P(None, "head"),
        P(None, "head"),
        P("head", None),
        P("head", "seq"),
        P("seq", "head"),
    )
    out_specs = P("seq", None)
    return jax.shard_map(shards, mesh=mesh, in_specs=in_specs, out_specs=out_specs, check_vma=False)
```
